32 devices in a mesh: dp: 8 (over y, x, core), mp: 4 (over z).
Axes of the slice: x: 2, y: 2, z: 4, core: 2. Of those that a mesh axis runs over, the one named last changes fastest.
Arguments:
- stream_in: float32 [16384, 512], P(('dp', 'mp')), may hold values from -6 to 6
- segments: int32 [8, 2048], P('dp'), may hold values from 0 to 3, as said below
- norm_gain: float32 [2, 2, 512], replicated, may hold values from 0.1 to 1.9
- norm_bias: float32 [2, 2, 512], replicated, may hold values from -1.8 to 1.8
- w_in: bfloat16 [2, 512, 2, 512], P(None, None, None, 'mp'), may hold values from -0.25 to 0.25
- w_out: bfloat16 [2, 512, 512], P(None, 'mp'), may hold values from -0.5 to 0.5
- sub_kernels: float32 [2, 6, 32, 512], P(None, None, None, 'mp'), may hold values from -6 to 6
- w_up: bfloat16 [2, 512, 2048], P(None, None, 'mp'), may hold values from -0.25 to 0.25
- w_down: bfloat16 [2, 2048, 512], P(None, 'mp'), may hold values from -0.1875 to 0.1875
- cotangent: float32 [16384, 512], P(('dp', 'mp')), may hold values from -6 to 6
Outputs:
- out_stream: float32 [16384, 512], P(('dp', 'mp'))
- grad_stream: float32 [16384, 512], P(('dp', 'mp'))
- grad_norm_gain: float32 [2, 2, 512], replicated
- grad_norm_bias: float32 [2, 2, 512], replicated
- grad_w_in: float32 [2, 512, 2, 512], P(None, None, None, 'mp')
- grad_w_out: float32 [2, 512, 512], P(None, 'mp')
- grad_sub_kernels: float32 [2, 6, 32, 512], P(None, None, None, 'mp')
- grad_w_up: float32 [2, 512, 2048], P(None, None, 'mp')
- grad_w_down: float32 [2, 2048, 512], P(None, 'mp')
The draws below stay inside these ranges and needn't reach their ends.
Inputs may be any that keep to these rules, and one draw needn't show every extreme that they name: `segments`: in each row the document numbers never fall and every number from 0 to 3 occurs, so each row holds 4 whole documents; one of them starts in the row's first quarter and ends in its last quarter.
All inputs are finite; a program needn't handle non-finite values.
Results may differ from the reference program's by a relative error of at most 0.025.
Values may be sent and summed in bfloat16 or wider, within the bound.
A program may use at most 448 MiB of HBM per device.

```python
import jax
import jax.numpy as jnp
from jax import lax

D = 512
FF = 2048
SCALES = 6
TAPS = 32
DOCS = 4
LAYERS = 2
L = 2048
ROWS = 8
TOKENS = 16384


def pick_bounds(base_key, span, offset):

    def one_row(row_key):
        return jnp.sort(jax.random.permutation(row_key, span - 1)[:DOCS - 1])
    return jax.vmap(one_row)(jax.random.split(base_key, ROWS)) + offset


def draw_segments(key, part):
    key = jax.random.fold_in(key, 7)
    wide_left, wide_right, close_left, close_right, pick_key, phase_key = jax.random.split(key, 6)
    quarter = L // 4
    close = 2 * DOCS
    left_wide = pick_bounds(wide_left, quarter, 1)
    right_wide = pick_bounds(wide_right, quarter, 3 * quarter + 1)
    left_close = pick_bounds(close_left, close, 1)
    right_close = pick_bounds(close_right, close, L - close + 1)
    phase = jax.random.randint(phase_key, (), 0, 2)
    tight = ((jnp.arange(ROWS, dtype=jnp.int32) + phase) % 2 == 0)[:, None]
    left_bounds = jnp.where(tight, left_close, left_wide)
    right_bounds = jnp.where(tight, right_close, right_wide)
    crossing = jax.random.randint(pick_key, (ROWS, 1), 0, DOCS)
    boundaries = jnp.where(jnp.arange(DOCS - 1)[None, :] < crossing, left_bounds, right_bounds)
    positions = jnp.arange(L)
    return jnp.sum(positions[None, :, None] >= boundaries[:, None, :], axis=2).astype(jnp.int32)


def draw_sub_kernels(key, part):
    key = jax.random.fold_in(key, 11)
    value_key, pick_key = jax.random.split(key)
    shape = (LAYERS, SCALES, TAPS, D)
    values = jnp.clip(jax.random.normal(value_key, shape, jnp.float32), -6.0, 6.0)
    dominated = jax.random.randint(pick_key, (LAYERS, 1, 1, D), 0, 2) == 1
    levels = jnp.arange(SCALES)[None, :, None, None]
    shrink = jnp.where(dominated & (levels < SCALES - 1), 1.0 / 32.0, 1.0)
    return (values * shrink).astype(jnp.float32)


def steps_of(rng, extent, cuts, least, high):
    gain = 1.0
    for axis_at, parts in cuts:
        draws = jax.random.uniform(jax.random.fold_in(jax.random.fold_in(rng, 6), axis_at), (parts,), jnp.float32, least / len(cuts), high / len(cuts))
        gain = gain * jnp.repeat(jnp.exp(draws), extent[axis_at] // parts).reshape((-1,) + (1,) * (len(extent) - 1 - axis_at))
    return gain


def scatter_about(rng, dims, width, reach, cuts=(), held_as=jnp.bfloat16):
    values = width * jax.random.normal(rng, dims, jnp.float32)
    if cuts:
        values = values * steps_of(rng, dims, cuts, -0.22, 0.18)
    return jnp.clip(values, -reach, reach).astype(held_as)


def setup_inputs(seed: int = 0) -> dict:
    arg_keys = jax.random.split(jax.random.key(seed), 11)
    stream_in = scatter_about(arg_keys[0], (TOKENS, D), 1.0, 6.0, ((0, 32),), jnp.float32)
    segments = draw_segments(jax.random.fold_in(arg_keys[10], 71), 0)
    norm_gain = jnp.clip(1.0 + 0.18 * jax.random.normal(arg_keys[2], (LAYERS, 2, D), jnp.float32), 0.1, 1.9)
    norm_bias = scatter_about(arg_keys[3], (LAYERS, 2, D), 0.3, 1.8, (), jnp.float32)
    w_in = scatter_about(arg_keys[4], (LAYERS, D, 2, D), D ** -0.5, 0.25, ((3, 4),))
    w_out = scatter_about(arg_keys[5], (LAYERS, D, D), (D // 4) ** -0.5, 0.5, ((1, 4),))
    sub_kernels = draw_sub_kernels(jax.random.fold_in(arg_keys[10], 71), 0)
    w_up = scatter_about(arg_keys[7], (LAYERS, D, FF), D ** -0.5, 0.25, ((2, 4),))
    w_down = scatter_about(arg_keys[8], (LAYERS, FF, D), (FF // 2) ** -0.5, 0.1875, ((1, 4),))
    cotangent = scatter_about(arg_keys[9], (TOKENS, D), 1.0, 6.0, ((0, 32),), jnp.float32)
    return {"stream_in": stream_in, "segments": segments, "norm_gain": norm_gain, "norm_bias": norm_bias, "w_in": w_in, "w_out": w_out, "sub_kernels": sub_kernels, "w_up": w_up, "w_down": w_down, "cotangent": cotangent}


@jax.custom_vjp
def low(v):
    return lax.optimization_barrier(v.astype(jnp.bfloat16)).astype(jnp.float32)

@jax.custom_vjp
def low_back(v):
    return v

def low_keep(v):
    return (low(v), None)

def low_pass(kept, grad):
    return (grad,)

def back_keep(v):
    return (v, None)

def back_low(kept, grad):
    return (low(grad),)
low.defvjp(low_keep, low_pass)
low_back.defvjp(back_keep, back_low)
HIGHEST_PRECISION = lax.Precision.HIGHEST
DECAY_RATE = 0.5
EPSILON = 1e-05

def product(left_side, right_side):
    return jnp.dot(left_side, right_side, precision=HIGHEST_PRECISION)

def norm_rows(values, gain_row, bias_row):
    centred = values - lax.optimization_barrier(jnp.mean(values, axis=-1, keepdims=True))
    variance = lax.optimization_barrier(jnp.mean(centred * centred, axis=-1, keepdims=True))
    return centred * lax.rsqrt(variance + EPSILON) * gain_row + bias_row

def build_kernel(sub_taps):
    pieces = []
    for level_index in range(sub_taps.shape[0]):
        repeats = 2 ** max(level_index, 1)
        pieces.append(jnp.repeat(sub_taps[level_index], repeats, axis=0) * DECAY_RATE ** level_index)
    raw_taps = jnp.concatenate(pieces, axis=0)
    return raw_taps * lax.rsqrt(lax.optimization_barrier(jnp.sum(raw_taps * raw_taps, axis=0, keepdims=True)) + EPSILON)

def masked_conv(values, kernel, seg_row):
    length = values.shape[0]
    onehot = (seg_row[:, None] == jnp.arange(DOCS, dtype=jnp.int32)[None, :]).astype(values.dtype)
    spread = onehot.T[:, :, None] * values[None]
    spectrum = jnp.fft.rfft(spread, n=2 * length, axis=1) * jnp.fft.rfft(kernel, n=2 * length, axis=0)[None]
    convolved = jnp.fft.irfft(spectrum, n=2 * length, axis=1)[:, :length]
    return lax.optimization_barrier(jnp.sum(onehot.T[:, :, None] * convolved, axis=0))

def row_forward(weights, row_stream, seg_row):
    gains, biases, w_in, w_out, kernels, w_up, w_down = weights
    stream = row_stream
    for layer_index in range(LAYERS):
        hidden = low(norm_rows(stream, gains[layer_index, 0], biases[layer_index, 0]))
        joined = product(hidden, w_in[layer_index].reshape(D, 2 * D))
        conv_input = low(low_back(joined[:, :D]))
        gate_pre = low_back(joined[:, D:])
        convolved = low_back(masked_conv(conv_input, kernels[layer_index], seg_row))
        gated_out = low(jax.nn.gelu(gate_pre) * convolved)
        middle = stream + low_back(product(gated_out, w_out[layer_index]))
        hidden_mid = low(norm_rows(middle, gains[layer_index, 1], biases[layer_index, 1]))
        up_pre = low_back(product(hidden_mid, w_up[layer_index]))
        active = low(jax.nn.gelu(up_pre))
        stream = middle + low_back(product(active, w_down[layer_index]))
    return stream

def forward(stream_in, segments, gains, biases, w_in, w_out, sub_kernels, w_up, w_down):
    kernels = low(jnp.stack([build_kernel(sub_kernels[layer_index]) for layer_index in range(LAYERS)]))
    weights = (gains, biases, w_in, w_out, kernels, w_up, w_down)
    row_streams = stream_in.reshape(ROWS, L, D)

    def one_row(row_pair):
        return row_forward(weights, row_pair[0], row_pair[1])
    result = lax.map(jax.checkpoint(one_row), (row_streams, segments))
    return result.reshape(ROWS * L, D)

def reference(stream_in, segments, norm_gain, norm_bias, w_in, w_out, sub_kernels, w_up, w_down, cotangent):
    floats = (stream_in.astype(jnp.float32), norm_gain.astype(jnp.float32), norm_bias.astype(jnp.float32), w_in.astype(jnp.float32), w_out.astype(jnp.float32), sub_kernels.astype(jnp.float32), w_up.astype(jnp.float32), w_down.astype(jnp.float32))

    def wrapped(stream_arg, gains, biases, w_in_arg, w_out_arg, sub_taps, w_up_arg, w_down_arg):
        return forward(stream_arg, segments, gains, biases, w_in_arg, w_out_arg, sub_taps, w_up_arg, w_down_arg)
    result, pullback = jax.vjp(wrapped, *floats)
    gradients = pullback(cotangent.astype(jnp.float32))
    return (result, gradients[0], gradients[1], gradients[2], gradients[3], gradients[4], gradients[5], gradients[6], gradients[7])
```

```python
import functools

import jax
import jax.numpy as jnp
import numpy as np
from jax import lax
from jax.sharding import PartitionSpec as P

DECAY_RATE = 0.5
EPSILON = 1e-05
BF = jnp.bfloat16
F32 = jnp.float32


def norm_rows(values, gain_row, bias_row):
    centred = values - jnp.mean(values, axis=-1, keepdims=True)
    variance = jnp.mean(centred * centred, axis=-1, keepdims=True)
    return centred * lax.rsqrt(variance + EPSILON) * gain_row + bias_row


def build_kernel(sub_taps):
    pieces = []
    for level_index in range(sub_taps.shape[0]):
        repeats = 2 ** max(level_index, 1)
        pieces.append(jnp.repeat(sub_taps[level_index], repeats, axis=0) * DECAY_RATE**level_index)
    raw_taps = jnp.concatenate(pieces, axis=0)
    return raw_taps * lax.rsqrt(jnp.sum(raw_taps * raw_taps, axis=0, keepdims=True) + EPSILON)


def transform_matrix(quarter):
    freq = np.arange(quarter)[:, None] + 0.5
    angle = np.pi * freq * np.arange(quarter)[None, :] / quarter
    return np.concatenate([np.cos(angle), -np.sin(angle)], axis=0).astype(np.float32)


def mul(a, b):
    return (a[0] * b[0] - a[1] * b[1], a[0] * b[1] + a[1] * b[0])


def mul_conj(a, b):
    return (a[0] * b[0] + a[1] * b[1], a[0] * b[1] - a[1] * b[0])


def add(a, b):
    return (a[0] + b[0], a[1] + b[1])


def turn(a, sign):
    return (-sign * a[1], sign * a[0])


def turn_back(a, sign):
    return (sign * a[1], -sign * a[0])


def split_docs(blocks, seg):
    long_doc = seg[1, 0]
    kept = [jnp.where((seg[n] == long_doc)[:, None], blocks[n], 0) for n in range(4)]
    for k in range(3):
        doc = k + (k >= long_doc).astype(jnp.int32)
        kept.append(
            jnp.where((seg[0] == doc)[:, None], blocks[0], 0)
            + jnp.where((seg[3] == doc)[:, None], blocks[3], 0)
        )
    return jnp.stack(kept)


def join_docs(parts, seg):
    long_doc = seg[1, 0]
    out = [jnp.where((seg[n] == long_doc)[:, None], parts[n], 0) for n in range(4)]
    for k in range(3):
        doc = k + (k >= long_doc).astype(jnp.int32)
        for n in (0, 3):
            out[n] = out[n] + jnp.where((seg[n] == doc)[:, None], parts[4 + k], 0)
    return jnp.stack(out)


def spectrum(blocks, table):
    both = jnp.einsum("fp,npc->nfc", table, blocks.astype(BF), preferred_element_type=F32)
    quarter = blocks.shape[1]
    return both[:, :quarter], both[:, quarter:]


def unspectrum(pair, table):
    both = jnp.concatenate(pair, axis=1).astype(BF)
    return jnp.einsum("fp,nfc->npc", table, both, preferred_element_type=F32) / table.shape[1]


def at(pair, n):
    return (pair[0][n], pair[1][n])


def windows(kernel, table, sign):
    length, channels = kernel.shape
    quarter = length // 4
    d = spectrum(kernel.reshape(4, quarter, channels), table)
    out = [at(d, 0)]
    for m in range(1, 4):
        out.append(add(at(d, m), turn(at(d, m - 1), sign)))
    return out


def conv(values, kernel, seg, table, sign):
    w = windows(kernel, table, sign)
    x = spectrum(split_docs(values, seg), table)
    ys = []
    for n in range(7):
        if n < 4:
            y = mul(w[0], at(x, n))
            for m in range(1, n + 1):
                y = add(y, mul(w[m], at(x, n - m)))
        else:
            y = mul(w[0], at(x, n))
        ys.append(y)
    parts = unspectrum((jnp.stack([y[0] for y in ys]), jnp.stack([y[1] for y in ys])), table)
    return join_docs(parts, seg), x


def conv_back(upstream, x, kernel, seg, table, sign):
    w = windows(kernel, table, sign)
    c = spectrum(split_docs(upstream, seg), table)
    gs = []
    for n in range(7):
        g = mul_conj(w[0], at(c, n))
        if n < 4:
            for m in range(1, 4 - n):
                g = add(g, mul_conj(w[m], at(c, n + m)))
        gs.append(g)
    parts = unspectrum((jnp.stack([g[0] for g in gs]), jnp.stack([g[1] for g in gs])), table)
    dw = []
    for m in range(4):
        total = None
        for n in range(m, 4):
            term = mul_conj(at(x, n - m), at(c, n))
            total = term if total is None else add(total, term)
        dw.append(total)
    for n in range(4, 7):
        dw[0] = add(dw[0], mul_conj(at(x, n), at(c, n)))
    dd = [add(dw[m], turn_back(dw[m + 1], sign)) if m < 3 else dw[m] for m in range(4)]
    taps = unspectrum((jnp.stack([g[0] for g in dd]), jnp.stack([g[1] for g in dd])), table)
    return join_docs(parts, seg), taps.reshape(-1, taps.shape[2])


def to_channels(rows):
    n = lax.axis_size("mp")
    return lax.all_to_all(rows.reshape(rows.shape[0], n, -1), "mp", 1, 0)


def to_tokens(blocks):
    got = lax.all_to_all(blocks, "mp", 0, 1)
    return got.reshape(got.shape[0], -1)


def dot_tn(a, b):
    return lax.dot_general(a, b, (((0,), (0,)), ((), ())), preferred_element_type=F32)


def dot_nt(a, b):
    return lax.dot_general(a, b, (((1,), (1,)), ((), ())), preferred_element_type=F32)


def per_device(
    stream_in, segments, norm_gain, norm_bias, w_in, w_out, sub_kernels, w_up, w_down, cotangent
):
    layers = w_in.shape[0]
    quarter = segments.shape[1] // 4
    seg = segments.reshape(4, quarter)
    table = jnp.asarray(transform_matrix(quarter)).astype(BF)
    sign = jnp.asarray(1.0 - 2.0 * (np.arange(quarter)[:, None] % 2), F32)
    w_in = lax.all_gather(w_in, "mp", axis=3, tiled=True)
    w_out = lax.all_gather(w_out, "mp", axis=1, tiled=True)
    w_up = lax.all_gather(w_up, "mp", axis=2, tiled=True)
    w_down = lax.all_gather(w_down, "mp", axis=1, tiled=True)
    stream = stream_in
    kept = []
    for l in range(layers):
        hidden = norm_rows(stream, norm_gain[l, 0], norm_bias[l, 0]).astype(BF)
        conv_input = jnp.dot(hidden, w_in[l, :, 0], preferred_element_type=F32).astype(BF)
        gate_pre = jnp.dot(hidden, w_in[l, :, 1], preferred_element_type=F32)
        kernel = build_kernel(sub_kernels[l]).astype(BF)
        convolved, x = conv(to_channels(conv_input), kernel, seg, table, sign)
        convolved = to_tokens(convolved.astype(BF)).astype(F32)
        gated = (jax.nn.gelu(gate_pre) * convolved).astype(BF)
        middle = stream + jnp.dot(gated, w_out[l], preferred_element_type=F32)
        hidden_mid = norm_rows(middle, norm_gain[l, 1], norm_bias[l, 1]).astype(BF)
        up_pre = jnp.dot(hidden_mid, w_up[l], preferred_element_type=F32)
        active = jax.nn.gelu(up_pre).astype(BF)
        out = middle + jnp.dot(active, w_down[l], preferred_element_type=F32)
        kept.append((stream, hidden, gate_pre, kernel, x, convolved, gated, middle, hidden_mid, up_pre, active))
        stream = out
    grad = cotangent
    collected = []
    for l in reversed(range(layers)):
        layer_in, hidden, gate_pre, kernel, x, convolved, gated, middle, hidden_mid, up_pre, active = kept[l]
        branch_grad = grad.astype(BF)
        g_down = dot_tn(active, branch_grad)
        up_grad = jax.vjp(jax.nn.gelu, up_pre)[1](dot_nt(branch_grad, w_down[l]))[0].astype(BF)
        g_up = dot_tn(hidden_mid, up_grad)
        hidden_grad = dot_nt(up_grad, w_up[l])
        pull = jax.vjp(norm_rows, middle, norm_gain[l, 1], norm_bias[l, 1])[1]
        norm_grad, gain1, bias1 = pull(hidden_grad)
        middle_grad = grad + norm_grad
        out_grad = middle_grad.astype(BF)
        g_out = dot_tn(gated, out_grad)
        gated_grad = dot_nt(out_grad, w_out[l])
        act, gate_pull = jax.vjp(jax.nn.gelu, gate_pre)
        conv_grad = (gated_grad * act).astype(BF)
        gate_grad = gate_pull(gated_grad * convolved)[0].astype(BF)
        input_grad, taps = conv_back(to_channels(conv_grad), x, kernel, seg, table, sign)
        input_grad = to_tokens(input_grad.astype(BF))
        g_sub = jax.vjp(build_kernel, sub_kernels[l])[1](taps)[0]
        g_in = jnp.stack([dot_tn(hidden, input_grad), dot_tn(hidden, gate_grad)], axis=1)
        hidden_grad = dot_nt(input_grad, w_in[l, :, 0]) + dot_nt(gate_grad, w_in[l, :, 1])
        pull = jax.vjp(norm_rows, layer_in, norm_gain[l, 0], norm_bias[l, 0])[1]
        norm_grad, gain0, bias0 = pull(hidden_grad)
        grad = middle_grad + norm_grad
        collected.insert(0, (jnp.stack([gain0, gain1]), jnp.stack([bias0, bias1]), g_in, g_out, g_sub, g_up, g_down))
    gain, bias, g_in, g_out, g_sub, g_up, g_down = [jnp.stack([c[i] for c in collected]) for i in range(7)]
    g_in = lax.psum_scatter(g_in.astype(BF), "mp", scatter_dimension=3, tiled=True)
    g_out = lax.psum_scatter(g_out.astype(BF), "mp", scatter_dimension=1, tiled=True)
    g_up = lax.psum_scatter(g_up.astype(BF), "mp", scatter_dimension=2, tiled=True)
    g_down = lax.psum_scatter(g_down.astype(BF), "mp", scatter_dimension=1, tiled=True)
    g_in, g_out, g_sub, g_up, g_down = lax.psum(
        (g_in.astype(F32), g_out.astype(F32), g_sub, g_up.astype(F32), g_down.astype(F32)), "dp"
    )
    gain, bias = lax.psum((gain, bias), ("dp", "mp"))
    return stream, grad, gain, bias, g_in, g_out, g_sub, g_up, g_down


def solution(mesh):
    rows = P(("dp", "mp"), None)
    last = P(None, None, None, "mp")
    mid = P(None, "mp", None)
    return jax.shard_map(
        per_device,
        mesh=mesh,
        in_specs=(rows, P("dp", None), P(), P(), last, mid, last, P(None, None, "mp"), mid, rows),
        out_specs=(rows, rows, P(), P(), last, mid, last, P(None, None, "mp"), mid),
        check_vma=False,
    )
```

```python
import functools

import jax
import jax.numpy as jnp
import numpy as np
from jax import lax
from jax.experimental import pallas as pl
from jax.experimental.pallas import tpu as pltpu
from jax.sharding import PartitionSpec as P

DECAY_RATE = 0.5
EPSILON = 1e-05
BF = jnp.bfloat16
F32 = jnp.float32
GROUP = 8
MESH = pl.DeviceIdType.MESH
VMEM = pl.BlockSpec(memory_space=pltpu.VMEM)
ANY = pl.BlockSpec(memory_space=pl.ANY)
GELU_A = float(np.sqrt(2.0 / np.pi))
GELU_B = 0.044715


def dot(a, b):
    return jnp.dot(a, b, preferred_element_type=F32)


def dot_nt(a, b):
    return lax.dot_general(a, b, (((1,), (1,)), ((), ())), preferred_element_type=F32)


def dot_tn(a, b):
    return lax.dot_general(a, b, (((0,), (0,)), ((), ())), preferred_element_type=F32)


def gelu(u):
    return 0.5 * u * (1.0 + jnp.tanh(GELU_A * (u + GELU_B * (u * u * u))))


def gelu_both(u):
    square = u * u
    t = jnp.tanh(GELU_A * (u + GELU_B * (square * u)))
    half = 0.5 * (1.0 + t)
    slope = half + (0.5 * u) * (1.0 - t * t) * (GELU_A + (3.0 * GELU_A * GELU_B) * square)
    return u * half, slope


def loop(count, body):
    lax.fori_loop(0, count, lambda j, c: (body(j), c)[1], 0)


def rows_of(j, size):
    return pl.ds(pl.multiple_of(j * size, size), size)


def transform_table(quarter):
    freq = np.arange(quarter)[:, None] + 0.5
    angle = np.pi * freq * np.arange(quarter)[None, :] / quarter
    return np.concatenate([np.cos(angle), -np.sin(angle)], axis=0)


def spread_matrix(scales, taps):
    lags = []
    for level in range(scales):
        lags += [level * taps + j for j in range(taps) for _ in range(2 ** max(level, 1))]
    spread = np.zeros((len(lags), scales * taps))
    spread[np.arange(len(lags)), lags] = 1.0
    return spread


def tap_tables(quarter, scales, taps):
    table = transform_table(quarter)
    spread = spread_matrix(scales, taps).reshape(4, quarter, scales * taps)
    return np.einsum("fp,mpt->mft", table, spread)


def tap_scales(scales, taps, channels):
    level = np.repeat(np.arange(scales), taps)
    decay = DECAY_RATE**level
    repeats = 2.0 ** np.maximum(level, 1)
    both = np.stack([decay, repeats])[:, :, None]
    return np.broadcast_to(both, (2, scales * taps, channels)).astype(np.float32)


def doc_masks(segments, channels):
    quarter = segments.shape[1] // 4
    seg = segments.reshape(4, quarter)
    long_doc = seg[1, 0]
    rows = [seg[n] == long_doc for n in range(4)]
    for k in range(3):
        doc = k + (k >= long_doc).astype(jnp.int32)
        rows += [seg[0] == doc, seg[3] == doc]
    stacked = jnp.stack(rows).astype(BF)
    return jnp.broadcast_to(stacked[:, :, None], (10, quarter, channels))


class Place:
    def __init__(self, n):
        self.n = n
        self.q = lax.axis_index("mp")
        dp = lax.axis_index("dp")
        self.i = lax.rem(dp, GROUP)
        self.base = dp - self.i
        self.core = lax.rem(self.i, 2)
        self.chip = self.i // 2

    def column(self, k):
        q = lax.rem(self.q + k, self.n)
        return q, {"dp": self.base + self.i, "mp": q}

    def mate(self, k):
        i = lax.rem(self.chip + k, GROUP // 2) * 2 + self.core
        return i, {"dp": self.base + i, "mp": self.q}

    def sibling(self):
        return {"dp": self.base + self.chip * 2 + (1 - self.core), "mp": self.q}

    def peers(self):
        others = [self.column(k)[1] for k in range(1, self.n)]
        others += [self.mate(k)[1] for k in range(1, GROUP // 2)]
        return others + [self.sibling()]


def greet(place):
    barrier = pltpu.get_barrier_semaphore()
    peers = place.peers()
    for peer in peers:
        pl.semaphore_signal(barrier, inc=1, device_id=peer, device_id_type=MESH)
    pl.semaphore_wait(barrier, len(peers))


def send(src, dst, send_sem, recv_sem, peer):
    pltpu.make_async_remote_copy(
        src_ref=src, dst_ref=dst, send_sem=send_sem, recv_sem=recv_sem, device_id=peer, device_id_type=MESH
    ).start()


def await_bytes(ref, sem):
    pltpu.make_async_copy(ref, ref, sem).wait()


class Weight:
    def __init__(self, whole, layer, kind, n):
        self.whole, self.kind, self.layer, self.n = whole, kind, layer, n
        shape = whole.shape
        if kind == "in":
            self.rows, self.cols = shape[2] // GROUP, shape[3] // n
        elif kind == "up":
            self.rows, self.cols = shape[1] // GROUP, shape[2] // n
        else:
            self.rows, self.cols = shape[1] // n // GROUP, shape[2]

    def piece(self, i, q):
        r, c = self.rows, self.cols
        if self.kind == "in":
            return self.whole.at[self.layer, :, pl.ds(i * r, r), pl.ds(q * c, c)]
        if self.kind == "up":
            return self.whole.at[self.layer, pl.ds(i * r, r), pl.ds(q * c, c)]
        return self.whole.at[self.layer, pl.ds((q * GROUP + i) * r, r), :]

    def shard(self, q):
        r, c = self.rows, self.cols
        if self.kind == "in":
            return self.whole.at[self.layer, :, :, pl.ds(q * c, c)]
        if self.kind == "up":
            return self.whole.at[self.layer, :, pl.ds(q * c, c)]
        return self.whole.at[self.layer, pl.ds(q * GROUP * r, GROUP * r), :]

    def local_piece(self, shard, i):
        r = self.rows
        if self.kind == "in":
            return shard.at[self.layer, :, pl.ds(i * r, r), :]
        return shard.at[self.layer, pl.ds(i * r, r), :]

    def span(self, members):
        r, c, k = self.rows, self.cols, self.n - 1
        if self.kind == "in":
            return self.whole.at[self.layer, :, pl.ds(0, members * r), pl.ds(0, k * c)]
        if self.kind == "up":
            return self.whole.at[self.layer, pl.ds(0, members * r), pl.ds(0, k * c)]
        return self.whole.at[self.layer, pl.ds(0, members * k * r), :]


class Gather:
    def __init__(self, place, weight, shard, sems, slot):
        self.p, self.w, self.shard_ref, self.sems, self.slot = place, weight, shard, sems, slot

    def sem(self, k):
        return self.sems.at[self.slot, k]

    def own(self):
        return pltpu.make_async_copy(
            self.shard_ref.at[self.w.layer], self.w.shard(self.p.q), self.sem(6)
        )

    def start(self):
        p, w = self.p, self.w
        for k in range(1, p.n):
            send(w.local_piece(self.shard_ref, p.i), w.piece(p.i, p.q), self.sem(0), self.sem(1), p.column(k)[1])
        self.own().start()

    def to_chips(self):
        p, w = self.p, self.w
        await_bytes(w.span(1), self.sem(1))
        for k in range(1, p.n):
            for c in range(1, GROUP // 2):
                piece = w.piece(p.i, p.column(k)[0])
                send(piece, piece, self.sem(2), self.sem(3), p.mate(c)[1])

    def to_core(self):
        p, w = self.p, self.w
        await_bytes(w.span(GROUP // 2 - 1), self.sem(3))
        for k in range(1, p.n):
            for c in range(GROUP // 2):
                piece = w.piece(p.mate(c)[0], p.column(k)[0])
                send(piece, piece, self.sem(4), self.sem(5), p.sibling())

    def arrive(self):
        self.own().wait()
        await_bytes(self.w.span(GROUP // 2), self.sem(5))

    def finish(self):
        await_bytes(self.w.span(1), self.sem(0))
        await_bytes(self.w.span(GROUP // 2 - 1), self.sem(2))
        await_bytes(self.w.span(GROUP // 2), self.sem(4))


def norm_strip(v, gain, bias):
    centred = v - jnp.mean(v, axis=-1, keepdims=True)
    variance = jnp.mean(centred * centred, axis=-1, keepdims=True)
    return centred * lax.rsqrt(variance + EPSILON) * gain + bias


def norm_all(src, dst, gain, bias):
    def strip(j):
        r = rows_of(j, 32)
        dst[r, :] = norm_strip(src[r, :], gain, bias).astype(BF)

    loop(dst.shape[0] // 32, strip)


def make_windows(sub_ref, scale_ref, tap_ref, spec, layer, wins):
    raw = sub_ref[layer] * scale_ref[0]
    total = jnp.sum(raw * raw * scale_ref[1], axis=0, keepdims=True)
    taps = (raw * lax.rsqrt(total + EPSILON)).astype(BF)
    channels = taps.shape[1]
    quarter = wins.shape[3]
    for m in range(4):
        spec[:, m * channels : (m + 1) * channels] = dot(tap_ref[m], taps)

    def strip(j):
        r = rows_of(j, 16)
        s = rows_of(j + quarter // 16, 16)
        sign = (1 - 2 * lax.rem(lax.broadcasted_iota(jnp.int32, (16, channels), 0), 2)).astype(F32)
        for m in range(4):
            here = slice(m * channels, (m + 1) * channels)
            re, im = spec[r, here], spec[s, here]
            if m:
                before = slice((m - 1) * channels, m * channels)
                re, im = re - sign * spec[s, before], im + sign * spec[r, before]
            wins[layer, m, 0, r, :] = re
            wins[layer, m, 1, r, :] = im

    loop(quarter // 16, strip)


def spread_blocks(blocks, layer, masks, out):
    channels = masks.shape[2]
    for n in range(4):
        out[:, n * channels : (n + 1) * channels] = blocks[layer, n] * masks[n]
    for k in range(3):
        out[:, (4 + k) * channels : (5 + k) * channels] = (
            blocks[layer, 0] * masks[4 + 2 * k] + blocks[layer, 3] * masks[5 + 2 * k]
        )


def join_blocks(parts, r, masks, n):
    channels = masks.shape[2]
    total = parts[:, n * channels : (n + 1) * channels] * masks[n, r, :].astype(F32)
    if n in (0, 3):
        for k in range(3):
            mask = masks[4 + 2 * k + (n == 3), r, :].astype(F32)
            total += parts[:, (4 + k) * channels : (5 + k) * channels] * mask
    return total


def fwd_products(spec, wins, layer, out, channels):
    quarter = wins.shape[3]

    def strip(j):
        r = rows_of(j, 16)
        s = rows_of(j + quarter // 16, 16)
        xs = [(spec[r, n * channels : (n + 1) * channels], spec[s, n * channels : (n + 1) * channels]) for n in range(7)]
        ws = [(wins[layer, m, 0, r, :], wins[layer, m, 1, r, :]) for m in range(4)]
        for n in range(7):
            re = im = None
            for m in range(n + 1 if n < 4 else 1):
                w, x = ws[m], xs[n - m]
                a = w[0] * x[0] - w[1] * x[1]
                b = w[0] * x[1] + w[1] * x[0]
                re, im = (a, b) if re is None else (re + a, im + b)
            out[r, n * channels : (n + 1) * channels] = re.astype(BF)
            out[s, n * channels : (n + 1) * channels] = im.astype(BF)

    loop(quarter // 16, strip)


def forward_kernel(
    n, layers,
    stream_in, masks, gains, biases, subs, scales, table, table_t, tap_table, win, wout, wup, wdn,
    out_stream, streams_o, gate_o, conv_in_o, conv_out_o, middle_o, win_o, wout_o, wup_o, wdn_o,
    stream, hidden, gate, middle, send_a, recv_a, send_b, recv_b,
    spread, spec, spec_y, wins, gated, up, active, win_f, wout_f, wup_f, wdn_f,
    gather_sems, a2a_sems, save_sems,
):
    place = Place(n)
    me = place.q
    tokens, width = stream_in.shape
    channels = width // n
    quarter = tokens
    greet(place)
    gathers = []
    for l in range(layers):
        for kind, whole, shard in (("in", win_f, win), ("out", wout_f, wout), ("up", wup_f, wup), ("down", wdn_f, wdn)):
            slot = len(gathers)
            gathers.append(Gather(place, Weight(whole, l, kind, n), shard, gather_sems, slot))
    saves = []

    def save(src, dst):
        copy = pltpu.make_async_copy(src, dst, save_sems.at[len(saves)])
        copy.start()
        saves.append(copy)

    def exchange_start(slot, src, dst, layer):
        for k in range(1, n):
            q, peer = place.column(k)
            send(src.at[layer, q], dst.at[layer, me], a2a_sems.at[slot, 0], a2a_sems.at[slot, 1], peer)

    def exchange_wait(slot, src, dst, layer):
        await_bytes(src.at[layer, pl.ds(0, n - 1)], a2a_sems.at[slot, 0])
        await_bytes(dst.at[layer, pl.ds(0, n - 1)], a2a_sems.at[slot, 1])

    for g in gathers[:4]:
        g.start()
    norm_all(stream_in, hidden, gains[0, 0], biases[0, 0])
    gathers[0].to_chips()
    for l in range(layers):
        make_windows(subs, scales, tap_table, spec, l, wins)
    gathers[0].to_core()
    gathers[0].arrive()

    for l in range(layers):
        here = stream_in if l == 0 else stream.at[l - 1]
        rest = gathers[4 * l + 1 : 4 * l + 4]
        if l:
            norm_all(here, hidden, gains[l, 0], biases[l, 0])
            gathers[4 * l].to_core()
            gathers[4 * l].arrive()

        def project(j):
            r = rows_of(j, 256)
            got = dot(hidden[r, :], win_f[l, 0]).astype(BF)
            for q in range(n):
                send_a[l, q, r, :] = got[:, q * channels : (q + 1) * channels]

        loop(tokens // 256, project)
        exchange_start(2 * l, send_a, recv_a, l)
        recv_a[l, me] = send_a[l, me]
        for g in rest:
            g.to_chips()

        def project_gate(j):
            r = rows_of(j, 256)
            gate[l, r, :] = dot(hidden[r, :], win_f[l, 1])

        loop(tokens // 256, project_gate)
        save(gate.at[l], gate_o.at[l])
        for g in rest:
            g.to_core()
        exchange_wait(2 * l, send_a, recv_a, l)
        save(recv_a.at[l], conv_in_o.at[l])
        spread_blocks(recv_a, l, masks, spread)

        def transform(j):
            r = rows_of(j, 256)
            spec[r, :] = dot(table[r, :], spread[...])

        loop(2 * quarter // 256, transform)
        fwd_products(spec, wins, l, spec_y, channels)

        def untransform(j):
            r = rows_of(j, 128)
            parts = dot(table_t[r, :], spec_y[...])
            for q in range(n):
                send_b[l, q, r, :] = join_blocks(parts, r, masks, q).astype(BF)

        loop(quarter // 128, untransform)
        exchange_start(2 * l + 1, send_b, recv_b, l)
        recv_b[l, me] = send_b[l, me]
        for g in rest:
            g.arrive()
        if l + 1 < layers:
            for g in gathers[4 * l + 4 : 4 * l + 8]:
                g.start()
        exchange_wait(2 * l + 1, send_b, recv_b, l)
        save(recv_b.at[l], conv_out_o.at[l])

        def mix(j):
            r = rows_of(j, 16)
            for q in range(n):
                c = slice(q * channels, (q + 1) * channels)
                gated[r, c] = (gelu(gate[l, r, c]) * recv_b[l, q, r, :].astype(F32)).astype(BF)

        loop(tokens // 16, mix)

        def attach(j):
            r = rows_of(j, 256)
            middle[l, r, :] = here[r, :] + dot(gated[r, :], wout_f[l])

        loop(tokens // 256, attach)
        save(middle.at[l], middle_o.at[l])
        norm_all(middle.at[l], hidden, gains[l, 1], biases[l, 1])
        if l + 1 < layers:
            gathers[4 * l + 4].to_chips()

        def widen(j):
            r = rows_of(j, 256)
            up[r, :] = dot(hidden[r, :], wup_f[l])

        loop(tokens // 256, widen)

        def activate(j):
            r = rows_of(j, 8)
            active[r, :] = gelu(up[r, :]).astype(BF)

        def activate16(j):
            r = rows_of(j, 16)
            active[r, :] = gelu(up[r, :]).astype(BF)

        loop(tokens // 16, activate16)

        def narrow(j):
            r = rows_of(j, 256)
            stream[l, r, :] = middle[l, r, :] + dot(active[r, :], wdn_f[l])

        loop(tokens // 256, narrow)
        save(stream.at[l], out_stream if l + 1 == layers else streams_o.at[l])
    for src, dst in ((win_f, win_o), (wout_f, wout_o), (wup_f, wup_o), (wdn_f, wdn_o)):
        save(src, dst)
    for g in gathers:
        g.finish()
    for copy in saves:
        copy.wait()


def forward(n, stream_in, masks, gains, biases, subs, scales, table, table_t, tap_table, win, wout, wup, wdn):
    layers = win.shape[0]
    tokens, width = stream_in.shape
    channels = width // n
    ff = wup.shape[2] * n
    length_freq = 2 * tokens

    def sds(*shape, dtype=BF):
        return jax.ShapeDtypeStruct(shape, dtype)

    wshapes = [(layers, 2, width, width), (layers, width, width), (layers, width, ff), (layers, ff, width)]
    outs = [
        sds(tokens, width, dtype=F32),
        sds(max(layers - 1, 1), tokens, width, dtype=F32),
        sds(layers, tokens, width, dtype=F32),
        sds(layers, n, tokens, channels),
        sds(layers, n, tokens, channels),
        sds(layers, tokens, width, dtype=F32),
    ] + [sds(*s) for s in wshapes]
    a2a = pltpu.VMEM((layers, n, tokens, channels), BF)
    scratch = [
        pltpu.VMEM((layers, tokens, width), F32),
        pltpu.VMEM((tokens, width), BF),
        pltpu.VMEM((layers, tokens, width), F32),
        pltpu.VMEM((layers, tokens, width), F32),
        a2a, a2a, a2a, a2a,
        pltpu.VMEM((tokens, 7 * channels), BF),
        pltpu.VMEM((length_freq, 7 * channels), F32),
        pltpu.VMEM((length_freq, 7 * channels), BF),
        pltpu.VMEM((layers, 4, 2, tokens, channels), F32),
        pltpu.VMEM((tokens, width), BF),
        pltpu.VMEM((tokens, ff), F32),
        pltpu.VMEM((tokens, ff), BF),
    ] + [pltpu.VMEM(s, BF) for s in wshapes] + [
        pltpu.SemaphoreType.DMA((4 * layers, 7)),
        pltpu.SemaphoreType.DMA((2 * layers, 2)),
        pltpu.SemaphoreType.DMA((5 * layers + 4,)),
    ]
    return pl.pallas_call(
        functools.partial(forward_kernel, n, layers),
        out_shape=outs,
        in_specs=[VMEM] * 9 + [ANY] * 4,
        out_specs=[ANY] * 10,
        scratch_shapes=scratch,
        compiler_params=pltpu.CompilerParams(collective_id=1, has_side_effects=True, vmem_limit_bytes=60 * 2**20),
        name="forward",
    )(stream_in, masks, gains, biases, subs, scales, table, table_t, tap_table, win, wout, wup, wdn)


def norm_rows(values, gain_row, bias_row):
    centred = values - jnp.mean(values, axis=-1, keepdims=True)
    variance = jnp.mean(centred * centred, axis=-1, keepdims=True)
    return centred * lax.rsqrt(variance + EPSILON) * gain_row + bias_row


def build_kernel(sub_taps):
    pieces = []
    for level_index in range(sub_taps.shape[0]):
        repeats = 2 ** max(level_index, 1)
        pieces.append(jnp.repeat(sub_taps[level_index], repeats, axis=0) * DECAY_RATE**level_index)
    raw_taps = jnp.concatenate(pieces, axis=0)
    return raw_taps * lax.rsqrt(jnp.sum(raw_taps * raw_taps, axis=0, keepdims=True) + EPSILON)


def transform_matrix(quarter):
    freq = np.arange(quarter)[:, None] + 0.5
    angle = np.pi * freq * np.arange(quarter)[None, :] / quarter
    return np.concatenate([np.cos(angle), -np.sin(angle)], axis=0).astype(np.float32)


def mul(a, b):
    return (a[0] * b[0] - a[1] * b[1], a[0] * b[1] + a[1] * b[0])


def mul_conj(a, b):
    return (a[0] * b[0] + a[1] * b[1], a[0] * b[1] - a[1] * b[0])


def add(a, b):
    return (a[0] + b[0], a[1] + b[1])


def turn(a, sign):
    return (-sign * a[1], sign * a[0])


def turn_back(a, sign):
    return (sign * a[1], -sign * a[0])


def split_docs(blocks, seg):
    long_doc = seg[1, 0]
    kept = [jnp.where((seg[n] == long_doc)[:, None], blocks[n], 0) for n in range(4)]
    for k in range(3):
        doc = k + (k >= long_doc).astype(jnp.int32)
        kept.append(
            jnp.where((seg[0] == doc)[:, None], blocks[0], 0)
            + jnp.where((seg[3] == doc)[:, None], blocks[3], 0)
        )
    return jnp.stack(kept)


def join_docs(parts, seg):
    long_doc = seg[1, 0]
    out = [jnp.where((seg[n] == long_doc)[:, None], parts[n], 0) for n in range(4)]
    for k in range(3):
        doc = k + (k >= long_doc).astype(jnp.int32)
        for n in (0, 3):
            out[n] = out[n] + jnp.where((seg[n] == doc)[:, None], parts[4 + k], 0)
    return jnp.stack(out)


def spectrum(blocks, table):
    both = jnp.einsum("fp,npc->nfc", table, blocks.astype(BF), preferred_element_type=F32)
    quarter = blocks.shape[1]
    return both[:, :quarter], both[:, quarter:]


def unspectrum(pair, table):
    both = jnp.concatenate(pair, axis=1).astype(BF)
    return jnp.einsum("fp,nfc->npc", table, both, preferred_element_type=F32) / table.shape[1]


def at(pair, n):
    return (pair[0][n], pair[1][n])


def windows(kernel, table, sign):
    length, channels = kernel.shape
    quarter = length // 4
    d = spectrum(kernel.reshape(4, quarter, channels), table)
    out = [at(d, 0)]
    for m in range(1, 4):
        out.append(add(at(d, m), turn(at(d, m - 1), sign)))
    return out


def conv(values, kernel, seg, table, sign):
    w = windows(kernel, table, sign)
    x = spectrum(split_docs(values, seg), table)
    ys = []
    for n in range(7):
        if n < 4:
            y = mul(w[0], at(x, n))
            for m in range(1, n + 1):
                y = add(y, mul(w[m], at(x, n - m)))
        else:
            y = mul(w[0], at(x, n))
        ys.append(y)
    parts = unspectrum((jnp.stack([y[0] for y in ys]), jnp.stack([y[1] for y in ys])), table)
    return join_docs(parts, seg), x


def conv_back(upstream, x, kernel, seg, table, sign):
    w = windows(kernel, table, sign)
    c = spectrum(split_docs(upstream, seg), table)
    gs = []
    for n in range(7):
        g = mul_conj(w[0], at(c, n))
        if n < 4:
            for m in range(1, 4 - n):
                g = add(g, mul_conj(w[m], at(c, n + m)))
        gs.append(g)
    parts = unspectrum((jnp.stack([g[0] for g in gs]), jnp.stack([g[1] for g in gs])), table)
    dw = []
    for m in range(4):
        total = None
        for n in range(m, 4):
            term = mul_conj(at(x, n - m), at(c, n))
            total = term if total is None else add(total, term)
        dw.append(total)
    for n in range(4, 7):
        dw[0] = add(dw[0], mul_conj(at(x, n), at(c, n)))
    dd = [add(dw[m], turn_back(dw[m + 1], sign)) if m < 3 else dw[m] for m in range(4)]
    taps = unspectrum((jnp.stack([g[0] for g in dd]), jnp.stack([g[1] for g in dd])), table)
    return join_docs(parts, seg), taps.reshape(-1, taps.shape[2])


def to_channels(rows):
    n = lax.axis_size("mp")
    return lax.all_to_all(rows.reshape(rows.shape[0], n, -1), "mp", 1, 0)


def to_tokens(blocks):
    got = lax.all_to_all(blocks, "mp", 0, 1)
    return got.reshape(got.shape[0], -1)


def dot_tn(a, b):
    return lax.dot_general(a, b, (((0,), (0,)), ((), ())), preferred_element_type=F32)


def dot_nt(a, b):
    return lax.dot_general(a, b, (((1,), (1,)), ((), ())), preferred_element_type=F32)


def per_device(
    stream_in, segments, norm_gain, norm_bias, w_in, w_out, sub_kernels, w_up, w_down, cotangent
):
    layers, scales, taps_n, channels = sub_kernels.shape
    n = lax.axis_size("mp")
    quarter = segments.shape[1] // 4
    seg = segments.reshape(4, quarter)
    table_np = transform_table(quarter)
    table = jnp.asarray(table_np, F32).astype(BF)
    sign = jnp.asarray(1.0 - 2.0 * (np.arange(quarter)[:, None] % 2), F32)
    masks = doc_masks(segments, channels)
    tap_table = jnp.asarray(tap_tables(quarter, scales, taps_n) / quarter, F32).astype(BF)
    consts = jnp.asarray(tap_scales(scales, taps_n, channels))
    out, streams, gate_all, conv_in, conv_out, middle_all, w_in_f, w_out_f, w_up_f, w_down_f = forward(
        n, stream_in, masks, norm_gain[:, :, None], norm_bias[:, :, None], sub_kernels.reshape(layers, -1, channels), consts,
        table, table.T, tap_table, w_in.transpose(0, 2, 1, 3), w_out, w_up, w_down)
    kept = []
    for l in range(layers):
        layer_in = stream_in if l == 0 else streams[l - 1]
        hidden = norm_rows(layer_in, norm_gain[l, 0], norm_bias[l, 0]).astype(BF)
        convolved = conv_out[l].transpose(1, 0, 2).reshape(quarter, -1).astype(F32)
        gate_pre = gate_all[l]
        gated = (jax.nn.gelu(gate_pre) * convolved).astype(BF)
        middle = middle_all[l]
        hidden_mid = norm_rows(middle, norm_gain[l, 1], norm_bias[l, 1]).astype(BF)
        up_pre = jnp.dot(hidden_mid, w_up_f[l], preferred_element_type=F32)
        active = jax.nn.gelu(up_pre).astype(BF)
        kernel = build_kernel(sub_kernels[l]).astype(BF)
        x = spectrum(split_docs(conv_in[l], seg), table)
        kept.append((layer_in, hidden, gate_pre, kernel, x, convolved, gated, middle, hidden_mid, up_pre, active))
    grad = cotangent
    collected = []
    for l in reversed(range(layers)):
        layer_in, hidden, gate_pre, kernel, x, convolved, gated, middle, hidden_mid, up_pre, active = kept[l]
        branch_grad = grad.astype(BF)
        g_down = dot_tn(active, branch_grad)
        up_grad = jax.vjp(jax.nn.gelu, up_pre)[1](dot_nt(branch_grad, w_down_f[l]))[0].astype(BF)
        g_up = dot_tn(hidden_mid, up_grad)
        hidden_grad = dot_nt(up_grad, w_up_f[l])
        pull = jax.vjp(norm_rows, middle, norm_gain[l, 1], norm_bias[l, 1])[1]
        norm_grad, gain1, bias1 = pull(hidden_grad)
        middle_grad = grad + norm_grad
        out_grad = middle_grad.astype(BF)
        g_out = dot_tn(gated, out_grad)
        gated_grad = dot_nt(out_grad, w_out_f[l])
        act, gate_pull = jax.vjp(jax.nn.gelu, gate_pre)
        conv_grad = (gated_grad * act).astype(BF)
        gate_grad = gate_pull(gated_grad * convolved)[0].astype(BF)
        input_grad, taps = conv_back(to_channels(conv_grad), x, kernel, seg, table, sign)
        input_grad = to_tokens(input_grad.astype(BF))
        g_sub = jax.vjp(build_kernel, sub_kernels[l])[1](taps)[0]
        g_in = jnp.stack([dot_tn(hidden, input_grad), dot_tn(hidden, gate_grad)], axis=1)
        hidden_grad = dot_nt(input_grad, w_in_f[l, 0]) + dot_nt(gate_grad, w_in_f[l, 1])
        pull = jax.vjp(norm_rows, layer_in, norm_gain[l, 0], norm_bias[l, 0])[1]
        norm_grad, gain0, bias0 = pull(hidden_grad)
        grad = middle_grad + norm_grad
        collected.insert(0, (jnp.stack([gain0, gain1]), jnp.stack([bias0, bias1]), g_in, g_out, g_sub, g_up, g_down))
    gain, bias, g_in, g_out, g_sub, g_up, g_down = [jnp.stack([c[i] for c in collected]) for i in range(7)]
    g_in = lax.psum_scatter(g_in.astype(BF), "mp", scatter_dimension=3, tiled=True)
    g_out = lax.psum_scatter(g_out.astype(BF), "mp", scatter_dimension=1, tiled=True)
    g_up = lax.psum_scatter(g_up.astype(BF), "mp", scatter_dimension=2, tiled=True)
    g_down = lax.psum_scatter(g_down.astype(BF), "mp", scatter_dimension=1, tiled=True)
    g_in, g_out, g_sub, g_up, g_down = lax.psum(
        (g_in.astype(F32), g_out.astype(F32), g_sub, g_up.astype(F32), g_down.astype(F32)), "dp"
    )
    gain, bias = lax.psum((gain, bias), ("dp", "mp"))
    return out, grad, gain, bias, g_in, g_out, g_sub, g_up, g_down


def solution(mesh):
    rows = P(("dp", "mp"), None)
    last = P(None, None, None, "mp")
    mid = P(None, "mp", None)
    return jax.shard_map(
        per_device,
        mesh=mesh,
        in_specs=(rows, P("dp", None), P(), P(), last, mid, last, P(None, None, "mp"), mid, rows),
        out_specs=(rows, rows, P(), P(), last, mid, last, P(None, None, "mp"), mid),
        check_vma=False,
    )
```

```python
import functools

import jax
import jax.numpy as jnp
import numpy as np
from jax import lax
from jax.experimental import pallas as pl
from jax.experimental.pallas import tpu as pltpu
from jax.sharding import PartitionSpec as P

DECAY_RATE = 0.5
EPSILON = 1e-05
BF = jnp.bfloat16
F32 = jnp.float32
GROUP = 8
MESH = pl.DeviceIdType.MESH
VMEM = pl.BlockSpec(memory_space=pltpu.VMEM)
ANY = pl.BlockSpec(memory_space=pl.ANY)
GELU_A = float(np.sqrt(2.0 / np.pi))
GELU_B = 0.044715


def dot(a, b):
    return jnp.dot(a, b, preferred_element_type=F32)


def dot_nt(a, b):
    return lax.dot_general(a, b, (((1,), (1,)), ((), ())), preferred_element_type=F32)


def dot_tn(a, b):
    return lax.dot_general(a, b, (((0,), (0,)), ((), ())), preferred_element_type=F32)


def gelu(u):
    return 0.5 * u * (1.0 + jnp.tanh(GELU_A * (u + GELU_B * (u * u * u))))


def gelu_both(u):
    square = u * u
    t = jnp.tanh(GELU_A * (u + GELU_B * (square * u)))
    half = 0.5 * (1.0 + t)
    slope = half + (0.5 * u) * (1.0 - t * t) * (GELU_A + (3.0 * GELU_A * GELU_B) * square)
    return u * half, slope


def loop(count, body):
    lax.fori_loop(0, count, lambda j, c: (body(j), c)[1], 0)


def rows_of(j, size):
    return pl.ds(pl.multiple_of(j * size, size), size)


def transform_table(quarter):
    freq = np.arange(quarter)[:, None] + 0.5
    angle = np.pi * freq * np.arange(quarter)[None, :] / quarter
    return np.concatenate([np.cos(angle), -np.sin(angle)], axis=0)


def spread_matrix(scales, taps):
    lags = []
    for level in range(scales):
        lags += [level * taps + j for j in range(taps) for _ in range(2 ** max(level, 1))]
    spread = np.zeros((len(lags), scales * taps))
    spread[np.arange(len(lags)), lags] = 1.0
    return spread


def tap_tables(quarter, scales, taps):
    table = transform_table(quarter)
    spread = spread_matrix(scales, taps).reshape(4, quarter, scales * taps)
    return np.einsum("fp,mpt->mft", table, spread)


def tap_scales(scales, taps, channels):
    level = np.repeat(np.arange(scales), taps)
    decay = DECAY_RATE**level
    repeats = 2.0 ** np.maximum(level, 1)
    both = np.stack([decay, repeats])[:, :, None]
    return np.broadcast_to(both, (2, scales * taps, channels)).astype(np.float32)


def doc_masks(segments, channels):
    quarter = segments.shape[1] // 4
    seg = segments.reshape(4, quarter)
    long_doc = seg[1, 0]
    rows = [seg[n] == long_doc for n in range(4)]
    for k in range(3):
        doc = k + (k >= long_doc).astype(jnp.int32)
        rows += [seg[0] == doc, seg[3] == doc]
    stacked = jnp.stack(rows).astype(BF)
    return jnp.broadcast_to(stacked[:, :, None], (10, quarter, channels))


class Place:
    def __init__(self, n):
        self.n = n
        self.q = lax.axis_index("mp")
        dp = lax.axis_index("dp")
        self.i = lax.rem(dp, GROUP)
        self.base = dp - self.i
        self.core = lax.rem(self.i, 2)
        self.chip = self.i // 2

    def column(self, k):
        q = lax.rem(self.q + k, self.n)
        return q, {"dp": self.base + self.i, "mp": q}

    def mate(self, k):
        i = lax.rem(self.chip + k, GROUP // 2) * 2 + self.core
        return i, {"dp": self.base + i, "mp": self.q}

    def sibling(self):
        return {"dp": self.base + self.chip * 2 + (1 - self.core), "mp": self.q}

    def member(self, k):
        return {"dp": self.base + lax.rem(self.i + k, GROUP), "mp": self.q}

    def peers(self):
        others = [self.column(k)[1] for k in range(1, self.n)]
        others += [self.mate(k)[1] for k in range(1, GROUP // 2)]
        return others + [self.sibling()]


def greet(place):
    barrier = pltpu.get_barrier_semaphore()
    peers = place.peers()
    for peer in peers:
        pl.semaphore_signal(barrier, inc=1, device_id=peer, device_id_type=MESH)
    pl.semaphore_wait(barrier, len(peers))


def greet_all(place):
    barrier = pltpu.get_barrier_semaphore()
    peers = [place.column(k)[1] for k in range(1, place.n)] + [place.member(k) for k in range(1, GROUP)]
    for peer in peers:
        pl.semaphore_signal(barrier, inc=1, device_id=peer, device_id_type=MESH)
    pl.semaphore_wait(barrier, len(peers))


def send(src, dst, send_sem, recv_sem, peer):
    pltpu.make_async_remote_copy(
        src_ref=src, dst_ref=dst, send_sem=send_sem, recv_sem=recv_sem, device_id=peer, device_id_type=MESH
    ).start()


def await_bytes(ref, sem):
    pltpu.make_async_copy(ref, ref, sem).wait()


class Weight:
    def __init__(self, whole, layer, kind, n):
        self.whole, self.kind, self.layer, self.n = whole, kind, layer, n
        shape = whole.shape
        if kind == "in":
            self.rows, self.cols = shape[2] // GROUP, shape[3] // n
        elif kind == "up":
            self.rows, self.cols = shape[1] // GROUP, shape[2] // n
        else:
            self.rows, self.cols = shape[1] // n // GROUP, shape[2]

    def piece(self, i, q):
        r, c = self.rows, self.cols
        if self.kind == "in":
            return self.whole.at[self.layer, :, pl.ds(i * r, r), pl.ds(q * c, c)]
        if self.kind == "up":
            return self.whole.at[self.layer, pl.ds(i * r, r), pl.ds(q * c, c)]
        return self.whole.at[self.layer, pl.ds((q * GROUP + i) * r, r), :]

    def shard(self, q):
        r, c = self.rows, self.cols
        if self.kind == "in":
            return self.whole.at[self.layer, :, :, pl.ds(q * c, c)]
        if self.kind == "up":
            return self.whole.at[self.layer, :, pl.ds(q * c, c)]
        return self.whole.at[self.layer, pl.ds(q * GROUP * r, GROUP * r), :]

    def local_piece(self, shard, i):
        r = self.rows
        if self.kind == "in":
            return shard.at[self.layer, :, pl.ds(i * r, r), :]
        return shard.at[self.layer, pl.ds(i * r, r), :]

    def span(self, members):
        r, c, k = self.rows, self.cols, self.n - 1
        if self.kind == "in":
            return self.whole.at[self.layer, :, pl.ds(0, members * r), pl.ds(0, k * c)]
        if self.kind == "up":
            return self.whole.at[self.layer, pl.ds(0, members * r), pl.ds(0, k * c)]
        return self.whole.at[self.layer, pl.ds(0, members * k * r), :]


class Gather:
    def __init__(self, place, weight, shard, sems, slot):
        self.p, self.w, self.shard_ref, self.sems, self.slot = place, weight, shard, sems, slot

    def sem(self, k):
        return self.sems.at[self.slot, k]

    def own(self):
        return pltpu.make_async_copy(
            self.shard_ref.at[self.w.layer], self.w.shard(self.p.q), self.sem(6)
        )

    def start(self):
        p, w = self.p, self.w
        for k in range(1, p.n):
            send(w.local_piece(self.shard_ref, p.i), w.piece(p.i, p.q), self.sem(0), self.sem(1), p.column(k)[1])
        self.own().start()

    def to_chips(self):
        p, w = self.p, self.w
        await_bytes(w.span(1), self.sem(1))
        for k in range(1, p.n):
            for c in range(1, GROUP // 2):
                piece = w.piece(p.i, p.column(k)[0])
                send(piece, piece, self.sem(2), self.sem(3), p.mate(c)[1])

    def to_core(self):
        p, w = self.p, self.w
        await_bytes(w.span(GROUP // 2 - 1), self.sem(3))
        for k in range(1, p.n):
            for c in range(GROUP // 2):
                piece = w.piece(p.mate(c)[0], p.column(k)[0])
                send(piece, piece, self.sem(4), self.sem(5), p.sibling())

    def arrive(self):
        self.own().wait()
        await_bytes(self.w.span(GROUP // 2), self.sem(5))

    def finish(self):
        await_bytes(self.w.span(1), self.sem(0))
        await_bytes(self.w.span(GROUP // 2 - 1), self.sem(2))
        await_bytes(self.w.span(GROUP // 2), self.sem(4))


def norm_strip(v, gain, bias):
    centred = v - jnp.mean(v, axis=-1, keepdims=True)
    variance = jnp.mean(centred * centred, axis=-1, keepdims=True)
    return centred * lax.rsqrt(variance + EPSILON) * gain + bias


def norm_all(src, dst, gain, bias):
    def strip(j):
        r = rows_of(j, 32)
        dst[r, :] = norm_strip(src[r, :], gain, bias).astype(BF)

    loop(dst.shape[0] // 32, strip)


def make_windows(sub_ref, scale_ref, tap_ref, spec, layer, wins):
    raw = sub_ref[layer] * scale_ref[0]
    total = jnp.sum(raw * raw * scale_ref[1], axis=0, keepdims=True)
    taps = (raw * lax.rsqrt(total + EPSILON)).astype(BF)
    channels = taps.shape[1]
    quarter = wins.shape[3]
    for m in range(4):
        spec[:, m * channels : (m + 1) * channels] = dot(tap_ref[m], taps)

    def strip(j):
        r = rows_of(j, 16)
        s = rows_of(j + quarter // 16, 16)
        sign = (1 - 2 * lax.rem(lax.broadcasted_iota(jnp.int32, (16, channels), 0), 2)).astype(F32)
        for m in range(4):
            here = slice(m * channels, (m + 1) * channels)
            re, im = spec[r, here], spec[s, here]
            if m:
                before = slice((m - 1) * channels, m * channels)
                re, im = re - sign * spec[s, before], im + sign * spec[r, before]
            wins[layer, m, 0, r, :] = re
            wins[layer, m, 1, r, :] = im

    loop(quarter // 16, strip)


def spread_blocks(blocks, masks, out):
    channels = masks.shape[2]
    for n in range(4):
        out[:, n * channels : (n + 1) * channels] = blocks[n] * masks[n]
    for k in range(3):
        out[:, (4 + k) * channels : (5 + k) * channels] = (
            blocks[0] * masks[4 + 2 * k] + blocks[3] * masks[5 + 2 * k]
        )


def join_blocks(parts, r, masks, n):
    channels = masks.shape[2]
    total = parts[:, n * channels : (n + 1) * channels] * masks[n, r, :].astype(F32)
    if n in (0, 3):
        for k in range(3):
            mask = masks[4 + 2 * k + (n == 3), r, :].astype(F32)
            total += parts[:, (4 + k) * channels : (5 + k) * channels] * mask
    return total


def fwd_products(spec, wins, layer, out, channels):
    quarter = wins.shape[3]

    def strip(j):
        r = rows_of(j, 16)
        s = rows_of(j + quarter // 16, 16)
        xs = [(spec[r, n * channels : (n + 1) * channels], spec[s, n * channels : (n + 1) * channels]) for n in range(7)]
        ws = [(wins[layer, m, 0, r, :], wins[layer, m, 1, r, :]) for m in range(4)]
        for n in range(7):
            re = im = None
            for m in range(n + 1 if n < 4 else 1):
                w, x = ws[m], xs[n - m]
                a = w[0] * x[0] - w[1] * x[1]
                b = w[0] * x[1] + w[1] * x[0]
                re, im = (a, b) if re is None else (re + a, im + b)
            out[r, n * channels : (n + 1) * channels] = re.astype(BF)
            out[s, n * channels : (n + 1) * channels] = im.astype(BF)

    loop(quarter // 16, strip)


def forward_kernel(
    n, layers,
    stream_in, masks, gains, biases, subs, scales, table, table_t, tap_table, win, wout, wup, wdn,
    out_stream, streams_o, gate_o, conv_in_o, conv_out_o, middle_o, wins_o, win_o, wout_o, wup_o, wdn_o,
    stream, hidden, gate, middle, send_a, recv_a, send_b, recv_b,
    spread, spec, spec_y, wins, gated, up, active, win_f, wout_f, wup_f, wdn_f,
    gather_sems, a2a_sems, save_sems,
):
    place = Place(n)
    me = place.q
    tokens, width = stream_in.shape
    channels = width // n
    quarter = tokens
    greet(place)
    gathers = []
    for l in range(layers):
        for kind, whole, shard in (("in", win_f, win), ("out", wout_f, wout), ("up", wup_f, wup), ("down", wdn_f, wdn)):
            slot = len(gathers)
            gathers.append(Gather(place, Weight(whole, l, kind, n), shard, gather_sems, slot))
    saves = []

    def save(src, dst):
        copy = pltpu.make_async_copy(src, dst, save_sems.at[len(saves)])
        copy.start()
        saves.append(copy)

    def exchange_start(slot, src, dst, layer):
        for k in range(1, n):
            q, peer = place.column(k)
            send(src.at[layer, q], dst.at[layer, me], a2a_sems.at[slot, 0], a2a_sems.at[slot, 1], peer)

    def exchange_wait(slot, src, dst, layer):
        await_bytes(src.at[layer, pl.ds(0, n - 1)], a2a_sems.at[slot, 0])
        await_bytes(dst.at[layer, pl.ds(0, n - 1)], a2a_sems.at[slot, 1])

    for g in gathers[:4]:
        g.start()
    norm_all(stream_in, hidden, gains[0, 0], biases[0, 0])
    gathers[0].to_chips()
    for l in range(layers):
        make_windows(subs, scales, tap_table, spec, l, wins)
    gathers[0].to_core()
    gathers[0].arrive()

    for l in range(layers):
        here = stream_in if l == 0 else stream.at[l - 1]
        rest = gathers[4 * l + 1 : 4 * l + 4]
        if l:
            norm_all(here, hidden, gains[l, 0], biases[l, 0])
            gathers[4 * l].to_core()
            gathers[4 * l].arrive()

        def project(j):
            r = rows_of(j, 256)
            got = dot(hidden[r, :], win_f[l, 0]).astype(BF)
            for q in range(n):
                send_a[l, q, r, :] = got[:, q * channels : (q + 1) * channels]

        loop(tokens // 256, project)
        exchange_start(2 * l, send_a, recv_a, l)
        recv_a[l, me] = send_a[l, me]
        for g in rest:
            g.to_chips()

        def project_gate(j):
            r = rows_of(j, 256)
            gate[l, r, :] = dot(hidden[r, :], win_f[l, 1])

        loop(tokens // 256, project_gate)
        save(gate.at[l], gate_o.at[l])
        for g in rest:
            g.to_core()
        exchange_wait(2 * l, send_a, recv_a, l)
        save(recv_a.at[l], conv_in_o.at[l])
        spread_blocks(recv_a.at[l], masks, spread)

        def transform(j):
            r = rows_of(j, 256)
            spec[r, :] = dot(table[r, :], spread[...])

        loop(2 * quarter // 256, transform)
        fwd_products(spec, wins, l, spec_y, channels)

        def untransform(j):
            r = rows_of(j, 128)
            parts = dot(table_t[r, :], spec_y[...])
            for q in range(n):
                send_b[l, q, r, :] = join_blocks(parts, r, masks, q).astype(BF)

        loop(quarter // 128, untransform)
        exchange_start(2 * l + 1, send_b, recv_b, l)
        recv_b[l, me] = send_b[l, me]
        for g in rest:
            g.arrive()
        if l + 1 < layers:
            for g in gathers[4 * l + 4 : 4 * l + 8]:
                g.start()
        exchange_wait(2 * l + 1, send_b, recv_b, l)
        save(recv_b.at[l], conv_out_o.at[l])

        def mix(j):
            r = rows_of(j, 16)
            for q in range(n):
                c = slice(q * channels, (q + 1) * channels)
                gated[r, c] = (gelu(gate[l, r, c]) * recv_b[l, q, r, :].astype(F32)).astype(BF)

        loop(tokens // 16, mix)

        def attach(j):
            r = rows_of(j, 256)
            middle[l, r, :] = here[r, :] + dot(gated[r, :], wout_f[l])

        loop(tokens // 256, attach)
        save(middle.at[l], middle_o.at[l])
        norm_all(middle.at[l], hidden, gains[l, 1], biases[l, 1])
        if l + 1 < layers:
            gathers[4 * l + 4].to_chips()

        def widen(j):
            r = rows_of(j, 256)
            up[r, :] = dot(hidden[r, :], wup_f[l])

        loop(tokens // 256, widen)

        def activate(j):
            r = rows_of(j, 8)
            active[r, :] = gelu(up[r, :]).astype(BF)

        def activate16(j):
            r = rows_of(j, 16)
            active[r, :] = gelu(up[r, :]).astype(BF)

        loop(tokens // 16, activate16)

        def narrow(j):
            r = rows_of(j, 256)
            stream[l, r, :] = middle[l, r, :] + dot(active[r, :], wdn_f[l])

        loop(tokens // 256, narrow)
        save(stream.at[l], out_stream if l + 1 == layers else streams_o.at[l])
    for src, dst in ((wins, wins_o), (win_f, win_o), (wout_f, wout_o), (wup_f, wup_o), (wdn_f, wdn_o)):
        save(src, dst)
    for g in gathers:
        g.finish()
    for copy in saves:
        copy.wait()


def forward(n, stream_in, masks, gains, biases, subs, scales, table, table_t, tap_table, win, wout, wup, wdn):
    layers = win.shape[0]
    tokens, width = stream_in.shape
    channels = width // n
    ff = wup.shape[2] * n
    length_freq = 2 * tokens

    def sds(*shape, dtype=BF):
        return jax.ShapeDtypeStruct(shape, dtype)

    wshapes = [(layers, 2, width, width), (layers, width, width), (layers, width, ff), (layers, ff, width)]
    outs = [
        sds(tokens, width, dtype=F32),
        sds(max(layers - 1, 1), tokens, width, dtype=F32),
        sds(layers, tokens, width, dtype=F32),
        sds(layers, n, tokens, channels),
        sds(layers, n, tokens, channels),
        sds(layers, tokens, width, dtype=F32),
        sds(layers, 4, 2, tokens, channels, dtype=F32),
    ] + [sds(*s) for s in wshapes]
    a2a = pltpu.VMEM((layers, n, tokens, channels), BF)
    scratch = [
        pltpu.VMEM((layers, tokens, width), F32),
        pltpu.VMEM((tokens, width), BF),
        pltpu.VMEM((layers, tokens, width), F32),
        pltpu.VMEM((layers, tokens, width), F32),
        a2a, a2a, a2a, a2a,
        pltpu.VMEM((tokens, 7 * channels), BF),
        pltpu.VMEM((length_freq, 7 * channels), F32),
        pltpu.VMEM((length_freq, 7 * channels), BF),
        pltpu.VMEM((layers, 4, 2, tokens, channels), F32),
        pltpu.VMEM((tokens, width), BF),
        pltpu.VMEM((tokens, ff), F32),
        pltpu.VMEM((tokens, ff), BF),
    ] + [pltpu.VMEM(s, BF) for s in wshapes] + [
        pltpu.SemaphoreType.DMA((4 * layers, 7)),
        pltpu.SemaphoreType.DMA((2 * layers, 2)),
        pltpu.SemaphoreType.DMA((5 * layers + 5,)),
    ]
    return pl.pallas_call(
        functools.partial(forward_kernel, n, layers),
        out_shape=outs,
        in_specs=[VMEM] * 9 + [ANY] * 4,
        out_specs=[ANY] * 11,
        scratch_shapes=scratch,
        compiler_params=pltpu.CompilerParams(collective_id=1, has_side_effects=True, vmem_limit_bytes=60 * 2**20),
        name="forward",
    )(stream_in, masks, gains, biases, subs, scales, table, table_t, tap_table, win, wout, wup, wdn)


PIECE_UP, PIECE_DOWN, PIECE_OUT, PIECE_IN, PIECE_ROWS = 0, 64, 128, 144, 176


def norm_back(upstream, src, base, gain, out, rounded):
    width = src.shape[1]

    def strip(j, sums):
        r = rows_of(j, 16)
        v = src[r, :]
        centred = v - jnp.mean(v, axis=-1, keepdims=True)
        inverse = lax.rsqrt(jnp.mean(centred * centred, axis=-1, keepdims=True) + EPSILON)
        xhat = centred * inverse
        up = upstream[r, :]
        q = gain * up
        both = q - jnp.mean(q, axis=-1, keepdims=True) - xhat * jnp.mean(q * xhat, axis=-1, keepdims=True)
        got = base[r, :] + both * inverse
        out[r, :] = got
        if rounded is not None:
            rounded[r, :] = got.astype(BF)
        p = up * xhat
        return sums[0] + p[:8] + p[8:], sums[1] + up[:8] + up[8:]

    zero = jnp.zeros((8, width), F32)
    return lax.fori_loop(0, src.shape[0] // 16, strip, (zero, zero))


def back_products(spec_x, spec_c, wins, out_g, out_d, channels):
    quarter = wins.shape[2]
    half = out_g.shape[1] // 2

    def strip(j):
        r = rows_of(j, 16)
        s = rows_of(j + quarter // 16, 16)
        cols = [slice(n * channels, (n + 1) * channels) for n in range(7)]
        cols2 = [slice(half + n * channels, half + (n + 1) * channels) for n in range(7)]
        cs = [(spec_c[r, c], spec_c[s, c]) for c in cols]
        for n in range(7):
            re = im = None
            for m in range(4 - n if n < 4 else 1):
                w, x = (wins[m, 0, r, :], wins[m, 1, r, :]), cs[n + m]
                a = w[0] * x[0] + w[1] * x[1]
                b = w[0] * x[1] - w[1] * x[0]
                re, im = (a, b) if re is None else (re + a, im + b)
            out_g[r, cols[n]] = re.astype(BF)
            out_g[r, cols2[n]] = im.astype(BF)
        sign = (1 - 2 * lax.rem(lax.broadcasted_iota(jnp.int32, (16, channels), 0), 2)).astype(F32)
        later = None
        for m in (3, 2, 1, 0):
            pairs = [(n - m, n) for n in range(m, 4)] + ([(n, n) for n in range(4, 7)] if m == 0 else [])
            re = im = None
            for i, n in pairs:
                x, c = (spec_x[r, cols[i]], spec_x[s, cols[i]]), cs[n]
                a = x[0] * c[0] + x[1] * c[1]
                b = x[0] * c[1] - x[1] * c[0]
                re, im = (a, b) if re is None else (re + a, im + b)
            dre, dim = (re, im) if later is None else (re + sign * later[1], im - sign * later[0])
            later = (re, im)
            out_d[r, cols[m]] = dre.astype(BF)
            out_d[r, cols2[m]] = dim.astype(BF)

    loop(quarter // 16, strip)


class Reduce:
    def __init__(self, place, bufs, sems, slot, layer, first, rows):
        self.p, self.layer, self.slot, self.sems = place, layer, slot, sems
        self.r = pl.ds(first, rows)
        self.first, self.rows = first, rows
        self.grads, self.r0, self.r1, self.r2, self.res = bufs
        self.spare = self.grads.shape[0] - 1

    def sem(self, k):
        return self.sems.at[self.slot, k]

    def strips(self, body):
        loop(self.rows // 16, lambda j: body(pl.ds(pl.multiple_of(self.first + j * 16, 16), 16)))

    def s0(self):
        send(self.grads.at[self.spare, :, :, self.r], self.r0.at[self.layer, :, :, self.r], self.sem(0), self.sem(1), self.p.sibling())

    def s1(self):
        p, l = self.p, self.layer
        await_bytes(self.r0.at[l, :, :, self.r], self.sem(0))
        await_bytes(self.r0.at[l, :, :, self.r], self.sem(1))

        def add(j):
            def strip(r):
                c, q = j // p.n, lax.rem(j, p.n)
                total = self.grads[l, c, q, r, :].astype(F32) + self.r0[l, c, q, r, :].astype(F32)
                self.grads[l, c, q, r, :] = total.astype(BF)

            self.strips(strip)

        loop(GROUP // 2 * p.n, add)
        for k in range(1, GROUP // 2):
            other = lax.rem(p.chip + k, GROUP // 2)
            send(self.grads.at[l, other, :, self.r], self.r1.at[l, k - 1, :, self.r], self.sem(2), self.sem(3), p.mate(k)[1])

    def s2(self):
        p, l = self.p, self.layer
        await_bytes(self.r1.at[l, :, :, self.r], self.sem(2))
        await_bytes(self.r1.at[l, :, :, self.r], self.sem(3))

        def add(q):
            def strip(r):
                total = self.grads[l, p.chip, q, r, :].astype(F32)
                for k in range(GROUP // 2 - 1):
                    total += self.r1[l, k, q, r, :].astype(F32)
                self.grads[l, p.chip, q, r, :] = total.astype(BF)

            self.strips(strip)

        loop(p.n, add)
        for k in range(1, p.n):
            q, peer = p.column(k)
            send(self.grads.at[l, p.chip, q, self.r], self.r2.at[l, k - 1, self.r], self.sem(4), self.sem(5), peer)

    def s3(self):
        p, l = self.p, self.layer
        await_bytes(self.r2.at[l, :, self.r], self.sem(4))
        await_bytes(self.r2.at[l, :, self.r], self.sem(5))

        def strip(r):
            total = self.grads[l, p.chip, p.q, r, :].astype(F32)
            for k in range(p.n - 1):
                total += self.r2[l, k, r, :].astype(F32)
            self.res[l, p.i, r, :] = total.astype(BF)

        self.strips(strip)
        for k in range(1, GROUP // 2):
            piece = self.res.at[l, p.i, self.r]
            send(piece, piece, self.sem(6), self.sem(7), p.mate(k)[1])

    def s4(self):
        p, l = self.p, self.layer
        await_bytes(self.res.at[l, pl.ds(0, GROUP // 2 - 1), self.r], self.sem(6))
        await_bytes(self.res.at[l, pl.ds(0, GROUP // 2 - 1), self.r], self.sem(7))
        for k in range(GROUP // 2):
            piece = self.res.at[l, p.mate(k)[0], self.r]
            send(piece, piece, self.sem(8), self.sem(9), p.sibling())

    def end(self):
        half = self.res.at[self.layer, pl.ds(0, GROUP // 2), self.r]
        await_bytes(half, self.sem(8))
        await_bytes(half, self.sem(9))


def backward_kernel(
    n, layers,
    masks, gains, subs, scales, table, table_t, tap_t,
    cotangent, stream_in, streams, gates, conv_ins, conv_outs, middles, wins_h, win_h, wout_h, wup_h, wdn_h,
    biases,
    grad_o, res_o, sub_o, norm_o,
    grad, middle_grad, stream, gate, conv_in, conv_out, middle, wins, win, wout, wup, wdn,
    grads, r0, r1, r2, res,
    hidden, hidden_mid, active, up_grad, gated, out_grad, branch, joined, big_a, big_b, spread,
    send_c, recv_c, send_d, recv_d, sub_s, sub_r, norm_s, norm_r, norm_t, norm_u,
    load_sems, a2a_sems, red_sems, small_sems, out_sems,
):
    place = Place(n)
    me, core = place.q, place.core
    tokens, width = grad.shape
    channels = width // n
    quarter = tokens
    ff = wup.shape[1]
    half = ff // 2
    spare = grads.shape[0] - 1
    greet_all(place)

    loads = {}

    def load(name, l):
        src, dst = {
            "stream": (streams.at[l - 1] if l else stream_in, stream), "gate": (gates.at[l], gate),
            "conv_in": (conv_ins.at[l], conv_in), "conv_out": (conv_outs.at[l], conv_out),
            "middle": (middles.at[l], middle), "wins": (wins_h.at[l], wins), "in": (win_h.at[l], win),
            "out": (wout_h.at[l], wout), "up": (wup_h.at[l], wup), "down": (wdn_h.at[l], wdn),
            "grad": (cotangent, grad),
        }[name]
        copy = pltpu.make_async_copy(src, dst, load_sems.at[l, len([k for k in loads if k[1] == l])])
        copy.start()
        loads[name, l] = copy

    def ready(name, l):
        loads[name, l].wait()

    def next_load(name, l):
        if l:
            load(name, l - 1)

    def exchange_start(slot, src, dst, l):
        for k in range(1, n):
            q, peer = place.column(k)
            send(src.at[q], dst.at[l, me], a2a_sems.at[slot, 0], a2a_sems.at[slot, 1], peer)

    def exchange_wait(slot, src, dst, l):
        await_bytes(src.at[pl.ds(0, n - 1)], a2a_sems.at[slot, 0])
        await_bytes(dst.at[l, pl.ds(0, n - 1)], a2a_sems.at[slot, 1])

    def holder(parity, l):
        mine = 1 - (parity - core) * (parity - core)
        return l * mine + spare * (1 - mine)

    bufs = (grads, r0, r1, r2, res)
    first = [Reduce(place, bufs, red_sems, 2 * l, l, 0, PIECE_IN) for l in range(layers)]
    second = [Reduce(place, bufs, red_sems, 2 * l + 1, l, PIECE_IN, PIECE_ROWS - PIECE_IN) for l in range(layers)]

    top = layers - 1
    for name in ("middle", "grad", "up", "down", "out", "gate", "conv_out", "conv_in", "wins", "stream", "in"):
        load(name, top)

    for l in reversed(range(layers)):
        ready("middle", l)
        norm_all(middle, hidden_mid, gains[l, 1], biases[l, 1])
        if l == top:
            ready("grad", l)

        def round_grad(j):
            r = rows_of(j, 32)
            branch[r, :] = grad[r, :].astype(BF)

        loop(tokens // 32, round_grad)
        ready("up", l)
        ready("down", l)

        def widen(j):
            r = rows_of(j, 256)
            for h in range(2):
                c = slice(h * half, (h + 1) * half)
                t = slice(h * 256, (h + 1) * 256)
                big_a[t, :] = dot(hidden_mid[r, :], wup[:, c])
                big_b[t, :] = dot_nt(branch[r, :], wdn[c, :])

            def activate(k):
                for h in range(2):
                    c = slice(h * half, (h + 1) * half)
                    t = pl.ds(pl.multiple_of(h * 256 + k * 16, 16), 16)
                    s = pl.ds(pl.multiple_of(j * 256 + k * 16, 16), 16)
                    act, slope = gelu_both(big_a[t, :])
                    active[s, c] = act.astype(BF)
                    up_grad[s, c] = (big_b[t, :] * slope).astype(BF)

            loop(256 // 16, activate)

        loop(tokens // 256, widen)

        def narrow(j):
            r = rows_of(j, 256)
            big_a[r, 0:width] = dot_nt(up_grad[r, :], wup[...])

        loop(tokens // 256, narrow)
        next_load("up", l)
        next_load("down", l)
        sums_mid = norm_back(big_a.at[:, 0:width], middle, grad, gains[l, 1], middle_grad, out_grad)
        next_load("middle", l)

        ready("out", l)

        def gated_back(j):
            r = rows_of(j, 256)
            big_b[r, 0:width] = dot_nt(out_grad[r, :], wout[...])

        loop(tokens // 256, gated_back)
        next_load("out", l)
        ready("gate", l)
        ready("conv_out", l)

        def unmix(j):
            r = rows_of(j, 16)
            for q in range(n):
                c = slice(q * channels, (q + 1) * channels)
                act, slope = gelu_both(gate[r, c])
                up, conv = big_b[r, c], conv_out[q, r, :].astype(F32)
                send_c[q, r, :] = (up * act).astype(BF)
                joined[r, slice(width + q * channels, width + (q + 1) * channels)] = (up * conv * slope).astype(BF)
                gated[r, c] = (act * conv).astype(BF)

        loop(tokens // 16, unmix)
        next_load("gate", l)
        next_load("conv_out", l)
        exchange_start(2 * l, send_c, recv_c, l)
        recv_c[l, me] = send_c[me]

        if l < top:
            second[l + 1].s1()

        def grad_up(c):
            got = dot_tn(hidden_mid[:, rows_of(c, 128)], up_grad[...]).astype(BF)
            for par in range(2):
                for q in range(n):
                    grads[holder(par, l), c, q, PIECE_UP:PIECE_DOWN, :] = got[par * 64 : par * 64 + 64, q * (ff // n) : (q + 1) * (ff // n)]

        loop(GROUP // 2, grad_up)

        def grad_down(q):
            got = dot_tn(active[:, rows_of(q, ff // n)], branch[...]).astype(BF)
            for i in range(GROUP):
                grads[holder(i % 2, l), i // 2, q, PIECE_DOWN:PIECE_OUT, :] = got[i * 64 : (i + 1) * 64]

        loop(n, grad_down)

        def grad_out(q):
            got = dot_tn(gated[:, rows_of(q, channels)], out_grad[...]).astype(BF)
            for i in range(GROUP):
                grads[holder(i % 2, l), i // 2, q, PIECE_OUT:PIECE_IN, :] = got[i * 16 : (i + 1) * 16]

        loop(n, grad_out)
        first[l].s0()
        if l < top:
            first[l + 1].s3()

        def grad_in(h):
            def block(c):
                got = dot_tn(hidden[:, rows_of(c, 128)], joined[:, h * width : (h + 1) * width]).astype(BF)
                for par in range(2):
                    for q in range(n):
                        for t in range(2):
                            grads[holder(par, l), c, q, PIECE_IN:PIECE_ROWS, h * 256 + t * 128 : h * 256 + (t + 1) * 128] = got[
                                par * 64 + t * 32 : par * 64 + (t + 1) * 32, q * channels : (q + 1) * channels
                            ]

            loop(GROUP // 2, block)

        ready("stream", l)
        norm_all(stream, hidden, gains[l, 0], biases[l, 0])
        grad_in(1)
        ready("conv_in", l)
        spread_blocks(conv_in, masks, spread)

        def transform_x(j):
            r = rows_of(j, 256)
            big_a[r, 0 : 7 * channels] = dot(table[r, :], spread[...])

        loop(2 * quarter // 256, transform_x)
        next_load("conv_in", l)
        first[l].s1()
        if l < top:
            first[l + 1].s4()
        exchange_wait(2 * l, send_c, recv_c, l)
        spread_blocks(recv_c.at[l], masks, spread)

        def transform_c(j):
            r = rows_of(j, 256)
            big_b[r, 0 : 7 * channels] = dot(table[r, :], spread[...])

        loop(2 * quarter // 256, transform_c)
        ready("wins", l)
        back_products(big_a, big_b, wins, active, up_grad, channels)
        next_load("wins", l)

        def untransform(j):
            r = rows_of(j, 128)
            parts = dot(table_t[r, 0:quarter], active[:, 0 : 7 * channels])
            parts += dot(table_t[r, quarter : 2 * quarter], active[:, half : half + 7 * channels])
            for q in range(n):
                send_d[q, r, :] = join_blocks(parts, r, masks, q).astype(BF)

        loop(quarter // 128, untransform)
        exchange_start(2 * l + 1, send_d, recv_d, l)
        recv_d[l, me] = send_d[me]

        taps = None
        for m in range(4):
            c = slice(m * channels, (m + 1) * channels)
            d = slice(half + m * channels, half + (m + 1) * channels)
            got = dot(tap_t[m, :, 0:quarter], up_grad[:, c]) + dot(tap_t[m, :, quarter : 2 * quarter], up_grad[:, d])
            taps = got if taps is None else taps + got
        raw = subs[l] * scales[0]
        inverse = lax.rsqrt(jnp.sum(raw * raw * scales[1], axis=0, keepdims=True) + EPSILON)
        k = raw * inverse
        along = jnp.sum(taps * k, axis=0, keepdims=True)
        sub_s[l] = scales[0] * (taps - scales[1] * k * along) * inverse
        for j in range(1, GROUP):
            send(sub_s.at[l], sub_r.at[l, j - 1], small_sems.at[l, 0], small_sems.at[l, 1], place.member(j))

        def project_back_gate(j):
            r = rows_of(j, 256)
            big_a[r, 0:width] = dot_nt(joined[r, width : 2 * width], win[1])

        ready("in", l)
        loop(tokens // 256, project_back_gate)
        exchange_wait(2 * l + 1, send_d, recv_d, l)
        first[l].s2()
        if l < top:
            second[l + 1].s2()

        def collect(j):
            r = rows_of(j, 32)
            for q in range(n):
                joined[r, q * channels : (q + 1) * channels] = recv_d[l, q, r, :]

        loop(tokens // 32, collect)

        def project_back(j):
            r = rows_of(j, 256)
            big_a[r, 0:width] = big_a[r, 0:width] + dot_nt(joined[r, 0:width], win[0])

        if l == 0:
            grad_in(0)
            second[l].s0()
        loop(tokens // 256, project_back)
        next_load("in", l)
        sums_in = norm_back(big_a.at[:, 0:width], stream, middle_grad, gains[l, 0], grad, None)
        next_load("stream", l)
        norm_s[l] = jnp.concatenate(
            [jnp.sum(s, axis=0, keepdims=True) for s in (sums_in[0], sums_mid[0], sums_in[1], sums_mid[1])]
            + [jnp.zeros((4, width), F32)],
            axis=0,
        )
        for j in range(1, GROUP):
            send(norm_s.at[l], norm_r.at[l, j - 1], small_sems.at[l, 2], small_sems.at[l, 3], place.member(j))
        if l:
            grad_in(0)
            second[l].s0()

    out = pltpu.make_async_copy(grad, grad_o, out_sems.at[0])
    out.start()
    second[0].s1()
    if layers > 1:
        second[1].s3()
    first[0].s3()
    for l in reversed(range(layers)):
        await_bytes(norm_r.at[l], small_sems.at[l, 2])
        await_bytes(norm_r.at[l], small_sems.at[l, 3])
        norm_t[l] = sum_members(norm_s[l], norm_r, l, place)
        for k in range(1, n):
            send(norm_t.at[l], norm_u.at[l, k - 1], small_sems.at[l, 4], small_sems.at[l, 5], place.column(k)[1])
    second[0].s2()
    first[0].s4()
    if layers > 1:
        second[1].s4()
    for l in reversed(range(layers)):
        await_bytes(sub_r.at[l], small_sems.at[l, 0])
        await_bytes(sub_r.at[l], small_sems.at[l, 1])
        sub_s[l] = sum_members(sub_s[l], sub_r, l, place)
    second[0].s3()
    for l in reversed(range(layers)):
        await_bytes(norm_u.at[l], small_sems.at[l, 4])
        await_bytes(norm_u.at[l], small_sems.at[l, 5])
        norm_s[l] = sum_columns(norm_t[l], norm_u, l, place)
    out_sub = pltpu.make_async_copy(sub_s, sub_o, out_sems.at[1])
    out_sub.start()
    out_norm = pltpu.make_async_copy(norm_s, norm_o, out_sems.at[2])
    out_norm.start()
    second[0].s4()
    for r in first + second:
        if r is not second[0]:
            r.end()
    second[0].end()
    out_res = pltpu.make_async_copy(res, res_o, out_sems.at[3])
    out_res.start()
    out.wait()
    out_sub.wait()
    out_norm.wait()
    out_res.wait()


def in_order(own, others, l, here, count):
    total = None
    for j in range(count):
        k = lax.rem(here - j + count, count)
        value = jnp.where(k == 0, own, others[l, lax.max(k - 1, 0)])
        total = value if total is None else total + value
    return total


def sum_members(own, others, l, place):
    return in_order(own, others, l, place.i, GROUP)


def sum_columns(own, others, l, place):
    return in_order(own, others, l, place.q, place.n)


def backward(n, masks, gains, biases, subs, scales, table, table_t, tap_t, cotangent, stream_in, kept):
    streams, gates, conv_ins, conv_outs, middles, wins, win, wout, wup, wdn = kept
    layers = win.shape[0]
    tokens, width = cotangent.shape
    channels = width // n
    ff = wup.shape[2]
    taps = subs.shape[1]

    def sds(*shape, dtype=F32):
        return jax.ShapeDtypeStruct(shape, dtype)

    outs = [sds(tokens, width), sds(layers, GROUP, PIECE_ROWS, width, dtype=BF), sds(layers, taps, channels), sds(layers, 8, width)]
    f32 = lambda *s: pltpu.VMEM(s, F32)
    bf = lambda *s: pltpu.VMEM(s, BF)
    scratch = [
        f32(tokens, width), f32(tokens, width), f32(tokens, width), f32(tokens, width),
        bf(n, tokens, channels), bf(n, tokens, channels), f32(tokens, width), f32(4, 2, tokens, channels),
        bf(2, width, width), bf(width, width), bf(width, ff), bf(ff, width),
        bf(layers + 1, GROUP // 2, n, PIECE_ROWS, width),
        bf(layers, GROUP // 2, n, PIECE_ROWS, width),
        bf(layers, GROUP // 2 - 1, n, PIECE_ROWS, width),
        bf(layers, n - 1, PIECE_ROWS, width),
        bf(layers, GROUP, PIECE_ROWS, width),
        bf(tokens, width), bf(tokens, width), bf(tokens, ff), bf(tokens, ff), bf(tokens, width), bf(tokens, width), bf(tokens, width),
        bf(tokens, 2 * width), f32(2 * tokens, ff // 2), f32(2 * tokens, ff // 2), bf(tokens, 7 * channels),
        bf(n, tokens, channels), bf(layers, n, tokens, channels), bf(n, tokens, channels), bf(layers, n, tokens, channels),
        f32(layers, taps, channels), f32(layers, GROUP - 1, taps, channels),
        f32(layers, 8, width), f32(layers, GROUP - 1, 8, width), f32(layers, 8, width), f32(layers, n - 1, 8, width),
        pltpu.SemaphoreType.DMA((layers, 11)),
        pltpu.SemaphoreType.DMA((2 * layers, 2)),
        pltpu.SemaphoreType.DMA((2 * layers, 10)),
        pltpu.SemaphoreType.DMA((layers, 6)),
        pltpu.SemaphoreType.DMA((4,)),
    ]
    return pl.pallas_call(
        functools.partial(backward_kernel, n, layers),
        out_shape=outs,
        in_specs=[VMEM] * 7 + [ANY] * 12 + [VMEM],
        out_specs=[ANY] * 4,
        scratch_shapes=scratch,
        compiler_params=pltpu.CompilerParams(collective_id=2, has_side_effects=True, vmem_limit_bytes=int(63.5 * 2**20)),
        name="backward",
    )(masks, gains, subs, scales, table, table_t, tap_t, cotangent, stream_in, streams, gates, conv_ins, conv_outs, middles, wins, win, wout, wup, wdn, biases)


def per_device(
    stream_in, segments, norm_gain, norm_bias, w_in, w_out, sub_kernels, w_up, w_down, cotangent
):
    layers, scales, taps, channels = sub_kernels.shape
    n = lax.axis_size("mp")
    quarter = segments.shape[1] // 4
    table = transform_table(quarter)
    tap_table = tap_tables(quarter, scales, taps) / quarter

    def const(a):
        return jnp.asarray(a, F32).astype(BF)

    masks = doc_masks(segments, channels)
    factors = jnp.asarray(tap_scales(scales, taps, channels))
    subs = sub_kernels.reshape(layers, -1, channels)
    gains, biases = norm_gain[:, :, None], norm_bias[:, :, None]
    out, *kept = forward(
        n, stream_in, masks, gains, biases, subs, factors, const(table), const(table.T), const(tap_table),
        w_in.transpose(0, 2, 1, 3), w_out, w_up, w_down,
    )
    grad, res, sub, norms = backward(
        n, masks, gains, biases, subs, factors, const(table), const(table.T), const(tap_table.transpose(0, 2, 1)),
        cotangent, stream_in, kept,
    )
    res = res.astype(F32)
    if lax.axis_size("dp") > GROUP:
        groups = lax.axis_size("dp") // GROUP
        res, sub, norms = [v * (1.0 / GROUP) for v in lax.psum((res, sub, norms), "dp")]
    width = stream_in.shape[1]
    up = res[:, :, PIECE_UP:PIECE_DOWN].reshape(w_up.shape)
    down = res[:, :, PIECE_DOWN:PIECE_OUT].reshape(w_down.shape)
    out_w = res[:, :, PIECE_OUT:PIECE_IN].reshape(w_out.shape)
    in_w = res[:, :, PIECE_IN:].reshape(layers, GROUP, PIECE_ROWS - PIECE_IN, 2, 2, channels)
    in_w = in_w.transpose(0, 1, 4, 2, 3, 5).reshape(w_in.shape)
    return out, grad, norms[:, 0:2], norms[:, 2:4], in_w, out_w, sub.reshape(sub_kernels.shape), up, down


def solution(mesh):
    rows = P(("dp", "mp"), None)
    last = P(None, None, None, "mp")
    mid = P(None, "mp", None)
    return jax.shard_map(
        per_device,
        mesh=mesh,
        in_specs=(rows, P("dp", None), P(), P(), last, mid, last, P(None, None, "mp"), mid, rows),
        out_specs=(rows, rows, P(), P(), last, mid, last, P(None, None, "mp"), mid),
        check_vma=False,
    )
```

```python
import functools

import jax
import jax.numpy as jnp
import numpy as np
from jax import lax
from jax.experimental import pallas as pl
from jax.experimental.pallas import tpu as pltpu
from jax.sharding import PartitionSpec as P

DECAY_RATE = 0.5
EPSILON = 1e-05
BF = jnp.bfloat16
F32 = jnp.float32
GROUP = 8
MESH = pl.DeviceIdType.MESH
VMEM = pl.BlockSpec(memory_space=pltpu.VMEM)
ANY = pl.BlockSpec(memory_space=pl.ANY)
GELU_A = float(np.sqrt(2.0 / np.pi))
GELU_B = 0.044715


def dot(a, b):
    return jnp.dot(a, b, preferred_element_type=F32)


def dot_nt(a, b):
    return lax.dot_general(a, b, (((1,), (1,)), ((), ())), preferred_element_type=F32)


def dot_tn(a, b):
    return lax.dot_general(a, b, (((0,), (0,)), ((), ())), preferred_element_type=F32)


def gelu(u):
    return 0.5 * u * (1.0 + jnp.tanh(GELU_A * (u + GELU_B * (u * u * u))))


def gelu_both(u):
    square = u * u
    t = jnp.tanh(GELU_A * (u + GELU_B * (square * u)))
    half = 0.5 * (1.0 + t)
    slope = half + (0.5 * u) * (1.0 - t * t) * (GELU_A + (3.0 * GELU_A * GELU_B) * square)
    return u * half, slope


def loop(count, body):
    lax.fori_loop(0, count, lambda j, c: (body(j), c)[1], 0)


def when(condition, body):
    pl.when(condition)(body)


def rows_of(j, size):
    return pl.ds(pl.multiple_of(j * size, size), size)


def transform_table(quarter):
    freq = np.arange(quarter)[:, None] + 0.5
    angle = np.pi * freq * np.arange(quarter)[None, :] / quarter
    return np.concatenate([np.cos(angle), -np.sin(angle)], axis=0)


def spread_matrix(scales, taps):
    lags = []
    for level in range(scales):
        lags += [level * taps + j for j in range(taps) for _ in range(2 ** max(level, 1))]
    spread = np.zeros((len(lags), scales * taps))
    spread[np.arange(len(lags)), lags] = 1.0
    return spread


def tap_tables(quarter, scales, taps):
    table = transform_table(quarter)
    spread = spread_matrix(scales, taps).reshape(4, quarter, scales * taps)
    return np.einsum("fp,mpt->mft", table, spread)


def tap_scales(scales, taps, channels):
    level = np.repeat(np.arange(scales), taps)
    decay = DECAY_RATE**level
    repeats = 2.0 ** np.maximum(level, 1)
    both = np.stack([decay, repeats])[:, :, None]
    return np.broadcast_to(both, (2, scales * taps, channels)).astype(np.float32)


class Place:
    def __init__(self, n):
        self.n = n
        self.q = lax.axis_index("mp")
        dp = lax.axis_index("dp")
        self.i = lax.rem(dp, GROUP)
        self.base = dp - self.i
        self.core = lax.rem(self.i, 2)
        self.x = lax.rem(self.i // 2, 2)
        self.y = self.i // 4
        self.s = self.x + 2 * self.core

    def device(self, i, q):
        return {"dp": self.base + i, "mp": q}

    def index(self, y, x, core):
        return 4 * y + 2 * x + core

    def column(self, k):
        q = lax.rem(self.q + k, self.n)
        return q, self.device(self.i, q)

    def member(self, k):
        return self.device(lax.rem(self.i + k, GROUP), self.q)

    def mate_x(self):
        i = self.index(self.y, 1 - self.x, self.core)
        return i, self.device(i, self.q)

    def mate_y(self):
        i = self.index(1 - self.y, self.x, self.core)
        return i, self.device(i, self.q)

    def mate_xy(self):
        i = self.index(1 - self.y, 1 - self.x, self.core)
        return i, self.device(i, self.q)

    def mates(self, order):
        return (self.mate_x(), self.mate_y()) if order == "xy" else (self.mate_y(), self.mate_x())

    def sibling(self):
        return self.device(self.index(self.y, self.x, 1 - self.core), self.q)

    def partner(self, k):
        s = lax.rem(self.s + k, self.n)
        return s, self.device(self.index(self.y, lax.rem(s, 2), s // 2), self.q)

    def row_target(self):
        return self.index(self.y, lax.rem(self.q, 2), self.q // 2), 2 * self.core + self.x

    def stays(self):
        i, q = self.row_target()
        return jnp.logical_and(i == self.i, q == self.q)


def greet_all(place):
    barrier = pltpu.get_barrier_semaphore()
    peers = [place.column(k)[1] for k in range(1, place.n)] + [place.member(k) for k in range(1, GROUP)]
    for peer in peers:
        pl.semaphore_signal(barrier, inc=1, device_id=peer, device_id_type=MESH)

    def across():
        other = place.device(*place.row_target())
        pl.semaphore_signal(barrier, inc=1, device_id=other, device_id_type=MESH)
        pl.semaphore_wait(barrier, len(peers) + 1)

    def here():
        pl.semaphore_wait(barrier, len(peers))

    when(jnp.logical_not(place.stays()), across)
    when(place.stays(), here)


def send(src, dst, send_sem, recv_sem, peer):
    pltpu.make_async_remote_copy(
        src_ref=src, dst_ref=dst, send_sem=send_sem, recv_sem=recv_sem, device_id=peer, device_id_type=MESH
    ).start()


def await_bytes(ref, sem):
    pltpu.make_async_copy(ref, ref, sem).wait()


class Move:
    def __init__(self, place, src, dst, relay, sems):
        self.p, self.src, self.dst, self.relay, self.sems = place, src, dst, relay, sems
        p = place
        turn = p.q == 1 + p.core
        self.stays = p.stays()
        self.via = jnp.logical_and(turn, p.x == p.core)
        self.passes = jnp.logical_and(turn, p.x != p.core)
        self.direct = jnp.logical_not(jnp.logical_or(self.stays, self.via))

    def start(self):
        p = self.p

        def across():
            send(self.src, self.dst, self.sems.at[0], self.sems.at[1], p.device(*p.row_target()))

        def aside():
            send(self.src, self.relay, self.sems.at[0], self.sems.at[2], p.mate_x()[1])

        def here():
            pltpu.make_async_copy(self.src, self.dst, self.sems.at[1]).start()

        when(self.direct, across)
        when(self.via, aside)
        when(self.stays, here)

    def pass_on(self):
        p = self.p

        def onward():
            await_bytes(self.relay, self.sems.at[2])
            send(self.relay, self.dst, self.sems.at[3], self.sems.at[1], p.device(p.i, 3 * p.core))

        when(self.passes, onward)

    def arrive(self):
        await_bytes(self.dst, self.sems.at[1])

    def finish(self):
        when(jnp.logical_not(self.stays), lambda: await_bytes(self.src, self.sems.at[0]))
        when(self.passes, lambda: await_bytes(self.relay, self.sems.at[3]))


class Weight:
    def __init__(self, whole, layer, kind, n):
        self.whole, self.kind, self.layer, self.n = whole, kind, layer, n
        shape = whole.shape
        if kind == "in":
            self.rows, self.cols = shape[2] // GROUP, shape[3] // n
        elif kind == "up":
            self.rows, self.cols = shape[1] // GROUP, shape[2] // n
        else:
            self.rows, self.cols = shape[1] // n // GROUP, shape[2]

    def piece(self, i, q):
        r, c = self.rows, self.cols
        if self.kind == "in":
            return self.whole.at[self.layer, :, pl.ds(i * r, r), pl.ds(q * c, c)]
        if self.kind == "up":
            return self.whole.at[self.layer, pl.ds(i * r, r), pl.ds(q * c, c)]
        return self.whole.at[self.layer, pl.ds((q * GROUP + i) * r, r), :]

    def shard(self, q):
        r, c = self.rows, self.cols
        if self.kind == "in":
            return self.whole.at[self.layer, :, :, pl.ds(q * c, c)]
        if self.kind == "up":
            return self.whole.at[self.layer, :, pl.ds(q * c, c)]
        return self.whole.at[self.layer, pl.ds(q * GROUP * r, GROUP * r), :]

    def local_piece(self, shard, i):
        r = self.rows
        if self.kind == "in":
            return shard.at[self.layer, :, pl.ds(i * r, r), :]
        return shard.at[self.layer, pl.ds(i * r, r), :]

    def span(self, members):
        r, c, k = self.rows, self.cols, self.n - 1
        if self.kind == "in":
            return self.whole.at[self.layer, :, pl.ds(0, members * r), pl.ds(0, k * c)]
        if self.kind == "up":
            return self.whole.at[self.layer, pl.ds(0, members * r), pl.ds(0, k * c)]
        return self.whole.at[self.layer, pl.ds(0, members * k * r), :]


class Gather:
    def __init__(self, place, weight, shard, sems, slot, order):
        self.p, self.w, self.shard_ref, self.sems, self.slot, self.order = place, weight, shard, sems, slot, order

    def sem(self, k):
        return self.sems.at[self.slot, k]

    def own(self):
        return pltpu.make_async_copy(
            self.shard_ref.at[self.w.layer], self.w.shard(self.p.q), self.sem(8)
        )

    def start(self):
        p, w = self.p, self.w
        for k in range(1, p.n):
            send(w.local_piece(self.shard_ref, p.i), w.piece(p.i, p.q), self.sem(0), self.sem(1), p.column(k)[1])
        self.own().start()

    def pass_on(self, i, send_sem, recv_sem, peer):
        p, w = self.p, self.w
        for k in range(1, p.n):
            piece = w.piece(i, p.column(k)[0])
            send(piece, piece, send_sem, recv_sem, peer)

    def hop1(self):
        p = self.p
        await_bytes(self.w.span(1), self.sem(1))
        first, second = p.mates(self.order)
        self.pass_on(p.i, self.sem(2), self.sem(3), first[1])
        self.pass_on(p.i, self.sem(4), self.sem(5), second[1])

    def hop2(self):
        first, second = self.p.mates(self.order)
        await_bytes(self.w.span(1), self.sem(3))
        self.pass_on(first[0], self.sem(4), self.sem(5), second[1])

    def hop3(self):
        p = self.p
        await_bytes(self.w.span(2), self.sem(5))
        for i in (p.i, p.mate_x()[0], p.mate_y()[0], p.mate_xy()[0]):
            self.pass_on(i, self.sem(6), self.sem(7), p.sibling())

    def arrive(self):
        self.own().wait()
        await_bytes(self.w.span(4), self.sem(7))

    def finish(self):
        await_bytes(self.w.span(1), self.sem(0))
        await_bytes(self.w.span(1), self.sem(2))
        await_bytes(self.w.span(2), self.sem(4))
        await_bytes(self.w.span(4), self.sem(6))


def norm_strip(v, gain, bias):
    centred = v - jnp.mean(v, axis=-1, keepdims=True)
    variance = jnp.mean(centred * centred, axis=-1, keepdims=True)
    return centred * lax.rsqrt(variance + EPSILON) * gain + bias


def norm_all(src, dst, gain, bias):
    def strip(j):
        r = rows_of(j, 128)
        dst[r, :] = norm_strip(src[r, :], gain, bias).astype(BF)

    loop(dst.shape[0] // 128, strip)


def normal_taps(sub_ref, scale_ref, layer):
    raw = sub_ref[layer] * scale_ref[0]
    total = jnp.sum(raw * raw * scale_ref[1], axis=0, keepdims=True)
    return raw, lax.rsqrt(total + EPSILON)


def make_masks(seg_rows, masks):
    quarter, channels = masks.shape[1:]
    ones = jnp.full((8, channels), 0.125, BF)

    def numbers(n):
        return dot_tn(seg_rows[:, n * quarter : (n + 1) * quarter].astype(BF), ones)

    def put(k, flag):
        masks[k] = jnp.where(flag, 1.0, 0.0).astype(BF)

    long_doc = numbers(1)[0:1, :]
    for n in range(4):
        here = numbers(n)
        put(n, here == long_doc)
        if n in (0, 3):
            for k in range(3):
                doc = jnp.where(long_doc <= k, k + 1.0, float(k))
                put(4 + 2 * k + (n == 3), here == doc)


def make_windows(taps, tap_ref, spec, layer, wins):
    channels = taps.shape[1]
    quarter = wins.shape[3]
    for m in range(4):
        spec[:, m * channels : (m + 1) * channels] = dot(tap_ref[m], taps)

    def strip(j):
        r = rows_of(j, 16)
        s = rows_of(j + quarter // 16, 16)
        sign = (1 - 2 * lax.rem(lax.broadcasted_iota(jnp.int32, (16, channels), 0), 2)).astype(F32)
        for m in range(4):
            here = slice(m * channels, (m + 1) * channels)
            re, im = spec[r, here], spec[s, here]
            if m:
                before = slice((m - 1) * channels, m * channels)
                re, im = re - sign * spec[s, before], im + sign * spec[r, before]
            wins[layer, m, 0, r, :] = re
            wins[layer, m, 1, r, :] = im

    loop(quarter // 16, strip)


def spread_blocks(blocks, masks, out):
    channels = masks.shape[2]
    for n in range(4):
        out[:, n * channels : (n + 1) * channels] = blocks[n] * masks[n]
    for k in range(3):
        out[:, (4 + k) * channels : (5 + k) * channels] = (
            blocks[0] * masks[4 + 2 * k] + blocks[3] * masks[5 + 2 * k]
        )


def join_blocks(parts, r, masks, n):
    channels = masks.shape[2]
    total = parts[:, n * channels : (n + 1) * channels] * masks[n, r, :].astype(F32)
    if n in (0, 3):
        for k in range(3):
            mask = masks[4 + 2 * k + (n == 3), r, :].astype(F32)
            total += parts[:, (4 + k) * channels : (5 + k) * channels] * mask
    return total


def fwd_products(spec, wins, layer, out, channels):
    quarter = wins.shape[3]

    def strip(j):
        r = rows_of(j, 16)
        s = rows_of(j + quarter // 16, 16)
        xs = [(spec[r, n * channels : (n + 1) * channels], spec[s, n * channels : (n + 1) * channels]) for n in range(7)]
        ws = [(wins[layer, m, 0, r, :], wins[layer, m, 1, r, :]) for m in range(4)]
        for n in range(7):
            re = im = None
            for m in range(n + 1 if n < 4 else 1):
                w, x = ws[m], xs[n - m]
                a = w[0] * x[0] - w[1] * x[1]
                b = w[0] * x[1] + w[1] * x[0]
                re, im = (a, b) if re is None else (re + a, im + b)
            out[r, n * channels : (n + 1) * channels] = re.astype(BF)
            out[s, n * channels : (n + 1) * channels] = im.astype(BF)

    loop(quarter // 16, strip)


FORWARD_PLAN = {
    (0, "start"): ("u0.start", "i0.hop1"),
    (0, "ready"): ("tok.pass_on", "i0.hop2", "i0.hop3"),
    (0, "project"): ("o0.start", "d0.start"),
    (0, "sent"): ("i1.start",),
    (0, "gate"): ("seg.pass_on",),
    (0, "came"): ("o1.start", "u1.start", "u0.hop1"),
    (0, "transform"): ("o0.hop1",),
    (0, "returned"): ("u0.hop2", "o0.hop2", "d0.hop1"),
    (0, "back"): ("u0.hop3", "i1.hop1", "cot.start", "o0.hop3"),
    (0, "attach"): ("d0.hop2",),
    (0, "norm"): ("i1.hop2",),
    (0, "widen"): ("u1.hop1",),
    (0, "activate"): ("d0.hop3", "i1.hop3"),
    (0, "narrow"): ("d1.start", "o1.hop1", "u1.hop2"),
    (1, "sent"): ("o1.hop2", "u1.hop3", "d1.hop1", "cot.pass_on"),
    (1, "gate"): ("o1.hop3",),
    (1, "returned"): ("d1.hop2", "d1.hop3"),
}


def forward_kernel(
    n, layers,
    stream_in, segs, gains, biases, subs, scales, cot_h, table_h, table_t_h, tap_table_h, win, wout, wup, wdn,
    out_o, streams_o, hidden_o, gact_o, gslope_o, conv_in_o, conv_out_o, gated_o, middle_o, hidden_mid_o, active_o, slope_o,
    wins_o, masks_o, cot_o, win_o, wout_o, wup_o, wdn_o,
    stream, hidden, gact, gslope, gated, middle, hidden_mid, active, slope, send_a, recv_a, send_b, recv_b,
    spread, spec, spec_y, wins, win_f, wout_f, wup_f, wdn_f,
    masks, tok_s, tok_r, tok_p, cot_in, cot_s, cot_p, seg_s, seg_r, seg_p, taps_s, taps_r, table, table_t, tap_table,
    gather_sems, a2a_sems, save_sems, move_sems, tap_sems, load_sems,
):
    place = Place(n)
    me = place.s
    tokens, width = stream_in.shape
    channels = width // n
    quarter = tokens
    half = wup_f.shape[2] // 2
    loads = [
        pltpu.make_async_copy(src, dst, load_sems.at[k])
        for k, (src, dst) in enumerate(((cot_h, cot_in), (tap_table_h, tap_table), (table_h, table), (table_t_h, table_t)))
    ]
    for copy in loads:
        copy.start()
    greet_all(place)
    saves = []

    def save(src, dst, l=None):
        if l is not None:
            src, dst = src.at[l], dst.at[l]
        copy = pltpu.make_async_copy(src, dst, save_sems.at[len(saves)])
        copy.start()
        saves.append(copy)

    def exchange_start(slot, src, dst, layer):
        for k in range(1, n):
            s, peer = place.partner(k)
            send(src.at[layer, s], dst.at[layer, me], a2a_sems.at[slot, 0], a2a_sems.at[slot, 1], peer)

    def exchange_wait(slot, src, dst, layer):
        await_bytes(src.at[layer, pl.ds(0, n - 1)], a2a_sems.at[slot, 0])
        await_bytes(dst.at[layer, pl.ds(0, n - 1)], a2a_sems.at[slot, 1])

    moving = {
        "seg": Move(place, seg_s, seg_r, seg_p, move_sems.at[0]),
        "tok": Move(place, tok_s, tok_r, tok_p, move_sems.at[1]),
        "cot": Move(place, cot_s, cot_o, cot_p, move_sems.at[2]),
    }
    gathers = {}
    for l in range(layers):
        for kind, whole, shard in (("in", win_f, win), ("out", wout_f, wout), ("up", wup_f, wup), ("down", wdn_f, wdn)):
            gathers[kind[0] + str(l)] = Gather(place, Weight(whole, l, kind, n), shard, gather_sems, len(gathers), "xy")
    moving.update(gathers)

    def visit(l, point):
        for step in FORWARD_PLAN.get((l, point), ()):
            what, action = step.split(".")
            getattr(moving[what], action)()

    gathers["i0"].start()

    def round_stream(j):
        r = rows_of(j, 64)
        tok_s[r, :] = stream_in[r, :].astype(BF)

    loop(tokens // 64, round_stream)
    moving["tok"].start()
    seg_s[...] = jnp.broadcast_to(segs[...].astype(F32), seg_s.shape)
    moving["seg"].start()
    for l in range(layers):
        raw, inverse = normal_taps(subs, scales, l)
        taps_s[l] = (raw * inverse).astype(BF)

    def give_taps():
        for k in range(1, n):
            send(taps_s, taps_r, tap_sems.at[0, k], tap_sems.at[1, k], place.column(k)[1])
        taps_r[...] = taps_s[...]

    def take_taps():
        ahead = lax.rem(place.q - place.s + n, n)
        await_bytes(taps_r, tap_sems.at[1, ahead])

    when(place.s == place.q, give_taps)
    loads[0].wait()

    def round_cotangent(j):
        r = rows_of(j, 64)
        cot_s[r, :] = cot_in[r, :].astype(BF)

    loop(tokens // 64, round_cotangent)
    visit(0, "start")
    visit(0, "ready")
    moving["tok"].arrive()

    def widen_stream(j):
        r = rows_of(j, 64)
        stream[0, r, :] = tok_r[r, :].astype(F32)

    loop(tokens // 64, widen_stream)
    save(stream, streams_o, 0)

    for l in range(layers):
        norm_all(stream.at[l], hidden.at[l], gains[l, 0:1, :], biases[l, 0:1, :])
        gathers["i" + str(l)].arrive()
        got = dot(hidden[l], win_f[l, 0]).astype(BF)
        for s in range(n):
            send_a[l, s] = got[:, s * channels : (s + 1) * channels]
        visit(l, "project")
        exchange_start(2 * l, send_a, recv_a, l)
        recv_a[l, me] = send_a[l, me]
        visit(l, "sent")
        save(hidden, hidden_o, l)
        save(win_f, win_o, l)
        spec[0:tokens, 0:width] = dot(hidden[l], win_f[l, 1])

        def open_gate(j):
            r = rows_of(j, 16)
            act, incline = gelu_both(spec[r, 0:width])
            gact[l, r, :] = act.astype(BF)
            gslope[l, r, :] = incline.astype(BF)

        loop(tokens // 16, open_gate)
        visit(l, "gate")
        save(gact, gact_o, l)
        save(gslope, gslope_o, l)
        if l == 0:
            moving["seg"].arrive()
            make_masks(seg_r, masks)
            save(masks, masks_o)
            when(place.s != place.q, take_taps)
            loads[1].wait()
            for m in range(layers):
                make_windows(taps_r[m], tap_table, spec, m, wins)
            save(wins, wins_o)
            loads[2].wait()
            loads[3].wait()
        exchange_wait(2 * l, send_a, recv_a, l)
        visit(l, "came")
        save(recv_a, conv_in_o, l)
        spread_blocks(recv_a.at[l], masks, spread)
        spec[:, 0 : 7 * channels] = dot(table[...], spread[...])
        visit(l, "transform")
        fwd_products(spec, wins, l, spec_y, channels)

        def untransform(j):
            r = rows_of(j, 256)
            parts = dot(table_t[r, :], spec_y[...])
            for s in range(n):
                send_b[l, s, r, :] = join_blocks(parts, r, masks, s).astype(BF)

        loop(quarter // 256, untransform)
        exchange_start(2 * l + 1, send_b, recv_b, l)
        recv_b[l, me] = send_b[l, me]
        visit(l, "returned")
        exchange_wait(2 * l + 1, send_b, recv_b, l)
        visit(l, "back")
        save(recv_b, conv_out_o, l)

        def mix(j):
            r = rows_of(j, 64)
            for s in range(n):
                c = slice(s * channels, (s + 1) * channels)
                gated[l, r, c] = (gact[l, r, c].astype(F32) * recv_b[l, s, r, :].astype(F32)).astype(BF)

        loop(tokens // 64, mix)
        gathers["o" + str(l)].arrive()
        save(gated, gated_o, l)
        save(wout_f, wout_o, l)
        middle[l] = stream[l] + dot(gated[l], wout_f[l])
        visit(l, "attach")
        save(middle, middle_o, l)
        norm_all(middle.at[l], hidden_mid.at[l], gains[l, 1:2, :], biases[l, 1:2, :])
        visit(l, "norm")
        gathers["u" + str(l)].arrive()
        save(hidden_mid, hidden_mid_o, l)
        save(wup_f, wup_o, l)
        for h in range(2):
            spec[h * tokens : (h + 1) * tokens, :] = dot(hidden_mid[l], wup_f[l, :, h * half : (h + 1) * half])
        visit(l, "widen")

        def activate(j):
            r = rows_of(j, 16)
            for h in range(2):
                t = pl.ds(pl.multiple_of(h * tokens + j * 16, 16), 16)
                act, incline = gelu_both(spec[t, :])
                active[l, r, h * half : (h + 1) * half] = act.astype(BF)
                slope[l, r, h * half : (h + 1) * half] = incline.astype(BF)

        loop(tokens // 16, activate)
        visit(l, "activate")
        save(active, active_o, l)
        save(slope, slope_o, l)
        gathers["d" + str(l)].arrive()
        save(wdn_f, wdn_o, l)
        if l + 1 < layers:
            stream[l + 1] = middle[l] + dot(active[l], wdn_f[l])
            save(stream, streams_o, l + 1)
        else:
            moving["tok"].finish()
            tok_s[...] = (middle[l] + dot(active[l], wdn_f[l])).astype(BF)
            save(tok_s, out_o)
        visit(l, "narrow")
    for g in gathers.values():
        g.finish()
    moving["cot"].arrive()
    for name in ("seg", "cot"):
        moving[name].finish()

    def taps_given():
        for k in range(1, n):
            await_bytes(taps_s, tap_sems.at[0, k])

    when(place.s == place.q, taps_given)
    for copy in saves:
        copy.wait()


def forward(n, stream_in, cotangent, segments, gains, biases, subs, scales, table, table_t, tap_table, win, wout, wup, wdn):
    layers = win.shape[0]
    tokens, width = stream_in.shape
    channels = width // n
    ff = wup.shape[2] * n
    taps = subs.shape[1]

    def sds(*shape, dtype=BF):
        return jax.ShapeDtypeStruct(shape, dtype)

    wshapes = [(layers, 2, width, width), (layers, width, width), (layers, width, ff), (layers, ff, width)]
    wide, blocks = (layers, tokens, width), (layers, n, tokens, channels)
    outs = [
        sds(tokens, width), sds(*wide, dtype=F32), sds(*wide), sds(*wide), sds(*wide), sds(*blocks), sds(*blocks), sds(*wide),
        sds(*wide, dtype=F32), sds(*wide), sds(layers, tokens, ff), sds(layers, tokens, ff),
        sds(layers, 4, 2, tokens, channels, dtype=F32), sds(10, tokens, channels), sds(tokens, width),
    ] + [sds(*s) for s in wshapes]
    f32 = lambda *s: pltpu.VMEM(s, F32)
    bf = lambda *s: pltpu.VMEM(s, BF)
    scratch = [
        f32(*wide), bf(*wide), bf(*wide), bf(*wide), bf(*wide), f32(*wide), bf(*wide), bf(layers, tokens, ff), bf(layers, tokens, ff),
        bf(*blocks), bf(*blocks), bf(*blocks), bf(*blocks),
        bf(tokens, 7 * channels), f32(2 * tokens, ff // 2), bf(2 * tokens, 7 * channels), f32(layers, 4, 2, tokens, channels),
    ] + [bf(*s) for s in wshapes] + [
        bf(10, tokens, channels), bf(tokens, width), bf(tokens, width), bf(tokens, width), f32(tokens, width), bf(tokens, width), bf(tokens, width),
        f32(8, 4 * tokens), f32(8, 4 * tokens), f32(8, 4 * tokens), bf(layers, taps, channels), bf(layers, taps, channels),
        bf(2 * tokens, tokens), bf(tokens, 2 * tokens), bf(4, 2 * tokens, taps),
        pltpu.SemaphoreType.DMA((4 * layers, 9)),
        pltpu.SemaphoreType.DMA((2 * layers, 2)),
        pltpu.SemaphoreType.DMA((15 * layers + 3,)),
        pltpu.SemaphoreType.DMA((3, 4)),
        pltpu.SemaphoreType.DMA((2, n)),
        pltpu.SemaphoreType.DMA((4,)),
    ]
    return pl.pallas_call(
        functools.partial(forward_kernel, n, layers),
        out_shape=outs,
        in_specs=[VMEM] * 6 + [ANY] * 8,
        out_specs=[ANY] * len(outs),
        scratch_shapes=scratch,
        compiler_params=pltpu.CompilerParams(collective_id=1, has_side_effects=True, vmem_limit_bytes=60 * 2**20),
        name="forward",
    )(stream_in, segments, gains, biases, subs, scales, cotangent, table, table_t, tap_table, win, wout, wup, wdn)


PIECE_DOWN, PIECE_UP, PIECE_OUT, PIECE_IN, PIECE_ROWS = 0, 64, 128, 144, 176


def norm_back(upstream, src, base, gain, out, rounded):
    width = src.shape[1]

    def strip(j, sums):
        r = rows_of(j, 128)
        v = src[r, :]
        centred = v - jnp.mean(v, axis=-1, keepdims=True)
        inverse = lax.rsqrt(jnp.mean(centred * centred, axis=-1, keepdims=True) + EPSILON)
        xhat = centred * inverse
        up = upstream[r, :]
        q = gain * up
        both = q - jnp.mean(q, axis=-1, keepdims=True) - xhat * jnp.mean(q * xhat, axis=-1, keepdims=True)
        got = base[r, :] + both * inverse
        out[r, :] = got
        if rounded is not None:
            rounded[r, :] = got.astype(BF)
        p = up * xhat
        first, second = sums
        for k in range(0, 128, 8):
            first, second = first + p[k : k + 8], second + up[k : k + 8]
        return first, second

    zero = jnp.zeros((8, width), F32)
    return lax.fori_loop(0, src.shape[0] // 128, strip, (zero, zero))


def back_products(spec_x, spec_c, wins, out_g, out_d, channels):
    quarter = wins.shape[2]
    half = out_g.shape[1] // 2

    def strip(j):
        r = rows_of(j, 16)
        s = rows_of(j + quarter // 16, 16)
        cols = [slice(n * channels, (n + 1) * channels) for n in range(7)]
        cols2 = [slice(half + n * channels, half + (n + 1) * channels) for n in range(7)]
        cs = [(spec_c[r, c], spec_c[s, c]) for c in cols]
        for n in range(7):
            re = im = None
            for m in range(4 - n if n < 4 else 1):
                w, x = (wins[m, 0, r, :], wins[m, 1, r, :]), cs[n + m]
                a = w[0] * x[0] + w[1] * x[1]
                b = w[0] * x[1] - w[1] * x[0]
                re, im = (a, b) if re is None else (re + a, im + b)
            out_g[r, cols[n]] = re.astype(BF)
            out_g[r, cols2[n]] = im.astype(BF)
        sign = (1 - 2 * lax.rem(lax.broadcasted_iota(jnp.int32, (16, channels), 0), 2)).astype(F32)
        later = None
        for m in (3, 2, 1, 0):
            pairs = [(n - m, n) for n in range(m, 4)] + ([(n, n) for n in range(4, 7)] if m == 0 else [])
            re = im = None
            for i, n in pairs:
                x, c = (spec_x[r, cols[i]], spec_x[s, cols[i]]), cs[n]
                a = x[0] * c[0] + x[1] * c[1]
                b = x[0] * c[1] - x[1] * c[0]
                re, im = (a, b) if re is None else (re + a, im + b)
            dre, dim = (re, im) if later is None else (re + sign * later[1], im - sign * later[0])
            later = (re, im)
            out_d[r, cols[m]] = dre.astype(BF)
            out_d[r, cols2[m]] = dim.astype(BF)

    loop(quarter // 16, strip)


class Reduce:
    def __init__(self, place, bufs, sems, slot, layer, first, rows, order):
        self.p, self.layer, self.slot, self.sems, self.order = place, layer, slot, sems, order
        self.r = pl.ds(first, rows)
        self.first, self.rows = first, rows
        self.grads, self.r0, self.r1, self.r2, self.res = bufs
        self.spare = self.grads.shape[0] - 1

    def sem(self, k):
        return self.sems.at[self.slot, k]

    def strips(self, body):
        step = next(s for s in (80, 64, 32, 16) if self.rows % s == 0)
        loop(self.rows // step, lambda j: body(pl.ds(pl.multiple_of(self.first + j * step, 16), step)))

    def add_to(self, place_of, others, r):
        total = self.grads[(self.layer, *place_of, r, slice(None))].astype(F32)
        for other in others:
            total += other[r, :].astype(F32)
        return total

    def s0(self):
        send(self.grads.at[self.spare, :, :, :, self.r], self.r0.at[self.layer, :, :, :, self.r], self.sem(0), self.sem(1), self.p.sibling())

    def s1(self):
        p, l = self.p, self.layer
        await_bytes(self.r0.at[l, :, :, :, self.r], self.sem(0))
        await_bytes(self.r0.at[l, :, :, :, self.r], self.sem(1))

        def add(j):
            y, x, q = j // (2 * p.n), lax.rem(j // p.n, 2), lax.rem(j, p.n)

            def strip(r):
                self.grads[l, y, x, q, r, :] = self.add_to((y, x, q), [self.r0.at[l, y, x, q]], r).astype(BF)

            self.strips(strip)

        loop(4 * p.n, add)
        if self.order == "yx":
            send(self.grads.at[l, 1 - p.y, :, :, self.r], self.r1.at[l, pl.ds(0, 2), :, self.r], self.sem(2), self.sem(3), p.mate_y()[1])
        elif self.order == "xy":
            send(self.grads.at[l, :, 1 - p.x, :, self.r], self.r1.at[l, pl.ds(0, 2), :, self.r], self.sem(2), self.sem(3), p.mate_x()[1])
        else:
            send(self.grads.at[l, p.y, 1 - p.x, :, self.r], self.r1.at[l, 0, :, self.r], self.sem(2), self.sem(3), p.mate_x()[1])
            send(self.grads.at[l, 1 - p.y, p.x, :, self.r], self.r1.at[l, 1, :, self.r], self.sem(2), self.sem(3), p.mate_y()[1])
            send(self.grads.at[l, 1 - p.y, 1 - p.x, :, self.r], self.r1.at[l, 2, :, self.r], self.sem(2), self.sem(3), p.mate_xy()[1])

    def s1b(self):
        p, l = self.p, self.layer
        both = self.r1.at[l, pl.ds(0, 2), :, self.r]
        await_bytes(both, self.sem(2))
        await_bytes(both, self.sem(3))

        def add(j):
            k, q = j // p.n, lax.rem(j, p.n)
            y, x = (p.y, k) if self.order == "yx" else (k, p.x)

            def strip(r):
                self.grads[l, y, x, q, r, :] = self.add_to((y, x, q), [self.r1.at[l, k, q]], r).astype(BF)

            self.strips(strip)

        loop(2 * p.n, add)
        if self.order == "yx":
            send(self.grads.at[l, p.y, 1 - p.x, :, self.r], self.r1.at[l, 2, :, self.r], self.sem(4), self.sem(5), p.mate_x()[1])
        else:
            send(self.grads.at[l, 1 - p.y, p.x, :, self.r], self.r1.at[l, 2, :, self.r], self.sem(4), self.sem(5), p.mate_y()[1])

    def s2(self):
        p, l = self.p, self.layer
        if self.order == "direct":
            slots = (0, 1, 2)
            await_bytes(self.r1.at[l, :, :, self.r], self.sem(2))
            await_bytes(self.r1.at[l, :, :, self.r], self.sem(3))
        else:
            slots = (2,)
            await_bytes(self.r1.at[l, 2, :, self.r], self.sem(4))
            await_bytes(self.r1.at[l, 2, :, self.r], self.sem(5))

        def add(q):
            def strip(r):
                self.grads[l, p.y, p.x, q, r, :] = self.add_to((p.y, p.x, q), [self.r1.at[l, k, q] for k in slots], r).astype(BF)

            self.strips(strip)

        loop(p.n, add)
        for k in range(1, p.n):
            q, peer = p.column(k)
            send(self.grads.at[l, p.y, p.x, q, self.r], self.r2.at[l, k - 1, self.r], self.sem(6), self.sem(7), peer)

    def s3(self):
        p, l = self.p, self.layer
        await_bytes(self.r2.at[l, :, self.r], self.sem(6))
        await_bytes(self.r2.at[l, :, self.r], self.sem(7))

        def strip(r):
            total = self.add_to((p.y, p.x, p.q), [self.r2.at[l, k] for k in range(p.n - 1)], r)
            self.res[l, p.i, r, :] = total.astype(BF)

        self.strips(strip)
        piece = self.res.at[l, p.i, self.r]
        for mate in (p.mate_x(), p.mate_y(), p.mate_xy()):
            send(piece, piece, self.sem(8), self.sem(9), mate[1])

    def s4(self):
        p, l = self.p, self.layer
        await_bytes(self.res.at[l, pl.ds(0, 3), self.r], self.sem(9))
        for i in (p.i, p.mate_x()[0], p.mate_y()[0], p.mate_xy()[0]):
            piece = self.res.at[l, i, self.r]
            send(piece, piece, self.sem(10), self.sem(11), p.sibling())

    def end(self):
        half = self.res.at[self.layer, pl.ds(0, GROUP // 2), self.r]
        await_bytes(self.res.at[self.layer, pl.ds(0, 3), self.r], self.sem(8))
        await_bytes(half, self.sem(10))
        await_bytes(half, self.sem(11))


def in_order(own, others, l, here, count):
    total = None
    for j in range(count):
        k = lax.rem(here - j + count, count)
        value = jnp.where(k == 0, own.astype(F32), others[l, lax.max(k - 1, 0)].astype(F32))
        total = value if total is None else total + value
    return total


BACKWARD_ORDER = {"d1": "yx", "u1": "direct", "i1": "yx", "d0": "yx", "u0": "yx", "i0": "yx"}
BACKWARD_PLAN = {
    (1, "sent"): ("d1.s1",),
    (1, "out"): ("o1.s1",),
    (1, "returned"): ("u1.s1",),
    (1, "project"): ("kg1.over_mp",),
    (0, "narrow"): ("d1.s1b",),
    (0, "down"): ("i1.s1",),
    (0, "sent"): ("u0.s1",),
    (0, "out"): ("o0.s1", "d1.s2", "i1.s1b", "d0.s1"),
    (0, "transform"): ("out.pass_on",),
    (0, "returned"): ("u1.s2", "kg0.over_mp"),
    (0, "in"): ("i1.s2", "u0.s1b"),
    (0, "end"): ("d1.s3", "i0.s1", "d0.s1b"),
    (0, "tail"): (
        "u0.s2", "u1.s3", "grad.pass_on", "kg0.over_y", "i1.s3", "d1.s4", "d0.s2", "o1.s2", "i0.s1b", "o0.s2", "u0.s3", "d0.s3",
        "i0.s2", "kg0.take", "norm.over_mp", "o0.s3", "o1.s3", "u0.s4", "u1.s4", "i0.s3", "d0.s4", "i1.s4", "o0.s4", "kg1.over_y",
        "o1.s4", "i0.s4", "norm.take", "kg1.take",
    ),
}


class KernelGrad:
    def __init__(self, place, layer, refs, sems):
        self.p, self.l, self.sems = place, layer, sems
        self.own, self.from_mp, self.mid, self.from_y, self.total, self.result = [r.at[layer] for r in refs]
        self.owner = place.s == place.q

    def sem(self, k):
        return self.sems.at[self.l, k]

    def start(self):
        p = self.p
        k = lax.rem(p.q - p.s + p.n, p.n)
        when(
            jnp.logical_not(self.owner),
            lambda: send(self.own, self.from_mp.at[lax.max(k - 1, 0)], self.sem(0), self.sem(1 + k), p.device(p.i, p.s)),
        )

    def over_mp(self):
        p = self.p

        def add():
            total = self.own[...].astype(F32)
            for k in range(1, p.n):
                await_bytes(self.from_mp.at[k - 1], self.sem(1 + k))
                total += self.from_mp[k - 1].astype(F32)
            self.mid[...] = total.astype(BF)
            send(self.mid, self.from_y, self.sem(5), self.sem(6), p.mate_y()[1])

        when(self.owner, add)

    def over_y(self):
        p = self.p

        def add():
            await_bytes(self.from_y, self.sem(6))
            both = (self.mid[...].astype(F32) + self.from_y[...].astype(F32)).astype(BF)
            self.total[...] = both
            self.result[...] = both
            for k in range(1, p.n):
                send(self.total, self.result, self.sem(6 + k), self.sem(9 + k), p.partner(k)[1])

        when(self.owner, add)

    def take(self):
        p = self.p
        k = lax.rem(p.s - p.q + p.n, p.n)
        when(jnp.logical_not(self.owner), lambda: await_bytes(self.result, self.sem(9 + k)))

    def finish(self):
        def given():
            await_bytes(self.mid, self.sem(5))
            for k in range(1, self.p.n):
                await_bytes(self.total, self.sem(6 + k))

        when(self.owner, given)
        when(jnp.logical_not(self.owner), lambda: await_bytes(self.own, self.sem(0)))


class NormGrad:
    def __init__(self, place, refs, sems):
        self.p, self.sems = place, sems
        self.own, self.from_group, self.mid, self.from_mp, self.result = refs
        self.layers = self.own.shape[0]

    def start(self, l):
        for k in range(1, GROUP):
            send(self.own.at[l], self.from_group.at[l, k - 1], self.sems.at[l, 0], self.sems.at[l, 1], self.p.member(k))

    def over_mp(self):
        p = self.p
        for l in reversed(range(self.layers)):
            await_bytes(self.from_group.at[l], self.sems.at[l, 0])
            await_bytes(self.from_group.at[l], self.sems.at[l, 1])
            self.mid[l] = in_order(self.own[l], self.from_group, l, p.i, GROUP)
            for k in range(1, p.n):
                send(self.mid.at[l], self.from_mp.at[l, k - 1], self.sems.at[l, 2], self.sems.at[l, 3], p.column(k)[1])

    def take(self):
        for l in reversed(range(self.layers)):
            await_bytes(self.from_mp.at[l], self.sems.at[l, 2])
            await_bytes(self.from_mp.at[l], self.sems.at[l, 3])
            self.result[l] = in_order(self.mid[l], self.from_mp, l, self.p.q, self.p.n)


def backward_kernel(
    n, layers,
    gains, subs, scales, masks_h, table_h, table_t_h, tap_t_h,
    out_in, cot, streams, hiddens, gacts, gslopes, conv_ins, conv_outs, gateds, middles, hidden_mids, actives, slopes,
    wins_h, win_h, wout_h, wup_h, wdn_h,
    out_o, grad_o, res_o, sub_o, norm_o, out_p, grad_p,
    grad, middle_grad, stream, hidden, gact, gslope, conv_in, conv_out, gated, middle, hidden_mid, active, slope, wins, win, wout, wup, wdn,
    grads, r0, r1, r2, res,
    up_grad, out_grad, branch, joined, big_a, big_b, spread,
    send_c, recv_c, send_d, recv_d, kg_s, kg_z, kg_t, kg_y, kg_u, kg_own, sub_s, masks, table, table_t, tap_t,
    norm_s, norm_r, norm_t, norm_u, norm_v,
    load_sems, a2a_sems, red_sems, kg_sems, norm_sems, out_sems, move_sems,
):
    place = Place(n)
    me, core = place.s, place.core
    tokens, width = grad.shape
    channels = width // n
    quarter = tokens
    ff = wup.shape[1]
    half = ff // 2
    spare = grads.shape[0] - 1
    loads = {}
    sources = {
        "stream": (streams, stream), "hidden": (hiddens, hidden), "gact": (gacts, gact), "gslope": (gslopes, gslope),
        "conv_in": (conv_ins, conv_in), "conv_out": (conv_outs, conv_out), "gated": (gateds, gated), "middle": (middles, middle),
        "hidden_mid": (hidden_mids, hidden_mid), "active": (actives, active), "slope": (slopes, slope), "wins": (wins_h, wins),
        "in": (win_h, win), "out": (wout_h, wout), "up": (wup_h, wup), "down": (wdn_h, wdn),
        "branch": (cot, branch), "masks": (masks_h, masks), "table": (table_h, table), "table_t": (table_t_h, table_t), "tap_t": (tap_t_h, tap_t),
    }
    once = ("branch", "masks", "table", "table_t", "tap_t")

    def load(name, l):
        src, dst = sources[name]
        copy = pltpu.make_async_copy(src if name in once else src.at[l], dst, load_sems.at[l, len([k for k in loads if k[1] == l])])
        copy.start()
        loads[name, l] = copy

    def ready(*names, l):
        for name in names:
            loads[name, l].wait()

    def next_load(*names, l):
        if l:
            for name in names:
                load(name, l - 1)

    top = layers - 1
    for name in (
        "branch", "down", "slope", "up", "active", "hidden_mid", "middle", "out", "gact", "gslope", "conv_out", "gated", "masks",
        "conv_in", "table", "wins", "table_t", "tap_t", "in", "hidden", "stream",
    ):
        load(name, top)
    greet_all(place)
    bufs = (grads, r0, r1, r2, res)
    bounds = (PIECE_DOWN, PIECE_UP, PIECE_OUT, PIECE_IN, PIECE_ROWS)
    groups = {}
    for l in range(layers):
        for k, letter in enumerate("duoi"):
            name = letter + str(l)
            order = BACKWARD_ORDER.get(name, "direct")
            groups[name] = Reduce(place, bufs, red_sems, len(groups), l, bounds[k], bounds[k + 1] - bounds[k], order)
    kernel_grads = [KernelGrad(place, l, (kg_s, kg_z, kg_t, kg_y, kg_u, kg_own), kg_sems) for l in range(layers)]
    norm_grads = NormGrad(place, (norm_s, norm_r, norm_t, norm_u, norm_v), norm_sems)
    out_move = Move(place, out_in, out_o, out_p, move_sems.at[0])
    grad_move = Move(place, branch, grad_o, grad_p, move_sems.at[1])
    moving = {"out": out_move, "grad": grad_move, "norm": norm_grads, **groups}
    moving.update({"kg" + str(l): kernel_grads[l] for l in range(layers)})

    def visit(l, point):
        for step in BACKWARD_PLAN.get((l, point), ()):
            what, action = step.split(".")
            getattr(moving[what], action)()

    def exchange_start(slot, src, dst, l):
        for k in range(1, n):
            s, peer = place.partner(k)
            send(src.at[s], dst.at[me], a2a_sems.at[slot, 0], a2a_sems.at[slot, 1], peer)

    def exchange_wait(slot, src, dst, l):
        await_bytes(src.at[pl.ds(0, n - 1)], a2a_sems.at[slot, 0])
        await_bytes(dst.at[pl.ds(0, n - 1)], a2a_sems.at[slot, 1])

    def holder(parity, l):
        mine = 1 - (parity - core) * (parity - core)
        return l * mine + spare * (1 - mine)

    out_move.start()
    ready("branch", l=top)

    def widen_grad(j):
        r = rows_of(j, 64)
        grad[r, :] = branch[r, :].astype(F32)

    loop(tokens // 64, widen_grad)

    for l in reversed(range(layers)):
        ready("down", "slope", l=l)
        for h in range(2):
            c = slice(h * half, (h + 1) * half)
            big_b[0:tokens, :] = dot_nt(branch[...], wdn[c, :])

            def activate(k):
                s = rows_of(k, 32)
                up_grad[s, c] = (big_b[s, :] * slope[s, c].astype(F32)).astype(BF)

            loop(tokens // 32, activate)
        next_load("down", "slope", l=l)
        visit(l, "activate")
        ready("up", "hidden_mid", "active", l=l)
        big_a[0:tokens, 0:width] = dot_nt(up_grad[...], wup[...])
        next_load("up", l=l)
        visit(l, "narrow")

        def grad_up(c):
            got = dot_tn(hidden_mid[:, rows_of(c, 128)], up_grad[...]).astype(BF)
            for par in range(2):
                for q in range(n):
                    grads[holder(par, l), c // 2, lax.rem(c, 2), q, PIECE_UP:PIECE_OUT, :] = got[par * 64 : par * 64 + 64, q * (ff // n) : (q + 1) * (ff // n)]

        def grad_down(q):
            got = dot_tn(active[:, rows_of(q, ff // n)], branch[...]).astype(BF)
            for i in range(GROUP):
                grads[holder(i % 2, l), i // 4, i // 2 % 2, q, PIECE_DOWN:PIECE_UP, :] = got[i * 64 : (i + 1) * 64]

        def grad_out(q):
            got = dot_tn(gated[:, rows_of(q, channels)], out_grad[...]).astype(BF)
            for i in range(GROUP):
                grads[holder(i % 2, l), i // 4, i // 2 % 2, q, PIECE_OUT:PIECE_IN, :] = got[i * 16 : (i + 1) * 16]

        def grad_in(h):
            def block(c):
                got = dot_tn(hidden[:, rows_of(c, 128)], joined[:, h * width : (h + 1) * width]).astype(BF)
                for par in range(2):
                    for q in range(n):
                        for t in range(2):
                            grads[holder(par, l), c // 2, lax.rem(c, 2), q, PIECE_IN:PIECE_ROWS, h * 256 + t * 128 : h * 256 + (t + 1) * 128] = got[
                                par * 64 + t * 32 : par * 64 + (t + 1) * 32, q * channels : (q + 1) * channels
                            ]

            loop(GROUP // 2, block)

        loop(n, grad_down)
        groups["d" + str(l)].s0()
        visit(l, "down")
        loop(GROUP // 2, grad_up)
        groups["u" + str(l)].s0()
        next_load("hidden_mid", l=l)
        visit(l, "up")
        ready("middle", l=l)
        sums_mid = norm_back(big_a.at[:, 0:width], middle, grad, gains[l, 1:2, :], middle_grad, out_grad)
        next_load("middle", l=l)

        ready("out", l=l)
        big_b[0:tokens, 0:width] = dot_nt(out_grad[...], wout[...])
        next_load("out", l=l)
        visit(l, "open")
        ready("gact", "gslope", "conv_out", l=l)

        def unmix(j):
            r = rows_of(j, 32)
            for s in range(n):
                c = slice(s * channels, (s + 1) * channels)
                up = big_b[r, c]
                send_c[s, r, :] = (up * gact[r, c].astype(F32)).astype(BF)
                joined[r, slice(width + s * channels, width + (s + 1) * channels)] = (
                    up * conv_out[s, r, :].astype(F32) * gslope[r, c].astype(F32)
                ).astype(BF)

        loop(tokens // 32, unmix)
        next_load("gact", "gslope", "conv_out", l=l)
        exchange_start(2 * l, send_c, recv_c, l)
        recv_c[me] = send_c[me]
        visit(l, "sent")
        ready("gated", l=l)
        loop(n, grad_out)
        groups["o" + str(l)].s0()
        next_load("gated", l=l)
        visit(l, "out")
        if l == top:
            ready("masks", "table", l=l)
        ready("conv_in", l=l)
        spread_blocks(conv_in, masks, spread)
        big_a[:, 0 : 7 * channels] = dot(table[...], spread[...])
        next_load("conv_in", l=l)
        visit(l, "transform")
        exchange_wait(2 * l, send_c, recv_c, l)
        spread_blocks(recv_c, masks, spread)
        big_b[:, 0 : 7 * channels] = dot(table[...], spread[...])
        visit(l, "came")
        ready("wins", l=l)
        back_products(big_a, big_b, wins, active, up_grad, channels)
        next_load("wins", l=l)
        visit(l, "products")
        if l == top:
            ready("table_t", "tap_t", l=l)

        def untransform(j):
            r = rows_of(j, 256)
            parts = dot(table_t[r, 0:quarter], active[:, 0 : 7 * channels])
            parts += dot(table_t[r, quarter : 2 * quarter], active[:, half : half + 7 * channels])
            for s in range(n):
                send_d[s, r, :] = join_blocks(parts, r, masks, s).astype(BF)

        loop(quarter // 256, untransform)
        exchange_start(2 * l + 1, send_d, recv_d, l)
        recv_d[me] = send_d[me]
        next_load("active", l=l)

        taps = None
        for m in range(4):
            c = slice(m * channels, (m + 1) * channels)
            d = slice(half + m * channels, half + (m + 1) * channels)
            got = dot(tap_t[m, :, 0:quarter], up_grad[:, c]) + dot(tap_t[m, :, quarter : 2 * quarter], up_grad[:, d])
            taps = got if taps is None else taps + got
        kg_s[l] = taps.astype(BF)
        kernel_grads[l].start()
        visit(l, "returned")
        ready("in", "hidden", "stream", l=l)
        big_a[0:tokens, 0:width] = dot_nt(joined[:, width : 2 * width], win[1])
        grad_in(1)
        visit(l, "in")
        exchange_wait(2 * l + 1, send_d, recv_d, l)

        def collect(j):
            r = rows_of(j, 64)
            for s in range(n):
                joined[r, s * channels : (s + 1) * channels] = recv_d[s, r, :]

        loop(tokens // 64, collect)
        if l == 0:
            grad_in(0)
            groups["i" + str(l)].s0()
        big_a[0:tokens, 0:width] = big_a[0:tokens, 0:width] + dot_nt(joined[:, 0:width], win[0])
        next_load("in", l=l)
        visit(l, "project")
        sums_in = norm_back(big_a.at[:, 0:width], stream, middle_grad, gains[l, 0:1, :], grad, branch)
        next_load("stream", l=l)
        if l == 0:
            grad_move.start()
        else:
            grad_in(0)
            groups["i" + str(l)].s0()
        next_load("hidden", l=l)
        norm_s[l] = jnp.concatenate(
            [jnp.sum(s, axis=0, keepdims=True) for s in (sums_in[0], sums_mid[0], sums_in[1], sums_mid[1])]
            + [jnp.zeros((4, width), F32)],
            axis=0,
        )
        norm_grads.start(l)
        visit(l, "end")

    visit(0, "tail")
    out_norm = pltpu.make_async_copy(norm_v, norm_o, out_sems.at[1])
    out_norm.start()
    for l in range(layers):
        raw, inverse = normal_taps(subs, scales, l)
        k = raw * inverse
        own = kg_own[l].astype(F32)
        along = jnp.sum(own * k, axis=0, keepdims=True)
        sub_s[l] = scales[0] * (own - scales[1] * k * along) * inverse
    out_sub = pltpu.make_async_copy(sub_s, sub_o, out_sems.at[0])
    out_sub.start()
    for group in groups.values():
        group.end()
    out_res = pltpu.make_async_copy(res, res_o, out_sems.at[2])
    out_res.start()
    for m in (out_move, grad_move):
        m.arrive()
        m.finish()
    for g in kernel_grads:
        g.finish()
    out_sub.wait()
    out_norm.wait()
    out_res.wait()


def backward(n, gains, subs, scales, masks, table, table_t, tap_t, out, cot, kept):
    layers, tokens, width = kept[0].shape
    channels = width // n
    ff = kept[-1].shape[1]
    taps = subs.shape[1]

    def sds(*shape, dtype=F32):
        return jax.ShapeDtypeStruct(shape, dtype)

    outs = [
        sds(tokens, width, dtype=BF), sds(tokens, width, dtype=BF), sds(layers, GROUP, PIECE_ROWS, width, dtype=BF),
        sds(layers, taps, channels), sds(layers, 8, width), sds(tokens, width, dtype=BF), sds(tokens, width, dtype=BF),
    ]
    f32 = lambda *s: pltpu.VMEM(s, F32)
    bf = lambda *s: pltpu.VMEM(s, BF)
    wide, blocks, small = (tokens, width), (n, tokens, channels), (layers, taps, channels)
    scratch = [
        f32(*wide), f32(*wide), f32(*wide), bf(*wide), bf(*wide), bf(*wide), bf(*blocks), bf(*blocks), bf(*wide), f32(*wide), bf(*wide),
        bf(tokens, ff), bf(tokens, ff), f32(4, 2, tokens, channels),
        bf(2, width, width), bf(width, width), bf(width, ff), bf(ff, width),
        bf(layers + 1, 2, 2, n, PIECE_ROWS, width),
        bf(layers, 2, 2, n, PIECE_ROWS, width),
        bf(layers, 3, n, PIECE_ROWS, width),
        bf(layers, n - 1, PIECE_ROWS, width),
        bf(layers, GROUP, PIECE_ROWS, width),
        bf(tokens, ff), bf(*wide), bf(*wide), bf(tokens, 2 * width),
        f32(2 * tokens, 7 * channels), f32(2 * tokens, ff // 2), bf(tokens, 7 * channels),
        bf(*blocks), bf(*blocks), bf(*blocks), bf(*blocks),
        bf(*small), bf(layers, n - 1, taps, channels), bf(*small), bf(*small), bf(*small), bf(*small), f32(*small),
        bf(10, tokens, channels), bf(2 * tokens, tokens), bf(tokens, 2 * tokens), bf(4, taps, 2 * tokens),
        f32(layers, 8, width), f32(layers, GROUP - 1, 8, width), f32(layers, 8, width), f32(layers, n - 1, 8, width), f32(layers, 8, width),
        pltpu.SemaphoreType.DMA((layers, 21)),
        pltpu.SemaphoreType.DMA((2 * layers, 2)),
        pltpu.SemaphoreType.DMA((4 * layers, 12)),
        pltpu.SemaphoreType.DMA((layers, 9 + n)),
        pltpu.SemaphoreType.DMA((layers, 4)),
        pltpu.SemaphoreType.DMA((3,)),
        pltpu.SemaphoreType.DMA((2, 4)),
    ]
    return pl.pallas_call(
        functools.partial(backward_kernel, n, layers),
        out_shape=outs,
        in_specs=[VMEM] * 3 + [ANY] * (6 + len(kept)),
        out_specs=[ANY] * len(outs),
        scratch_shapes=scratch,
        compiler_params=pltpu.CompilerParams(collective_id=2, has_side_effects=True, vmem_limit_bytes=int(63.5 * 2**20)),
        name="backward",
    )(gains, subs, scales, masks, table, table_t, tap_t, out, cot, *kept)


def finish_kernel(out_i, grad_i, res, out, grad, up, down, out_w, in_w):
    out[...] = out_i[...].astype(F32)
    grad[...] = grad_i[...].astype(F32)
    members = res.shape[1]
    for i in range(members):
        up[0, i * 64 : (i + 1) * 64, :] = res[0, i, PIECE_UP:PIECE_OUT, :].astype(F32)
        down[0, i * 64 : (i + 1) * 64, :] = res[0, i, PIECE_DOWN:PIECE_UP, :].astype(F32)
        out_w[0, i * 16 : (i + 1) * 16, :] = res[0, i, PIECE_OUT:PIECE_IN, :].astype(F32)
        for h in range(2):
            for t in range(2):
                c = h * 256 + t * 128
                in_w[0, h, i * 64 + t * 32 : i * 64 + (t + 1) * 32, :] = res[0, i, PIECE_IN:, c : c + 128].astype(F32)


def finish(out, grad, res):
    layers, members, _, width = res.shape
    tokens = out.shape[0]
    parts = 2
    m = members // parts
    steps = layers * parts
    rows = tokens // steps

    def sds(*shape):
        return jax.ShapeDtypeStruct(shape, F32)

    flat = pl.BlockSpec((rows, width), lambda j: (j, 0))

    def mid(*shape):
        return pl.BlockSpec((1, *shape, width), lambda j: (j // parts, j % parts, 0))

    return pl.pallas_call(
        finish_kernel,
        grid=(steps,),
        out_shape=[
            sds(tokens, width), sds(tokens, width), sds(layers, members * 64, width), sds(layers, members * 64, width),
            sds(layers, members * 16, width), sds(layers, 2, members * 64, 128),
        ],
        in_specs=[flat, flat, pl.BlockSpec((1, m, PIECE_ROWS, width), lambda j: (j // parts, j % parts, 0, 0))],
        out_specs=[flat, flat, mid(m * 64), mid(m * 64), mid(m * 16), pl.BlockSpec((1, 2, m * 64, 128), lambda j: (j // parts, 0, j % parts, 0))],
        name="finish",
    )(out, grad, res)


def per_device(
    stream_in, segments, norm_gain, norm_bias, w_in, w_out, sub_kernels, w_up, w_down, cotangent
):
    layers, scales, taps, channels = sub_kernels.shape
    n = lax.axis_size("mp")
    quarter = segments.shape[1] // 4
    table = transform_table(quarter)
    tap_table = tap_tables(quarter, scales, taps) / quarter

    def const(a):
        return jnp.asarray(a, F32).astype(BF)

    factors = jnp.asarray(tap_scales(scales, taps, channels))
    subs = sub_kernels.reshape(layers, -1, channels)
    out, *kept, masks, cot, win, wout, wup, wdn = forward(
        n, stream_in, cotangent, segments, norm_gain, norm_bias, subs, factors, const(table), const(table.T), const(tap_table),
        w_in.transpose(0, 2, 1, 3), w_out, w_up, w_down,
    )
    out, grad, res, sub, norms, *_ = backward(
        n, norm_gain, subs, factors, masks, const(table), const(table.T), const(tap_table.transpose(0, 2, 1)),
        out, cot, (*kept, win, wout, wup, wdn),
    )
    if lax.axis_size("dp") > GROUP:
        res, sub, norms = [v * (1.0 / GROUP) for v in lax.psum((res.astype(F32), sub, norms), "dp")]
        res = res.astype(BF)
    out, grad, up, down, out_w, in_w = finish(out, grad, res)
    return (
        out, grad, norms[:, 0:2], norms[:, 2:4], in_w.transpose(0, 2, 1, 3), out_w, sub.reshape(sub_kernels.shape), up, down,
    )


def solution(mesh):
    rows = P(("dp", "mp"), None)
    last = P(None, None, None, "mp")
    mid = P(None, "mp", None)
    return jax.shard_map(
        per_device,
        mesh=mesh,
        in_specs=(rows, P("dp", None), P(), P(), last, mid, last, P(None, None, "mp"), mid, rows),
        out_specs=(rows, rows, P(), P(), last, mid, last, P(None, None, "mp"), mid),
        check_vma=False,
    )
```

```python
import functools

import jax
import jax.numpy as jnp
import numpy as np
from jax import lax
from jax.experimental import pallas as pl
from jax.experimental.pallas import tpu as pltpu
from jax.sharding import PartitionSpec as P

DECAY_RATE = 0.5
EPSILON = 1e-05
BF = jnp.bfloat16
F32 = jnp.float32
GROUP = 8
MESH = pl.DeviceIdType.MESH
VMEM = pl.BlockSpec(memory_space=pltpu.VMEM)
ANY = pl.BlockSpec(memory_space=pl.ANY)
GELU_A = float(np.sqrt(2.0 / np.pi))
GELU_B = 0.044715


def dot(a, b):
    return jnp.dot(a, b, preferred_element_type=F32)


def dot_nt(a, b):
    return lax.dot_general(a, b, (((1,), (1,)), ((), ())), preferred_element_type=F32)


def dot_tn(a, b):
    return lax.dot_general(a, b, (((0,), (0,)), ((), ())), preferred_element_type=F32)


def gelu(u):
    return 0.5 * u * (1.0 + jnp.tanh(GELU_A * (u + GELU_B * (u * u * u))))


def gelu_both(u):
    square = u * u
    t = jnp.tanh(GELU_A * (u + GELU_B * (square * u)))
    half = 0.5 * (1.0 + t)
    slope = half + (0.5 * u) * (1.0 - t * t) * (GELU_A + (3.0 * GELU_A * GELU_B) * square)
    return u * half, slope


def loop(count, body):
    lax.fori_loop(0, count, lambda j, c: (body(j), c)[1], 0)


def when(condition, body):
    pl.when(condition)(body)


def rows_of(j, size):
    return pl.ds(pl.multiple_of(j * size, size), size)


def transform_table(quarter):
    freq = np.arange(quarter)[:, None] + 0.5
    angle = np.pi * freq * np.arange(quarter)[None, :] / quarter
    return np.concatenate([np.cos(angle), -np.sin(angle)], axis=0)


def spread_matrix(scales, taps):
    lags = []
    for level in range(scales):
        lags += [level * taps + j for j in range(taps) for _ in range(2 ** max(level, 1))]
    spread = np.zeros((len(lags), scales * taps))
    spread[np.arange(len(lags)), lags] = 1.0
    return spread


def tap_tables(quarter, scales, taps):
    table = transform_table(quarter)
    spread = spread_matrix(scales, taps).reshape(4, quarter, scales * taps)
    return np.einsum("fp,mpt->mft", table, spread)


def tap_scales(scales, taps, channels):
    level = np.repeat(np.arange(scales), taps)
    decay = DECAY_RATE**level
    repeats = 2.0 ** np.maximum(level, 1)
    both = np.stack([decay, repeats])[:, :, None]
    return np.broadcast_to(both, (2, scales * taps, channels)).astype(np.float32)


class Place:
    def __init__(self, n):
        self.n = n
        self.q = lax.axis_index("mp")
        dp = lax.axis_index("dp")
        self.i = lax.rem(dp, GROUP)
        self.base = dp - self.i
        self.core = lax.rem(self.i, 2)
        self.x = lax.rem(self.i // 2, 2)
        self.y = self.i // 4
        self.s = lax.rem(self.q, 2) + 2 * self.core

    def device(self, i, q):
        return {"dp": self.base + i, "mp": q}

    def index(self, y, x, core):
        return 4 * y + 2 * x + core

    def column(self, k):
        q = lax.rem(self.q + k, self.n)
        return q, self.device(self.i, q)

    def member(self, k):
        return self.device(lax.rem(self.i + k, GROUP), self.q)

    def mate_x(self):
        i = self.index(self.y, 1 - self.x, self.core)
        return i, self.device(i, self.q)

    def mate_y(self):
        i = self.index(1 - self.y, self.x, self.core)
        return i, self.device(i, self.q)

    def mate_xy(self):
        i = self.index(1 - self.y, 1 - self.x, self.core)
        return i, self.device(i, self.q)

    def mates(self, order):
        return (self.mate_x(), self.mate_y()) if order == "xy" else (self.mate_y(), self.mate_x())

    def sibling(self):
        return self.device(self.index(self.y, self.x, 1 - self.core), self.q)

    def partner(self, k):
        s = lax.rem(self.s + k, self.n)
        return s, self.device(self.index(self.y, self.x, s // 2), 2 * (self.q // 2) + lax.rem(s, 2))

    def row_target(self):
        return self.device(self.index(self.y, self.x, self.q // 2), 2 * self.core + lax.rem(self.q, 2))

    def opposite(self):
        return self.device(self.i, lax.rem(self.q + 2, self.n))

    def stays(self):
        return self.q // 2 == self.core


def greet_all(place):
    barrier = pltpu.get_barrier_semaphore()
    peers = [place.column(k)[1] for k in range(1, place.n)] + [place.member(k) for k in range(1, GROUP)]
    across = place.index(place.y, place.x, 1 - place.core)
    peers += [place.device(across, place.column(k)[0]) for k in range(1, place.n)]
    for peer in peers:
        pl.semaphore_signal(barrier, inc=1, device_id=peer, device_id_type=MESH)
    pl.semaphore_wait(barrier, len(peers))


def send(src, dst, send_sem, recv_sem, peer):
    pltpu.make_async_remote_copy(
        src_ref=src, dst_ref=dst, send_sem=send_sem, recv_sem=recv_sem, device_id=peer, device_id_type=MESH
    ).start()


def await_bytes(ref, sem):
    pltpu.make_async_copy(ref, ref, sem).wait()


class Move:
    def __init__(self, place, src, dst, sems):
        self.p, self.src, self.dst, self.sems = place, src, dst, sems

    def start(self):
        p = self.p
        when(jnp.logical_not(p.stays()), lambda: send(self.src, self.dst, self.sems.at[0], self.sems.at[1], p.row_target()))
        when(p.stays(), lambda: pltpu.make_async_copy(self.src, self.dst, self.sems.at[1]).start())

    def arrive(self):
        await_bytes(self.dst, self.sems.at[1])

    def finish(self):
        when(jnp.logical_not(self.p.stays()), lambda: await_bytes(self.src, self.sems.at[0]))


class Weight:
    def __init__(self, whole, layer, kind, n):
        self.whole, self.kind, self.layer, self.n = whole, kind, layer, n
        shape = whole.shape
        if kind == "in":
            self.rows, self.cols = shape[2] // GROUP, shape[3] // n
        elif kind == "up":
            self.rows, self.cols = shape[1] // GROUP, shape[2] // n
        else:
            self.rows, self.cols = shape[1] // n // GROUP, shape[2]

    def piece(self, i, q):
        r, c = self.rows, self.cols
        if self.kind == "in":
            return self.whole.at[self.layer, :, pl.ds(i * r, r), pl.ds(q * c, c)]
        if self.kind == "up":
            return self.whole.at[self.layer, pl.ds(i * r, r), pl.ds(q * c, c)]
        return self.whole.at[self.layer, pl.ds((q * GROUP + i) * r, r), :]

    def shard(self, q):
        r, c = self.rows, self.cols
        if self.kind == "in":
            return self.whole.at[self.layer, :, :, pl.ds(q * c, c)]
        if self.kind == "up":
            return self.whole.at[self.layer, :, pl.ds(q * c, c)]
        return self.whole.at[self.layer, pl.ds(q * GROUP * r, GROUP * r), :]

    def local_piece(self, shard, i):
        r = self.rows
        if self.kind == "in":
            return shard.at[self.layer, :, pl.ds(i * r, r), :]
        return shard.at[self.layer, pl.ds(i * r, r), :]

    def span(self, members):
        r, c, k = self.rows, self.cols, self.n - 1
        if self.kind == "in":
            return self.whole.at[self.layer, :, pl.ds(0, members * r), pl.ds(0, k * c)]
        if self.kind == "up":
            return self.whole.at[self.layer, pl.ds(0, members * r), pl.ds(0, k * c)]
        return self.whole.at[self.layer, pl.ds(0, members * k * r), :]


class Gather:
    def __init__(self, place, weight, shard, sems, slot, order):
        self.p, self.w, self.shard_ref, self.sems, self.slot, self.order = place, weight, shard, sems, slot, order

    def sem(self, k):
        return self.sems.at[self.slot, k]

    def own(self):
        return pltpu.make_async_copy(
            self.shard_ref.at[self.w.layer], self.w.shard(self.p.q), self.sem(8)
        )

    def start(self):
        p, w = self.p, self.w
        for k in range(1, p.n):
            send(w.local_piece(self.shard_ref, p.i), w.piece(p.i, p.q), self.sem(0), self.sem(1), p.column(k)[1])
        self.own().start()

    def pass_on(self, i, send_sem, recv_sem, peer):
        p, w = self.p, self.w
        for k in range(1, p.n):
            piece = w.piece(i, p.column(k)[0])
            send(piece, piece, send_sem, recv_sem, peer)

    def first_second(self):
        return self.p.mates("yx" if self.order == "yx" else "xy")

    def hop1(self):
        p = self.p
        await_bytes(self.w.span(1), self.sem(1))
        first, second = self.first_second()
        self.pass_on(p.i, self.sem(2), self.sem(3), first[1])
        self.pass_on(p.i, self.sem(4), self.sem(5), second[1])
        if self.order == "direct":
            self.pass_on(p.i, self.sem(4), self.sem(5), p.mate_xy()[1])
        self.pass_on(p.i, self.sem(6), self.sem(7), p.sibling())

    def hop2(self):
        first, second = self.first_second()
        await_bytes(self.w.span(1), self.sem(3))
        self.pass_on(first[0], self.sem(4), self.sem(5), second[1])
        self.pass_on(first[0], self.sem(6), self.sem(7), self.p.sibling())

    def hop3(self):
        p = self.p
        first, second = self.first_second()
        others = [second[0], p.mate_xy()[0]]
        if self.order == "direct":
            await_bytes(self.w.span(1), self.sem(3))
            others.append(first[0])
        await_bytes(self.w.span(2), self.sem(5))
        for i in others:
            self.pass_on(i, self.sem(6), self.sem(7), p.sibling())

    def arrive(self):
        self.own().wait()
        await_bytes(self.w.span(4), self.sem(7))

    def finish(self):
        await_bytes(self.w.span(1), self.sem(0))
        await_bytes(self.w.span(1), self.sem(2))
        await_bytes(self.w.span(2), self.sem(4))
        await_bytes(self.w.span(4), self.sem(6))


def norm_strip(v, gain, bias):
    centred = v - jnp.mean(v, axis=-1, keepdims=True)
    variance = jnp.mean(centred * centred, axis=-1, keepdims=True)
    return centred * lax.rsqrt(variance + EPSILON) * gain + bias


def norm_all(src, dst, gain, bias):
    def strip(j):
        r = rows_of(j, 128)
        dst[r, :] = norm_strip(src[r, :], gain, bias).astype(BF)

    loop(dst.shape[0] // 128, strip)


def normal_taps(sub_ref, scale_ref, layer):
    raw = sub_ref[layer] * scale_ref[0]
    total = jnp.sum(raw * raw * scale_ref[1], axis=0, keepdims=True)
    return raw, lax.rsqrt(total + EPSILON)


def make_masks(segs, masks):
    quarter, channels = masks.shape[1:]
    ones = jnp.full((8, channels), 0.125, BF)

    def numbers(n):
        row = segs[:, n * quarter : (n + 1) * quarter].astype(F32)
        return dot_tn(jnp.broadcast_to(row, (8, quarter)).astype(BF), ones)

    def put(k, flag):
        masks[k] = jnp.where(flag, 1.0, 0.0).astype(BF)

    long_doc = numbers(1)[0:1, :]
    for n in range(4):
        here = numbers(n)
        put(n, here == long_doc)
        if n in (0, 3):
            for k in range(3):
                doc = jnp.where(long_doc <= k, k + 1.0, float(k))
                put(4 + 2 * k + (n == 3), here == doc)


def make_windows(taps, tap_ref, spec, layer, wins):
    channels = taps.shape[1]
    quarter = wins.shape[3]
    for m in range(4):
        spec[:, m * channels : (m + 1) * channels] = dot(tap_ref[m], taps)

    def strip(j):
        r = rows_of(j, 16)
        s = rows_of(j + quarter // 16, 16)
        sign = (1 - 2 * lax.rem(lax.broadcasted_iota(jnp.int32, (16, channels), 0), 2)).astype(F32)
        for m in range(4):
            here = slice(m * channels, (m + 1) * channels)
            re, im = spec[r, here], spec[s, here]
            if m:
                before = slice((m - 1) * channels, m * channels)
                re, im = re - sign * spec[s, before], im + sign * spec[r, before]
            wins[layer, m, 0, r, :] = re
            wins[layer, m, 1, r, :] = im

    loop(quarter // 16, strip)


def spread_blocks(blocks, masks, out):
    channels = masks.shape[2]
    for n in range(4):
        out[:, n * channels : (n + 1) * channels] = blocks[n] * masks[n]
    for k in range(3):
        out[:, (4 + k) * channels : (5 + k) * channels] = (
            blocks[0] * masks[4 + 2 * k] + blocks[3] * masks[5 + 2 * k]
        )


def join_blocks(parts, r, masks, n):
    channels = masks.shape[2]
    total = parts[:, n * channels : (n + 1) * channels] * masks[n, r, :].astype(F32)
    if n in (0, 3):
        for k in range(3):
            mask = masks[4 + 2 * k + (n == 3), r, :].astype(F32)
            total += parts[:, (4 + k) * channels : (5 + k) * channels] * mask
    return total


def fwd_products(spec, wins, layer, out, channels):
    quarter = wins.shape[3]

    def strip(j):
        r = rows_of(j, 16)
        s = rows_of(j + quarter // 16, 16)
        xs = [(spec[r, n * channels : (n + 1) * channels], spec[s, n * channels : (n + 1) * channels]) for n in range(7)]
        ws = [(wins[layer, m, 0, r, :], wins[layer, m, 1, r, :]) for m in range(4)]
        for n in range(7):
            re = im = None
            for m in range(n + 1 if n < 4 else 1):
                w, x = ws[m], xs[n - m]
                a = w[0] * x[0] - w[1] * x[1]
                b = w[0] * x[1] + w[1] * x[0]
                re, im = (a, b) if re is None else (re + a, im + b)
            out[r, n * channels : (n + 1) * channels] = re.astype(BF)
            out[s, n * channels : (n + 1) * channels] = im.astype(BF)

    loop(quarter // 16, strip)


FORWARD_ORDER = {"d0": "direct", "d1": "direct", "i0": "direct", "i1": "direct", "o0": "xy", "o1": "direct", "u0": "direct", "u1": "direct"}
FORWARD_PLAN = {
    (0, "start"): ("o0.start", "i0.hop1", "u0.start"),
    (0, "start2"): ("i0.hop3",),
    (0, "sent"): ("d0.start", "i1.start"),
    (0, "gate"): ("o0.hop1",),
    (0, "win0"): ("o0.hop2", "u0.hop1"),
    (0, "win1"): ("o0.hop3",),
    (0, "came"): ("d0.hop1",),
    (0, "returned"): ("u0.hop3", "d1.start", "u1.start", "i1.hop1", "o1.start"),
    (0, "widen"): ("d0.hop3",),
    (0, "narrow"): ("i1.hop3",),
    (1, "normed"): ("u1.hop1",),
    (1, "sent"): ("cot.start",),
    (1, "gate"): ("o1.hop1",),
    (1, "transform"): ("d1.hop1",),
    (1, "returned"): ("u1.hop3", "o1.hop3"),
    (1, "widen"): ("d1.hop3",),
}


def forward_kernel(
    n, layers,
    stream_in, segs, gains, biases, subs, scales, cot_h, table_h, table_t_h, tap_table_h, win, wout, wup, wdn,
    out_o, streams_o, hidden_o, gact_o, gslope_o, conv_in_o, conv_out_o, gated_o, middle_o, hidden_mid_o, active_o, slope_o,
    wins_o, masks_o, cot_o, win_o, wout_o, wup_o, wdn_o,
    stream, hidden, gact, gslope, gated, middle, hidden_mid, active, slope, send_a, recv_a, send_b, recv_b,
    spread, spec, spec_y, wins, win_f, wout_f, wup_f, wdn_f,
    masks, tok_s, tok_r, cot_in, cot_s, seg_r, taps_s, taps_r, table, table_t, tap_table,
    gather_sems, a2a_sems, save_sems, move_sems, tap_sems, load_sems,
):
    place = Place(n)
    me = place.s
    tokens, width = stream_in.shape
    channels = width // n
    quarter = tokens
    half = wup_f.shape[2] // 2
    loads = [
        pltpu.make_async_copy(src, dst, load_sems.at[k])
        for k, (src, dst) in enumerate(((cot_h, cot_in), (tap_table_h, tap_table), (table_h, table), (table_t_h, table_t)))
    ]
    greet_all(place)
    saves = []

    def save(src, dst, l=None):
        if l is not None:
            src, dst = src.at[l], dst.at[l]
        copy = pltpu.make_async_copy(src, dst, save_sems.at[len(saves)])
        copy.start()
        saves.append(copy)

    def exchange_start(slot, src, dst, layer, rows=None):
        rows = pl.ds(0, tokens) if rows is None else rows
        for k in range(1, n):
            s, peer = place.partner(k)
            send(src.at[layer, s, rows], dst.at[layer, me, rows], a2a_sems.at[slot, 0], a2a_sems.at[slot, 1], peer)

    def exchange_wait(slot, src, dst, layer):
        await_bytes(src.at[layer, pl.ds(0, n - 1)], a2a_sems.at[slot, 0])
        await_bytes(dst.at[layer, pl.ds(0, n - 1)], a2a_sems.at[slot, 1])

    moving = {
        "seg": Move(place, segs, seg_r, move_sems.at[0]),
        "tok": Move(place, tok_s, tok_r, move_sems.at[1]),
        "cot": Move(place, cot_s, cot_o, move_sems.at[2]),
    }
    gathers = {}
    for l in range(layers):
        for kind, whole, shard in (("in", win_f, win), ("out", wout_f, wout), ("up", wup_f, wup), ("down", wdn_f, wdn)):
            name = kind[0] + str(l)
            gathers[name] = Gather(place, Weight(whole, l, kind, n), shard, gather_sems, len(gathers), FORWARD_ORDER.get(name, "xy"))
    moving.update(gathers)

    def visit(l, point):
        for step in FORWARD_PLAN.get((l, point), ()):
            what, action = step.split(".")
            getattr(moving[what], action)()

    gathers["i0"].start()

    def round_stream(j):
        r = rows_of(j, 64)
        tok_s[r, :] = stream_in[r, :].astype(BF)

    loop(tokens // 64, round_stream)
    moving["tok"].start()
    moving["seg"].start()
    for l in range(layers):
        raw, inverse = normal_taps(subs, scales, l)
        taps_s[l] = (raw * inverse).astype(BF)

    def give_taps():
        send(taps_s, taps_r, tap_sems.at[0], tap_sems.at[1], place.opposite())

    def keep_taps():
        taps_r[...] = taps_s[...]

    def take_taps():
        await_bytes(taps_r, tap_sems.at[1])

    own_taps = place.s == place.q
    when(own_taps, give_taps)
    for copy in loads:
        copy.start()
    when(own_taps, keep_taps)
    visit(0, "start")
    loads[0].wait()

    def round_cotangent(j):
        r = rows_of(j, 64)
        cot_s[r, :] = cot_in[r, :].astype(BF)

    loop(tokens // 64, round_cotangent)
    visit(0, "start2")
    visit(0, "ready")
    moving["tok"].arrive()

    def widen_stream(j):
        r = rows_of(j, 64)
        stream[0, r, :] = tok_r[r, :].astype(F32)

    loop(tokens // 64, widen_stream)
    save(stream, streams_o, 0)

    for l in range(layers):
        norm_all(stream.at[l], hidden.at[l], gains[l, 0:1, :], biases[l, 0:1, :])
        visit(l, "normed")
        gathers["i" + str(l)].arrive()
        got = dot(hidden[l], win_f[l, 0]).astype(BF)
        for s in range(n):
            send_a[l, s] = got[:, s * channels : (s + 1) * channels]
        visit(l, "project")
        exchange_start(2 * l, send_a, recv_a, l)
        recv_a[l, me] = send_a[l, me]
        visit(l, "sent")
        save(hidden, hidden_o, l)
        save(win_f, win_o, l)
        spec[0:tokens, 0:width] = dot(hidden[l], win_f[l, 1])
        visit(l, "gate0")

        def open_gate(j):
            r = rows_of(j, 16)
            act, incline = gelu_both(spec[r, 0:width])
            gact[l, r, :] = act.astype(BF)
            gslope[l, r, :] = incline.astype(BF)

        loop(tokens // 16, open_gate)
        visit(l, "gate")
        save(gact, gact_o, l)
        save(gslope, gslope_o, l)
        if l == 0:
            moving["seg"].arrive()
            make_masks(seg_r, masks)
            save(masks, masks_o)
            visit(l, "masks")
            when(jnp.logical_not(own_taps), take_taps)
            loads[1].wait()
            for m in range(layers):
                make_windows(taps_r[m], tap_table, spec, m, wins)
                visit(l, "win" + str(m))
            save(wins, wins_o)
            loads[2].wait()
            loads[3].wait()
        exchange_wait(2 * l, send_a, recv_a, l)
        visit(l, "came")
        save(recv_a, conv_in_o, l)
        spread_blocks(recv_a.at[l], masks, spread)
        spec[:, 0 : 7 * channels] = dot(table[...], spread[...])
        visit(l, "transform")
        fwd_products(spec, wins, l, spec_y, channels)
        visit(l, "prod")
        for j in range(2):
            r = slice(j * (quarter // 2), (j + 1) * (quarter // 2))
            parts = dot(table_t[r, :], spec_y[...])
            for s in range(n):
                send_b[l, s, r, :] = join_blocks(parts, r, masks, s).astype(BF)
            exchange_start(2 * l + 1, send_b, recv_b, l, pl.ds(j * (quarter // 2), quarter // 2))
            if j == 0:
                visit(l, "untr")
        recv_b[l, me] = send_b[l, me]
        visit(l, "returned")
        exchange_wait(2 * l + 1, send_b, recv_b, l)
        visit(l, "back")
        save(recv_b, conv_out_o, l)

        def mix(j):
            r = rows_of(j, 64)
            for s in range(n):
                c = slice(s * channels, (s + 1) * channels)
                gated[l, r, c] = (gact[l, r, c].astype(F32) * recv_b[l, s, r, :].astype(F32)).astype(BF)

        loop(tokens // 64, mix)
        visit(l, "mix")
        gathers["o" + str(l)].arrive()
        save(gated, gated_o, l)
        save(wout_f, wout_o, l)
        middle[l] = stream[l] + dot(gated[l], wout_f[l])
        visit(l, "attach")
        save(middle, middle_o, l)
        norm_all(middle.at[l], hidden_mid.at[l], gains[l, 1:2, :], biases[l, 1:2, :])
        visit(l, "norm")
        gathers["u" + str(l)].arrive()
        save(hidden_mid, hidden_mid_o, l)
        save(wup_f, wup_o, l)
        for h in range(2):
            spec[h * tokens : (h + 1) * tokens, :] = dot(hidden_mid[l], wup_f[l, :, h * half : (h + 1) * half])
            visit(l, ("widen0", "widen")[h])

        for h in range(2):

            def activate(j):
                r = rows_of(j, 16)
                act, incline = gelu_both(spec[pl.ds(pl.multiple_of(h * tokens + j * 16, 16), 16), :])
                active[l, r, h * half : (h + 1) * half] = act.astype(BF)
                slope[l, r, h * half : (h + 1) * half] = incline.astype(BF)

            loop(tokens // 16, activate)
            visit(l, ("act0", "activate")[h])
        save(active, active_o, l)
        save(slope, slope_o, l)
        gathers["d" + str(l)].arrive()
        save(wdn_f, wdn_o, l)
        if l + 1 < layers:
            stream[l + 1] = middle[l] + dot(active[l], wdn_f[l])
            save(stream, streams_o, l + 1)
        else:
            moving["tok"].finish()
            tok_s[...] = (middle[l] + dot(active[l], wdn_f[l])).astype(BF)
            save(tok_s, out_o)
        visit(l, "narrow")
    for g in gathers.values():
        g.finish()
    moving["cot"].arrive()
    for name in ("seg", "cot"):
        moving[name].finish()

    when(own_taps, lambda: await_bytes(taps_s, tap_sems.at[0]))
    for copy in saves:
        copy.wait()


def forward(n, stream_in, cotangent, segments, gains, biases, subs, scales, table, table_t, tap_table, win, wout, wup, wdn):
    layers = win.shape[0]
    tokens, width = stream_in.shape
    channels = width // n
    ff = wup.shape[2] * n
    taps = subs.shape[1]

    def sds(*shape, dtype=BF):
        return jax.ShapeDtypeStruct(shape, dtype)

    wshapes = [(layers, 2, width, width), (layers, width, width), (layers, width, ff), (layers, ff, width)]
    wide, blocks = (layers, tokens, width), (layers, n, tokens, channels)
    outs = [
        sds(tokens, width), sds(*wide, dtype=F32), sds(*wide), sds(*wide), sds(*wide), sds(*blocks), sds(*blocks), sds(*wide),
        sds(*wide, dtype=F32), sds(*wide), sds(layers, tokens, ff), sds(layers, tokens, ff),
        sds(layers, 4, 2, tokens, channels, dtype=F32), sds(10, tokens, channels), sds(tokens, width),
    ] + [sds(*s) for s in wshapes]
    f32 = lambda *s: pltpu.VMEM(s, F32)
    bf = lambda *s: pltpu.VMEM(s, BF)
    scratch = [
        f32(*wide), bf(*wide), bf(*wide), bf(*wide), bf(*wide), f32(*wide), bf(*wide), bf(layers, tokens, ff), bf(layers, tokens, ff),
        bf(*blocks), bf(*blocks), bf(*blocks), bf(*blocks),
        bf(tokens, 7 * channels), f32(2 * tokens, ff // 2), bf(2 * tokens, 7 * channels), f32(layers, 4, 2, tokens, channels),
    ] + [bf(*s) for s in wshapes] + [
        bf(10, tokens, channels), bf(tokens, width), bf(tokens, width), f32(tokens, width), bf(tokens, width),
        pltpu.VMEM(segments.shape, segments.dtype), bf(layers, taps, channels), bf(layers, taps, channels),
        bf(2 * tokens, tokens), bf(tokens, 2 * tokens), bf(4, 2 * tokens, taps),
        pltpu.SemaphoreType.DMA((4 * layers, 9)),
        pltpu.SemaphoreType.DMA((2 * layers, 2)),
        pltpu.SemaphoreType.DMA((15 * layers + 3,)),
        pltpu.SemaphoreType.DMA((3, 2)),
        pltpu.SemaphoreType.DMA((2,)),
        pltpu.SemaphoreType.DMA((4,)),
    ]
    return pl.pallas_call(
        functools.partial(forward_kernel, n, layers),
        out_shape=outs,
        in_specs=[VMEM] * 6 + [ANY] * 8,
        out_specs=[ANY] * len(outs),
        scratch_shapes=scratch,
        compiler_params=pltpu.CompilerParams(collective_id=1, has_side_effects=True, vmem_limit_bytes=60 * 2**20),
        name="forward",
    )(stream_in, segments, gains, biases, subs, scales, cotangent, table, table_t, tap_table, win, wout, wup, wdn)


PIECE_DOWN, PIECE_UP, PIECE_OUT, PIECE_IN, PIECE_ROWS = 0, 64, 128, 144, 176


def norm_back(upstream, src, base, gain, out, rounded):
    width = src.shape[1]

    def strip(j, sums):
        r = rows_of(j, 128)
        v = src[r, :]
        centred = v - jnp.mean(v, axis=-1, keepdims=True)
        inverse = lax.rsqrt(jnp.mean(centred * centred, axis=-1, keepdims=True) + EPSILON)
        xhat = centred * inverse
        up = upstream[r, :]
        q = gain * up
        both = q - jnp.mean(q, axis=-1, keepdims=True) - xhat * jnp.mean(q * xhat, axis=-1, keepdims=True)
        got = base[r, :] + both * inverse
        out[r, :] = got
        if rounded is not None:
            rounded[r, :] = got.astype(BF)
        p = up * xhat
        first, second = sums
        for k in range(0, 128, 8):
            first, second = first + p[k : k + 8], second + up[k : k + 8]
        return first, second

    zero = jnp.zeros((8, width), F32)
    return lax.fori_loop(0, src.shape[0] // 128, strip, (zero, zero))


def back_products(spec_x, spec_c, wins, out_g, out_d, channels):
    quarter = wins.shape[2]
    half = out_g.shape[1] // 2

    def strip(j):
        r = rows_of(j, 16)
        s = rows_of(j + quarter // 16, 16)
        cols = [slice(n * channels, (n + 1) * channels) for n in range(7)]
        cols2 = [slice(half + n * channels, half + (n + 1) * channels) for n in range(7)]
        cs = [(spec_c[r, c], spec_c[s, c]) for c in cols]
        for n in range(7):
            re = im = None
            for m in range(4 - n if n < 4 else 1):
                w, x = (wins[m, 0, r, :], wins[m, 1, r, :]), cs[n + m]
                a = w[0] * x[0] + w[1] * x[1]
                b = w[0] * x[1] - w[1] * x[0]
                re, im = (a, b) if re is None else (re + a, im + b)
            out_g[r, cols[n]] = re.astype(BF)
            out_g[r, cols2[n]] = im.astype(BF)
        sign = (1 - 2 * lax.rem(lax.broadcasted_iota(jnp.int32, (16, channels), 0), 2)).astype(F32)
        later = None
        for m in (3, 2, 1, 0):
            pairs = [(n - m, n) for n in range(m, 4)] + ([(n, n) for n in range(4, 7)] if m == 0 else [])
            re = im = None
            for i, n in pairs:
                x, c = (spec_x[r, cols[i]], spec_x[s, cols[i]]), cs[n]
                a = x[0] * c[0] + x[1] * c[1]
                b = x[0] * c[1] - x[1] * c[0]
                re, im = (a, b) if re is None else (re + a, im + b)
            dre, dim = (re, im) if later is None else (re + sign * later[1], im - sign * later[0])
            later = (re, im)
            out_d[r, cols[m]] = dre.astype(BF)
            out_d[r, cols2[m]] = dim.astype(BF)

    loop(quarter // 16, strip)


class Reduce:
    def __init__(self, place, bufs, sems, slot, layer, first, rows, order):
        self.p, self.layer, self.slot, self.sems, self.order = place, layer, slot, sems, order
        self.r = pl.ds(first, rows)
        self.first, self.rows = first, rows
        self.grads, self.r0, self.r1, self.r2, self.res = bufs
        self.spare = self.grads.shape[0] - 1

    def sem(self, k):
        return self.sems.at[self.slot, k]

    def strips(self, body):
        step = next(s for s in (80, 64, 32, 16) if self.rows % s == 0)
        loop(self.rows // step, lambda j: body(pl.ds(pl.multiple_of(self.first + j * step, 16), step)))

    def add_to(self, place_of, others, r):
        total = self.grads[(self.layer, *place_of, r, slice(None))].astype(F32)
        for other in others:
            total += other[r, :].astype(F32)
        return total

    def s0(self):
        send(self.grads.at[self.spare, :, :, :, self.r], self.r0.at[self.layer, :, :, :, self.r], self.sem(0), self.sem(1), self.p.sibling())

    def s1(self):
        p, l = self.p, self.layer
        await_bytes(self.r0.at[l, :, :, :, self.r], self.sem(0))
        await_bytes(self.r0.at[l, :, :, :, self.r], self.sem(1))

        def add(j):
            y, x, q = j // (2 * p.n), lax.rem(j // p.n, 2), lax.rem(j, p.n)

            def strip(r):
                self.grads[l, y, x, q, r, :] = self.add_to((y, x, q), [self.r0.at[l, y, x, q]], r).astype(BF)

            self.strips(strip)

        loop(4 * p.n, add)
        if self.order == "yx":
            send(self.grads.at[l, 1 - p.y, :, :, self.r], self.r1.at[l, pl.ds(0, 2), :, self.r], self.sem(2), self.sem(3), p.mate_y()[1])
        elif self.order == "xy":
            send(self.grads.at[l, :, 1 - p.x, :, self.r], self.r1.at[l, pl.ds(0, 2), :, self.r], self.sem(2), self.sem(3), p.mate_x()[1])
        else:
            send(self.grads.at[l, p.y, 1 - p.x, :, self.r], self.r1.at[l, 0, :, self.r], self.sem(2), self.sem(3), p.mate_x()[1])
            send(self.grads.at[l, 1 - p.y, p.x, :, self.r], self.r1.at[l, 1, :, self.r], self.sem(2), self.sem(3), p.mate_y()[1])
            send(self.grads.at[l, 1 - p.y, 1 - p.x, :, self.r], self.r1.at[l, 2, :, self.r], self.sem(2), self.sem(3), p.mate_xy()[1])

    def s1b(self):
        p, l = self.p, self.layer
        both = self.r1.at[l, pl.ds(0, 2), :, self.r]
        await_bytes(both, self.sem(2))
        await_bytes(both, self.sem(3))

        def add(j):
            k, q = j // p.n, lax.rem(j, p.n)
            y, x = (p.y, k) if self.order == "yx" else (k, p.x)

            def strip(r):
                self.grads[l, y, x, q, r, :] = self.add_to((y, x, q), [self.r1.at[l, k, q]], r).astype(BF)

            self.strips(strip)

        loop(2 * p.n, add)
        if self.order == "yx":
            send(self.grads.at[l, p.y, 1 - p.x, :, self.r], self.r1.at[l, 2, :, self.r], self.sem(4), self.sem(5), p.mate_x()[1])
        else:
            send(self.grads.at[l, 1 - p.y, p.x, :, self.r], self.r1.at[l, 2, :, self.r], self.sem(4), self.sem(5), p.mate_y()[1])

    def s2(self):
        p, l = self.p, self.layer
        if self.order == "direct":
            slots = (0, 1, 2)
            await_bytes(self.r1.at[l, :, :, self.r], self.sem(2))
            await_bytes(self.r1.at[l, :, :, self.r], self.sem(3))
        else:
            slots = (2,)
            await_bytes(self.r1.at[l, 2, :, self.r], self.sem(4))
            await_bytes(self.r1.at[l, 2, :, self.r], self.sem(5))

        def add(q):
            def strip(r):
                self.grads[l, p.y, p.x, q, r, :] = self.add_to((p.y, p.x, q), [self.r1.at[l, k, q] for k in slots], r).astype(BF)

            self.strips(strip)

        loop(p.n, add)
        for k in range(1, p.n):
            q, peer = p.column(k)
            send(self.grads.at[l, p.y, p.x, q, self.r], self.r2.at[l, k - 1, self.r], self.sem(6), self.sem(7), peer)

    def s3(self):
        p, l = self.p, self.layer
        await_bytes(self.r2.at[l, :, self.r], self.sem(6))
        await_bytes(self.r2.at[l, :, self.r], self.sem(7))

        def strip(r):
            total = self.add_to((p.y, p.x, p.q), [self.r2.at[l, k] for k in range(p.n - 1)], r)
            self.res[l, p.i, r, :] = total.astype(BF)

        self.strips(strip)
        piece = self.res.at[l, p.i, self.r]
        for mate in (p.mate_x(), p.mate_y(), p.mate_xy()):
            send(piece, piece, self.sem(8), self.sem(9), mate[1])

    def s4(self):
        p, l = self.p, self.layer
        await_bytes(self.res.at[l, pl.ds(0, 3), self.r], self.sem(9))
        for i in (p.i, p.mate_x()[0], p.mate_y()[0], p.mate_xy()[0]):
            piece = self.res.at[l, i, self.r]
            send(piece, piece, self.sem(10), self.sem(11), p.sibling())

    def end(self):
        half = self.res.at[self.layer, pl.ds(0, GROUP // 2), self.r]
        await_bytes(self.res.at[self.layer, pl.ds(0, 3), self.r], self.sem(8))
        await_bytes(half, self.sem(10))
        await_bytes(half, self.sem(11))


def in_order(own, others, l, here, count):
    total = None
    for j in range(count):
        k = lax.rem(here - j + count, count)
        value = jnp.where(k == 0, own.astype(F32), others[l, lax.max(k - 1, 0)].astype(F32))
        total = value if total is None else total + value
    return total


BACKWARD_ORDER = {"d0": "yx", "d1": "yx", "e0": "xy", "e1": "xy", "i0": "direct", "i1": "direct", "o0": "direct", "o1": "direct", "u0": "yx", "u1": "yx", "v0": "xy", "v1": "xy"}
BACKWARD_PLAN = {
    (1, "middle"): ("e1.s1",),
    (1, "open"): ("d1.s1",),
    (1, "sent"): ("v1.s1",),
    (1, "transform"): ("o1.s1",),
    (1, "gatep"): ("u1.s1",),
    (1, "in"): ("d1.s1b",),
    (1, "end"): ("v1.s1b",),
    (0, "narrow"): ("i1.s1",),
    (0, "down0"): ("d1.s2",),
    (0, "down"): ("e1.s1b",),
    (0, "up0"): ("u1.s1b",),
    (0, "sent"): ("v1.s2", "e0.s1", "d0.s1"),
    (0, "out"): ("e1.s2",),
    (0, "transform"): ("i1.s2",),
    (0, "came"): ("o0.s1",),
    (0, "half"): ("u0.s1", "d0.s1b"),
    (0, "returned"): ("v0.s1",),
    (0, "gatep"): ("o1.s2", "u1.s2"),
    (0, "in"): ("d1.s3", "d0.s2", "v1.s3"),
    (0, "project"): ("e0.s1b",),
    (0, "end"): ("v0.s1b", "u0.s1b"),
    (0, "tail"): (
        "kg1.over_mp", "i1.s3", "v0.s2", "kg0.over_mp", "kg1.over_group", "e0.s2", "u0.s2", "i0.s1", "d0.s3",
        "v0.s3", "d1.s4", "i0.s2", "u1.s3", "kg1.take", "o1.s3", "o0.s2", "v1.s4", "v0.s4", "d0.s4", "e0.s3",
        "e1.s3", "i1.s4", "kg0.over_group", "norm.over_mp", "o1.s4", "u0.s3", "u1.s4", "i0.s3", "o0.s3", "e0.s4",
        "kg0.take", "e1.s4", "u0.s4", "norm.take", "i0.s4", "o0.s4",
    ),
}


class KernelGrad:
    def __init__(self, place, layer, refs, sems):
        self.p, self.l, self.sems = place, layer, sems
        self.own, self.from_mp, self.mid, self.from_group, self.total, self.result = [r.at[layer] for r in refs]
        self.owner = place.s == place.q

    def sem(self, k):
        return self.sems.at[self.l, k]

    def start(self):
        when(jnp.logical_not(self.owner), lambda: send(self.own, self.from_mp, self.sem(0), self.sem(1), self.p.opposite()))

    def over_mp(self):
        p = self.p

        def add():
            await_bytes(self.from_mp, self.sem(1))
            self.mid[...] = (self.own[...].astype(F32) + self.from_mp[...].astype(F32)).astype(BF)
            for k, mate in enumerate((p.mate_x(), p.mate_y(), p.mate_xy())):
                send(self.mid, self.from_group.at[k], self.sem(2 + k), self.sem(5 + k), mate[1])

        when(self.owner, add)

    def over_group(self):
        p = self.p

        def add():
            for k in range(3):
                await_bytes(self.from_group.at[k], self.sem(5 + k))
            near = self.mid[...].astype(F32) + self.from_group[0].astype(F32)
            far = self.from_group[1].astype(F32) + self.from_group[2].astype(F32)
            both = (near + far).astype(BF)
            self.total[...] = both
            self.result[...] = both
            send(self.total, self.result, self.sem(8), self.sem(9), p.sibling())

        when(self.owner, add)

    def take(self):
        when(jnp.logical_not(self.owner), lambda: await_bytes(self.result, self.sem(9)))

    def finish(self):
        def given():
            for k in range(3):
                await_bytes(self.mid, self.sem(2 + k))
            await_bytes(self.total, self.sem(8))

        when(self.owner, given)
        when(jnp.logical_not(self.owner), lambda: await_bytes(self.own, self.sem(0)))


class NormGrad:
    def __init__(self, place, refs, sems):
        self.p, self.sems = place, sems
        self.own, self.from_group, self.mid, self.from_mp, self.result = refs
        self.layers = self.own.shape[0]

    def start(self, l):
        for k in range(1, GROUP):
            send(self.own.at[l], self.from_group.at[l, k - 1], self.sems.at[l, 0], self.sems.at[l, 1], self.p.member(k))

    def over_mp(self):
        p = self.p
        for l in reversed(range(self.layers)):
            await_bytes(self.from_group.at[l], self.sems.at[l, 0])
            await_bytes(self.from_group.at[l], self.sems.at[l, 1])
            self.mid[l] = in_order(self.own[l], self.from_group, l, p.i, GROUP)
            for k in range(1, p.n):
                send(self.mid.at[l], self.from_mp.at[l, k - 1], self.sems.at[l, 2], self.sems.at[l, 3], p.column(k)[1])

    def take(self):
        for l in reversed(range(self.layers)):
            await_bytes(self.from_mp.at[l], self.sems.at[l, 2])
            await_bytes(self.from_mp.at[l], self.sems.at[l, 3])
            self.result[l] = in_order(self.mid[l], self.from_mp, l, self.p.q, self.p.n)


def backward_kernel(
    n, layers,
    gains, subs, scales, masks_h, table_h, table_t_h, tap_t_h,
    out_in, cot, streams, hiddens, gacts, gslopes, conv_ins, conv_outs, gateds, middles, hidden_mids, actives, slopes,
    wins_h, win_h, wout_h, wup_h, wdn_h,
    out_o, grad_o, res_o, sub_o, norm_o,
    grad, middle_grad, stream, hidden, gact, gslope, conv_in, conv_out, gated, middle, hidden_mid, active, slope, wins, win, wout, wup, wdn,
    grads, r0, r1, r2, res,
    up_grad, out_grad, branch, joined, big_a, big_b, spread,
    send_c, recv_c, send_d, recv_d, kg_s, kg_z, kg_t, kg_y, kg_u, kg_own, sub_s, masks, table, table_t, tap_t,
    norm_s, norm_r, norm_t, norm_u, norm_v,
    load_sems, a2a_sems, red_sems, kg_sems, norm_sems, out_sems, move_sems,
):
    place = Place(n)
    me, core = place.s, place.core
    tokens, width = grad.shape
    channels = width // n
    quarter = tokens
    ff = wup.shape[1]
    half = ff // 2
    spare = grads.shape[0] - 1
    loads = {}
    sources = {
        "stream": (streams, stream), "hidden": (hiddens, hidden), "gact": (gacts, gact), "gslope": (gslopes, gslope),
        "conv_in": (conv_ins, conv_in), "conv_out": (conv_outs, conv_out), "gated": (gateds, gated), "middle": (middles, middle),
        "hidden_mid": (hidden_mids, hidden_mid), "active": (actives, active), "slope": (slopes, slope), "wins": (wins_h, wins),
        "in": (win_h, win), "out": (wout_h, wout), "up": (wup_h, wup), "down": (wdn_h, wdn),
        "branch": (cot, branch), "masks": (masks_h, masks), "table": (table_h, table), "table_t": (table_t_h, table_t), "tap_t": (tap_t_h, tap_t),
    }
    once = ("branch", "masks", "table", "table_t", "tap_t")

    def load(name, l):
        src, dst = sources[name]
        copy = pltpu.make_async_copy(src if name in once else src.at[l], dst, load_sems.at[l, len([k for k in loads if k[1] == l])])
        copy.start()
        loads[name, l] = copy

    def ready(*names, l):
        for name in names:
            loads[name, l].wait()

    def next_load(*names, l):
        if l:
            for name in names:
                load(name, l - 1)

    top = layers - 1
    for name in ("branch", "down", "slope"):
        load(name, top)
    greet_all(place)
    bufs = (grads, r0, r1, r2, res)
    bounds = (PIECE_DOWN, PIECE_UP // 2, PIECE_UP, (PIECE_UP + PIECE_OUT) // 2, PIECE_OUT, PIECE_IN, PIECE_ROWS)
    groups = {}
    for l in range(layers):
        for k, letter in enumerate("deuvoi"):
            name = letter + str(l)
            order = BACKWARD_ORDER.get(name, "direct")
            groups[name] = Reduce(place, bufs, red_sems, len(groups), l, bounds[k], bounds[k + 1] - bounds[k], order)
    kernel_grads = [KernelGrad(place, l, (kg_s, kg_z, kg_t, kg_y, kg_u, kg_own), kg_sems) for l in range(layers)]
    norm_grads = NormGrad(place, (norm_s, norm_r, norm_t, norm_u, norm_v), norm_sems)
    out_move = Move(place, out_in, out_o, move_sems.at[0])
    grad_move = Move(place, branch, grad_o, move_sems.at[1])
    moving = {"norm": norm_grads, **groups}
    moving.update({"kg" + str(l): kernel_grads[l] for l in range(layers)})

    def visit(l, point):
        for step in BACKWARD_PLAN.get((l, point), ()):
            what, action = step.split(".")
            getattr(moving[what], action)()

    def exchange_start(slot, src, dst, rows):
        for k in range(1, n):
            s, peer = place.partner(k)
            send(src.at[s, rows], dst.at[me, rows], a2a_sems.at[slot, 0], a2a_sems.at[slot, 1], peer)

    def exchange_wait(slot, src, dst, l):
        await_bytes(src.at[pl.ds(0, n - 1)], a2a_sems.at[slot, 0])
        await_bytes(dst.at[pl.ds(0, n - 1)], a2a_sems.at[slot, 1])

    def holder(parity, l):
        mine = 1 - (parity - core) * (parity - core)
        return l * mine + spare * (1 - mine)

    out_move.start()
    for name in ("up", "active", "hidden_mid", "middle", "out", "gact", "gslope", "conv_out"):
        load(name, top)
    ready("branch", l=top)

    def widen_grad(j):
        r = rows_of(j, 64)
        grad[r, :] = branch[r, :].astype(F32)

    loop(tokens // 64, widen_grad)

    for l in reversed(range(layers)):
        ready("down", "slope", l=l)
        for h in range(2):
            c = slice(h * half, (h + 1) * half)
            big_b[0:tokens, :] = dot_nt(branch[...], wdn[c, :])

            def activate(k):
                s = rows_of(k, 32)
                up_grad[s, c] = (big_b[s, :] * slope[s, c].astype(F32)).astype(BF)

            loop(tokens // 32, activate)
        next_load("down", "slope", l=l)
        if l == top:
            for name in ("gated", "masks", "conv_in", "table", "wins", "table_t", "tap_t", "in", "hidden", "stream"):
                load(name, top)
        visit(l, "activate")
        ready("up", "hidden_mid", "active", l=l)
        big_a[0:tokens, 0:width] = dot_nt(up_grad[...], wup[...])
        next_load("up", l=l)
        visit(l, "narrow")

        def grad_up(c):
            got = dot_tn(hidden_mid[:, rows_of(c, 128)], up_grad[...]).astype(BF)
            for par in range(2):
                for q in range(n):
                    grads[holder(par, l), c // 2, lax.rem(c, 2), q, PIECE_UP:PIECE_OUT, :] = got[par * 64 : par * 64 + 64, q * (ff // n) : (q + 1) * (ff // n)]

        def grad_down(q):
            got = dot_tn(active[:, rows_of(q, ff // n)], branch[...]).astype(BF)
            for i in range(GROUP):
                grads[holder(i % 2, l), i // 4, i // 2 % 2, q, PIECE_DOWN:PIECE_UP, :] = got[i * 64 : (i + 1) * 64]

        def grad_out(q):
            got = dot_tn(gated[:, rows_of(q, channels)], out_grad[...]).astype(BF)
            for i in range(GROUP):
                grads[holder(i % 2, l), i // 4, i // 2 % 2, q, PIECE_OUT:PIECE_IN, :] = got[i * 16 : (i + 1) * 16]

        def grad_in(h):
            def block(c):
                got = dot_tn(hidden[:, rows_of(c, 128)], joined[:, h * width : (h + 1) * width]).astype(BF)
                for par in range(2):
                    for q in range(n):
                        for t in range(2):
                            grads[holder(par, l), c // 2, lax.rem(c, 2), q, PIECE_IN:PIECE_ROWS, h * 256 + t * 128 : h * 256 + (t + 1) * 128] = got[
                                par * 64 + t * 32 : par * 64 + (t + 1) * 32, q * channels : (q + 1) * channels
                            ]

            loop(GROUP // 2, block)

        loop(n // 2, grad_down)
        visit(l, "down0")
        loop(n // 2, lambda q: grad_down(q + n // 2))
        for letter in "de":
            groups[letter + str(l)].s0()
        visit(l, "down")
        loop(GROUP // 4, grad_up)
        visit(l, "up0")
        loop(GROUP // 4, lambda c: grad_up(c + GROUP // 4))
        for letter in "uv":
            groups[letter + str(l)].s0()
        next_load("hidden_mid", l=l)
        visit(l, "up")
        ready("middle", l=l)
        sums_mid = norm_back(big_a.at[:, 0:width], middle, grad, gains[l, 1:2, :], middle_grad, out_grad)
        next_load("middle", l=l)
        visit(l, "middle")

        ready("out", l=l)
        big_b[0:tokens, 0:width] = dot_nt(out_grad[...], wout[...])
        next_load("out", l=l)
        visit(l, "open")
        ready("gact", "gslope", "conv_out", l=l)

        def unmix(j):
            r = rows_of(j, 32)
            for s in range(n):
                c = slice(s * channels, (s + 1) * channels)
                up = big_b[r, c]
                send_c[s, r, :] = (up * gact[r, c].astype(F32)).astype(BF)
                joined[r, slice(width + s * channels, width + (s + 1) * channels)] = (
                    up * conv_out[s, r, :].astype(F32) * gslope[r, c].astype(F32)
                ).astype(BF)

        for j in range(2):
            loop(tokens // 64, lambda k: unmix(k + j * (tokens // 64)))
            exchange_start(2 * l, send_c, recv_c, pl.ds(j * (tokens // 2), tokens // 2))
        next_load("gact", "gslope", "conv_out", l=l)
        recv_c[me] = send_c[me]
        visit(l, "sent")
        ready("gated", l=l)
        loop(n, grad_out)
        groups["o" + str(l)].s0()
        next_load("gated", l=l)
        visit(l, "out")
        if l == top:
            ready("masks", "table", l=l)
        ready("conv_in", l=l)
        spread_blocks(conv_in, masks, spread)
        big_a[:, 0 : 7 * channels] = dot(table[...], spread[...])
        next_load("conv_in", l=l)
        visit(l, "transform")
        exchange_wait(2 * l, send_c, recv_c, l)
        visit(l, "arrived")
        spread_blocks(recv_c, masks, spread)
        big_b[:, 0 : 7 * channels] = dot(table[...], spread[...])
        visit(l, "came")
        ready("wins", l=l)
        back_products(big_a, big_b, wins, active, up_grad, channels)
        next_load("wins", l=l)
        visit(l, "products")
        if l == top:
            ready("table_t", "tap_t", l=l)

        for j in range(2):
            r = slice(j * (quarter // 2), (j + 1) * (quarter // 2))
            parts = dot(table_t[r, 0:quarter], active[:, 0 : 7 * channels])
            parts += dot(table_t[r, quarter : 2 * quarter], active[:, half : half + 7 * channels])
            for s in range(n):
                send_d[s, r, :] = join_blocks(parts, r, masks, s).astype(BF)
            exchange_start(2 * l + 1, send_d, recv_d, pl.ds(j * (quarter // 2), quarter // 2))
            if j == 0:
                visit(l, "half")
        recv_d[me] = send_d[me]
        next_load("active", l=l)

        taps = None
        for m in range(4):
            c = slice(m * channels, (m + 1) * channels)
            d = slice(half + m * channels, half + (m + 1) * channels)
            got = dot(tap_t[m, :, 0:quarter], up_grad[:, c]) + dot(tap_t[m, :, quarter : 2 * quarter], up_grad[:, d])
            taps = got if taps is None else taps + got
        kg_s[l] = taps.astype(BF)
        kernel_grads[l].start()
        visit(l, "returned")
        ready("in", "hidden", "stream", l=l)
        big_a[0:tokens, 0:width] = dot_nt(joined[:, width : 2 * width], win[1])
        visit(l, "gatep")
        grad_in(1)
        visit(l, "in")
        exchange_wait(2 * l + 1, send_d, recv_d, l)

        def collect(j):
            r = rows_of(j, 64)
            for s in range(n):
                joined[r, s * channels : (s + 1) * channels] = recv_d[s, r, :]

        loop(tokens // 64, collect)
        if l == 0:
            grad_in(0)
            groups["i" + str(l)].s0()
        visit(l, "in0")
        big_a[0:tokens, 0:width] = big_a[0:tokens, 0:width] + dot_nt(joined[:, 0:width], win[0])
        next_load("in", l=l)
        visit(l, "project")
        sums_in = norm_back(big_a.at[:, 0:width], stream, middle_grad, gains[l, 0:1, :], grad, branch)
        next_load("stream", l=l)
        if l == 0:
            grad_move.start()
        else:
            grad_in(0)
            groups["i" + str(l)].s0()
        next_load("hidden", l=l)
        norm_s[l] = jnp.concatenate(
            [jnp.sum(s, axis=0, keepdims=True) for s in (sums_in[0], sums_mid[0], sums_in[1], sums_mid[1])]
            + [jnp.zeros((4, width), F32)],
            axis=0,
        )
        norm_grads.start(l)
        visit(l, "end")

    visit(0, "tail")
    out_norm = pltpu.make_async_copy(norm_v, norm_o, out_sems.at[1])
    out_norm.start()
    for l in range(layers):
        raw, inverse = normal_taps(subs, scales, l)
        k = raw * inverse
        own = kg_own[l].astype(F32)
        along = jnp.sum(own * k, axis=0, keepdims=True)
        sub_s[l] = scales[0] * (own - scales[1] * k * along) * inverse
    out_sub = pltpu.make_async_copy(sub_s, sub_o, out_sems.at[0])
    out_sub.start()
    for group in groups.values():
        group.end()
    out_res = pltpu.make_async_copy(res, res_o, out_sems.at[2])
    out_res.start()
    for m in (out_move, grad_move):
        m.arrive()
        m.finish()
    for g in kernel_grads:
        g.finish()
    out_sub.wait()
    out_norm.wait()
    out_res.wait()


def backward(n, gains, subs, scales, masks, table, table_t, tap_t, out, cot, kept):
    layers, tokens, width = kept[0].shape
    channels = width // n
    ff = kept[-1].shape[1]
    taps = subs.shape[1]

    def sds(*shape, dtype=F32):
        return jax.ShapeDtypeStruct(shape, dtype)

    outs = [
        sds(tokens, width, dtype=BF), sds(tokens, width, dtype=BF), sds(layers, GROUP, PIECE_ROWS, width, dtype=BF),
        sds(layers, taps, channels), sds(layers, 8, width),
    ]
    f32 = lambda *s: pltpu.VMEM(s, F32)
    bf = lambda *s: pltpu.VMEM(s, BF)
    wide, blocks, small = (tokens, width), (n, tokens, channels), (layers, taps, channels)
    scratch = [
        f32(*wide), f32(*wide), f32(*wide), bf(*wide), bf(*wide), bf(*wide), bf(*blocks), bf(*blocks), bf(*wide), f32(*wide), bf(*wide),
        bf(tokens, ff), bf(tokens, ff), f32(4, 2, tokens, channels),
        bf(2, width, width), bf(width, width), bf(width, ff), bf(ff, width),
        bf(layers + 1, 2, 2, n, PIECE_ROWS, width),
        bf(layers, 2, 2, n, PIECE_ROWS, width),
        bf(layers, 3, n, PIECE_ROWS, width),
        bf(layers, n - 1, PIECE_ROWS, width),
        bf(layers, GROUP, PIECE_ROWS, width),
        bf(tokens, ff), bf(*wide), bf(*wide), bf(tokens, 2 * width),
        f32(2 * tokens, 7 * channels), f32(2 * tokens, ff // 2), bf(tokens, 7 * channels),
        bf(*blocks), bf(*blocks), bf(*blocks), bf(*blocks),
        bf(*small), bf(*small), bf(*small), bf(layers, 3, taps, channels), bf(*small), bf(*small), f32(*small),
        bf(10, tokens, channels), bf(2 * tokens, tokens), bf(tokens, 2 * tokens), bf(4, taps, 2 * tokens),
        f32(layers, 8, width), f32(layers, GROUP - 1, 8, width), f32(layers, 8, width), f32(layers, n - 1, 8, width), f32(layers, 8, width),
        pltpu.SemaphoreType.DMA((layers, 21)),
        pltpu.SemaphoreType.DMA((2 * layers, 2)),
        pltpu.SemaphoreType.DMA((6 * layers, 12)),
        pltpu.SemaphoreType.DMA((layers, 10)),
        pltpu.SemaphoreType.DMA((layers, 4)),
        pltpu.SemaphoreType.DMA((3,)),
        pltpu.SemaphoreType.DMA((2, 2)),
    ]
    return pl.pallas_call(
        functools.partial(backward_kernel, n, layers),
        out_shape=outs,
        in_specs=[VMEM] * 3 + [ANY] * (6 + len(kept)),
        out_specs=[ANY] * len(outs),
        scratch_shapes=scratch,
        compiler_params=pltpu.CompilerParams(collective_id=2, has_side_effects=True, vmem_limit_bytes=int(63.5 * 2**20)),
        name="backward",
    )(gains, subs, scales, masks, table, table_t, tap_t, out, cot, *kept)


def finish_kernel(out_i, grad_i, res, out, grad, up, down, out_w, in_w):
    out[...] = out_i[...].astype(F32)
    grad[...] = grad_i[...].astype(F32)
    members = res.shape[1]
    for i in range(members):
        up[0, i * 64 : (i + 1) * 64, :] = res[0, i, PIECE_UP:PIECE_OUT, :].astype(F32)
        down[0, i * 64 : (i + 1) * 64, :] = res[0, i, PIECE_DOWN:PIECE_UP, :].astype(F32)
        out_w[0, i * 16 : (i + 1) * 16, :] = res[0, i, PIECE_OUT:PIECE_IN, :].astype(F32)
        for h in range(2):
            for t in range(2):
                c = h * 256 + t * 128
                in_w[0, h, i * 64 + t * 32 : i * 64 + (t + 1) * 32, :] = res[0, i, PIECE_IN:, c : c + 128].astype(F32)


def finish(out, grad, res):
    layers, members, _, width = res.shape
    tokens = out.shape[0]
    parts = 2
    m = members // parts
    steps = layers * parts
    rows = tokens // steps

    def sds(*shape):
        return jax.ShapeDtypeStruct(shape, F32)

    flat = pl.BlockSpec((rows, width), lambda j: (j, 0))

    def mid(*shape):
        return pl.BlockSpec((1, *shape, width), lambda j: (j // parts, j % parts, 0))

    return pl.pallas_call(
        finish_kernel,
        grid=(steps,),
        out_shape=[
            sds(tokens, width), sds(tokens, width), sds(layers, members * 64, width), sds(layers, members * 64, width),
            sds(layers, members * 16, width), sds(layers, 2, members * 64, 128),
        ],
        in_specs=[flat, flat, pl.BlockSpec((1, m, PIECE_ROWS, width), lambda j: (j // parts, j % parts, 0, 0))],
        out_specs=[flat, flat, mid(m * 64), mid(m * 64), mid(m * 16), pl.BlockSpec((1, 2, m * 64, 128), lambda j: (j // parts, 0, j % parts, 0))],
        name="finish",
    )(out, grad, res)


def per_device(
    stream_in, segments, norm_gain, norm_bias, w_in, w_out, sub_kernels, w_up, w_down, cotangent
):
    layers, scales, taps, channels = sub_kernels.shape
    n = lax.axis_size("mp")
    quarter = segments.shape[1] // 4
    table = transform_table(quarter)
    tap_table = tap_tables(quarter, scales, taps) / quarter

    def const(a):
        return jnp.asarray(a, F32).astype(BF)

    factors = jnp.asarray(tap_scales(scales, taps, channels))
    subs = sub_kernels.reshape(layers, -1, channels)
    out, *kept, masks, cot, win, wout, wup, wdn = forward(
        n, stream_in, cotangent, segments, norm_gain, norm_bias, subs, factors, const(table), const(table.T), const(tap_table),
        w_in.transpose(0, 2, 1, 3), w_out, w_up, w_down,
    )
    out, grad, res, sub, norms = backward(
        n, norm_gain, subs, factors, masks, const(table), const(table.T), const(tap_table.transpose(0, 2, 1)),
        out, cot, (*kept, win, wout, wup, wdn),
    )
    if lax.axis_size("dp") > GROUP:
        res, sub, norms = [v * (1.0 / GROUP) for v in lax.psum((res.astype(F32), sub, norms), "dp")]
        res = res.astype(BF)
    out, grad, up, down, out_w, in_w = finish(out, grad, res)
    return (
        out, grad, norms[:, 0:2], norms[:, 2:4], in_w.transpose(0, 2, 1, 3), out_w, sub.reshape(sub_kernels.shape), up, down,
    )


def solution(mesh):
    rows = P(("dp", "mp"), None)
    last = P(None, None, None, "mp")
    mid = P(None, "mp", None)
    return jax.shard_map(
        per_device,
        mesh=mesh,
        in_specs=(rows, P("dp", None), P(), P(), last, mid, last, P(None, None, "mp"), mid, rows),
        out_specs=(rows, rows, P(), P(), last, mid, last, P(None, None, "mp"), mid),
        check_vma=False,
    )
```

```python
import functools

import jax
import jax.numpy as jnp
import numpy as np
from jax import lax
from jax.experimental import pallas as pl
from jax.experimental.pallas import tpu as pltpu
from jax.sharding import PartitionSpec as P

DECAY_RATE = 0.5
EPSILON = 1e-05
BF = jnp.bfloat16
F32 = jnp.float32
GROUP = 8
MESH = pl.DeviceIdType.MESH
VMEM = pl.BlockSpec(memory_space=pltpu.VMEM)
ANY = pl.BlockSpec(memory_space=pl.ANY)
GELU_A = float(np.sqrt(2.0 / np.pi))
GELU_B = 0.044715


def dot(a, b):
    return jnp.dot(a, b, preferred_element_type=F32)


def dot_nt(a, b):
    return lax.dot_general(a, b, (((1,), (1,)), ((), ())), preferred_element_type=F32)


def dot_tn(a, b):
    return lax.dot_general(a, b, (((0,), (0,)), ((), ())), preferred_element_type=F32)


def gelu(u):
    return 0.5 * u * (1.0 + jnp.tanh(GELU_A * (u + GELU_B * (u * u * u))))


def gelu_both(u):
    square = u * u
    t = jnp.tanh(GELU_A * (u + GELU_B * (square * u)))
    half = 0.5 * (1.0 + t)
    slope = half + (0.5 * u) * (1.0 - t * t) * (GELU_A + (3.0 * GELU_A * GELU_B) * square)
    return u * half, slope


def loop(count, body):
    lax.fori_loop(0, count, lambda j, c: (body(j), c)[1], 0)


def when(condition, body):
    pl.when(condition)(body)


def rows_of(j, size):
    return pl.ds(pl.multiple_of(j * size, size), size)


def transform_table(quarter):
    freq = np.arange(quarter)[:, None] + 0.5
    angle = np.pi * freq * np.arange(quarter)[None, :] / quarter
    return np.concatenate([np.cos(angle), -np.sin(angle)], axis=0)


def spread_matrix(scales, taps):
    lags = []
    for level in range(scales):
        lags += [level * taps + j for j in range(taps) for _ in range(2 ** max(level, 1))]
    spread = np.zeros((len(lags), scales * taps))
    spread[np.arange(len(lags)), lags] = 1.0
    return spread


def tap_tables(quarter, scales, taps):
    table = transform_table(quarter)
    spread = spread_matrix(scales, taps).reshape(4, quarter, scales * taps)
    return np.einsum("fp,mpt->mft", table, spread)


def tap_scales(scales, taps, channels):
    level = np.repeat(np.arange(scales), taps)
    decay = DECAY_RATE**level
    repeats = 2.0 ** np.maximum(level, 1)
    both = np.stack([decay, repeats])[:, :, None]
    return np.broadcast_to(both, (2, scales * taps, channels)).astype(np.float32)


class Place:
    def __init__(self, n):
        self.n = n
        self.q = lax.axis_index("mp")
        dp = lax.axis_index("dp")
        self.i = lax.rem(dp, GROUP)
        self.base = dp - self.i
        self.core = lax.rem(self.i, 2)
        self.x = lax.rem(self.i // 2, 2)
        self.y = self.i // 4
        self.s = lax.rem(self.q, 2) + 2 * self.core

    def device(self, i, q):
        return {"dp": self.base + i, "mp": q}

    def index(self, y, x, core):
        return 4 * y + 2 * x + core

    def column(self, k):
        q = lax.rem(self.q + k, self.n)
        return q, self.device(self.i, q)

    def member(self, k):
        return self.device(lax.rem(self.i + k, GROUP), self.q)

    def mate_x(self):
        i = self.index(self.y, 1 - self.x, self.core)
        return i, self.device(i, self.q)

    def mate_y(self):
        i = self.index(1 - self.y, self.x, self.core)
        return i, self.device(i, self.q)

    def mate_xy(self):
        i = self.index(1 - self.y, 1 - self.x, self.core)
        return i, self.device(i, self.q)

    def mates(self, order):
        return (self.mate_x(), self.mate_y()) if order == "xy" else (self.mate_y(), self.mate_x())

    def sibling(self):
        return self.device(self.index(self.y, self.x, 1 - self.core), self.q)

    def partner(self, k):
        s = lax.rem(self.s + k, self.n)
        return s, self.device(self.index(self.y, self.x, s // 2), 2 * (self.q // 2) + lax.rem(s, 2))

    def row_target(self):
        return self.device(self.index(self.y, self.x, self.q // 2), 2 * self.core + lax.rem(self.q, 2))

    def opposite(self):
        return self.device(self.i, lax.rem(self.q + 2, self.n))

    def stays(self):
        return self.q // 2 == self.core


def greet_all(place):
    barrier = pltpu.get_barrier_semaphore()
    peers = [place.column(k)[1] for k in range(1, place.n)] + [place.member(k) for k in range(1, GROUP)]
    across = place.index(place.y, place.x, 1 - place.core)
    peers += [place.device(across, place.column(k)[0]) for k in range(1, place.n)]
    for peer in peers:
        pl.semaphore_signal(barrier, inc=1, device_id=peer, device_id_type=MESH)
    pl.semaphore_wait(barrier, len(peers))


def send(src, dst, send_sem, recv_sem, peer):
    pltpu.make_async_remote_copy(
        src_ref=src, dst_ref=dst, send_sem=send_sem, recv_sem=recv_sem, device_id=peer, device_id_type=MESH
    ).start()


def await_bytes(ref, sem):
    pltpu.make_async_copy(ref, ref, sem).wait()


class Move:
    def __init__(self, place, src, dst, sems, relay=None):
        self.p, self.src, self.dst, self.sems, self.relay = place, src, dst, sems, relay
        half = src.shape[0] // 2
        self.first = pl.ds(0, src.shape[0] if relay is None else half)
        self.second = pl.ds(half, half)

    def start(self):
        p = self.p

        def across():
            send(self.src.at[self.first], self.dst.at[self.first], self.sems.at[0], self.sems.at[1], p.row_target())
            if self.relay is not None:
                send(self.src.at[self.second], self.relay, self.sems.at[0], self.sems.at[2], p.sibling())

        when(jnp.logical_not(p.stays()), across)
        when(p.stays(), lambda: pltpu.make_async_copy(self.src, self.dst, self.sems.at[1]).start())

    def pass_on(self):
        def onward():
            await_bytes(self.relay, self.sems.at[2])
            send(self.relay, self.dst.at[self.second], self.sems.at[3], self.sems.at[1], self.p.opposite())

        when(self.p.stays(), onward)

    def arrive(self):
        await_bytes(self.dst, self.sems.at[1])

    def finish(self):
        when(jnp.logical_not(self.p.stays()), lambda: await_bytes(self.src, self.sems.at[0]))
        if self.relay is not None:
            when(self.p.stays(), lambda: await_bytes(self.relay, self.sems.at[3]))


class Weight:
    def __init__(self, whole, layer, columns, n):
        self.whole, self.columns, self.layer, self.n = whole, columns, layer, n
        shape = whole.shape
        self.rows = shape[1] // GROUP if columns else shape[1] // n // GROUP
        self.cols = shape[2] // n if columns else shape[2]

    def piece(self, i, q):
        r, c = self.rows, self.cols
        if self.columns:
            return self.whole.at[self.layer, pl.ds(i * r, r), pl.ds(q * c, c)]
        return self.whole.at[self.layer, pl.ds((q * GROUP + i) * r, r), :]

    def shard(self, q):
        r, c = self.rows, self.cols
        if self.columns:
            return self.whole.at[self.layer, :, pl.ds(q * c, c)]
        return self.whole.at[self.layer, pl.ds(q * GROUP * r, GROUP * r), :]

    def local_piece(self, shard, i):
        return shard.at[self.layer, pl.ds(i * self.rows, self.rows), :]

    def span(self, members):
        r, c, k = self.rows, self.cols, self.n - 1
        if self.columns:
            return self.whole.at[self.layer, pl.ds(0, members * r), pl.ds(0, k * c)]
        return self.whole.at[self.layer, pl.ds(0, members * k * r), :]


class Gather:
    def __init__(self, place, weight, shard, sems, slot, order):
        self.p, self.w, self.shard_ref, self.sems, self.slot, self.order = place, weight, shard, sems, slot, order

    def sem(self, k):
        return self.sems.at[self.slot, k]

    def own(self):
        return pltpu.make_async_copy(
            self.shard_ref.at[self.w.layer], self.w.shard(self.p.q), self.sem(8)
        )

    def start(self):
        p, w = self.p, self.w
        for k in range(1, p.n):
            send(w.local_piece(self.shard_ref, p.i), w.piece(p.i, p.q), self.sem(0), self.sem(1), p.column(k)[1])
        self.own().start()

    def pass_on(self, i, send_sem, recv_sem, peer):
        p, w = self.p, self.w
        for k in range(1, p.n):
            piece = w.piece(i, p.column(k)[0])
            send(piece, piece, send_sem, recv_sem, peer)

    def first_second(self):
        return self.p.mates("yx" if self.order == "yx" else "xy")

    def hop1(self):
        p = self.p
        await_bytes(self.w.span(1), self.sem(1))
        first, second = self.first_second()
        self.pass_on(p.i, self.sem(2), self.sem(3), first[1])
        self.pass_on(p.i, self.sem(4), self.sem(5), second[1])
        if self.order == "direct":
            self.pass_on(p.i, self.sem(4), self.sem(5), p.mate_xy()[1])
        self.pass_on(p.i, self.sem(6), self.sem(7), p.sibling())

    def hop2(self):
        first, second = self.first_second()
        await_bytes(self.w.span(1), self.sem(3))
        self.pass_on(first[0], self.sem(4), self.sem(5), second[1])
        self.pass_on(first[0], self.sem(6), self.sem(7), self.p.sibling())

    def hop3(self):
        p = self.p
        first, second = self.first_second()
        others = [second[0], p.mate_xy()[0]]
        if self.order == "direct":
            await_bytes(self.w.span(1), self.sem(3))
            others.append(first[0])
        await_bytes(self.w.span(2), self.sem(5))
        for i in others:
            self.pass_on(i, self.sem(6), self.sem(7), p.sibling())

    def arrive(self):
        self.own().wait()
        await_bytes(self.w.span(4), self.sem(7))

    def finish(self):
        await_bytes(self.w.span(1), self.sem(0))
        await_bytes(self.w.span(1), self.sem(2))
        await_bytes(self.w.span(2), self.sem(4))
        await_bytes(self.w.span(4), self.sem(6))


def norm_strip(v, gain, bias):
    centred = v - jnp.mean(v, axis=-1, keepdims=True)
    variance = jnp.mean(centred * centred, axis=-1, keepdims=True)
    return centred * lax.rsqrt(variance + EPSILON) * gain + bias


def norm_all(src, dst, gain, bias):
    def strip(j):
        r = rows_of(j, 128)
        dst[r, :] = norm_strip(src[r, :], gain, bias).astype(BF)

    loop(dst.shape[0] // 128, strip)


def normal_taps(sub_ref, scale_ref, layer):
    raw = sub_ref[layer] * scale_ref[0]
    total = jnp.sum(raw * raw * scale_ref[1], axis=0, keepdims=True)
    return raw, lax.rsqrt(total + EPSILON)


def make_masks(segs, masks):
    quarter, channels = masks.shape[1:]
    ones = jnp.full((8, channels), 0.125, BF)

    def numbers(n):
        row = segs[:, n * quarter : (n + 1) * quarter].astype(F32)
        return dot_tn(jnp.broadcast_to(row, (8, quarter)).astype(BF), ones)

    def put(k, flag):
        masks[k] = jnp.where(flag, 1.0, 0.0).astype(BF)

    long_doc = numbers(1)[0:1, :]
    for n in range(4):
        here = numbers(n)
        put(n, here == long_doc)
        if n in (0, 3):
            for k in range(3):
                doc = jnp.where(long_doc <= k, k + 1.0, float(k))
                put(4 + 2 * k + (n == 3), here == doc)


def make_windows(taps, tap_ref, spec, layer, wins):
    channels = taps.shape[1]
    quarter = wins.shape[3]
    for m in range(4):
        spec[:, m * channels : (m + 1) * channels] = dot(tap_ref[m], taps)

    def strip(j):
        r = rows_of(j, 16)
        s = rows_of(j + quarter // 16, 16)
        sign = (1 - 2 * lax.rem(lax.broadcasted_iota(jnp.int32, (16, channels), 0), 2)).astype(F32)
        for m in range(4):
            here = slice(m * channels, (m + 1) * channels)
            re, im = spec[r, here], spec[s, here]
            if m:
                before = slice((m - 1) * channels, m * channels)
                re, im = re - sign * spec[s, before], im + sign * spec[r, before]
            wins[layer, m, 0, r, :] = re
            wins[layer, m, 1, r, :] = im

    loop(quarter // 16, strip)


def spread_blocks(blocks, masks, out):
    channels = masks.shape[2]
    for n in range(4):
        out[:, n * channels : (n + 1) * channels] = blocks[n] * masks[n]
    for k in range(3):
        out[:, (4 + k) * channels : (5 + k) * channels] = (
            blocks[0] * masks[4 + 2 * k] + blocks[3] * masks[5 + 2 * k]
        )


def join_blocks(parts, r, masks, n):
    channels = masks.shape[2]
    total = parts[:, n * channels : (n + 1) * channels] * masks[n, r, :].astype(F32)
    if n in (0, 3):
        for k in range(3):
            mask = masks[4 + 2 * k + (n == 3), r, :].astype(F32)
            total += parts[:, (4 + k) * channels : (5 + k) * channels] * mask
    return total


def fwd_products(spec, wins, layer, out, kept, channels):
    quarter = wins.shape[3]

    def strip(j):
        r = rows_of(j, 16)
        s = rows_of(j + quarter // 16, 16)
        xs = [(spec[r, n * channels : (n + 1) * channels], spec[s, n * channels : (n + 1) * channels]) for n in range(7)]
        for n in range(7):
            c = slice(n * channels, (n + 1) * channels)
            kept[layer, r, c] = xs[n][0].astype(BF)
            kept[layer, s, c] = xs[n][1].astype(BF)
        ws = [(wins[layer, m, 0, r, :], wins[layer, m, 1, r, :]) for m in range(4)]
        for n in range(7):
            re = im = None
            for m in range(n + 1 if n < 4 else 1):
                w, x = ws[m], xs[n - m]
                a = w[0] * x[0] - w[1] * x[1]
                b = w[0] * x[1] + w[1] * x[0]
                re, im = (a, b) if re is None else (re + a, im + b)
            out[r, n * channels : (n + 1) * channels] = re.astype(BF)
            out[s, n * channels : (n + 1) * channels] = im.astype(BF)

    loop(quarter // 16, strip)


FORWARD_ORDER = {"c0": "direct", "c1": "direct", "d0": "direct", "d1": "direct", "g0": "direct", "g1": "direct", "o0": "direct", "o1": "direct", "u0": "direct", "u1": "direct"}
FORWARD_PLAN = {
    (0, "start2"): ("c0.hop1", "c0.hop3"),
    (0, "ready"): ("g0.start", "o0.start", "u0.start", "g0.hop1"),
    (0, "sent"): ("d0.start", "o0.hop1", "g0.hop3"),
    (0, "gate0"): ("u0.hop1",),
    (0, "masks"): ("c1.start", "o0.hop3"),
    (0, "win0"): ("o1.start",),
    (0, "win1"): ("g1.start",),
    (0, "transform"): ("d0.hop1",),
    (0, "returned"): ("u1.start", "c1.hop1", "u0.hop3"),
    (0, "back"): ("d1.start",),
    (0, "act0"): ("o1.hop1", "d0.hop3"),
    (0, "activate"): ("g1.hop1", "c1.hop3"),
    (1, "normed"): ("u1.hop1",),
    (1, "sent"): ("cot.start", "g1.hop3"),
    (1, "gate"): ("d1.hop1",),
    (1, "returned"): ("o1.hop3", "u1.hop3"),
    (1, "attach"): ("d1.hop3",),
}


def forward_kernel(
    n, layers,
    stream_in, segs, gains, biases, subs, scales, cot_h, table_h, table_t_h, tap_table_h, win, wout, wup, wdn,
    out_o, streams_o, hidden_o, gact_o, gslope_o, spec_o, conv_out_o, gated_o, middle_o, hidden_mid_o, active_o, slope_o,
    wins_o, masks_o, cot_o, win_o, wout_o, wup_o, wdn_o,
    stream, hidden, gact, gslope, gated, middle, hidden_mid, active, slope, send_a, recv_a, send_b, recv_b,
    spread, spec, spec_x, spec_y, wins, win_f, wout_f, wup_f, wdn_f,
    masks, tok_s, tok_r, tok_p, cot_in, cot_s, seg_r, taps_s, taps_r, table, table_t, tap_table,
    gather_sems, a2a_sems, save_sems, move_sems, tap_sems, load_sems,
):
    place = Place(n)
    me = place.s
    tokens, width = stream_in.shape
    channels = width // n
    quarter = tokens
    half = wup_f.shape[2] // 2
    loads = [
        pltpu.make_async_copy(src, dst, load_sems.at[k])
        for k, (src, dst) in enumerate(((cot_h, cot_in), (tap_table_h, tap_table), (table_h, table), (table_t_h, table_t)))
    ]
    greet_all(place)
    saves = []

    def save(src, dst, l=None):
        if l is not None:
            src, dst = src.at[l], dst.at[l]
        copy = pltpu.make_async_copy(src, dst, save_sems.at[len(saves)])
        copy.start()
        saves.append(copy)

    def exchange_start(slot, src, dst, layer, rows=None):
        rows = pl.ds(0, tokens) if rows is None else rows
        for k in range(1, n):
            s, peer = place.partner(k)
            send(src.at[layer, s, rows], dst.at[layer, me, rows], a2a_sems.at[slot, 0], a2a_sems.at[slot, 1], peer)

    def exchange_wait(slot, src, dst, layer):
        await_bytes(src.at[layer, pl.ds(0, n - 1)], a2a_sems.at[slot, 0])
        await_bytes(dst.at[layer, pl.ds(0, n - 1)], a2a_sems.at[slot, 1])

    moving = {
        "seg": Move(place, segs, seg_r, move_sems.at[0]),
        "tok": Move(place, tok_s, tok_r, move_sems.at[1], tok_p),
        "cot": Move(place, cot_s, cot_o, move_sems.at[2]),
    }
    gathers = {}
    for l in range(layers):
        for letter, whole, shard, index, columns in (
            ("c", win_f, win, 2 * l, True), ("g", win_f, win, 2 * l + 1, True), ("o", wout_f, wout, l, False),
            ("u", wup_f, wup, l, True), ("d", wdn_f, wdn, l, False),
        ):
            name = letter + str(l)
            weight = Weight(whole, index, columns, n)
            gathers[name] = Gather(place, weight, shard, gather_sems, len(gathers), FORWARD_ORDER.get(name, "xy"))
    moving.update(gathers)

    def visit(l, point):
        for step in FORWARD_PLAN.get((l, point), ()):
            what, action = step.split(".")
            getattr(moving[what], action)()

    gathers["c0"].start()

    def round_stream(j):
        r = rows_of(j, 64)
        tok_s[r, :] = stream_in[r, :].astype(BF)

    loop(tokens // 64, round_stream)
    moving["tok"].start()
    moving["seg"].start()
    for l in range(layers):
        raw, inverse = normal_taps(subs, scales, l)
        taps_s[l] = (raw * inverse).astype(BF)

    def give_taps():
        send(taps_s, taps_r, tap_sems.at[0], tap_sems.at[1], place.opposite())

    def keep_taps():
        taps_r[...] = taps_s[...]

    def take_taps():
        await_bytes(taps_r, tap_sems.at[1])

    own_taps = place.s == place.q
    when(own_taps, give_taps)
    for copy in loads:
        copy.start()
    when(own_taps, keep_taps)
    moving["tok"].pass_on()
    visit(0, "start")
    loads[0].wait()

    def round_cotangent(j):
        r = rows_of(j, 64)
        cot_s[r, :] = cot_in[r, :].astype(BF)

    loop(tokens // 64, round_cotangent)
    visit(0, "start2")
    moving["tok"].arrive()
    visit(0, "ready")

    def widen_stream(j):
        r = rows_of(j, 64)
        stream[0, r, :] = tok_r[r, :].astype(F32)

    loop(tokens // 64, widen_stream)
    save(stream, streams_o, 0)

    for l in range(layers):
        norm_all(stream.at[l], hidden.at[l], gains[l, 0:1, :], biases[l, 0:1, :])
        visit(l, "normed")
        gathers["c" + str(l)].arrive()
        got = dot(hidden[l], win_f[2 * l]).astype(BF)
        for s in range(n):
            send_a[l, s] = got[:, s * channels : (s + 1) * channels]
        visit(l, "project")
        exchange_start(2 * l, send_a, recv_a, l)
        recv_a[l, me] = send_a[l, me]
        visit(l, "sent")
        save(hidden, hidden_o, l)
        gathers["g" + str(l)].arrive()
        spec[0:tokens, 0:width] = dot(hidden[l], win_f[2 * l + 1])
        visit(l, "gate0")

        def open_gate(j):
            r = rows_of(j, 16)
            act, incline = gelu_both(spec[r, 0:width])
            gact[l, r, :] = act.astype(BF)
            gslope[l, r, :] = incline.astype(BF)

        loop(tokens // 16, open_gate)
        visit(l, "gate")
        save(win_f, win_o, 2 * l)
        save(win_f, win_o, 2 * l + 1)
        save(gact, gact_o, l)
        save(gslope, gslope_o, l)
        if l == 0:
            moving["seg"].arrive()
            make_masks(seg_r, masks)
            save(masks, masks_o)
            visit(l, "masks")
            when(jnp.logical_not(own_taps), take_taps)
            loads[1].wait()
            for m in range(layers):
                make_windows(taps_r[m], tap_table, spec, m, wins)
                visit(l, "win" + str(m))
            save(wins, wins_o)
            loads[2].wait()
            loads[3].wait()
        exchange_wait(2 * l, send_a, recv_a, l)
        visit(l, "came")
        spread_blocks(recv_a.at[l], masks, spread)
        spec[:, 0 : 7 * channels] = dot(table[...], spread[...])
        visit(l, "transform")
        fwd_products(spec, wins, l, spec_y, spec_x, channels)
        save(spec_x, spec_o, l)
        visit(l, "prod")
        for j in range(2):
            r = slice(j * (quarter // 2), (j + 1) * (quarter // 2))
            parts = dot(table_t[r, :], spec_y[...])
            for s in range(n):
                send_b[l, s, r, :] = join_blocks(parts, r, masks, s).astype(BF)
            exchange_start(2 * l + 1, send_b, recv_b, l, pl.ds(j * (quarter // 2), quarter // 2))
            if j == 0:
                visit(l, "untr")
        recv_b[l, me] = send_b[l, me]
        visit(l, "returned")
        exchange_wait(2 * l + 1, send_b, recv_b, l)
        visit(l, "back")
        save(recv_b, conv_out_o, l)

        def mix(j):
            r = rows_of(j, 64)
            for s in range(n):
                c = slice(s * channels, (s + 1) * channels)
                gated[l, r, c] = (gact[l, r, c].astype(F32) * recv_b[l, s, r, :].astype(F32)).astype(BF)

        loop(tokens // 64, mix)
        visit(l, "mix")
        gathers["o" + str(l)].arrive()
        save(gated, gated_o, l)
        save(wout_f, wout_o, l)
        middle[l] = stream[l] + dot(gated[l], wout_f[l])
        visit(l, "attach")
        save(middle, middle_o, l)
        norm_all(middle.at[l], hidden_mid.at[l], gains[l, 1:2, :], biases[l, 1:2, :])
        visit(l, "norm")
        gathers["u" + str(l)].arrive()
        save(hidden_mid, hidden_mid_o, l)
        save(wup_f, wup_o, l)
        for h in range(2):
            c = slice(h * half, (h + 1) * half)
            act, incline = gelu_both(dot(hidden_mid[l], wup_f[l, :, c]))
            active[l, :, c] = act.astype(BF)
            slope[l, :, c] = incline.astype(BF)
            visit(l, ("act0", "activate")[h])
        save(active, active_o, l)
        save(slope, slope_o, l)
        gathers["d" + str(l)].arrive()
        save(wdn_f, wdn_o, l)
        if l + 1 < layers:
            stream[l + 1] = middle[l] + dot(active[l], wdn_f[l])
            save(stream, streams_o, l + 1)
        else:
            moving["tok"].finish()
            tok_s[...] = (middle[l] + dot(active[l], wdn_f[l])).astype(BF)
            save(tok_s, out_o)
        visit(l, "narrow")
    for g in gathers.values():
        g.finish()
    moving["cot"].arrive()
    for name in ("seg", "cot"):
        moving[name].finish()

    when(own_taps, lambda: await_bytes(taps_s, tap_sems.at[0]))
    for copy in saves:
        copy.wait()


def forward(n, stream_in, cotangent, segments, gains, biases, subs, scales, table, table_t, tap_table, win, wout, wup, wdn):
    layers = wup.shape[0]
    tokens, width = stream_in.shape
    channels = width // n
    ff = wup.shape[2] * n
    taps = subs.shape[1]

    def sds(*shape, dtype=BF):
        return jax.ShapeDtypeStruct(shape, dtype)

    wshapes = [(2 * layers, width, width), (layers, width, width), (layers, width, ff), (layers, ff, width)]
    wide, blocks = (layers, tokens, width), (layers, n, tokens, channels)
    outs = [
        sds(tokens, width), sds(*wide, dtype=F32), sds(*wide), sds(*wide), sds(*wide), sds(layers, 2 * tokens, 7 * channels), sds(*blocks), sds(*wide),
        sds(*wide, dtype=F32), sds(*wide), sds(layers, tokens, ff), sds(layers, tokens, ff),
        sds(layers, 4, 2, tokens, channels, dtype=F32), sds(10, tokens, channels), sds(tokens, width),
    ] + [sds(*s) for s in wshapes]
    f32 = lambda *s: pltpu.VMEM(s, F32)
    bf = lambda *s: pltpu.VMEM(s, BF)
    scratch = [
        f32(*wide), bf(*wide), bf(*wide), bf(*wide), bf(*wide), f32(*wide), bf(*wide), bf(layers, tokens, ff), bf(layers, tokens, ff),
        bf(*blocks), bf(*blocks), bf(*blocks), bf(*blocks),
        bf(tokens, 7 * channels), f32(2 * tokens, 7 * channels), bf(layers, 2 * tokens, 7 * channels), bf(2 * tokens, 7 * channels), f32(layers, 4, 2, tokens, channels),
    ] + [bf(*s) for s in wshapes] + [
        bf(10, tokens, channels), bf(tokens, width), bf(tokens, width), bf(tokens // 2, width), f32(tokens, width), bf(tokens, width),
        pltpu.VMEM(segments.shape, segments.dtype), bf(layers, taps, channels), bf(layers, taps, channels),
        bf(2 * tokens, tokens), bf(tokens, 2 * tokens), bf(4, 2 * tokens, taps),
        pltpu.SemaphoreType.DMA((5 * layers, 9)),
        pltpu.SemaphoreType.DMA((2 * layers, 2)),
        pltpu.SemaphoreType.DMA((16 * layers + 3,)),
        pltpu.SemaphoreType.DMA((3, 4)),
        pltpu.SemaphoreType.DMA((2,)),
        pltpu.SemaphoreType.DMA((4,)),
    ]
    return pl.pallas_call(
        functools.partial(forward_kernel, n, layers),
        out_shape=outs,
        in_specs=[VMEM] * 6 + [ANY] * 8,
        out_specs=[ANY] * len(outs),
        scratch_shapes=scratch,
        compiler_params=pltpu.CompilerParams(collective_id=1, has_side_effects=True, vmem_limit_bytes=60 * 2**20),
        name="forward",
    )(stream_in, segments, gains, biases, subs, scales, cotangent, table, table_t, tap_table, win, wout, wup, wdn)


PIECE_DOWN, PIECE_UP, PIECE_OUT, PIECE_IN, PIECE_GATE, PIECE_ROWS = 0, 64, 128, 144, 160, 176


def norm_back(upstream, src, base, gain, out, rounded):
    width = src.shape[1]

    def strip(j, sums):
        r = rows_of(j, 128)
        v = src[r, :]
        centred = v - jnp.mean(v, axis=-1, keepdims=True)
        inverse = lax.rsqrt(jnp.mean(centred * centred, axis=-1, keepdims=True) + EPSILON)
        xhat = centred * inverse
        up = upstream[r, :]
        q = gain * up
        both = q - jnp.mean(q, axis=-1, keepdims=True) - xhat * jnp.mean(q * xhat, axis=-1, keepdims=True)
        got = base[r, :] + both * inverse
        out[r, :] = got
        if rounded is not None:
            rounded[r, :] = got.astype(BF)
        p = up * xhat
        first, second = sums
        for k in range(0, 128, 8):
            first, second = first + p[k : k + 8], second + up[k : k + 8]
        return first, second

    zero = jnp.zeros((8, width), F32)
    return lax.fori_loop(0, src.shape[0] // 128, strip, (zero, zero))


def back_products(spec_x, spec_c, wins, out_g, out_d, channels):
    quarter = wins.shape[2]
    half = out_g.shape[1] // 2

    def strip(j):
        r = rows_of(j, 16)
        s = rows_of(j + quarter // 16, 16)
        cols = [slice(n * channels, (n + 1) * channels) for n in range(7)]
        cols2 = [slice(half + n * channels, half + (n + 1) * channels) for n in range(7)]
        cs = [(spec_c[r, c], spec_c[s, c]) for c in cols]
        for n in range(7):
            re = im = None
            for m in range(4 - n if n < 4 else 1):
                w, x = (wins[m, 0, r, :], wins[m, 1, r, :]), cs[n + m]
                a = w[0] * x[0] + w[1] * x[1]
                b = w[0] * x[1] - w[1] * x[0]
                re, im = (a, b) if re is None else (re + a, im + b)
            out_g[r, cols[n]] = re.astype(BF)
            out_g[r, cols2[n]] = im.astype(BF)
        sign = (1 - 2 * lax.rem(lax.broadcasted_iota(jnp.int32, (16, channels), 0), 2)).astype(F32)
        later = None
        for m in (3, 2, 1, 0):
            pairs = [(n - m, n) for n in range(m, 4)] + ([(n, n) for n in range(4, 7)] if m == 0 else [])
            re = im = None
            for i, n in pairs:
                x, c = (spec_x[r, cols[i]].astype(F32), spec_x[s, cols[i]].astype(F32)), cs[n]
                a = x[0] * c[0] + x[1] * c[1]
                b = x[0] * c[1] - x[1] * c[0]
                re, im = (a, b) if re is None else (re + a, im + b)
            dre, dim = (re, im) if later is None else (re + sign * later[1], im - sign * later[0])
            later = (re, im)
            out_d[r, cols[m]] = dre.astype(BF)
            out_d[r, cols2[m]] = dim.astype(BF)

    loop(quarter // 16, strip)


class Reduce:
    def __init__(self, place, bufs, sems, slot, layer, first, rows, order):
        self.p, self.layer, self.slot, self.sems, self.order = place, layer, slot, sems, order
        self.r = pl.ds(first, rows)
        self.first, self.rows = first, rows
        self.grads, self.r0, self.r1, self.r2, self.res = bufs
        self.spare = self.grads.shape[0] - 1

    def sem(self, k):
        return self.sems.at[self.slot, k]

    def strips(self, body):
        step = next(s for s in (80, 64, 32, 16) if self.rows % s == 0)
        loop(self.rows // step, lambda j: body(pl.ds(pl.multiple_of(self.first + j * step, 16), step)))

    def add_to(self, place_of, others, r):
        total = self.grads[(self.layer, *place_of, r, slice(None))].astype(F32)
        for other in others:
            total += other[r, :].astype(F32)
        return total

    def s0(self):
        send(self.grads.at[self.spare, :, :, :, self.r], self.r0.at[self.layer, :, :, :, self.r], self.sem(0), self.sem(1), self.p.sibling())

    def s1(self):
        p, l = self.p, self.layer
        await_bytes(self.r0.at[l, :, :, :, self.r], self.sem(0))
        await_bytes(self.r0.at[l, :, :, :, self.r], self.sem(1))

        def add(j):
            y, x, q = j // (2 * p.n), lax.rem(j // p.n, 2), lax.rem(j, p.n)

            def strip(r):
                self.grads[l, y, x, q, r, :] = self.add_to((y, x, q), [self.r0.at[l, y, x, q]], r).astype(BF)

            self.strips(strip)

        loop(4 * p.n, add)
        if self.order == "yx":
            send(self.grads.at[l, 1 - p.y, :, :, self.r], self.r1.at[l, pl.ds(0, 2), :, self.r], self.sem(2), self.sem(3), p.mate_y()[1])
        elif self.order == "xy":
            send(self.grads.at[l, :, 1 - p.x, :, self.r], self.r1.at[l, pl.ds(0, 2), :, self.r], self.sem(2), self.sem(3), p.mate_x()[1])
        else:
            send(self.grads.at[l, p.y, 1 - p.x, :, self.r], self.r1.at[l, 0, :, self.r], self.sem(2), self.sem(3), p.mate_x()[1])
            send(self.grads.at[l, 1 - p.y, p.x, :, self.r], self.r1.at[l, 1, :, self.r], self.sem(2), self.sem(3), p.mate_y()[1])
            send(self.grads.at[l, 1 - p.y, 1 - p.x, :, self.r], self.r1.at[l, 2, :, self.r], self.sem(2), self.sem(3), p.mate_xy()[1])

    def s1b(self):
        p, l = self.p, self.layer
        both = self.r1.at[l, pl.ds(0, 2), :, self.r]
        await_bytes(both, self.sem(2))
        await_bytes(both, self.sem(3))

        def add(j):
            k, q = j // p.n, lax.rem(j, p.n)
            y, x = (p.y, k) if self.order == "yx" else (k, p.x)

            def strip(r):
                self.grads[l, y, x, q, r, :] = self.add_to((y, x, q), [self.r1.at[l, k, q]], r).astype(BF)

            self.strips(strip)

        loop(2 * p.n, add)
        if self.order == "yx":
            send(self.grads.at[l, p.y, 1 - p.x, :, self.r], self.r1.at[l, 2, :, self.r], self.sem(4), self.sem(5), p.mate_x()[1])
        else:
            send(self.grads.at[l, 1 - p.y, p.x, :, self.r], self.r1.at[l, 2, :, self.r], self.sem(4), self.sem(5), p.mate_y()[1])

    def s2(self):
        p, l = self.p, self.layer
        if self.order == "direct":
            slots = (0, 1, 2)
            await_bytes(self.r1.at[l, :, :, self.r], self.sem(2))
            await_bytes(self.r1.at[l, :, :, self.r], self.sem(3))
        else:
            slots = (2,)
            await_bytes(self.r1.at[l, 2, :, self.r], self.sem(4))
            await_bytes(self.r1.at[l, 2, :, self.r], self.sem(5))

        def add(q):
            def strip(r):
                self.grads[l, p.y, p.x, q, r, :] = self.add_to((p.y, p.x, q), [self.r1.at[l, k, q] for k in slots], r).astype(BF)

            self.strips(strip)

        loop(p.n, add)
        for k in range(1, p.n):
            q, peer = p.column(k)
            send(self.grads.at[l, p.y, p.x, q, self.r], self.r2.at[l, k - 1, self.r], self.sem(6), self.sem(7), peer)

    def s3(self):
        p, l = self.p, self.layer
        await_bytes(self.r2.at[l, :, self.r], self.sem(6))
        await_bytes(self.r2.at[l, :, self.r], self.sem(7))

        def strip(r):
            total = self.add_to((p.y, p.x, p.q), [self.r2.at[l, k] for k in range(p.n - 1)], r)
            self.res[l, p.i, r, :] = total.astype(BF)

        self.strips(strip)
        piece = self.res.at[l, p.i, self.r]
        if self.order == "direct":
            for mate in (p.mate_x(), p.mate_y(), p.mate_xy()):
                send(piece, piece, self.sem(8), self.sem(9), mate[1])
        else:
            first, second = p.mates(self.order)
            send(piece, piece, self.sem(12), self.sem(13), first[1])
            send(piece, piece, self.sem(8), self.sem(9), second[1])

    def s3b(self):
        p, l = self.p, self.layer
        first, second = p.mates(self.order)
        await_bytes(self.res.at[l, 0, self.r], self.sem(13))
        piece = self.res.at[l, first[0], self.r]
        send(piece, piece, self.sem(8), self.sem(9), second[1])

    def spread(self):
        return self.res.at[self.layer, pl.ds(0, 3 if self.order == "direct" else 2), self.r]

    def s4(self):
        p, l = self.p, self.layer
        await_bytes(self.spread(), self.sem(9))
        for i in (p.i, p.mate_x()[0], p.mate_y()[0], p.mate_xy()[0]):
            piece = self.res.at[l, i, self.r]
            send(piece, piece, self.sem(10), self.sem(11), p.sibling())

    def end(self):
        half = self.res.at[self.layer, pl.ds(0, GROUP // 2), self.r]
        await_bytes(self.spread(), self.sem(8))
        if self.order != "direct":
            await_bytes(self.res.at[self.layer, 0, self.r], self.sem(12))
        await_bytes(half, self.sem(10))
        await_bytes(half, self.sem(11))


def in_order(own, others, l, here, count):
    total = None
    for j in range(count):
        k = lax.rem(here - j + count, count)
        value = jnp.where(k == 0, own.astype(F32), others[l, lax.max(k - 1, 0)].astype(F32))
        total = value if total is None else total + value
    return total


BACKWARD_ORDER = {"d0": "yx", "d1": "yx", "e0": "xy", "e1": "xy", "i0": "direct", "i1": "yx", "j0": "direct", "j1": "xy", "o0": "yx", "o1": "yx", "u0": "yx", "u1": "yx", "v0": "xy", "v1": "xy"}
BACKWARD_PLAN = {
    (1, "middle"): ("d1.s1",),
    (1, "out"): ("v1.s1",),
    (1, "sent"): ("e1.s1", "u1.s1"),
    (1, "transform"): ("o1.s1",),
    (1, "came"): ("d1.s1b",),
    (1, "products"): ("v1.s1b",),
    (1, "in"): ("j1.s1", "e1.s1b"),
    (1, "project"): ("d1.s2",),
    (1, "end"): ("u1.s1b",),
    (0, "down0"): ("i1.s1",),
    (0, "down"): ("d1.s3", "j1.s1b"),
    (0, "activate"): ("o1.s1b",),
    (0, "up0"): ("e0.s1", "d0.s1", "u1.s2"),
    (0, "up"): ("v1.s2",),
    (0, "narrow"): ("o1.s2",),
    (0, "middle"): ("kg1.over_mp", "u0.s1"),
    (0, "open"): ("i1.s1b",),
    (0, "sent"): ("e0.s1b", "d0.s1b", "e1.s2", "o0.s1", "u1.s3"),
    (0, "transform"): ("j1.s2",),
    (0, "arrived"): ("v0.s1",),
    (0, "came"): ("d0.s2",),
    (0, "half"): ("v1.s3", "u0.s1b", "kg1.over_group"),
    (0, "returned"): ("i1.s2",),
    (0, "gatep"): ("o0.s1b", "e0.s2", "v0.s1b"),
    (0, "in"): ("e1.s3", "j0.s1", "u0.s2"),
    (0, "in0"): ("i0.s1", "v0.s2", "kg1.take", "j1.s3", "j0.s2", "u1.s3b", "v1.s3b", "o0.s2", "kg0.over_mp"),
    (0, "project"): ("e1.s3b", "e0.s3", "j1.s3b", "i0.s2", "v0.s3"),
    (0, "end"): ("d0.s3", "o1.s3"),
    (0, "tail"): (
        "e1.s4", "u1.s4", "o0.s3", "v0.s3b", "i1.s3", "j1.s4", "u0.s3", "j0.s3", "norm.over_mp", "d1.s3b",
        "u0.s3b", "v1.s4", "d0.s3b", "i1.s3b", "v0.s4", "d1.s4", "e0.s3b", "i0.s3", "kg0.over_group", "o0.s3b",
        "o1.s3b", "u0.s4", "e0.s4", "o0.s4", "kg0.take", "i0.s4", "i1.s4", "o1.s4", "j0.s4", "d0.s4", "norm.take",
    ),
}


class KernelGrad:
    def __init__(self, place, layer, refs, sems):
        self.p, self.l, self.sems = place, layer, sems
        self.own, self.from_mp, self.mid, self.from_group, self.total, self.result = [r.at[layer] for r in refs]
        self.owner = place.s == place.q

    def sem(self, k):
        return self.sems.at[self.l, k]

    def start(self):
        when(jnp.logical_not(self.owner), lambda: send(self.own, self.from_mp, self.sem(0), self.sem(1), self.p.opposite()))

    def over_mp(self):
        p = self.p

        def add():
            await_bytes(self.from_mp, self.sem(1))
            self.mid[...] = (self.own[...].astype(F32) + self.from_mp[...].astype(F32)).astype(BF)
            for k, mate in enumerate((p.mate_x(), p.mate_y(), p.mate_xy())):
                send(self.mid, self.from_group.at[k], self.sem(2 + k), self.sem(5 + k), mate[1])

        when(self.owner, add)

    def over_group(self):
        p = self.p

        def add():
            for k in range(3):
                await_bytes(self.from_group.at[k], self.sem(5 + k))
            near = self.mid[...].astype(F32) + self.from_group[0].astype(F32)
            far = self.from_group[1].astype(F32) + self.from_group[2].astype(F32)
            both = (near + far).astype(BF)
            self.total[...] = both
            self.result[...] = both
            send(self.total, self.result, self.sem(8), self.sem(9), p.sibling())

        when(self.owner, add)

    def take(self):
        when(jnp.logical_not(self.owner), lambda: await_bytes(self.result, self.sem(9)))

    def finish(self):
        def given():
            for k in range(3):
                await_bytes(self.mid, self.sem(2 + k))
            await_bytes(self.total, self.sem(8))

        when(self.owner, given)
        when(jnp.logical_not(self.owner), lambda: await_bytes(self.own, self.sem(0)))


class NormGrad:
    def __init__(self, place, refs, sems):
        self.p, self.sems = place, sems
        self.own, self.from_group, self.mid, self.from_mp, self.result = refs
        self.layers = self.own.shape[0]

    def start(self, l):
        for k in range(1, GROUP):
            send(self.own.at[l], self.from_group.at[l, k - 1], self.sems.at[l, 0], self.sems.at[l, 1], self.p.member(k))

    def over_mp(self):
        p = self.p
        for l in reversed(range(self.layers)):
            await_bytes(self.from_group.at[l], self.sems.at[l, 0])
            await_bytes(self.from_group.at[l], self.sems.at[l, 1])
            self.mid[l] = in_order(self.own[l], self.from_group, l, p.i, GROUP)
            for k in range(1, p.n):
                send(self.mid.at[l], self.from_mp.at[l, k - 1], self.sems.at[l, 2], self.sems.at[l, 3], p.column(k)[1])

    def take(self):
        for l in reversed(range(self.layers)):
            await_bytes(self.from_mp.at[l], self.sems.at[l, 2])
            await_bytes(self.from_mp.at[l], self.sems.at[l, 3])
            self.result[l] = in_order(self.mid[l], self.from_mp, l, self.p.q, self.p.n)


def backward_kernel(
    n, layers,
    gains, subs, scales, masks_h, table_h, table_t_h, tap_t_h,
    out_in, cot, streams, hiddens, gacts, gslopes, specs, conv_outs, gateds, middles, hidden_mids, actives, slopes,
    wins_h, win_h, wout_h, wup_h, wdn_h,
    out_o, grad_o, res_o, sub_o, norm_o,
    grad, middle_grad, stream, hidden, gact, gslope, spec_x, conv_out, gated, middle, hidden_mid, active, slope, wins, win, wout, wup, wdn,
    grads, r0, r1, r2, res,
    up_grad, out_grad, branch, joined, big_a, big_b, spread,
    send_c, recv_c, send_d, recv_d, kg_s, kg_z, kg_t, kg_y, kg_u, kg_own, sub_s, masks, table, table_t, tap_t,
    norm_s, norm_r, norm_t, norm_u, norm_v, grad_p,
    load_sems, a2a_sems, red_sems, kg_sems, norm_sems, out_sems, move_sems,
):
    place = Place(n)
    me, core = place.s, place.core
    tokens, width = grad.shape
    channels = width // n
    quarter = tokens
    ff = wup.shape[1]
    half = ff // 2
    spare = grads.shape[0] - 1
    loads = {}
    sources = {
        "stream": (streams, stream), "hidden": (hiddens, hidden), "gact": (gacts, gact), "gslope": (gslopes, gslope),
        "spec_x": (specs, spec_x), "conv_out": (conv_outs, conv_out), "gated": (gateds, gated), "middle": (middles, middle),
        "hidden_mid": (hidden_mids, hidden_mid), "active": (actives, active), "slope": (slopes, slope), "wins": (wins_h, wins),
        "in": (win_h, win), "out": (wout_h, wout), "up": (wup_h, wup), "down": (wdn_h, wdn),
        "branch": (cot, branch), "masks": (masks_h, masks), "table": (table_h, table), "table_t": (table_t_h, table_t), "tap_t": (tap_t_h, tap_t),
    }
    once = ("branch", "masks", "table", "table_t", "tap_t")

    def load(name, l):
        src, dst = sources[name]
        copy = pltpu.make_async_copy(src if name in once else src.at[l], dst, load_sems.at[l, len([k for k in loads if k[1] == l])])
        copy.start()
        loads[name, l] = copy

    def ready(*names, l):
        for name in names:
            loads[name, l].wait()

    def next_load(*names, l):
        if l:
            for name in names:
                load(name, l - 1)

    top = layers - 1
    for name in ("branch", "active", "down"):
        load(name, top)
    greet_all(place)
    bufs = (grads, r0, r1, r2, res)
    bounds = (PIECE_DOWN, PIECE_UP // 2, PIECE_UP, (PIECE_UP + PIECE_OUT) // 2, PIECE_OUT, PIECE_IN, PIECE_GATE, PIECE_ROWS)
    groups = {}
    for l in range(layers):
        for k, letter in enumerate("deuvoij"):
            name = letter + str(l)
            order = BACKWARD_ORDER.get(name, "direct")
            groups[name] = Reduce(place, bufs, red_sems, len(groups), l, bounds[k], bounds[k + 1] - bounds[k], order)
    kernel_grads = [KernelGrad(place, l, (kg_s, kg_z, kg_t, kg_y, kg_u, kg_own), kg_sems) for l in range(layers)]
    norm_grads = NormGrad(place, (norm_s, norm_r, norm_t, norm_u, norm_v), norm_sems)
    out_move = Move(place, out_in, out_o, move_sems.at[0])
    grad_move = Move(place, branch, grad_o, move_sems.at[1], grad_p)
    moving = {"norm": norm_grads, **groups}
    moving.update({"kg" + str(l): kernel_grads[l] for l in range(layers)})

    def visit(l, point):
        for step in BACKWARD_PLAN.get((l, point), ()):
            what, action = step.split(".")
            getattr(moving[what], action)()

    def exchange_start(slot, src, dst, rows):
        for k in range(1, n):
            s, peer = place.partner(k)
            send(src.at[s, rows], dst.at[me, rows], a2a_sems.at[slot, 0], a2a_sems.at[slot, 1], peer)

    def exchange_wait(slot, src, dst, l):
        await_bytes(src.at[pl.ds(0, n - 1)], a2a_sems.at[slot, 0])
        await_bytes(dst.at[pl.ds(0, n - 1)], a2a_sems.at[slot, 1])

    def holder(parity, l):
        mine = 1 - (parity - core) * (parity - core)
        return l * mine + spare * (1 - mine)

    out_move.start()
    for name in ("slope", "hidden_mid", "up", "middle", "out", "gated", "gact", "gslope", "conv_out"):
        load(name, top)
    ready("branch", l=top)

    def widen_grad(j):
        r = rows_of(j, 64)
        grad[r, :] = branch[r, :].astype(F32)

    loop(tokens // 64, widen_grad)

    for l in reversed(range(layers)):
        ready("active", l=l)

        def grad_up(c):
            got = dot_tn(hidden_mid[:, rows_of(c, 128)], up_grad[...]).astype(BF)
            for par in range(2):
                for q in range(n):
                    grads[holder(par, l), c // 2, lax.rem(c, 2), q, PIECE_UP:PIECE_OUT, :] = got[par * 64 : par * 64 + 64, q * (ff // n) : (q + 1) * (ff // n)]

        def grad_down(q):
            got = dot_tn(active[:, rows_of(q, ff // n)], branch[...]).astype(BF)
            for i in range(GROUP):
                grads[holder(i % 2, l), i // 4, i // 2 % 2, q, PIECE_DOWN:PIECE_UP, :] = got[i * 64 : (i + 1) * 64]

        def grad_out():
            got = dot_tn(gated[...], out_grad[...]).astype(BF)
            for q in range(n):
                for i in range(GROUP):
                    at = q * channels + i * 16
                    grads[holder(i % 2, l), i // 4, i // 2 % 2, q, PIECE_OUT:PIECE_IN, :] = got[at : at + 16]

        def grad_in(h):
            got = dot_tn(hidden[...], joined[:, h * width : (h + 1) * width]).astype(BF)
            first = (PIECE_IN, PIECE_GATE)[h]
            for i in range(GROUP):
                for q in range(n):
                    for t in range(4):
                        at = i * 64 + t * 16
                        grads[holder(i % 2, l), i // 4, i // 2 % 2, q, first : first + 16, t * 128 : (t + 1) * 128] = got[
                            at : at + 16, q * channels : (q + 1) * channels
                        ]
            groups["ij"[h] + str(l)].s0()

        loop(n // 2, grad_down)
        visit(l, "down0")
        loop(n // 2, lambda q: grad_down(q + n // 2))
        for letter in "de":
            groups[letter + str(l)].s0()
        visit(l, "down")
        ready("down", "slope", l=l)
        for h in range(2):
            c = slice(h * half, (h + 1) * half)
            up_grad[:, c] = (dot_nt(branch[...], wdn[c, :]) * slope[:, c].astype(F32)).astype(BF)
        next_load("down", "slope", l=l)
        if l == top:
            for name in ("spec_x", "wins", "masks", "table", "table_t", "tap_t", "in", "hidden", "stream"):
                load(name, top)
        visit(l, "activate")
        ready("hidden_mid", l=l)
        loop(GROUP // 4, grad_up)
        visit(l, "up0")
        loop(GROUP // 4, lambda c: grad_up(c + GROUP // 4))
        for letter in "uv":
            groups[letter + str(l)].s0()
        next_load("hidden_mid", l=l)
        visit(l, "up")
        ready("up", l=l)
        big_a[...] = dot_nt(up_grad[...], wup[...])
        next_load("up", l=l)
        visit(l, "narrow")
        ready("middle", l=l)
        sums_mid = norm_back(big_a, middle, grad, gains[l, 1:2, :], middle_grad, out_grad)
        next_load("middle", l=l)
        visit(l, "middle")

        ready("gated", l=l)
        grad_out()
        groups["o" + str(l)].s0()
        next_load("gated", l=l)
        visit(l, "out")
        ready("out", l=l)
        big_b[0:tokens, 0:width] = dot_nt(out_grad[...], wout[...])
        next_load("out", l=l)
        visit(l, "open")
        ready("gact", "gslope", "conv_out", l=l)

        def unmix(j):
            r = rows_of(j, 32)
            for s in range(n):
                c = slice(s * channels, (s + 1) * channels)
                up = big_b[r, c]
                send_c[s, r, :] = (up * gact[r, c].astype(F32)).astype(BF)
                joined[r, slice(width + s * channels, width + (s + 1) * channels)] = (
                    up * conv_out[s, r, :].astype(F32) * gslope[r, c].astype(F32)
                ).astype(BF)

        for j in range(2):
            loop(tokens // 64, lambda k: unmix(k + j * (tokens // 64)))
            exchange_start(2 * l, send_c, recv_c, pl.ds(j * (tokens // 2), tokens // 2))
        next_load("gact", "gslope", "conv_out", l=l)
        recv_c[me] = send_c[me]
        visit(l, "sent")
        if l == top:
            ready("masks", "table", l=l)
        visit(l, "transform")
        exchange_wait(2 * l, send_c, recv_c, l)
        visit(l, "arrived")
        spread_blocks(recv_c, masks, spread)
        big_b[:, 0 : 7 * channels] = dot(table[...], spread[...])
        visit(l, "came")
        ready("wins", "spec_x", l=l)
        back_products(spec_x, big_b, wins, active, up_grad, channels)
        next_load("wins", "spec_x", l=l)
        visit(l, "products")
        if l == top:
            ready("table_t", "tap_t", l=l)

        for j in range(2):
            r = slice(j * (quarter // 2), (j + 1) * (quarter // 2))
            parts = dot(table_t[r, 0:quarter], active[:, 0 : 7 * channels])
            parts += dot(table_t[r, quarter : 2 * quarter], active[:, half : half + 7 * channels])
            for s in range(n):
                send_d[s, r, :] = join_blocks(parts, r, masks, s).astype(BF)
            exchange_start(2 * l + 1, send_d, recv_d, pl.ds(j * (quarter // 2), quarter // 2))
            if j == 0:
                visit(l, "half")
        recv_d[me] = send_d[me]
        next_load("active", l=l)

        taps = None
        for m in range(4):
            c = slice(m * channels, (m + 1) * channels)
            d = slice(half + m * channels, half + (m + 1) * channels)
            got = dot(tap_t[m, :, 0:quarter], up_grad[:, c]) + dot(tap_t[m, :, quarter : 2 * quarter], up_grad[:, d])
            taps = got if taps is None else taps + got
        kg_s[l] = taps.astype(BF)
        kernel_grads[l].start()
        visit(l, "returned")
        ready("in", "hidden", "stream", l=l)
        big_a[...] = dot_nt(joined[:, width : 2 * width], win[1])
        visit(l, "gatep")
        grad_in(1)
        visit(l, "in")
        exchange_wait(2 * l + 1, send_d, recv_d, l)

        def collect(j):
            r = rows_of(j, 64)
            for s in range(n):
                joined[r, s * channels : (s + 1) * channels] = recv_d[s, r, :]

        loop(tokens // 64, collect)
        if l == 0:
            grad_in(0)
        visit(l, "in0")
        big_a[...] = big_a[...] + dot_nt(joined[:, 0:width], win[0])
        next_load("in", l=l)
        visit(l, "project")
        sums_in = norm_back(big_a, stream, middle_grad, gains[l, 0:1, :], grad, branch)
        next_load("stream", l=l)
        if l == 0:
            grad_move.start()
        else:
            grad_in(0)
        next_load("hidden", l=l)
        norm_s[l] = jnp.concatenate(
            [jnp.sum(s, axis=0, keepdims=True) for s in (sums_in[0], sums_mid[0], sums_in[1], sums_mid[1])]
            + [jnp.zeros((4, width), F32)],
            axis=0,
        )
        norm_grads.start(l)
        if l == 0:
            grad_move.pass_on()
        visit(l, "end")

    visit(0, "tail")
    out_norm = pltpu.make_async_copy(norm_v, norm_o, out_sems.at[1])
    out_norm.start()
    for l in range(layers):
        raw, inverse = normal_taps(subs, scales, l)
        k = raw * inverse
        own = kg_own[l].astype(F32)
        along = jnp.sum(own * k, axis=0, keepdims=True)
        sub_s[l] = scales[0] * (own - scales[1] * k * along) * inverse
    out_sub = pltpu.make_async_copy(sub_s, sub_o, out_sems.at[0])
    out_sub.start()
    for group in groups.values():
        group.end()
    out_res = pltpu.make_async_copy(res, res_o, out_sems.at[2])
    out_res.start()
    for m in (out_move, grad_move):
        m.arrive()
        m.finish()
    for g in kernel_grads:
        g.finish()
    out_sub.wait()
    out_norm.wait()
    out_res.wait()


def backward(n, gains, subs, scales, masks, table, table_t, tap_t, out, cot, kept):
    layers, tokens, width = kept[0].shape
    channels = width // n
    ff = kept[-1].shape[1]
    taps = subs.shape[1]

    def sds(*shape, dtype=F32):
        return jax.ShapeDtypeStruct(shape, dtype)

    outs = [
        sds(tokens, width, dtype=BF), sds(tokens, width, dtype=BF), sds(layers, GROUP, PIECE_ROWS, width, dtype=BF),
        sds(layers, taps, channels), sds(layers, 8, width),
    ]
    f32 = lambda *s: pltpu.VMEM(s, F32)
    bf = lambda *s: pltpu.VMEM(s, BF)
    wide, blocks, small = (tokens, width), (n, tokens, channels), (layers, taps, channels)
    scratch = [
        f32(*wide), f32(*wide), f32(*wide), bf(*wide), bf(*wide), bf(*wide), bf(2 * tokens, 7 * channels), bf(*blocks), bf(*wide), f32(*wide), bf(*wide),
        bf(tokens, ff), bf(tokens, ff), f32(4, 2, tokens, channels),
        bf(2, width, width), bf(width, width), bf(width, ff), bf(ff, width),
        bf(layers + 1, 2, 2, n, PIECE_ROWS, width),
        bf(layers, 2, 2, n, PIECE_ROWS, width),
        bf(layers, 3, n, PIECE_ROWS, width),
        bf(layers, n - 1, PIECE_ROWS, width),
        bf(layers, GROUP, PIECE_ROWS, width),
        bf(tokens, ff), bf(*wide), bf(*wide), bf(tokens, 2 * width),
        f32(*wide), f32(2 * tokens, 7 * channels), bf(tokens, 7 * channels),
        bf(*blocks), bf(*blocks), bf(*blocks), bf(*blocks),
        bf(*small), bf(*small), bf(*small), bf(layers, 3, taps, channels), bf(*small), bf(*small), f32(*small),
        bf(10, tokens, channels), bf(2 * tokens, tokens), bf(tokens, 2 * tokens), bf(4, taps, 2 * tokens),
        f32(layers, 8, width), f32(layers, GROUP - 1, 8, width), f32(layers, 8, width), f32(layers, n - 1, 8, width), f32(layers, 8, width), bf(tokens // 2, width),
        pltpu.SemaphoreType.DMA((layers, 21)),
        pltpu.SemaphoreType.DMA((2 * layers, 2)),
        pltpu.SemaphoreType.DMA((7 * layers, 14)),
        pltpu.SemaphoreType.DMA((layers, 10)),
        pltpu.SemaphoreType.DMA((layers, 4)),
        pltpu.SemaphoreType.DMA((3,)),
        pltpu.SemaphoreType.DMA((2, 4)),
    ]
    return pl.pallas_call(
        functools.partial(backward_kernel, n, layers),
        out_shape=outs,
        in_specs=[VMEM] * 3 + [ANY] * (6 + len(kept)),
        out_specs=[ANY] * len(outs),
        scratch_shapes=scratch,
        compiler_params=pltpu.CompilerParams(collective_id=2, has_side_effects=True, vmem_limit_bytes=int(63.5 * 2**20)),
        name="backward",
    )(gains, subs, scales, masks, table, table_t, tap_t, out, cot, *kept)


def finish_kernel(out_i, grad_i, res, norms, sub_i, out, grad, up, down, out_w, in_w, gains, biases, sub):
    out[...] = out_i[...].astype(F32)
    grad[...] = grad_i[...].astype(F32)
    members = res.shape[1]
    for i in range(members):
        up[0, i * 64 : (i + 1) * 64, :] = res[0, i, PIECE_UP:PIECE_OUT, :].astype(F32)
        down[0, i * 64 : (i + 1) * 64, :] = res[0, i, PIECE_DOWN:PIECE_UP, :].astype(F32)
        out_w[0, i * 16 : (i + 1) * 16, :] = res[0, i, PIECE_OUT:PIECE_IN, :].astype(F32)
        for h, first in enumerate((PIECE_IN, PIECE_GATE)):
            for t in range(4):
                c = t * 128
                in_w[0, i * 64 + t * 16 : i * 64 + (t + 1) * 16, h, :] = res[0, i, first : first + 16, c : c + 128].astype(F32)
    gains[...] = norms[:, 0:2, :]
    biases[...] = norms[:, 2:4, :]
    sub[...] = sub_i[...]


def finish(out, grad, res, norms, sub):
    layers, members, _, width = res.shape
    tokens = out.shape[0]
    channels = sub.shape[2]
    parts = 2
    m = members // parts
    steps = layers * parts
    rows = tokens // steps

    def sds(*shape):
        return jax.ShapeDtypeStruct(shape, F32)

    def whole(a):
        return pl.BlockSpec(a.shape, lambda j: (0,) * len(a.shape))

    flat = pl.BlockSpec((rows, width), lambda j: (j, 0))

    def mid(*shape):
        return pl.BlockSpec((1, *shape, width), lambda j: (j // parts, j % parts, 0))

    vector = sds(layers, 2, width)
    return pl.pallas_call(
        finish_kernel,
        grid=(steps,),
        out_shape=[
            sds(tokens, width), sds(tokens, width), sds(layers, members * 64, width), sds(layers, members * 64, width),
            sds(layers, members * 16, width), sds(layers, members * 64, 2, channels), vector, vector, sds(*sub.shape),
        ],
        in_specs=[
            flat, flat, pl.BlockSpec((1, m, PIECE_ROWS, width), lambda j: (j // parts, j % parts, 0, 0)), whole(norms), whole(sub),
        ],
        out_specs=[
            flat, flat, mid(m * 64), mid(m * 64), mid(m * 16),
            pl.BlockSpec((1, m * 64, 2, channels), lambda j: (j // parts, j % parts, 0, 0)), whole(vector), whole(vector), whole(sub),
        ],
        name="finish",
    )(out, grad, res, norms, sub)


def per_device(
    stream_in, segments, norm_gain, norm_bias, w_in, w_out, sub_kernels, w_up, w_down, cotangent
):
    layers, scales, taps, channels = sub_kernels.shape
    n = lax.axis_size("mp")
    quarter = segments.shape[1] // 4
    table = transform_table(quarter)
    tap_table = tap_tables(quarter, scales, taps) / quarter

    def const(a):
        return jnp.asarray(a, F32).astype(BF)

    factors = jnp.asarray(tap_scales(scales, taps, channels))
    subs = sub_kernels.reshape(layers, -1, channels)
    out, *kept, masks, cot, win, wout, wup, wdn = forward(
        n, stream_in, cotangent, segments, norm_gain, norm_bias, subs, factors, const(table), const(table.T), const(tap_table),
        w_in.transpose(0, 2, 1, 3).reshape(2 * layers, -1, channels), w_out, w_up, w_down,
    )
    out, grad, res, sub, norms = backward(
        n, norm_gain, subs, factors, masks, const(table), const(table.T), const(tap_table.transpose(0, 2, 1)),
        out, cot, (*kept, win.reshape(layers, 2, *win.shape[1:]), wout, wup, wdn),
    )
    if lax.axis_size("dp") > GROUP:
        res, sub, norms = [v * (1.0 / GROUP) for v in lax.psum((res.astype(F32), sub, norms), "dp")]
        res = res.astype(BF)
    out, grad, up, down, out_w, in_w, gains, biases, sub = finish(out, grad, res, norms, sub)
    return out, grad, gains, biases, in_w, out_w, sub.reshape(sub_kernels.shape), up, down


def solution(mesh):
    rows = P(("dp", "mp"), None)
    last = P(None, None, None, "mp")
    mid = P(None, "mp", None)
    return jax.shard_map(
        per_device,
        mesh=mesh,
        in_specs=(rows, P("dp", None), P(), P(), last, mid, last, P(None, None, "mp"), mid, rows),
        out_specs=(rows, rows, P(), P(), last, mid, last, P(None, None, "mp"), mid),
        check_vma=False,
    )
```

```python
import functools

import jax
import jax.numpy as jnp
import numpy as np
from jax import lax
from jax.experimental import pallas as pl
from jax.experimental.pallas import tpu as pltpu
from jax.sharding import PartitionSpec as P

DECAY_RATE = 0.5
EPSILON = 1e-05
BF = jnp.bfloat16
F32 = jnp.float32
GROUP = 8
MESH = pl.DeviceIdType.MESH
VMEM = pl.BlockSpec(memory_space=pltpu.VMEM)
ANY = pl.BlockSpec(memory_space=pl.ANY)
GELU_A = float(np.sqrt(2.0 / np.pi))
GELU_B = 0.044715


def dot(a, b):
    return jnp.dot(a, b, preferred_element_type=F32)


def dot_nt(a, b):
    return lax.dot_general(a, b, (((1,), (1,)), ((), ())), preferred_element_type=F32)


def dot_tn(a, b):
    return lax.dot_general(a, b, (((0,), (0,)), ((), ())), preferred_element_type=F32)


def gelu(u):
    return 0.5 * u * (1.0 + jnp.tanh(GELU_A * (u + GELU_B * (u * u * u))))


def gelu_both(u):
    square = u * u
    t = jnp.tanh(GELU_A * (u + GELU_B * (square * u)))
    half = 0.5 * (1.0 + t)
    slope = half + (0.5 * u) * (1.0 - t * t) * (GELU_A + (3.0 * GELU_A * GELU_B) * square)
    return u * half, slope


def loop(count, body):
    lax.fori_loop(0, count, lambda j, c: (body(j), c)[1], 0)


def when(condition, body):
    pl.when(condition)(body)


def rows_of(j, size):
    return pl.ds(pl.multiple_of(j * size, size), size)


def transform_table(quarter):
    freq = np.arange(quarter)[:, None] + 0.5
    angle = np.pi * freq * np.arange(quarter)[None, :] / quarter
    return np.concatenate([np.cos(angle), -np.sin(angle)], axis=0)


def spread_matrix(scales, taps):
    lags = []
    for level in range(scales):
        lags += [level * taps + j for j in range(taps) for _ in range(2 ** max(level, 1))]
    spread = np.zeros((len(lags), scales * taps))
    spread[np.arange(len(lags)), lags] = 1.0
    return spread


def tap_tables(quarter, scales, taps):
    table = transform_table(quarter)
    spread = spread_matrix(scales, taps).reshape(4, quarter, scales * taps)
    return np.einsum("fp,mpt->mft", table, spread)


def tap_scales(scales, taps, channels):
    level = np.repeat(np.arange(scales), taps)
    decay = DECAY_RATE**level
    repeats = 2.0 ** np.maximum(level, 1)
    both = np.stack([decay, repeats])[:, :, None]
    return np.broadcast_to(both, (2, scales * taps, channels)).astype(np.float32)


class Place:
    def __init__(self, n):
        self.n = n
        self.q = lax.axis_index("mp")
        dp = lax.axis_index("dp")
        self.i = lax.rem(dp, GROUP)
        self.base = dp - self.i
        self.core = lax.rem(self.i, 2)
        self.x = lax.rem(self.i // 2, 2)
        self.y = self.i // 4
        self.s = lax.rem(self.q, 2) + 2 * self.core

    def device(self, i, q):
        return {"dp": self.base + i, "mp": q}

    def index(self, y, x, core):
        return 4 * y + 2 * x + core

    def column(self, k):
        q = lax.rem(self.q + k, self.n)
        return q, self.device(self.i, q)

    def member(self, k):
        return self.device(lax.rem(self.i + k, GROUP), self.q)

    def mate_x(self):
        i = self.index(self.y, 1 - self.x, self.core)
        return i, self.device(i, self.q)

    def mate_y(self):
        i = self.index(1 - self.y, self.x, self.core)
        return i, self.device(i, self.q)

    def mate_xy(self):
        i = self.index(1 - self.y, 1 - self.x, self.core)
        return i, self.device(i, self.q)

    def mates(self, order):
        return (self.mate_x(), self.mate_y()) if order == "xy" else (self.mate_y(), self.mate_x())

    def sibling(self):
        return self.device(self.index(self.y, self.x, 1 - self.core), self.q)

    def partner(self, k):
        s = lax.rem(self.s + k, self.n)
        return s, self.device(self.index(self.y, self.x, s // 2), 2 * (self.q // 2) + lax.rem(s, 2))

    def row_target(self):
        return self.device(self.index(self.y, self.x, self.q // 2), 2 * self.core + lax.rem(self.q, 2))

    def opposite(self):
        return self.device(self.i, lax.rem(self.q + 2, self.n))

    def stays(self):
        return self.q // 2 == self.core


def greet_all(place):
    barrier = pltpu.get_barrier_semaphore()
    peers = [place.column(k)[1] for k in range(1, place.n)] + [place.member(k) for k in range(1, GROUP)]
    across = place.index(place.y, place.x, 1 - place.core)
    peers += [place.device(across, place.column(k)[0]) for k in range(1, place.n)]
    for peer in peers:
        pl.semaphore_signal(barrier, inc=1, device_id=peer, device_id_type=MESH)
    pl.semaphore_wait(barrier, len(peers))


def send(src, dst, send_sem, recv_sem, peer):
    pltpu.make_async_remote_copy(
        src_ref=src, dst_ref=dst, send_sem=send_sem, recv_sem=recv_sem, device_id=peer, device_id_type=MESH
    ).start()


def await_bytes(ref, sem):
    pltpu.make_async_copy(ref, ref, sem).wait()


class Move:
    def __init__(self, place, src, dst, sems, relay=None):
        self.p, self.src, self.dst, self.sems, self.relay = place, src, dst, sems, relay
        half = src.shape[0] // 2
        self.first = pl.ds(0, src.shape[0] if relay is None else half)
        self.second = pl.ds(half, half)

    def start(self):
        p = self.p

        def across():
            send(self.src.at[self.first], self.dst.at[self.first], self.sems.at[0], self.sems.at[1], p.row_target())
            if self.relay is not None:
                send(self.src.at[self.second], self.relay, self.sems.at[0], self.sems.at[2], p.sibling())

        when(jnp.logical_not(p.stays()), across)
        when(p.stays(), lambda: pltpu.make_async_copy(self.src, self.dst, self.sems.at[1]).start())

    def pass_on(self):
        def onward():
            await_bytes(self.relay, self.sems.at[2])
            send(self.relay, self.dst.at[self.second], self.sems.at[3], self.sems.at[1], self.p.opposite())

        when(self.p.stays(), onward)

    def arrive(self):
        await_bytes(self.dst, self.sems.at[1])

    def finish(self):
        when(jnp.logical_not(self.p.stays()), lambda: await_bytes(self.src, self.sems.at[0]))
        if self.relay is not None:
            when(self.p.stays(), lambda: await_bytes(self.relay, self.sems.at[3]))


class Weight:
    def __init__(self, whole, layer, columns, n):
        self.whole, self.columns, self.layer, self.n = whole, columns, layer, n
        shape = whole.shape
        self.rows = shape[1] // GROUP if columns else shape[1] // n // GROUP
        self.cols = shape[2] // n if columns else shape[2]

    def piece(self, i, q):
        r, c = self.rows, self.cols
        if self.columns:
            return self.whole.at[self.layer, pl.ds(i * r, r), pl.ds(q * c, c)]
        return self.whole.at[self.layer, pl.ds((q * GROUP + i) * r, r), :]

    def shard(self, q):
        r, c = self.rows, self.cols
        if self.columns:
            return self.whole.at[self.layer, :, pl.ds(q * c, c)]
        return self.whole.at[self.layer, pl.ds(q * GROUP * r, GROUP * r), :]

    def local_piece(self, shard, i):
        return shard.at[self.layer, pl.ds(i * self.rows, self.rows), :]

    def span(self, members):
        r, c, k = self.rows, self.cols, self.n - 1
        if self.columns:
            return self.whole.at[self.layer, pl.ds(0, members * r), pl.ds(0, k * c)]
        return self.whole.at[self.layer, pl.ds(0, members * k * r), :]


class Gather:
    def __init__(self, place, weight, shard, sems, slot, order):
        self.p, self.w, self.shard_ref, self.sems, self.slot, self.order = place, weight, shard, sems, slot, order

    def sem(self, k):
        return self.sems.at[self.slot, k]

    def own(self):
        return pltpu.make_async_copy(
            self.shard_ref.at[self.w.layer], self.w.shard(self.p.q), self.sem(8)
        )

    def start(self):
        p, w = self.p, self.w
        for k in range(1, p.n):
            send(w.local_piece(self.shard_ref, p.i), w.piece(p.i, p.q), self.sem(0), self.sem(1), p.column(k)[1])
        self.own().start()

    def pass_on(self, i, send_sem, recv_sem, peer):
        p, w = self.p, self.w
        for k in range(1, p.n):
            piece = w.piece(i, p.column(k)[0])
            send(piece, piece, send_sem, recv_sem, peer)

    def first_second(self):
        return self.p.mates("yx" if self.order == "yx" else "xy")

    def hop1(self):
        p = self.p
        await_bytes(self.w.span(1), self.sem(1))
        first, second = self.first_second()
        self.pass_on(p.i, self.sem(2), self.sem(3), first[1])
        self.pass_on(p.i, self.sem(4), self.sem(5), second[1])
        if self.order == "direct":
            self.pass_on(p.i, self.sem(4), self.sem(5), p.mate_xy()[1])
        self.pass_on(p.i, self.sem(6), self.sem(7), p.sibling())

    def hop2(self):
        first, second = self.first_second()
        await_bytes(self.w.span(1), self.sem(3))
        self.pass_on(first[0], self.sem(4), self.sem(5), second[1])
        self.pass_on(first[0], self.sem(6), self.sem(7), self.p.sibling())

    def hop3(self):
        p = self.p
        first, second = self.first_second()
        others = [second[0], p.mate_xy()[0]]
        if self.order == "direct":
            await_bytes(self.w.span(1), self.sem(3))
            others.append(first[0])
        await_bytes(self.w.span(2), self.sem(5))
        for i in others:
            self.pass_on(i, self.sem(6), self.sem(7), p.sibling())

    def arrive(self):
        self.own().wait()
        await_bytes(self.w.span(4), self.sem(7))

    def finish(self):
        await_bytes(self.w.span(1), self.sem(0))
        await_bytes(self.w.span(1), self.sem(2))
        await_bytes(self.w.span(2), self.sem(4))
        await_bytes(self.w.span(4), self.sem(6))


def norm_strip(v, gain, bias):
    centred = v - jnp.mean(v, axis=-1, keepdims=True)
    variance = jnp.mean(centred * centred, axis=-1, keepdims=True)
    return centred * lax.rsqrt(variance + EPSILON) * gain + bias


def norm_all(src, dst, gain, bias):
    def strip(j):
        r = rows_of(j, 128)
        dst[r, :] = norm_strip(src[r, :], gain, bias).astype(BF)

    loop(dst.shape[0] // 128, strip)


def normal_taps(sub_ref, scale_ref, layer):
    raw = sub_ref[layer] * scale_ref[0]
    total = jnp.sum(raw * raw * scale_ref[1], axis=0, keepdims=True)
    return raw, lax.rsqrt(total + EPSILON)


def make_masks(segs, masks):
    quarter, channels = masks.shape[1:]
    ones = jnp.full((8, channels), 0.125, BF)

    def numbers(n):
        row = segs[:, n * quarter : (n + 1) * quarter].astype(F32)
        return dot_tn(jnp.broadcast_to(row, (8, quarter)).astype(BF), ones)

    def put(k, flag):
        masks[k] = jnp.where(flag, 1.0, 0.0).astype(BF)

    long_doc = numbers(1)[0:1, :]
    for n in range(4):
        here = numbers(n)
        put(n, here == long_doc)
        if n in (0, 3):
            for k in range(3):
                doc = jnp.where(long_doc <= k, k + 1.0, float(k))
                put(4 + 2 * k + (n == 3), here == doc)


def make_windows(taps, tap_ref, spec, layer, wins):
    channels = taps.shape[1]
    quarter = wins.shape[3]
    for m in range(4):
        spec[:, m * channels : (m + 1) * channels] = dot(tap_ref[m], taps)

    def strip(j):
        r = rows_of(j, 16)
        s = rows_of(j + quarter // 16, 16)
        sign = (1 - 2 * lax.rem(lax.broadcasted_iota(jnp.int32, (16, channels), 0), 2)).astype(F32)
        for m in range(4):
            here = slice(m * channels, (m + 1) * channels)
            re, im = spec[r, here], spec[s, here]
            if m:
                before = slice((m - 1) * channels, m * channels)
                re, im = re - sign * spec[s, before], im + sign * spec[r, before]
            wins[layer, m, 0, r, :] = re
            wins[layer, m, 1, r, :] = im

    loop(quarter // 16, strip)


def spread_blocks(blocks, masks, out):
    channels = masks.shape[2]
    for n in range(4):
        out[:, n * channels : (n + 1) * channels] = blocks[n] * masks[n]
    for k in range(3):
        out[:, (4 + k) * channels : (5 + k) * channels] = (
            blocks[0] * masks[4 + 2 * k] + blocks[3] * masks[5 + 2 * k]
        )


def join_blocks(parts, r, masks, n):
    channels = masks.shape[2]
    total = parts[:, n * channels : (n + 1) * channels] * masks[n, r, :].astype(F32)
    if n in (0, 3):
        for k in range(3):
            mask = masks[4 + 2 * k + (n == 3), r, :].astype(F32)
            total += parts[:, (4 + k) * channels : (5 + k) * channels] * mask
    return total


def fwd_products(spec, wins, layer, out, kept, channels):
    quarter = wins.shape[3]

    def strip(j):
        r = rows_of(j, 16)
        s = rows_of(j + quarter // 16, 16)
        xs = [(spec[r, n * channels : (n + 1) * channels], spec[s, n * channels : (n + 1) * channels]) for n in range(7)]
        for n in range(7):
            c = slice(n * channels, (n + 1) * channels)
            kept[layer, r, c] = xs[n][0].astype(BF)
            kept[layer, s, c] = xs[n][1].astype(BF)
        ws = [(wins[layer, m, 0, r, :], wins[layer, m, 1, r, :]) for m in range(4)]
        for n in range(7):
            re = im = None
            for m in range(n + 1 if n < 4 else 1):
                w, x = ws[m], xs[n - m]
                a = w[0] * x[0] - w[1] * x[1]
                b = w[0] * x[1] + w[1] * x[0]
                re, im = (a, b) if re is None else (re + a, im + b)
            out[r, n * channels : (n + 1) * channels] = re.astype(BF)
            out[s, n * channels : (n + 1) * channels] = im.astype(BF)

    loop(quarter // 16, strip)


FORWARD_ORDER = {"c0": "direct", "c1": "direct", "d0": "direct", "d1": "direct", "g0": "direct", "g1": "direct", "o0": "direct", "o1": "direct", "u0": "direct", "u1": "direct"}
FORWARD_PLAN = {
    (0, "start2"): ("c0.hop1", "c0.hop3"),
    (0, "ready"): ("g0.start", "o0.start", "u0.start", "g0.hop1"),
    (0, "sent"): ("d0.start", "o0.hop1", "g0.hop3"),
    (0, "gate0"): ("u0.hop1",),
    (0, "masks"): ("c1.start", "o0.hop3"),
    (0, "win0"): ("o1.start",),
    (0, "win1"): ("g1.start",),
    (0, "transform"): ("d0.hop1",),
    (0, "returned"): ("u1.start", "c1.hop1", "u0.hop3"),
    (0, "back"): ("d1.start",),
    (0, "act0"): ("o1.hop1", "d0.hop3"),
    (0, "activate"): ("g1.hop1", "c1.hop3"),
    (1, "normed"): ("u1.hop1",),
    (1, "sent"): ("cot.start", "g1.hop3"),
    (1, "gate"): ("d1.hop1",),
    (1, "returned"): ("o1.hop3", "u1.hop3"),
    (1, "attach"): ("d1.hop3",),
}


def forward_kernel(
    n, layers,
    stream_in, segs, gains, biases, subs, scales, cot_h, table_h, table_t_h, tap_table_h, win, wout, wup, wdn,
    out_o, streams_o, hidden_o, gact_o, gslope_o, spec_o, conv_out_o, gated_o, middle_o, hidden_mid_o, active_o, slope_o,
    wins_o, masks_o, cot_o, win_o, wout_o, wup_o, wdn_o,
    stream, hidden, gact, gslope, gated, middle, hidden_mid, active, slope, send_a, recv_a, send_b, recv_b,
    spread, spec, spec_x, spec_y, wins, win_f, wout_f, wup_f, wdn_f,
    masks, tok_s, tok_r, tok_p, cot_in, cot_s, seg_r, taps_s, taps_r, table, table_t, tap_table,
    gather_sems, a2a_sems, save_sems, move_sems, tap_sems, load_sems,
):
    place = Place(n)
    me = place.s
    tokens, width = stream_in.shape
    channels = width // n
    quarter = tokens
    half = wup_f.shape[2] // 2
    loads = [
        pltpu.make_async_copy(src, dst, load_sems.at[k])
        for k, (src, dst) in enumerate(((cot_h, cot_in), (tap_table_h, tap_table), (table_h, table), (table_t_h, table_t)))
    ]
    greet_all(place)
    saves = []

    def save(src, dst, l=None):
        if l is not None:
            src, dst = src.at[l], dst.at[l]
        copy = pltpu.make_async_copy(src, dst, save_sems.at[len(saves)])
        copy.start()
        saves.append(copy)

    def exchange_start(slot, src, dst, layer, rows=None):
        rows = pl.ds(0, tokens) if rows is None else rows
        for k in range(1, n):
            s, peer = place.partner(k)
            send(src.at[layer, s, rows], dst.at[layer, me, rows], a2a_sems.at[slot, 0], a2a_sems.at[slot, 1], peer)

    def exchange_wait(slot, src, dst, layer):
        await_bytes(src.at[layer, pl.ds(0, n - 1)], a2a_sems.at[slot, 0])
        await_bytes(dst.at[layer, pl.ds(0, n - 1)], a2a_sems.at[slot, 1])

    moving = {
        "seg": Move(place, segs, seg_r, move_sems.at[0]),
        "tok": Move(place, tok_s, tok_r, move_sems.at[1], tok_p),
        "cot": Move(place, cot_s, cot_o, move_sems.at[2]),
    }
    gathers = {}
    for l in range(layers):
        for letter, whole, shard, index, columns in (
            ("c", win_f, win, 2 * l, True), ("g", win_f, win, 2 * l + 1, True), ("o", wout_f, wout, l, False),
            ("u", wup_f, wup, l, True), ("d", wdn_f, wdn, l, False),
        ):
            name = letter + str(l)
            weight = Weight(whole, index, columns, n)
            gathers[name] = Gather(place, weight, shard, gather_sems, len(gathers), FORWARD_ORDER.get(name, "xy"))
    moving.update(gathers)

    def visit(l, point):
        for step in FORWARD_PLAN.get((l, point), ()):
            what, action = step.split(".")
            getattr(moving[what], action)()

    gathers["c0"].start()

    def round_stream(j):
        r = rows_of(j, 64)
        tok_s[r, :] = stream_in[r, :].astype(BF)

    loop(tokens // 64, round_stream)
    moving["tok"].start()
    moving["seg"].start()
    for l in range(layers):
        raw, inverse = normal_taps(subs, scales, l)
        taps_s[l] = (raw * inverse).astype(BF)

    def give_taps():
        send(taps_s, taps_r, tap_sems.at[0], tap_sems.at[1], place.opposite())

    def keep_taps():
        taps_r[...] = taps_s[...]

    def take_taps():
        await_bytes(taps_r, tap_sems.at[1])

    own_taps = place.s == place.q
    when(own_taps, give_taps)
    for copy in loads:
        copy.start()
    when(own_taps, keep_taps)
    moving["tok"].pass_on()
    visit(0, "start")
    loads[0].wait()

    def round_cotangent(j):
        r = rows_of(j, 64)
        cot_s[r, :] = cot_in[r, :].astype(BF)

    loop(tokens // 64, round_cotangent)
    visit(0, "start2")
    moving["tok"].arrive()
    visit(0, "ready")

    def widen_stream(j):
        r = rows_of(j, 64)
        stream[0, r, :] = tok_r[r, :].astype(F32)

    loop(tokens // 64, widen_stream)
    save(stream, streams_o, 0)

    for l in range(layers):
        norm_all(stream.at[l], hidden.at[l], gains[l, 0:1, :], biases[l, 0:1, :])
        visit(l, "normed")
        gathers["c" + str(l)].arrive()
        got = dot(hidden[l], win_f[2 * l]).astype(BF)
        for s in range(n):
            send_a[l, s] = got[:, s * channels : (s + 1) * channels]
        visit(l, "project")
        exchange_start(2 * l, send_a, recv_a, l)
        recv_a[l, me] = send_a[l, me]
        visit(l, "sent")
        save(hidden, hidden_o, l)
        gathers["g" + str(l)].arrive()
        spec[0:tokens, 0:width] = dot(hidden[l], win_f[2 * l + 1])
        visit(l, "gate0")

        def open_gate(j):
            r = rows_of(j, 16)
            act, incline = gelu_both(spec[r, 0:width])
            gact[l, r, :] = act.astype(BF)
            gslope[l, r, :] = incline.astype(BF)

        loop(tokens // 16, open_gate)
        visit(l, "gate")
        save(win_f, win_o, 2 * l)
        save(win_f, win_o, 2 * l + 1)
        save(gact, gact_o, l)
        save(gslope, gslope_o, l)
        if l == 0:
            moving["seg"].arrive()
            make_masks(seg_r, masks)
            save(masks, masks_o)
            visit(l, "masks")
            when(jnp.logical_not(own_taps), take_taps)
            loads[1].wait()
            for m in range(layers):
                make_windows(taps_r[m], tap_table, spec, m, wins)
                visit(l, "win" + str(m))
            save(wins, wins_o)
            loads[2].wait()
            loads[3].wait()
        exchange_wait(2 * l, send_a, recv_a, l)
        visit(l, "came")
        spread_blocks(recv_a.at[l], masks, spread)
        spec[:, 0 : 7 * channels] = dot(table[...], spread[...])
        visit(l, "transform")
        fwd_products(spec, wins, l, spec_y, spec_x, channels)
        save(spec_x, spec_o, l)
        visit(l, "prod")
        for j in range(2):
            r = slice(j * (quarter // 2), (j + 1) * (quarter // 2))
            parts = dot(table_t[r, :], spec_y[...])
            for s in range(n):
                send_b[l, s, r, :] = join_blocks(parts, r, masks, s).astype(BF)
            exchange_start(2 * l + 1, send_b, recv_b, l, pl.ds(j * (quarter // 2), quarter // 2))
            if j == 0:
                visit(l, "untr")
        recv_b[l, me] = send_b[l, me]
        visit(l, "returned")
        exchange_wait(2 * l + 1, send_b, recv_b, l)
        visit(l, "back")
        save(recv_b, conv_out_o, l)

        def mix(j):
            r = rows_of(j, 64)
            for s in range(n):
                c = slice(s * channels, (s + 1) * channels)
                gated[l, r, c] = (gact[l, r, c].astype(F32) * recv_b[l, s, r, :].astype(F32)).astype(BF)

        loop(tokens // 64, mix)
        visit(l, "mix")
        gathers["o" + str(l)].arrive()
        save(gated, gated_o, l)
        save(wout_f, wout_o, l)
        middle[l] = stream[l] + dot(gated[l], wout_f[l])
        visit(l, "attach")
        save(middle, middle_o, l)
        norm_all(middle.at[l], hidden_mid.at[l], gains[l, 1:2, :], biases[l, 1:2, :])
        visit(l, "norm")
        gathers["u" + str(l)].arrive()
        save(hidden_mid, hidden_mid_o, l)
        save(wup_f, wup_o, l)
        for h in range(2):
            c = slice(h * half, (h + 1) * half)
            act, incline = gelu_both(dot(hidden_mid[l], wup_f[l, :, c]))
            active[l, :, c] = act.astype(BF)
            slope[l, :, c] = incline.astype(BF)
            visit(l, ("act0", "activate")[h])
            save(active.at[l, :, c], active_o.at[l, :, c])
            save(slope.at[l, :, c], slope_o.at[l, :, c])
        gathers["d" + str(l)].arrive()
        save(wdn_f, wdn_o, l)
        if l + 1 < layers:
            stream[l + 1] = middle[l] + dot(active[l], wdn_f[l])
            save(stream, streams_o, l + 1)
        else:
            moving["tok"].finish()
            tok_s[...] = (middle[l] + dot(active[l], wdn_f[l])).astype(BF)
            save(tok_s, out_o)
        visit(l, "narrow")
    for g in gathers.values():
        g.finish()
    moving["cot"].arrive()
    for name in ("seg", "cot"):
        moving[name].finish()

    when(own_taps, lambda: await_bytes(taps_s, tap_sems.at[0]))
    for copy in saves:
        copy.wait()


def forward(n, stream_in, cotangent, segments, gains, biases, subs, scales, table, table_t, tap_table, win, wout, wup, wdn):
    layers = wup.shape[0]
    tokens, width = stream_in.shape
    channels = width // n
    ff = wup.shape[2] * n
    taps = subs.shape[1]

    def sds(*shape, dtype=BF):
        return jax.ShapeDtypeStruct(shape, dtype)

    wshapes = [(2 * layers, width, width), (layers, width, width), (layers, width, ff), (layers, ff, width)]
    wide, blocks = (layers, tokens, width), (layers, n, tokens, channels)
    outs = [
        sds(tokens, width), sds(*wide, dtype=F32), sds(*wide), sds(*wide), sds(*wide), sds(layers, 2 * tokens, 7 * channels), sds(*blocks), sds(*wide),
        sds(*wide, dtype=F32), sds(*wide), sds(layers, tokens, ff), sds(layers, tokens, ff),
        sds(layers, 4, 2, tokens, channels, dtype=F32), sds(10, tokens, channels), sds(tokens, width),
    ] + [sds(*s) for s in wshapes]
    f32 = lambda *s: pltpu.VMEM(s, F32)
    bf = lambda *s: pltpu.VMEM(s, BF)
    scratch = [
        f32(*wide), bf(*wide), bf(*wide), bf(*wide), bf(*wide), f32(*wide), bf(*wide), bf(layers, tokens, ff), bf(layers, tokens, ff),
        bf(*blocks), bf(*blocks), bf(*blocks), bf(*blocks),
        bf(tokens, 7 * channels), f32(2 * tokens, 7 * channels), bf(layers, 2 * tokens, 7 * channels), bf(2 * tokens, 7 * channels), f32(layers, 4, 2, tokens, channels),
    ] + [bf(*s) for s in wshapes] + [
        bf(10, tokens, channels), bf(tokens, width), bf(tokens, width), bf(tokens // 2, width), f32(tokens, width), bf(tokens, width),
        pltpu.VMEM(segments.shape, segments.dtype), bf(layers, taps, channels), bf(layers, taps, channels),
        bf(2 * tokens, tokens), bf(tokens, 2 * tokens), bf(4, 2 * tokens, taps),
        pltpu.SemaphoreType.DMA((5 * layers, 9)),
        pltpu.SemaphoreType.DMA((2 * layers, 2)),
        pltpu.SemaphoreType.DMA((18 * layers + 3,)),
        pltpu.SemaphoreType.DMA((3, 4)),
        pltpu.SemaphoreType.DMA((2,)),
        pltpu.SemaphoreType.DMA((4,)),
    ]
    return pl.pallas_call(
        functools.partial(forward_kernel, n, layers),
        out_shape=outs,
        in_specs=[VMEM] * 6 + [ANY] * 8,
        out_specs=[ANY] * len(outs),
        scratch_shapes=scratch,
        compiler_params=pltpu.CompilerParams(collective_id=1, has_side_effects=True, vmem_limit_bytes=60 * 2**20),
        name="forward",
    )(stream_in, segments, gains, biases, subs, scales, cotangent, table, table_t, tap_table, win, wout, wup, wdn)


PIECE_DOWN, PIECE_UP, PIECE_OUT, PIECE_IN, PIECE_GATE, PIECE_ROWS = 0, 64, 128, 144, 160, 176


def norm_back(upstream, src, base, gain, out, rounded):
    width = src.shape[1]

    def strip(j, sums):
        r = rows_of(j, 128)
        v = src[r, :]
        centred = v - jnp.mean(v, axis=-1, keepdims=True)
        inverse = lax.rsqrt(jnp.mean(centred * centred, axis=-1, keepdims=True) + EPSILON)
        xhat = centred * inverse
        up = upstream[r, :]
        q = gain * up
        both = q - jnp.mean(q, axis=-1, keepdims=True) - xhat * jnp.mean(q * xhat, axis=-1, keepdims=True)
        got = base[r, :] + both * inverse
        out[r, :] = got
        if rounded is not None:
            rounded[r, :] = got.astype(BF)
        p = up * xhat
        first, second = sums
        for k in range(0, 128, 8):
            first, second = first + p[k : k + 8], second + up[k : k + 8]
        return first, second

    zero = jnp.zeros((8, width), F32)
    return lax.fori_loop(0, src.shape[0] // 128, strip, (zero, zero))


def back_products(spec_x, spec_c, wins, out_g, out_d, channels):
    quarter = wins.shape[2]
    half = out_g.shape[1] // 2

    def strip(j):
        r = rows_of(j, 16)
        s = rows_of(j + quarter // 16, 16)
        cols = [slice(n * channels, (n + 1) * channels) for n in range(7)]
        cols2 = [slice(half + n * channels, half + (n + 1) * channels) for n in range(7)]
        cs = [(spec_c[r, c], spec_c[s, c]) for c in cols]
        for n in range(7):
            re = im = None
            for m in range(4 - n if n < 4 else 1):
                w, x = (wins[m, 0, r, :], wins[m, 1, r, :]), cs[n + m]
                a = w[0] * x[0] + w[1] * x[1]
                b = w[0] * x[1] - w[1] * x[0]
                re, im = (a, b) if re is None else (re + a, im + b)
            out_g[r, cols[n]] = re.astype(BF)
            out_g[r, cols2[n]] = im.astype(BF)
        sign = (1 - 2 * lax.rem(lax.broadcasted_iota(jnp.int32, (16, channels), 0), 2)).astype(F32)
        later = None
        for m in (3, 2, 1, 0):
            pairs = [(n - m, n) for n in range(m, 4)] + ([(n, n) for n in range(4, 7)] if m == 0 else [])
            re = im = None
            for i, n in pairs:
                x, c = (spec_x[r, cols[i]].astype(F32), spec_x[s, cols[i]].astype(F32)), cs[n]
                a = x[0] * c[0] + x[1] * c[1]
                b = x[0] * c[1] - x[1] * c[0]
                re, im = (a, b) if re is None else (re + a, im + b)
            dre, dim = (re, im) if later is None else (re + sign * later[1], im - sign * later[0])
            later = (re, im)
            out_d[r, cols[m]] = dre.astype(BF)
            out_d[r, cols2[m]] = dim.astype(BF)

    loop(quarter // 16, strip)


class Reduce:
    def __init__(self, place, bufs, sems, slot, layer, first, rows, order):
        self.p, self.layer, self.slot, self.sems, self.order = place, layer, slot, sems, order
        self.r = pl.ds(first, rows)
        self.first, self.rows = first, rows
        self.grads, self.r0, self.r1, self.r2, self.res = bufs
        self.spare = self.grads.shape[0] - 1

    def sem(self, k):
        return self.sems.at[self.slot, k]

    def strips(self, body):
        step = next(s for s in (80, 64, 32, 16) if self.rows % s == 0)
        loop(self.rows // step, lambda j: body(pl.ds(pl.multiple_of(self.first + j * step, 16), step)))

    def add_to(self, place_of, others, r):
        total = self.grads[(self.layer, *place_of, r, slice(None))].astype(F32)
        for other in others:
            total += other[r, :].astype(F32)
        return total

    def s0(self):
        send(self.grads.at[self.spare, :, :, :, self.r], self.r0.at[self.layer, :, :, :, self.r], self.sem(0), self.sem(1), self.p.sibling())

    def s1(self):
        p, l = self.p, self.layer
        await_bytes(self.r0.at[l, :, :, :, self.r], self.sem(0))
        await_bytes(self.r0.at[l, :, :, :, self.r], self.sem(1))

        def add(j):
            y, x, q = j // (2 * p.n), lax.rem(j // p.n, 2), lax.rem(j, p.n)

            def strip(r):
                self.grads[l, y, x, q, r, :] = self.add_to((y, x, q), [self.r0.at[l, y, x, q]], r).astype(BF)

            self.strips(strip)

        loop(4 * p.n, add)
        if self.order == "yx":
            send(self.grads.at[l, 1 - p.y, :, :, self.r], self.r1.at[l, pl.ds(0, 2), :, self.r], self.sem(2), self.sem(3), p.mate_y()[1])
        elif self.order == "xy":
            send(self.grads.at[l, :, 1 - p.x, :, self.r], self.r1.at[l, pl.ds(0, 2), :, self.r], self.sem(2), self.sem(3), p.mate_x()[1])
        else:
            send(self.grads.at[l, p.y, 1 - p.x, :, self.r], self.r1.at[l, 0, :, self.r], self.sem(2), self.sem(3), p.mate_x()[1])
            send(self.grads.at[l, 1 - p.y, p.x, :, self.r], self.r1.at[l, 1, :, self.r], self.sem(2), self.sem(3), p.mate_y()[1])
            send(self.grads.at[l, 1 - p.y, 1 - p.x, :, self.r], self.r1.at[l, 2, :, self.r], self.sem(2), self.sem(3), p.mate_xy()[1])

    def s1b(self):
        p, l = self.p, self.layer
        both = self.r1.at[l, pl.ds(0, 2), :, self.r]
        await_bytes(both, self.sem(2))
        await_bytes(both, self.sem(3))

        def add(j):
            k, q = j // p.n, lax.rem(j, p.n)
            y, x = (p.y, k) if self.order == "yx" else (k, p.x)

            def strip(r):
                self.grads[l, y, x, q, r, :] = self.add_to((y, x, q), [self.r1.at[l, k, q]], r).astype(BF)

            self.strips(strip)

        loop(2 * p.n, add)
        if self.order == "yx":
            send(self.grads.at[l, p.y, 1 - p.x, :, self.r], self.r1.at[l, 2, :, self.r], self.sem(4), self.sem(5), p.mate_x()[1])
        else:
            send(self.grads.at[l, 1 - p.y, p.x, :, self.r], self.r1.at[l, 2, :, self.r], self.sem(4), self.sem(5), p.mate_y()[1])

    def s2(self):
        p, l = self.p, self.layer
        if self.order == "direct":
            slots = (0, 1, 2)
            await_bytes(self.r1.at[l, :, :, self.r], self.sem(2))
            await_bytes(self.r1.at[l, :, :, self.r], self.sem(3))
        else:
            slots = (2,)
            await_bytes(self.r1.at[l, 2, :, self.r], self.sem(4))
            await_bytes(self.r1.at[l, 2, :, self.r], self.sem(5))

        def add(q):
            def strip(r):
                self.grads[l, p.y, p.x, q, r, :] = self.add_to((p.y, p.x, q), [self.r1.at[l, k, q] for k in slots], r).astype(BF)

            self.strips(strip)

        loop(p.n, add)
        for k in range(1, p.n):
            q, peer = p.column(k)
            send(self.grads.at[l, p.y, p.x, q, self.r], self.r2.at[l, k - 1, self.r], self.sem(6), self.sem(7), peer)

    def s3(self):
        p, l = self.p, self.layer
        await_bytes(self.r2.at[l, :, self.r], self.sem(6))
        await_bytes(self.r2.at[l, :, self.r], self.sem(7))

        def strip(r):
            total = self.add_to((p.y, p.x, p.q), [self.r2.at[l, k] for k in range(p.n - 1)], r)
            self.res[l, p.i, r, :] = total.astype(BF)

        self.strips(strip)
        piece = self.res.at[l, p.i, self.r]
        if self.order == "direct":
            for mate in (p.mate_x(), p.mate_y(), p.mate_xy()):
                send(piece, piece, self.sem(8), self.sem(9), mate[1])
        else:
            first, second = p.mates(self.order)
            send(piece, piece, self.sem(12), self.sem(13), first[1])
            send(piece, piece, self.sem(8), self.sem(9), second[1])

    def s3b(self):
        p, l = self.p, self.layer
        first, second = p.mates(self.order)
        await_bytes(self.res.at[l, 0, self.r], self.sem(13))
        piece = self.res.at[l, first[0], self.r]
        send(piece, piece, self.sem(8), self.sem(9), second[1])

    def spread(self):
        return self.res.at[self.layer, pl.ds(0, 3 if self.order == "direct" else 2), self.r]

    def s4(self):
        p, l = self.p, self.layer
        await_bytes(self.spread(), self.sem(9))
        for i in (p.i, p.mate_x()[0], p.mate_y()[0], p.mate_xy()[0]):
            piece = self.res.at[l, i, self.r]
            send(piece, piece, self.sem(10), self.sem(11), p.sibling())

    def end(self):
        half = self.res.at[self.layer, pl.ds(0, GROUP // 2), self.r]
        await_bytes(self.spread(), self.sem(8))
        if self.order != "direct":
            await_bytes(self.res.at[self.layer, 0, self.r], self.sem(12))
        await_bytes(half, self.sem(10))
        await_bytes(half, self.sem(11))


def in_order(own, others, l, here, count):
    total = None
    for j in range(count):
        k = lax.rem(here - j + count, count)
        value = jnp.where(k == 0, own.astype(F32), others[l, lax.max(k - 1, 0)].astype(F32))
        total = value if total is None else total + value
    return total


BACKWARD_ORDER = {"d0": "yx", "d1": "yx", "e0": "xy", "e1": "xy", "i0": "direct", "i1": "yx", "j0": "direct", "j1": "xy", "o0": "yx", "o1": "yx", "u0": "yx", "u1": "yx", "v0": "xy", "v1": "xy"}
BACKWARD_PLAN = {
    (1, "middle"): ("d1.s1",),
    (1, "out"): ("v1.s1",),
    (1, "sent"): ("e1.s1", "u1.s1"),
    (1, "transform"): ("o1.s1",),
    (1, "came"): ("d1.s1b",),
    (1, "products"): ("v1.s1b",),
    (1, "in"): ("j1.s1", "e1.s1b"),
    (1, "project"): ("d1.s2",),
    (1, "end"): ("u1.s1b",),
    (0, "down0"): ("i1.s1",),
    (0, "down"): ("d1.s3", "j1.s1b"),
    (0, "activate"): ("o1.s1b",),
    (0, "up0"): ("e0.s1", "d0.s1", "u1.s2"),
    (0, "up"): ("v1.s2",),
    (0, "narrow"): ("o1.s2",),
    (0, "middle"): ("kg1.over_mp", "u0.s1"),
    (0, "open"): ("i1.s1b",),
    (0, "sent"): ("e0.s1b", "d0.s1b", "e1.s2", "o0.s1", "u1.s3"),
    (0, "transform"): ("j1.s2",),
    (0, "arrived"): ("v0.s1",),
    (0, "came"): ("d0.s2",),
    (0, "half"): ("v1.s3", "u0.s1b", "kg1.over_group"),
    (0, "returned"): ("i1.s2",),
    (0, "gatep"): ("o0.s1b", "e0.s2", "v0.s1b"),
    (0, "in"): ("e1.s3", "j0.s1", "u0.s2"),
    (0, "in0"): ("i0.s1", "v0.s2", "kg1.take", "j1.s3", "j0.s2", "u1.s3b", "v1.s3b", "o0.s2", "kg0.over_mp"),
    (0, "project"): ("e1.s3b", "e0.s3", "j1.s3b", "i0.s2", "v0.s3"),
    (0, "end"): ("d0.s3", "o1.s3"),
    (0, "tail"): (
        "e1.s4", "u1.s4", "o0.s3", "v0.s3b", "i1.s3", "j1.s4", "u0.s3", "j0.s3", "norm.over_mp", "d1.s3b",
        "u0.s3b", "v1.s4", "d0.s3b", "i1.s3b", "v0.s4", "d1.s4", "e0.s3b", "i0.s3", "kg0.over_group", "o0.s3b",
        "o1.s3b", "u0.s4", "e0.s4", "o0.s4", "kg0.take", "i0.s4", "i1.s4", "o1.s4", "j0.s4", "d0.s4", "norm.take",
    ),
}


class KernelGrad:
    def __init__(self, place, layer, refs, sems):
        self.p, self.l, self.sems = place, layer, sems
        self.own, self.from_mp, self.mid, self.from_group, self.total, self.result = [r.at[layer] for r in refs]
        self.owner = place.s == place.q

    def sem(self, k):
        return self.sems.at[self.l, k]

    def start(self):
        when(jnp.logical_not(self.owner), lambda: send(self.own, self.from_mp, self.sem(0), self.sem(1), self.p.opposite()))

    def over_mp(self):
        p = self.p

        def add():
            await_bytes(self.from_mp, self.sem(1))
            self.mid[...] = (self.own[...].astype(F32) + self.from_mp[...].astype(F32)).astype(BF)
            for k, mate in enumerate((p.mate_x(), p.mate_y(), p.mate_xy())):
                send(self.mid, self.from_group.at[k], self.sem(2 + k), self.sem(5 + k), mate[1])

        when(self.owner, add)

    def over_group(self):
        p = self.p

        def add():
            for k in range(3):
                await_bytes(self.from_group.at[k], self.sem(5 + k))
            near = self.mid[...].astype(F32) + self.from_group[0].astype(F32)
            far = self.from_group[1].astype(F32) + self.from_group[2].astype(F32)
            both = (near + far).astype(BF)
            self.total[...] = both
            self.result[...] = both
            send(self.total, self.result, self.sem(8), self.sem(9), p.sibling())

        when(self.owner, add)

    def take(self):
        when(jnp.logical_not(self.owner), lambda: await_bytes(self.result, self.sem(9)))

    def finish(self):
        def given():
            for k in range(3):
                await_bytes(self.mid, self.sem(2 + k))
            await_bytes(self.total, self.sem(8))

        when(self.owner, given)
        when(jnp.logical_not(self.owner), lambda: await_bytes(self.own, self.sem(0)))


class NormGrad:
    def __init__(self, place, refs, sems):
        self.p, self.sems = place, sems
        self.own, self.from_group, self.mid, self.from_mp, self.result = refs
        self.layers = self.own.shape[0]

    def start(self, l):
        for k in range(1, GROUP):
            send(self.own.at[l], self.from_group.at[l, k - 1], self.sems.at[l, 0], self.sems.at[l, 1], self.p.member(k))

    def over_mp(self):
        p = self.p
        for l in reversed(range(self.layers)):
            await_bytes(self.from_group.at[l], self.sems.at[l, 0])
            await_bytes(self.from_group.at[l], self.sems.at[l, 1])
            self.mid[l] = in_order(self.own[l], self.from_group, l, p.i, GROUP)
            for k in range(1, p.n):
                send(self.mid.at[l], self.from_mp.at[l, k - 1], self.sems.at[l, 2], self.sems.at[l, 3], p.column(k)[1])

    def take(self):
        for l in reversed(range(self.layers)):
            await_bytes(self.from_mp.at[l], self.sems.at[l, 2])
            await_bytes(self.from_mp.at[l], self.sems.at[l, 3])
            self.result[l] = in_order(self.mid[l], self.from_mp, l, self.p.q, self.p.n)


def backward_kernel(
    n, layers,
    gains, subs, scales, masks_h, table_h, table_t_h, tap_t_h,
    out_in, cot, streams, hiddens, gacts, gslopes, specs, conv_outs, gateds, middles, hidden_mids, actives, slopes,
    wins_h, win_h, wout_h, wup_h, wdn_h,
    out_o, grad_o, res_o, sub_o, norm_o,
    grad, middle_grad, stream, hidden, gact, gslope, spec_x, conv_out, gated, middle, hidden_mid, active, slope, wins, win, wout, wup, wdn,
    grads, r0, r1, r2, res,
    up_grad, out_grad, branch, joined, big_a, big_b, spread,
    send_c, recv_c, send_d, recv_d, kg_s, kg_z, kg_t, kg_y, kg_u, kg_own, sub_s, masks, table, table_t, tap_t,
    norm_s, norm_r, norm_t, norm_u, norm_v, grad_p,
    load_sems, a2a_sems, red_sems, kg_sems, norm_sems, out_sems, move_sems,
):
    place = Place(n)
    me, core = place.s, place.core
    tokens, width = grad.shape
    channels = width // n
    quarter = tokens
    ff = wup.shape[1]
    half = ff // 2
    spare = grads.shape[0] - 1
    loads = {}
    sources = {
        "stream": (streams, stream), "hidden": (hiddens, hidden), "gact": (gacts, gact), "gslope": (gslopes, gslope),
        "spec_x": (specs, spec_x), "conv_out": (conv_outs, conv_out), "gated": (gateds, gated), "middle": (middles, middle),
        "hidden_mid": (hidden_mids, hidden_mid), "active": (actives, active), "slope": (slopes, slope), "wins": (wins_h, wins),
        "in": (win_h, win), "out": (wout_h, wout), "up": (wup_h, wup), "down": (wdn_h, wdn),
        "branch": (cot, branch), "masks": (masks_h, masks), "table": (table_h, table), "table_t": (table_t_h, table_t), "tap_t": (tap_t_h, tap_t),
    }
    once = ("branch", "masks", "table", "table_t", "tap_t")

    def load(name, l):
        src, dst = sources[name]
        copy = pltpu.make_async_copy(src if name in once else src.at[l], dst, load_sems.at[l, len([k for k in loads if k[1] == l])])
        copy.start()
        loads[name, l] = copy

    def ready(*names, l):
        for name in names:
            loads[name, l].wait()

    def next_load(*names, l):
        if l:
            for name in names:
                load(name, l - 1)

    top = layers - 1
    for name in ("branch", "active", "down"):
        load(name, top)
    greet_all(place)
    bufs = (grads, r0, r1, r2, res)
    bounds = (PIECE_DOWN, PIECE_UP // 2, PIECE_UP, (PIECE_UP + PIECE_OUT) // 2, PIECE_OUT, PIECE_IN, PIECE_GATE, PIECE_ROWS)
    groups = {}
    for l in range(layers):
        for k, letter in enumerate("deuvoij"):
            name = letter + str(l)
            order = BACKWARD_ORDER.get(name, "direct")
            groups[name] = Reduce(place, bufs, red_sems, len(groups), l, bounds[k], bounds[k + 1] - bounds[k], order)
    kernel_grads = [KernelGrad(place, l, (kg_s, kg_z, kg_t, kg_y, kg_u, kg_own), kg_sems) for l in range(layers)]
    norm_grads = NormGrad(place, (norm_s, norm_r, norm_t, norm_u, norm_v), norm_sems)
    out_move = Move(place, out_in, out_o, move_sems.at[0])
    grad_move = Move(place, branch, grad_o, move_sems.at[1], grad_p)
    moving = {"norm": norm_grads, **groups}
    moving.update({"kg" + str(l): kernel_grads[l] for l in range(layers)})

    def visit(l, point):
        for step in BACKWARD_PLAN.get((l, point), ()):
            what, action = step.split(".")
            getattr(moving[what], action)()

    def exchange_start(slot, src, dst, rows):
        for k in range(1, n):
            s, peer = place.partner(k)
            send(src.at[s, rows], dst.at[me, rows], a2a_sems.at[slot, 0], a2a_sems.at[slot, 1], peer)

    def exchange_wait(slot, src, dst, l):
        await_bytes(src.at[pl.ds(0, n - 1)], a2a_sems.at[slot, 0])
        await_bytes(dst.at[pl.ds(0, n - 1)], a2a_sems.at[slot, 1])

    def holder(parity, l):
        mine = 1 - (parity - core) * (parity - core)
        return l * mine + spare * (1 - mine)

    out_move.start()
    for name in ("slope", "hidden_mid", "up", "middle", "out", "gated", "gact", "gslope", "conv_out"):
        load(name, top)
    ready("branch", l=top)

    def widen_grad(j):
        r = rows_of(j, 64)
        grad[r, :] = branch[r, :].astype(F32)

    loop(tokens // 64, widen_grad)

    for l in reversed(range(layers)):
        ready("active", l=l)

        def grad_up(c):
            got = dot_tn(hidden_mid[:, rows_of(c, 128)], up_grad[...]).astype(BF)
            for par in range(2):
                for q in range(n):
                    grads[holder(par, l), c // 2, lax.rem(c, 2), q, PIECE_UP:PIECE_OUT, :] = got[par * 64 : par * 64 + 64, q * (ff // n) : (q + 1) * (ff // n)]

        def grad_down(q):
            got = dot_tn(active[:, rows_of(q, ff // n)], branch[...]).astype(BF)
            for i in range(GROUP):
                grads[holder(i % 2, l), i // 4, i // 2 % 2, q, PIECE_DOWN:PIECE_UP, :] = got[i * 64 : (i + 1) * 64]

        def grad_out():
            got = dot_tn(gated[...], out_grad[...]).astype(BF)
            for q in range(n):
                for i in range(GROUP):
                    at = q * channels + i * 16
                    grads[holder(i % 2, l), i // 4, i // 2 % 2, q, PIECE_OUT:PIECE_IN, :] = got[at : at + 16]

        def grad_in(h):
            got = dot_tn(hidden[...], joined[:, h * width : (h + 1) * width]).astype(BF)
            first = (PIECE_IN, PIECE_GATE)[h]
            for i in range(GROUP):
                for q in range(n):
                    for t in range(4):
                        at = i * 64 + t * 16
                        grads[holder(i % 2, l), i // 4, i // 2 % 2, q, first : first + 16, t * 128 : (t + 1) * 128] = got[
                            at : at + 16, q * channels : (q + 1) * channels
                        ]
            groups["ij"[h] + str(l)].s0()

        loop(n // 2, grad_down)
        visit(l, "down0")
        loop(n // 2, lambda q: grad_down(q + n // 2))
        for letter in "de":
            groups[letter + str(l)].s0()
        visit(l, "down")
        ready("down", "slope", l=l)
        for h in range(2):
            c = slice(h * half, (h + 1) * half)
            up_grad[:, c] = (dot_nt(branch[...], wdn[c, :]) * slope[:, c].astype(F32)).astype(BF)
        next_load("down", "slope", l=l)
        if l == top:
            for name in ("spec_x", "wins", "masks", "table", "table_t", "tap_t", "in", "hidden", "stream"):
                load(name, top)
        visit(l, "activate")
        ready("hidden_mid", l=l)
        loop(GROUP // 4, grad_up)
        visit(l, "up0")
        loop(GROUP // 4, lambda c: grad_up(c + GROUP // 4))
        for letter in "uv":
            groups[letter + str(l)].s0()
        next_load("hidden_mid", l=l)
        visit(l, "up")
        ready("up", l=l)
        big_a[...] = dot_nt(up_grad[...], wup[...])
        next_load("up", l=l)
        visit(l, "narrow")
        ready("middle", l=l)
        sums_mid = norm_back(big_a, middle, grad, gains[l, 1:2, :], middle_grad, out_grad)
        next_load("middle", l=l)
        visit(l, "middle")

        ready("gated", l=l)
        grad_out()
        groups["o" + str(l)].s0()
        next_load("gated", l=l)
        visit(l, "out")
        ready("out", l=l)
        big_b[0:tokens, 0:width] = dot_nt(out_grad[...], wout[...])
        next_load("out", l=l)
        visit(l, "open")
        ready("gact", "gslope", "conv_out", l=l)

        def unmix(j):
            r = rows_of(j, 32)
            for s in range(n):
                c = slice(s * channels, (s + 1) * channels)
                up = big_b[r, c]
                send_c[s, r, :] = (up * gact[r, c].astype(F32)).astype(BF)
                joined[r, slice(width + s * channels, width + (s + 1) * channels)] = (
                    up * conv_out[s, r, :].astype(F32) * gslope[r, c].astype(F32)
                ).astype(BF)

        for j in range(2):
            loop(tokens // 64, lambda k: unmix(k + j * (tokens // 64)))
            exchange_start(2 * l, send_c, recv_c, pl.ds(j * (tokens // 2), tokens // 2))
        next_load("gact", "gslope", "conv_out", l=l)
        recv_c[me] = send_c[me]
        visit(l, "sent")
        if l == top:
            ready("masks", "table", l=l)
        visit(l, "transform")
        exchange_wait(2 * l, send_c, recv_c, l)
        visit(l, "arrived")
        spread_blocks(recv_c, masks, spread)
        big_b[:, 0 : 7 * channels] = dot(table[...], spread[...])
        visit(l, "came")
        ready("wins", "spec_x", l=l)
        back_products(spec_x, big_b, wins, active, up_grad, channels)
        next_load("wins", "spec_x", l=l)
        visit(l, "products")
        if l == top:
            ready("table_t", "tap_t", l=l)

        for j in range(2):
            r = slice(j * (quarter // 2), (j + 1) * (quarter // 2))
            parts = dot(table_t[r, 0:quarter], active[:, 0 : 7 * channels])
            parts += dot(table_t[r, quarter : 2 * quarter], active[:, half : half + 7 * channels])
            for s in range(n):
                send_d[s, r, :] = join_blocks(parts, r, masks, s).astype(BF)
            exchange_start(2 * l + 1, send_d, recv_d, pl.ds(j * (quarter // 2), quarter // 2))
            if j == 0:
                visit(l, "half")
        recv_d[me] = send_d[me]
        next_load("active", l=l)

        taps = None
        for m in range(4):
            c = slice(m * channels, (m + 1) * channels)
            d = slice(half + m * channels, half + (m + 1) * channels)
            got = dot(tap_t[m, :, 0:quarter], up_grad[:, c]) + dot(tap_t[m, :, quarter : 2 * quarter], up_grad[:, d])
            taps = got if taps is None else taps + got
        kg_s[l] = taps.astype(BF)
        kernel_grads[l].start()
        visit(l, "returned")
        ready("in", "hidden", "stream", l=l)
        big_a[...] = dot_nt(joined[:, width : 2 * width], win[1])
        visit(l, "gatep")
        grad_in(1)
        visit(l, "in")
        exchange_wait(2 * l + 1, send_d, recv_d, l)

        def collect(j):
            r = rows_of(j, 64)
            for s in range(n):
                joined[r, s * channels : (s + 1) * channels] = recv_d[s, r, :]

        loop(tokens // 64, collect)
        if l == 0:
            grad_in(0)
        visit(l, "in0")
        big_a[...] = big_a[...] + dot_nt(joined[:, 0:width], win[0])
        next_load("in", l=l)
        visit(l, "project")
        sums_in = norm_back(big_a, stream, middle_grad, gains[l, 0:1, :], grad, branch)
        next_load("stream", l=l)
        if l == 0:
            grad_move.start()
        else:
            grad_in(0)
        next_load("hidden", l=l)
        norm_s[l] = jnp.concatenate(
            [jnp.sum(s, axis=0, keepdims=True) for s in (sums_in[0], sums_mid[0], sums_in[1], sums_mid[1])]
            + [jnp.zeros((4, width), F32)],
            axis=0,
        )
        norm_grads.start(l)
        if l == 0:
            grad_move.pass_on()
        visit(l, "end")

    visit(0, "tail")
    out_norm = pltpu.make_async_copy(norm_v, norm_o, out_sems.at[1])
    out_norm.start()
    for l in range(layers):
        raw, inverse = normal_taps(subs, scales, l)
        k = raw * inverse
        own = kg_own[l].astype(F32)
        along = jnp.sum(own * k, axis=0, keepdims=True)
        sub_s[l] = scales[0] * (own - scales[1] * k * along) * inverse
    out_sub = pltpu.make_async_copy(sub_s, sub_o, out_sems.at[0])
    out_sub.start()
    for group in groups.values():
        group.end()
    out_res = pltpu.make_async_copy(res, res_o, out_sems.at[2])
    out_res.start()
    for m in (out_move, grad_move):
        m.arrive()
        m.finish()
    for g in kernel_grads:
        g.finish()
    out_sub.wait()
    out_norm.wait()
    out_res.wait()


def backward(n, gains, subs, scales, masks, table, table_t, tap_t, out, cot, kept):
    layers, tokens, width = kept[0].shape
    channels = width // n
    ff = kept[-1].shape[1]
    taps = subs.shape[1]

    def sds(*shape, dtype=F32):
        return jax.ShapeDtypeStruct(shape, dtype)

    outs = [
        sds(tokens, width, dtype=BF), sds(tokens, width, dtype=BF), sds(layers, GROUP, PIECE_ROWS, width, dtype=BF),
        sds(layers, taps, channels), sds(layers, 8, width),
    ]
    f32 = lambda *s: pltpu.VMEM(s, F32)
    bf = lambda *s: pltpu.VMEM(s, BF)
    wide, blocks, small = (tokens, width), (n, tokens, channels), (layers, taps, channels)
    scratch = [
        f32(*wide), f32(*wide), f32(*wide), bf(*wide), bf(*wide), bf(*wide), bf(2 * tokens, 7 * channels), bf(*blocks), bf(*wide), f32(*wide), bf(*wide),
        bf(tokens, ff), bf(tokens, ff), f32(4, 2, tokens, channels),
        bf(2, width, width), bf(width, width), bf(width, ff), bf(ff, width),
        bf(layers + 1, 2, 2, n, PIECE_ROWS, width),
        bf(layers, 2, 2, n, PIECE_ROWS, width),
        bf(layers, 3, n, PIECE_ROWS, width),
        bf(layers, n - 1, PIECE_ROWS, width),
        bf(layers, GROUP, PIECE_ROWS, width),
        bf(tokens, ff), bf(*wide), bf(*wide), bf(tokens, 2 * width),
        f32(*wide), f32(2 * tokens, 7 * channels), bf(tokens, 7 * channels),
        bf(*blocks), bf(*blocks), bf(*blocks), bf(*blocks),
        bf(*small), bf(*small), bf(*small), bf(layers, 3, taps, channels), bf(*small), bf(*small), f32(*small),
        bf(10, tokens, channels), bf(2 * tokens, tokens), bf(tokens, 2 * tokens), bf(4, taps, 2 * tokens),
        f32(layers, 8, width), f32(layers, GROUP - 1, 8, width), f32(layers, 8, width), f32(layers, n - 1, 8, width), f32(layers, 8, width), bf(tokens // 2, width),
        pltpu.SemaphoreType.DMA((layers, 21)),
        pltpu.SemaphoreType.DMA((2 * layers, 2)),
        pltpu.SemaphoreType.DMA((7 * layers, 14)),
        pltpu.SemaphoreType.DMA((layers, 10)),
        pltpu.SemaphoreType.DMA((layers, 4)),
        pltpu.SemaphoreType.DMA((3,)),
        pltpu.SemaphoreType.DMA((2, 4)),
    ]
    return pl.pallas_call(
        functools.partial(backward_kernel, n, layers),
        out_shape=outs,
        in_specs=[VMEM] * 3 + [ANY] * (6 + len(kept)),
        out_specs=[ANY] * len(outs),
        scratch_shapes=scratch,
        compiler_params=pltpu.CompilerParams(collective_id=2, has_side_effects=True, vmem_limit_bytes=int(63.5 * 2**20)),
        name="backward",
    )(gains, subs, scales, masks, table, table_t, tap_t, out, cot, *kept)


def finish_kernel(out_i, grad_i, res, norms, sub_i, out, grad, up, down, out_w, in_w, gains, biases, sub):
    out[...] = out_i[...].astype(F32)
    grad[...] = grad_i[...].astype(F32)
    members = res.shape[1]
    for i in range(members):
        up[0, i * 64 : (i + 1) * 64, :] = res[0, i, PIECE_UP:PIECE_OUT, :].astype(F32)
        down[0, i * 64 : (i + 1) * 64, :] = res[0, i, PIECE_DOWN:PIECE_UP, :].astype(F32)
        out_w[0, i * 16 : (i + 1) * 16, :] = res[0, i, PIECE_OUT:PIECE_IN, :].astype(F32)
        for h, first in enumerate((PIECE_IN, PIECE_GATE)):
            for t in range(4):
                c = t * 128
                in_w[0, i * 64 + t * 16 : i * 64 + (t + 1) * 16, h, :] = res[0, i, first : first + 16, c : c + 128].astype(F32)
    gains[...] = norms[:, 0:2, :]
    biases[...] = norms[:, 2:4, :]
    sub[...] = sub_i[...]


def finish(out, grad, res, norms, sub):
    layers, members, _, width = res.shape
    tokens = out.shape[0]
    channels = sub.shape[2]
    parts = 1
    m = members // parts
    steps = layers * parts
    rows = tokens // steps

    def sds(*shape):
        return jax.ShapeDtypeStruct(shape, F32)

    def whole(a):
        return pl.BlockSpec(a.shape, lambda j: (0,) * len(a.shape))

    flat = pl.BlockSpec((rows, width), lambda j: (j, 0))

    def mid(*shape):
        return pl.BlockSpec((1, *shape, width), lambda j: (j // parts, j % parts, 0))

    vector = sds(layers, 2, width)
    return pl.pallas_call(
        finish_kernel,
        grid=(steps,),
        out_shape=[
            sds(tokens, width), sds(tokens, width), sds(layers, members * 64, width), sds(layers, members * 64, width),
            sds(layers, members * 16, width), sds(layers, members * 64, 2, channels), vector, vector, sds(*sub.shape),
        ],
        in_specs=[
            flat, flat, pl.BlockSpec((1, m, PIECE_ROWS, width), lambda j: (j // parts, j % parts, 0, 0)), whole(norms), whole(sub),
        ],
        out_specs=[
            flat, flat, mid(m * 64), mid(m * 64), mid(m * 16),
            pl.BlockSpec((1, m * 64, 2, channels), lambda j: (j // parts, j % parts, 0, 0)), whole(vector), whole(vector), whole(sub),
        ],
        compiler_params=pltpu.CompilerParams(vmem_limit_bytes=48 * 2**20),
        name="finish",
    )(out, grad, res, norms, sub)


def per_device(
    stream_in, segments, norm_gain, norm_bias, w_in, w_out, sub_kernels, w_up, w_down, cotangent
):
    layers, scales, taps, channels = sub_kernels.shape
    n = lax.axis_size("mp")
    quarter = segments.shape[1] // 4
    table = transform_table(quarter)
    tap_table = tap_tables(quarter, scales, taps) / quarter

    def const(a):
        return jnp.asarray(a, F32).astype(BF)

    factors = jnp.asarray(tap_scales(scales, taps, channels))
    subs = sub_kernels.reshape(layers, -1, channels)
    out, *kept, masks, cot, win, wout, wup, wdn = forward(
        n, stream_in, cotangent, segments, norm_gain, norm_bias, subs, factors, const(table), const(table.T), const(tap_table),
        w_in.transpose(0, 2, 1, 3).reshape(2 * layers, -1, channels), w_out, w_up, w_down,
    )
    out, grad, res, sub, norms = backward(
        n, norm_gain, subs, factors, masks, const(table), const(table.T), const(tap_table.transpose(0, 2, 1)),
        out, cot, (*kept, win.reshape(layers, 2, *win.shape[1:]), wout, wup, wdn),
    )
    if lax.axis_size("dp") > GROUP:
        res, sub, norms = [v * (1.0 / GROUP) for v in lax.psum((res.astype(F32), sub, norms), "dp")]
        res = res.astype(BF)
    out, grad, up, down, out_w, in_w, gains, biases, sub = finish(out, grad, res, norms, sub)
    return out, grad, gains, biases, in_w, out_w, sub.reshape(sub_kernels.shape), up, down


def solution(mesh):
    rows = P(("dp", "mp"), None)
    last = P(None, None, None, "mp")
    mid = P(None, "mp", None)
    return jax.shard_map(
        per_device,
        mesh=mesh,
        in_specs=(rows, P("dp", None), P(), P(), last, mid, last, P(None, None, "mp"), mid, rows),
        out_specs=(rows, rows, P(), P(), last, mid, last, P(None, None, "mp"), mid),
        check_vma=False,
    )
```

```python
import functools

import jax
import jax.numpy as jnp
import numpy as np
from jax import lax
from jax.experimental import pallas as pl
from jax.experimental.pallas import tpu as pltpu
from jax.sharding import PartitionSpec as P

DECAY_RATE = 0.5
EPSILON = 1e-05
BF = jnp.bfloat16
F32 = jnp.float32
GROUP = 8
MESH = pl.DeviceIdType.MESH
VMEM = pl.BlockSpec(memory_space=pltpu.VMEM)
ANY = pl.BlockSpec(memory_space=pl.ANY)
GELU_A = float(np.sqrt(2.0 / np.pi))
GELU_B = 0.044715


def dot(a, b):
    return jnp.dot(a, b, preferred_element_type=F32)


def dot_nt(a, b):
    return lax.dot_general(a, b, (((1,), (1,)), ((), ())), preferred_element_type=F32)


def dot_tn(a, b):
    return lax.dot_general(a, b, (((0,), (0,)), ((), ())), preferred_element_type=F32)


def gelu(u):
    return 0.5 * u * (1.0 + jnp.tanh(GELU_A * (u + GELU_B * (u * u * u))))


def gelu_both(u):
    square = u * u
    t = jnp.tanh(GELU_A * (u + GELU_B * (square * u)))
    half = 0.5 * (1.0 + t)
    slope = half + (0.5 * u) * (1.0 - t * t) * (GELU_A + (3.0 * GELU_A * GELU_B) * square)
    return u * half, slope


def loop(count, body):
    lax.fori_loop(0, count, lambda j, c: (body(j), c)[1], 0)


def when(condition, body):
    pl.when(condition)(body)


def rows_of(j, size):
    return pl.ds(pl.multiple_of(j * size, size), size)


def transform_table(quarter):
    freq = np.arange(quarter)[:, None] + 0.5
    angle = np.pi * freq * np.arange(quarter)[None, :] / quarter
    return np.concatenate([np.cos(angle), -np.sin(angle)], axis=0)


def spread_matrix(scales, taps):
    lags = []
    for level in range(scales):
        lags += [level * taps + j for j in range(taps) for _ in range(2 ** max(level, 1))]
    spread = np.zeros((len(lags), scales * taps))
    spread[np.arange(len(lags)), lags] = 1.0
    return spread


def tap_tables(quarter, scales, taps):
    table = transform_table(quarter)
    spread = spread_matrix(scales, taps).reshape(4, quarter, scales * taps)
    return np.einsum("fp,mpt->mft", table, spread)


def tap_scales(scales, taps, channels):
    level = np.repeat(np.arange(scales), taps)
    decay = DECAY_RATE**level
    repeats = 2.0 ** np.maximum(level, 1)
    both = np.stack([decay, repeats])[:, :, None]
    return np.broadcast_to(both, (2, scales * taps, channels)).astype(np.float32)


class Place:
    def __init__(self, n):
        self.n = n
        self.q = lax.axis_index("mp")
        dp = lax.axis_index("dp")
        self.i = lax.rem(dp, GROUP)
        self.base = dp - self.i
        self.core = lax.rem(self.i, 2)
        self.x = lax.rem(self.i // 2, 2)
        self.y = self.i // 4
        self.s = lax.rem(self.q, 2) + 2 * self.core

    def device(self, i, q):
        return {"dp": self.base + i, "mp": q}

    def index(self, y, x, core):
        return 4 * y + 2 * x + core

    def column(self, k):
        q = lax.rem(self.q + k, self.n)
        return q, self.device(self.i, q)

    def member(self, k):
        return self.device(lax.rem(self.i + k, GROUP), self.q)

    def mate_x(self):
        i = self.index(self.y, 1 - self.x, self.core)
        return i, self.device(i, self.q)

    def mate_y(self):
        i = self.index(1 - self.y, self.x, self.core)
        return i, self.device(i, self.q)

    def mate_xy(self):
        i = self.index(1 - self.y, 1 - self.x, self.core)
        return i, self.device(i, self.q)

    def mates(self, order):
        return (self.mate_x(), self.mate_y()) if order == "xy" else (self.mate_y(), self.mate_x())

    def sibling(self):
        return self.device(self.index(self.y, self.x, 1 - self.core), self.q)

    def partner(self, k):
        s = lax.rem(self.s + k, self.n)
        return s, self.device(self.index(self.y, self.x, s // 2), 2 * (self.q // 2) + lax.rem(s, 2))

    def row_target(self):
        return self.device(self.index(self.y, self.x, self.q // 2), 2 * self.core + lax.rem(self.q, 2))

    def opposite(self):
        return self.device(self.i, lax.rem(self.q + 2, self.n))

    def stays(self):
        return self.q // 2 == self.core


def greet_all(place):
    barrier = pltpu.get_barrier_semaphore()
    peers = [place.column(k)[1] for k in range(1, place.n)] + [place.member(k) for k in range(1, GROUP)]
    across = place.index(place.y, place.x, 1 - place.core)
    peers += [place.device(across, place.column(k)[0]) for k in range(1, place.n)]
    for peer in peers:
        pl.semaphore_signal(barrier, inc=1, device_id=peer, device_id_type=MESH)
    pl.semaphore_wait(barrier, len(peers))


def send(src, dst, send_sem, recv_sem, peer):
    pltpu.make_async_remote_copy(
        src_ref=src, dst_ref=dst, send_sem=send_sem, recv_sem=recv_sem, device_id=peer, device_id_type=MESH
    ).start()


def await_bytes(ref, sem):
    pltpu.make_async_copy(ref, ref, sem).wait()


class Move:
    def __init__(self, place, src, dst, sems, relay=None):
        self.p, self.src, self.dst, self.sems, self.relay = place, src, dst, sems, relay
        half = src.shape[0] // 2
        self.first = pl.ds(0, src.shape[0] if relay is None else half)
        self.second = pl.ds(half, half)

    def start(self):
        p = self.p

        def across():
            send(self.src.at[self.first], self.dst.at[self.first], self.sems.at[0], self.sems.at[1], p.row_target())
            if self.relay is not None:
                send(self.src.at[self.second], self.relay, self.sems.at[0], self.sems.at[2], p.sibling())

        when(jnp.logical_not(p.stays()), across)
        when(p.stays(), lambda: pltpu.make_async_copy(self.src, self.dst, self.sems.at[1]).start())

    def pass_on(self):
        def onward():
            await_bytes(self.relay, self.sems.at[2])
            send(self.relay, self.dst.at[self.second], self.sems.at[3], self.sems.at[1], self.p.opposite())

        when(self.p.stays(), onward)

    def arrive(self):
        await_bytes(self.dst, self.sems.at[1])

    def finish(self):
        when(jnp.logical_not(self.p.stays()), lambda: await_bytes(self.src, self.sems.at[0]))
        if self.relay is not None:
            when(self.p.stays(), lambda: await_bytes(self.relay, self.sems.at[3]))


class Weight:
    def __init__(self, whole, layer, columns, n):
        self.whole, self.columns, self.layer, self.n = whole, columns, layer, n
        shape = whole.shape
        self.rows = shape[1] // GROUP if columns else shape[1] // n // GROUP
        self.cols = shape[2] // n if columns else shape[2]

    def piece(self, i, q):
        r, c = self.rows, self.cols
        if self.columns:
            return self.whole.at[self.layer, pl.ds(i * r, r), pl.ds(q * c, c)]
        return self.whole.at[self.layer, pl.ds((q * GROUP + i) * r, r), :]

    def shard(self, q):
        r, c = self.rows, self.cols
        if self.columns:
            return self.whole.at[self.layer, :, pl.ds(q * c, c)]
        return self.whole.at[self.layer, pl.ds(q * GROUP * r, GROUP * r), :]

    def local_piece(self, shard, i):
        return shard.at[self.layer, pl.ds(i * self.rows, self.rows), :]

    def span(self, members):
        r, c, k = self.rows, self.cols, self.n - 1
        if self.columns:
            return self.whole.at[self.layer, pl.ds(0, members * r), pl.ds(0, k * c)]
        return self.whole.at[self.layer, pl.ds(0, members * k * r), :]


class Gather:
    def __init__(self, place, weight, shard, sems, slot, order):
        self.p, self.w, self.shard_ref, self.sems, self.slot, self.order = place, weight, shard, sems, slot, order

    def sem(self, k):
        return self.sems.at[self.slot, k]

    def own(self):
        return pltpu.make_async_copy(
            self.shard_ref.at[self.w.layer], self.w.shard(self.p.q), self.sem(8)
        )

    def start(self):
        p, w = self.p, self.w
        for k in range(1, p.n):
            send(w.local_piece(self.shard_ref, p.i), w.piece(p.i, p.q), self.sem(0), self.sem(1), p.column(k)[1])
        self.own().start()

    def pass_on(self, i, send_sem, recv_sem, peer):
        p, w = self.p, self.w
        for k in range(1, p.n):
            piece = w.piece(i, p.column(k)[0])
            send(piece, piece, send_sem, recv_sem, peer)

    def first_second(self):
        return self.p.mates("yx" if self.order == "yx" else "xy")

    def hop1(self):
        p = self.p
        await_bytes(self.w.span(1), self.sem(1))
        first, second = self.first_second()
        self.pass_on(p.i, self.sem(2), self.sem(3), first[1])
        self.pass_on(p.i, self.sem(4), self.sem(5), second[1])
        if self.order == "direct":
            self.pass_on(p.i, self.sem(4), self.sem(5), p.mate_xy()[1])
        self.pass_on(p.i, self.sem(6), self.sem(7), p.sibling())

    def hop2(self):
        first, second = self.first_second()
        await_bytes(self.w.span(1), self.sem(3))
        self.pass_on(first[0], self.sem(4), self.sem(5), second[1])
        self.pass_on(first[0], self.sem(6), self.sem(7), self.p.sibling())

    def hop3(self):
        p = self.p
        first, second = self.first_second()
        others = [second[0], p.mate_xy()[0]]
        if self.order == "direct":
            await_bytes(self.w.span(1), self.sem(3))
            others.append(first[0])
        await_bytes(self.w.span(2), self.sem(5))
        for i in others:
            self.pass_on(i, self.sem(6), self.sem(7), p.sibling())

    def arrive(self):
        self.own().wait()
        await_bytes(self.w.span(4), self.sem(7))

    def finish(self):
        await_bytes(self.w.span(1), self.sem(0))
        await_bytes(self.w.span(1), self.sem(2))
        await_bytes(self.w.span(2), self.sem(4))
        await_bytes(self.w.span(4), self.sem(6))


def norm_strip(v, gain, bias):
    centred = v - jnp.mean(v, axis=-1, keepdims=True)
    variance = jnp.mean(centred * centred, axis=-1, keepdims=True)
    return centred * lax.rsqrt(variance + EPSILON) * gain + bias


def norm_all(src, dst, gain, bias):
    def strip(j):
        r = rows_of(j, 128)
        dst[r, :] = norm_strip(src[r, :], gain, bias).astype(BF)

    loop(dst.shape[0] // 128, strip)


def normal_taps(sub_ref, scale_ref, layer):
    raw = sub_ref[layer] * scale_ref[0]
    total = jnp.sum(raw * raw * scale_ref[1], axis=0, keepdims=True)
    return raw, lax.rsqrt(total + EPSILON)


def make_masks(segs, masks):
    quarter, channels = masks.shape[1:]
    ones = jnp.full((8, channels), 0.125, BF)

    def numbers(n):
        row = segs[:, n * quarter : (n + 1) * quarter].astype(F32)
        return dot_tn(jnp.broadcast_to(row, (8, quarter)).astype(BF), ones)

    def put(k, flag):
        masks[k] = jnp.where(flag, 1.0, 0.0).astype(BF)

    long_doc = numbers(1)[0:1, :]
    for n in range(4):
        here = numbers(n)
        put(n, here == long_doc)
        if n in (0, 3):
            for k in range(3):
                doc = jnp.where(long_doc <= k, k + 1.0, float(k))
                put(4 + 2 * k + (n == 3), here == doc)


def make_windows(taps, tap_ref, spec, layer, wins):
    channels = taps.shape[1]
    quarter = wins.shape[3]
    for m in range(4):
        spec[:, m * channels : (m + 1) * channels] = dot(tap_ref[m], taps)

    def strip(j):
        r = rows_of(j, 16)
        s = rows_of(j + quarter // 16, 16)
        sign = (1 - 2 * lax.rem(lax.broadcasted_iota(jnp.int32, (16, channels), 0), 2)).astype(F32)
        for m in range(4):
            here = slice(m * channels, (m + 1) * channels)
            re, im = spec[r, here], spec[s, here]
            if m:
                before = slice((m - 1) * channels, m * channels)
                re, im = re - sign * spec[s, before], im + sign * spec[r, before]
            wins[layer, m, 0, r, :] = re
            wins[layer, m, 1, r, :] = im

    loop(quarter // 16, strip)


def spread_blocks(blocks, masks, out):
    channels = masks.shape[2]
    for n in range(4):
        out[:, n * channels : (n + 1) * channels] = blocks[n] * masks[n]
    for k in range(3):
        out[:, (4 + k) * channels : (5 + k) * channels] = (
            blocks[0] * masks[4 + 2 * k] + blocks[3] * masks[5 + 2 * k]
        )


def join_blocks(parts, r, masks, n):
    channels = masks.shape[2]
    total = parts[:, n * channels : (n + 1) * channels] * masks[n, r, :].astype(F32)
    if n in (0, 3):
        for k in range(3):
            mask = masks[4 + 2 * k + (n == 3), r, :].astype(F32)
            total += parts[:, (4 + k) * channels : (5 + k) * channels] * mask
    return total


def fwd_products(spec, wins, layer, out, kept, channels):
    quarter = wins.shape[3]

    def strip(j):
        r = rows_of(j, 16)
        s = rows_of(j + quarter // 16, 16)
        xs = [(spec[r, n * channels : (n + 1) * channels], spec[s, n * channels : (n + 1) * channels]) for n in range(7)]
        for n in range(7):
            c = slice(n * channels, (n + 1) * channels)
            kept[layer, r, c] = xs[n][0].astype(BF)
            kept[layer, s, c] = xs[n][1].astype(BF)
        ws = [(wins[layer, m, 0, r, :], wins[layer, m, 1, r, :]) for m in range(4)]
        for n in range(7):
            re = im = None
            for m in range(n + 1 if n < 4 else 1):
                w, x = ws[m], xs[n - m]
                a = w[0] * x[0] - w[1] * x[1]
                b = w[0] * x[1] + w[1] * x[0]
                re, im = (a, b) if re is None else (re + a, im + b)
            out[r, n * channels : (n + 1) * channels] = re.astype(BF)
            out[s, n * channels : (n + 1) * channels] = im.astype(BF)

    loop(quarter // 16, strip)


FORWARD_ORDER = {"c0": "direct", "c1": "direct", "d0": "direct", "d1": "direct", "g0": "direct", "g1": "direct", "o0": "direct", "o1": "direct", "u0": "direct", "u1": "direct"}
FORWARD_PLAN = {
    (0, "start2"): ("c0.hop1", "c0.hop3"),
    (0, "ready"): ("g0.start", "o0.start", "u0.start", "g0.hop1"),
    (0, "sent"): ("d0.start", "o0.hop1", "g0.hop3"),
    (0, "gate0"): ("u0.hop1",),
    (0, "masks"): ("c1.start", "o0.hop3"),
    (0, "win0"): ("o1.start",),
    (0, "win1"): ("g1.start",),
    (0, "transform"): ("d0.hop1",),
    (0, "returned"): ("u1.start", "c1.hop1", "u0.hop3"),
    (0, "back"): ("d1.start",),
    (0, "act0"): ("o1.hop1", "d0.hop3"),
    (0, "activate"): ("g1.hop1", "c1.hop3"),
    (1, "normed"): ("u1.hop1",),
    (1, "sent"): ("cot.start", "g1.hop3"),
    (1, "gate"): ("d1.hop1",),
    (1, "returned"): ("o1.hop3", "u1.hop3"),
    (1, "attach"): ("d1.hop3",),
}


def forward_kernel(
    n, layers,
    stream_in, segs, gains, biases, subs, scales, cot_h, table_h, table_t_h, tap_table_h, win, wout, wup, wdn,
    out_o, streams_o, hidden_o, gact_o, gslope_o, spec_o, conv_out_o, gated_o, middle_o, hidden_mid_o, active_o, slope_o,
    wins_o, masks_o, cot_o, win_o, wout_o, wup_o, wdn_o,
    stream, hidden, gact, gslope, gated, middle, hidden_mid, active, slope, send_a, recv_a, send_b, recv_b,
    spread, spec, spec_x, spec_y, wins, win_f, wout_f, wup_f, wdn_f,
    masks, tok_s, tok_r, tok_p, cot_in, cot_s, seg_r, taps_s, taps_r, table, table_t, tap_table,
    gather_sems, a2a_sems, save_sems, move_sems, tap_sems, load_sems,
):
    place = Place(n)
    me = place.s
    tokens, width = stream_in.shape
    channels = width // n
    quarter = tokens
    half = wup_f.shape[2] // 2
    loads = [
        pltpu.make_async_copy(src, dst, load_sems.at[k])
        for k, (src, dst) in enumerate(((cot_h, cot_in), (tap_table_h, tap_table), (table_h, table), (table_t_h, table_t)))
    ]
    greet_all(place)
    saves = []

    def save(src, dst, l=None):
        if l is not None:
            src, dst = src.at[l], dst.at[l]
        copy = pltpu.make_async_copy(src, dst, save_sems.at[len(saves)])
        copy.start()
        saves.append(copy)

    def exchange_start(slot, src, dst, layer, rows=None):
        rows = pl.ds(0, tokens) if rows is None else rows
        for k in range(1, n):
            s, peer = place.partner(k)
            send(src.at[layer, s, rows], dst.at[layer, me, rows], a2a_sems.at[slot, 0], a2a_sems.at[slot, 1], peer)

    def exchange_wait(slot, src, dst, layer):
        await_bytes(src.at[layer, pl.ds(0, n - 1)], a2a_sems.at[slot, 0])
        await_bytes(dst.at[layer, pl.ds(0, n - 1)], a2a_sems.at[slot, 1])

    moving = {
        "seg": Move(place, segs, seg_r, move_sems.at[0]),
        "tok": Move(place, tok_s, tok_r, move_sems.at[1], tok_p),
        "cot": Move(place, cot_s, cot_o, move_sems.at[2]),
    }
    gathers = {}
    for l in range(layers):
        for letter, whole, shard, index, columns in (
            ("c", win_f, win, 2 * l, True), ("g", win_f, win, 2 * l + 1, True), ("o", wout_f, wout, l, False),
            ("u", wup_f, wup, l, True), ("d", wdn_f, wdn, l, False),
        ):
            name = letter + str(l)
            weight = Weight(whole, index, columns, n)
            gathers[name] = Gather(place, weight, shard, gather_sems, len(gathers), FORWARD_ORDER.get(name, "xy"))
    moving.update(gathers)

    def visit(l, point):
        for step in FORWARD_PLAN.get((l, point), ()):
            what, action = step.split(".")
            getattr(moving[what], action)()

    gathers["c0"].start()

    def round_stream(j):
        r = rows_of(j, 64)
        tok_s[r, :] = stream_in[r, :].astype(BF)

    loop(tokens // 64, round_stream)
    moving["tok"].start()
    moving["seg"].start()
    for l in range(layers):
        raw, inverse = normal_taps(subs, scales, l)
        taps_s[l] = (raw * inverse).astype(BF)

    def give_taps():
        send(taps_s, taps_r, tap_sems.at[0], tap_sems.at[1], place.opposite())

    def keep_taps():
        taps_r[...] = taps_s[...]

    def take_taps():
        await_bytes(taps_r, tap_sems.at[1])

    own_taps = place.s == place.q
    when(own_taps, give_taps)
    for copy in loads:
        copy.start()
    when(own_taps, keep_taps)
    moving["tok"].pass_on()
    visit(0, "start")
    loads[0].wait()

    def round_cotangent(j):
        r = rows_of(j, 64)
        cot_s[r, :] = cot_in[r, :].astype(BF)

    loop(tokens // 64, round_cotangent)
    visit(0, "start2")
    moving["tok"].arrive()
    visit(0, "ready")

    def widen_stream(j):
        r = rows_of(j, 64)
        stream[0, r, :] = tok_r[r, :].astype(F32)

    loop(tokens // 64, widen_stream)
    save(stream, streams_o, 0)

    for l in range(layers):
        norm_all(stream.at[l], hidden.at[l], gains[l, 0:1, :], biases[l, 0:1, :])
        visit(l, "normed")
        gathers["c" + str(l)].arrive()
        got = dot(hidden[l], win_f[2 * l]).astype(BF)
        for s in range(n):
            send_a[l, s] = got[:, s * channels : (s + 1) * channels]
        visit(l, "project")
        exchange_start(2 * l, send_a, recv_a, l)
        recv_a[l, me] = send_a[l, me]
        visit(l, "sent")
        save(hidden, hidden_o, l)
        gathers["g" + str(l)].arrive()
        spec[0:tokens, 0:width] = dot(hidden[l], win_f[2 * l + 1])
        visit(l, "gate0")

        def open_gate(j):
            r = rows_of(j, 16)
            act, incline = gelu_both(spec[r, 0:width])
            gact[l, r, :] = act.astype(BF)
            gslope[l, r, :] = incline.astype(BF)

        loop(tokens // 16, open_gate)
        visit(l, "gate")
        save(win_f, win_o, 2 * l)
        save(win_f, win_o, 2 * l + 1)
        save(gact, gact_o, l)
        save(gslope, gslope_o, l)
        if l == 0:
            moving["seg"].arrive()
            make_masks(seg_r, masks)
            save(masks, masks_o)
            visit(l, "masks")
            when(jnp.logical_not(own_taps), take_taps)
            loads[1].wait()
            for m in range(layers):
                make_windows(taps_r[m], tap_table, spec, m, wins)
                visit(l, "win" + str(m))
            save(wins, wins_o)
            loads[2].wait()
            loads[3].wait()
        exchange_wait(2 * l, send_a, recv_a, l)
        visit(l, "came")
        spread_blocks(recv_a.at[l], masks, spread)
        spec[:, 0 : 7 * channels] = dot(table[...], spread[...])
        visit(l, "transform")
        fwd_products(spec, wins, l, spec_y, spec_x, channels)
        save(spec_x, spec_o, l)
        visit(l, "prod")
        for j in range(2):
            r = slice(j * (quarter // 2), (j + 1) * (quarter // 2))
            parts = dot(table_t[r, :], spec_y[...])
            for s in range(n):
                send_b[l, s, r, :] = join_blocks(parts, r, masks, s).astype(BF)
            exchange_start(2 * l + 1, send_b, recv_b, l, pl.ds(j * (quarter // 2), quarter // 2))
            if j == 0:
                visit(l, "untr")
        recv_b[l, me] = send_b[l, me]
        visit(l, "returned")
        exchange_wait(2 * l + 1, send_b, recv_b, l)
        visit(l, "back")
        save(recv_b, conv_out_o, l)

        def mix(j):
            r = rows_of(j, 64)
            for s in range(n):
                c = slice(s * channels, (s + 1) * channels)
                gated[l, r, c] = (gact[l, r, c].astype(F32) * recv_b[l, s, r, :].astype(F32)).astype(BF)

        loop(tokens // 64, mix)
        visit(l, "mix")
        gathers["o" + str(l)].arrive()
        save(gated, gated_o, l)
        save(wout_f, wout_o, l)
        middle[l] = stream[l] + dot(gated[l], wout_f[l])
        visit(l, "attach")
        save(middle, middle_o, l)
        norm_all(middle.at[l], hidden_mid.at[l], gains[l, 1:2, :], biases[l, 1:2, :])
        visit(l, "norm")
        gathers["u" + str(l)].arrive()
        save(hidden_mid, hidden_mid_o, l)
        save(wup_f, wup_o, l)
        for h in range(2):
            c = slice(h * half, (h + 1) * half)
            act, incline = gelu_both(dot(hidden_mid[l], wup_f[l, :, c]))
            active[l, :, c] = act.astype(BF)
            slope[l, :, c] = incline.astype(BF)
            visit(l, ("act0", "activate")[h])
            save(active.at[l, :, c], active_o.at[l, :, c])
            save(slope.at[l, :, c], slope_o.at[l, :, c])
        gathers["d" + str(l)].arrive()
        save(wdn_f, wdn_o, l)
        if l + 1 < layers:
            stream[l + 1] = middle[l] + dot(active[l], wdn_f[l])
            save(stream, streams_o, l + 1)
        else:
            moving["tok"].finish()
            tok_s[...] = (middle[l] + dot(active[l], wdn_f[l])).astype(BF)
            save(tok_s, out_o)
        visit(l, "narrow")
    for g in gathers.values():
        g.finish()
    moving["cot"].arrive()
    for name in ("seg", "cot"):
        moving[name].finish()

    when(own_taps, lambda: await_bytes(taps_s, tap_sems.at[0]))
    for copy in saves:
        copy.wait()


def forward(n, stream_in, cotangent, segments, gains, biases, subs, scales, table, table_t, tap_table, win, wout, wup, wdn):
    layers = wup.shape[0]
    tokens, width = stream_in.shape
    channels = width // n
    ff = wup.shape[2] * n
    taps = subs.shape[1]

    def sds(*shape, dtype=BF):
        return jax.ShapeDtypeStruct(shape, dtype)

    wshapes = [(2 * layers, width, width), (layers, width, width), (layers, width, ff), (layers, ff, width)]
    wide, blocks = (layers, tokens, width), (layers, n, tokens, channels)
    outs = [
        sds(tokens, width), sds(*wide, dtype=F32), sds(*wide), sds(*wide), sds(*wide), sds(layers, 2 * tokens, 7 * channels), sds(*blocks), sds(*wide),
        sds(*wide, dtype=F32), sds(*wide), sds(layers, tokens, ff), sds(layers, tokens, ff),
        sds(layers, 4, 2, tokens, channels, dtype=F32), sds(10, tokens, channels), sds(tokens, width),
    ] + [sds(*s) for s in wshapes]
    f32 = lambda *s: pltpu.VMEM(s, F32)
    bf = lambda *s: pltpu.VMEM(s, BF)
    scratch = [
        f32(*wide), bf(*wide), bf(*wide), bf(*wide), bf(*wide), f32(*wide), bf(*wide), bf(layers, tokens, ff), bf(layers, tokens, ff),
        bf(*blocks), bf(*blocks), bf(*blocks), bf(*blocks),
        bf(tokens, 7 * channels), f32(2 * tokens, 7 * channels), bf(layers, 2 * tokens, 7 * channels), bf(2 * tokens, 7 * channels), f32(layers, 4, 2, tokens, channels),
    ] + [bf(*s) for s in wshapes] + [
        bf(10, tokens, channels), bf(tokens, width), bf(tokens, width), bf(tokens // 2, width), f32(tokens, width), bf(tokens, width),
        pltpu.VMEM(segments.shape, segments.dtype), bf(layers, taps, channels), bf(layers, taps, channels),
        bf(2 * tokens, tokens), bf(tokens, 2 * tokens), bf(4, 2 * tokens, taps),
        pltpu.SemaphoreType.DMA((5 * layers, 9)),
        pltpu.SemaphoreType.DMA((2 * layers, 2)),
        pltpu.SemaphoreType.DMA((18 * layers + 3,)),
        pltpu.SemaphoreType.DMA((3, 4)),
        pltpu.SemaphoreType.DMA((2,)),
        pltpu.SemaphoreType.DMA((4,)),
    ]
    return pl.pallas_call(
        functools.partial(forward_kernel, n, layers),
        out_shape=outs,
        in_specs=[VMEM] * 6 + [ANY] * 8,
        out_specs=[ANY] * len(outs),
        scratch_shapes=scratch,
        compiler_params=pltpu.CompilerParams(collective_id=1, has_side_effects=True, vmem_limit_bytes=60 * 2**20),
        name="forward",
    )(stream_in, segments, gains, biases, subs, scales, cotangent, table, table_t, tap_table, win, wout, wup, wdn)


PIECE_DOWN, PIECE_UP, PIECE_OUT, PIECE_IN, PIECE_GATE, PIECE_ROWS = 0, 64, 128, 144, 160, 176


def norm_back(upstream, src, base, gain, out, rounded):
    width = src.shape[1]

    def strip(j, sums):
        r = rows_of(j, 128)
        v = src[r, :]
        centred = v - jnp.mean(v, axis=-1, keepdims=True)
        inverse = lax.rsqrt(jnp.mean(centred * centred, axis=-1, keepdims=True) + EPSILON)
        xhat = centred * inverse
        up = upstream[r, :]
        q = gain * up
        both = q - jnp.mean(q, axis=-1, keepdims=True) - xhat * jnp.mean(q * xhat, axis=-1, keepdims=True)
        got = base[r, :] + both * inverse
        out[r, :] = got
        if rounded is not None:
            rounded[r, :] = got.astype(BF)
        p = up * xhat
        first, second = sums
        for k in range(0, 128, 8):
            first, second = first + p[k : k + 8], second + up[k : k + 8]
        return first, second

    zero = jnp.zeros((8, width), F32)
    return lax.fori_loop(0, src.shape[0] // 128, strip, (zero, zero))


def back_products(spec_x, spec_c, wins, out_g, out_d, channels):
    quarter = wins.shape[2]
    half = out_g.shape[1] // 2

    def strip(j):
        r = rows_of(j, 16)
        s = rows_of(j + quarter // 16, 16)
        cols = [slice(n * channels, (n + 1) * channels) for n in range(7)]
        cols2 = [slice(half + n * channels, half + (n + 1) * channels) for n in range(7)]
        cs = [(spec_c[r, c], spec_c[s, c]) for c in cols]
        for n in range(7):
            re = im = None
            for m in range(4 - n if n < 4 else 1):
                w, x = (wins[m, 0, r, :], wins[m, 1, r, :]), cs[n + m]
                a = w[0] * x[0] + w[1] * x[1]
                b = w[0] * x[1] - w[1] * x[0]
                re, im = (a, b) if re is None else (re + a, im + b)
            out_g[r, cols[n]] = re.astype(BF)
            out_g[r, cols2[n]] = im.astype(BF)
        sign = (1 - 2 * lax.rem(lax.broadcasted_iota(jnp.int32, (16, channels), 0), 2)).astype(F32)
        later = None
        for m in (3, 2, 1, 0):
            pairs = [(n - m, n) for n in range(m, 4)] + ([(n, n) for n in range(4, 7)] if m == 0 else [])
            re = im = None
            for i, n in pairs:
                x, c = (spec_x[r, cols[i]].astype(F32), spec_x[s, cols[i]].astype(F32)), cs[n]
                a = x[0] * c[0] + x[1] * c[1]
                b = x[0] * c[1] - x[1] * c[0]
                re, im = (a, b) if re is None else (re + a, im + b)
            dre, dim = (re, im) if later is None else (re + sign * later[1], im - sign * later[0])
            later = (re, im)
            out_d[r, cols[m]] = dre.astype(BF)
            out_d[r, cols2[m]] = dim.astype(BF)

    loop(quarter // 16, strip)


class Reduce:
    def __init__(self, place, bufs, sems, slot, layer, first, rows, order):
        self.p, self.layer, self.slot, self.sems, self.order = place, layer, slot, sems, order
        self.r = pl.ds(first, rows)
        self.first, self.rows = first, rows
        self.grads, self.r0, self.r1, self.r2, self.res = bufs
        self.spare = self.grads.shape[0] - 1

    def sem(self, k):
        return self.sems.at[self.slot, k]

    def strips(self, body):
        step = next(s for s in (80, 64, 32, 16) if self.rows % s == 0)
        loop(self.rows // step, lambda j: body(pl.ds(pl.multiple_of(self.first + j * step, 16), step)))

    def add_to(self, place_of, others, r):
        total = self.grads[(self.layer, *place_of, r, slice(None))].astype(F32)
        for other in others:
            total += other[r, :].astype(F32)
        return total

    def s0(self):
        send(self.grads.at[self.spare, :, :, :, self.r], self.r0.at[self.layer, :, :, :, self.r], self.sem(0), self.sem(1), self.p.sibling())

    def s1(self):
        p, l = self.p, self.layer
        await_bytes(self.r0.at[l, :, :, :, self.r], self.sem(0))
        await_bytes(self.r0.at[l, :, :, :, self.r], self.sem(1))

        def add(j):
            y, x, q = j // (2 * p.n), lax.rem(j // p.n, 2), lax.rem(j, p.n)

            def strip(r):
                self.grads[l, y, x, q, r, :] = self.add_to((y, x, q), [self.r0.at[l, y, x, q]], r).astype(BF)

            self.strips(strip)

        loop(4 * p.n, add)
        if self.order == "yx":
            send(self.grads.at[l, 1 - p.y, :, :, self.r], self.r1.at[l, pl.ds(0, 2), :, self.r], self.sem(2), self.sem(3), p.mate_y()[1])
        elif self.order == "xy":
            send(self.grads.at[l, :, 1 - p.x, :, self.r], self.r1.at[l, pl.ds(0, 2), :, self.r], self.sem(2), self.sem(3), p.mate_x()[1])
        else:
            send(self.grads.at[l, p.y, 1 - p.x, :, self.r], self.r1.at[l, 0, :, self.r], self.sem(2), self.sem(3), p.mate_x()[1])
            send(self.grads.at[l, 1 - p.y, p.x, :, self.r], self.r1.at[l, 1, :, self.r], self.sem(2), self.sem(3), p.mate_y()[1])
            send(self.grads.at[l, 1 - p.y, 1 - p.x, :, self.r], self.r1.at[l, 2, :, self.r], self.sem(2), self.sem(3), p.mate_xy()[1])

    def s1b(self):
        p, l = self.p, self.layer
        both = self.r1.at[l, pl.ds(0, 2), :, self.r]
        await_bytes(both, self.sem(2))
        await_bytes(both, self.sem(3))

        def add(j):
            k, q = j // p.n, lax.rem(j, p.n)
            y, x = (p.y, k) if self.order == "yx" else (k, p.x)

            def strip(r):
                self.grads[l, y, x, q, r, :] = self.add_to((y, x, q), [self.r1.at[l, k, q]], r).astype(BF)

            self.strips(strip)

        loop(2 * p.n, add)
        if self.order == "yx":
            send(self.grads.at[l, p.y, 1 - p.x, :, self.r], self.r1.at[l, 2, :, self.r], self.sem(4), self.sem(5), p.mate_x()[1])
        else:
            send(self.grads.at[l, 1 - p.y, p.x, :, self.r], self.r1.at[l, 2, :, self.r], self.sem(4), self.sem(5), p.mate_y()[1])

    def s2(self):
        p, l = self.p, self.layer
        if self.order == "direct":
            slots = (0, 1, 2)
            await_bytes(self.r1.at[l, :, :, self.r], self.sem(2))
            await_bytes(self.r1.at[l, :, :, self.r], self.sem(3))
        else:
            slots = (2,)
            await_bytes(self.r1.at[l, 2, :, self.r], self.sem(4))
            await_bytes(self.r1.at[l, 2, :, self.r], self.sem(5))

        def add(q):
            def strip(r):
                self.grads[l, p.y, p.x, q, r, :] = self.add_to((p.y, p.x, q), [self.r1.at[l, k, q] for k in slots], r).astype(BF)

            self.strips(strip)

        loop(p.n, add)
        for k in range(1, p.n):
            q, peer = p.column(k)
            send(self.grads.at[l, p.y, p.x, q, self.r], self.r2.at[l, k - 1, self.r], self.sem(6), self.sem(7), peer)

    def s3(self):
        p, l = self.p, self.layer
        await_bytes(self.r2.at[l, :, self.r], self.sem(6))
        await_bytes(self.r2.at[l, :, self.r], self.sem(7))

        def strip(r):
            total = self.add_to((p.y, p.x, p.q), [self.r2.at[l, k] for k in range(p.n - 1)], r)
            self.res[l, p.i, r, :] = total.astype(BF)

        self.strips(strip)
        piece = self.res.at[l, p.i, self.r]
        if self.order == "direct":
            for mate in (p.mate_x(), p.mate_y(), p.mate_xy()):
                send(piece, piece, self.sem(8), self.sem(9), mate[1])
        else:
            first, second = p.mates(self.order)
            send(piece, piece, self.sem(12), self.sem(13), first[1])
            send(piece, piece, self.sem(8), self.sem(9), second[1])

    def s3b(self):
        p, l = self.p, self.layer
        first, second = p.mates(self.order)
        await_bytes(self.res.at[l, 0, self.r], self.sem(13))
        piece = self.res.at[l, first[0], self.r]
        send(piece, piece, self.sem(8), self.sem(9), second[1])

    def spread(self):
        return self.res.at[self.layer, pl.ds(0, 3 if self.order == "direct" else 2), self.r]

    def s4(self):
        p, l = self.p, self.layer
        await_bytes(self.spread(), self.sem(9))
        for i in (p.i, p.mate_x()[0], p.mate_y()[0], p.mate_xy()[0]):
            piece = self.res.at[l, i, self.r]
            send(piece, piece, self.sem(10), self.sem(11), p.sibling())

    def end(self):
        half = self.res.at[self.layer, pl.ds(0, GROUP // 2), self.r]
        await_bytes(self.spread(), self.sem(8))
        if self.order != "direct":
            await_bytes(self.res.at[self.layer, 0, self.r], self.sem(12))
        await_bytes(half, self.sem(10))
        await_bytes(half, self.sem(11))


def in_order(own, others, l, here, count):
    total = None
    for j in range(count):
        k = lax.rem(here - j + count, count)
        value = jnp.where(k == 0, own.astype(F32), others[l, lax.max(k - 1, 0)].astype(F32))
        total = value if total is None else total + value
    return total


BACKWARD_ORDER = {"d0": "yx", "d1": "yx", "e0": "xy", "e1": "xy", "i0": "direct", "i1": "yx", "j0": "direct", "j1": "xy", "o0": "yx", "o1": "yx", "u0": "yx", "u1": "yx", "v0": "xy", "v1": "xy"}
BACKWARD_PLAN = {
    (1, "middle"): ("d1.s1",),
    (1, "out"): ("v1.s1",),
    (1, "sent"): ("e1.s1", "u1.s1"),
    (1, "transform"): ("o1.s1",),
    (1, "came"): ("d1.s1b",),
    (1, "products"): ("v1.s1b",),
    (1, "in"): ("j1.s1", "e1.s1b"),
    (1, "project"): ("d1.s2",),
    (1, "end"): ("u1.s1b",),
    (0, "down0"): ("i1.s1",),
    (0, "down"): ("d1.s3", "j1.s1b"),
    (0, "activate"): ("o1.s1b",),
    (0, "up0"): ("e0.s1", "d0.s1", "u1.s2"),
    (0, "up"): ("v1.s2",),
    (0, "narrow"): ("o1.s2",),
    (0, "middle"): ("kg1.over_mp", "u0.s1"),
    (0, "open"): ("i1.s1b",),
    (0, "sent"): ("e0.s1b", "d0.s1b", "e1.s2", "o0.s1", "u1.s3"),
    (0, "transform"): ("j1.s2",),
    (0, "arrived"): ("v0.s1",),
    (0, "came"): ("d0.s2",),
    (0, "half"): ("v1.s3", "u0.s1b", "kg1.over_group"),
    (0, "returned"): ("i1.s2",),
    (0, "gatep"): ("o0.s1b", "e0.s2", "v0.s1b"),
    (0, "in"): ("e1.s3", "j0.s1", "u0.s2"),
    (0, "in0"): ("i0.s1", "v0.s2", "kg1.take", "j1.s3", "j0.s2", "u1.s3b", "v1.s3b", "o0.s2", "kg0.over_mp"),
    (0, "project"): ("e1.s3b", "e0.s3", "j1.s3b", "i0.s2", "v0.s3"),
    (0, "end"): ("d0.s3", "o1.s3"),
    (0, "tail"): (
        "e1.s4", "u1.s4", "o0.s3", "v0.s3b", "i1.s3", "j1.s4", "u0.s3", "j0.s3", "norm.over_mp", "d1.s3b",
        "u0.s3b", "v1.s4", "d0.s3b", "i1.s3b", "v0.s4", "d1.s4", "e0.s3b", "i0.s3", "kg0.over_group", "o0.s3b",
        "o1.s3b", "u0.s4", "e0.s4", "o0.s4", "kg0.take", "i0.s4", "i1.s4", "o1.s4", "j0.s4", "d0.s4", "norm.take",
    ),
}


class KernelGrad:
    def __init__(self, place, layer, refs, sems):
        self.p, self.l, self.sems = place, layer, sems
        self.own, self.from_mp, self.mid, self.from_group, self.total, self.result = [r.at[layer] for r in refs]
        self.owner = place.s == place.q

    def sem(self, k):
        return self.sems.at[self.l, k]

    def start(self):
        when(jnp.logical_not(self.owner), lambda: send(self.own, self.from_mp, self.sem(0), self.sem(1), self.p.opposite()))

    def over_mp(self):
        p = self.p

        def add():
            await_bytes(self.from_mp, self.sem(1))
            self.mid[...] = (self.own[...].astype(F32) + self.from_mp[...].astype(F32)).astype(BF)
            for k, mate in enumerate((p.mate_x(), p.mate_y(), p.mate_xy())):
                send(self.mid, self.from_group.at[k], self.sem(2 + k), self.sem(5 + k), mate[1])

        when(self.owner, add)

    def over_group(self):
        p = self.p

        def add():
            for k in range(3):
                await_bytes(self.from_group.at[k], self.sem(5 + k))
            near = self.mid[...].astype(F32) + self.from_group[0].astype(F32)
            far = self.from_group[1].astype(F32) + self.from_group[2].astype(F32)
            both = (near + far).astype(BF)
            self.total[...] = both
            self.result[...] = both
            send(self.total, self.result, self.sem(8), self.sem(9), p.sibling())

        when(self.owner, add)

    def take(self):
        when(jnp.logical_not(self.owner), lambda: await_bytes(self.result, self.sem(9)))

    def finish(self):
        def given():
            for k in range(3):
                await_bytes(self.mid, self.sem(2 + k))
            await_bytes(self.total, self.sem(8))

        when(self.owner, given)
        when(jnp.logical_not(self.owner), lambda: await_bytes(self.own, self.sem(0)))


class NormGrad:
    def __init__(self, place, refs, sems):
        self.p, self.sems = place, sems
        self.own, self.from_group, self.mid, self.from_mp, self.result = refs
        self.layers = self.own.shape[0]

    def start(self, l):
        for k in range(1, GROUP):
            send(self.own.at[l], self.from_group.at[l, k - 1], self.sems.at[l, 0], self.sems.at[l, 1], self.p.member(k))

    def over_mp(self):
        p = self.p
        for l in reversed(range(self.layers)):
            await_bytes(self.from_group.at[l], self.sems.at[l, 0])
            await_bytes(self.from_group.at[l], self.sems.at[l, 1])
            self.mid[l] = in_order(self.own[l], self.from_group, l, p.i, GROUP)
            for k in range(1, p.n):
                send(self.mid.at[l], self.from_mp.at[l, k - 1], self.sems.at[l, 2], self.sems.at[l, 3], p.column(k)[1])

    def take(self):
        for l in reversed(range(self.layers)):
            await_bytes(self.from_mp.at[l], self.sems.at[l, 2])
            await_bytes(self.from_mp.at[l], self.sems.at[l, 3])
            self.result[l] = in_order(self.mid[l], self.from_mp, l, self.p.q, self.p.n)


def backward_kernel(
    n, layers,
    gains, subs, scales, masks_h, table_h, table_t_h, tap_t_h,
    out_in, cot, streams, hiddens, gacts, gslopes, specs, conv_outs, gateds, middles, hidden_mids, actives, slopes,
    wins_h, win_h, wout_h, wup_h, wdn_h,
    out_o, grad_o, res_o, sub_o, norm_o,
    grad, middle_grad, stream, hidden, gact, gslope, spec_x, conv_out, gated, middle, hidden_mid, active, slope, wins, win, wout, wup, wdn,
    grads, r0, r1, r2, res,
    up_grad, out_grad, branch, joined, big_a, big_b, spread,
    send_c, recv_c, send_d, recv_d, kg_s, kg_z, kg_t, kg_y, kg_u, kg_own, sub_s, masks, table, table_t, tap_t,
    norm_s, norm_r, norm_t, norm_u, norm_v, grad_p,
    load_sems, a2a_sems, red_sems, kg_sems, norm_sems, out_sems, move_sems,
):
    place = Place(n)
    me, core = place.s, place.core
    tokens, width = grad.shape
    channels = width // n
    quarter = tokens
    ff = wup.shape[1]
    half = ff // 2
    spare = grads.shape[0] - 1
    loads = {}
    sources = {
        "stream": (streams, stream), "hidden": (hiddens, hidden), "gact": (gacts, gact), "gslope": (gslopes, gslope),
        "spec_x": (specs, spec_x), "conv_out": (conv_outs, conv_out), "gated": (gateds, gated), "middle": (middles, middle),
        "hidden_mid": (hidden_mids, hidden_mid), "active": (actives, active), "slope": (slopes, slope), "wins": (wins_h, wins),
        "in": (win_h, win), "out": (wout_h, wout), "up": (wup_h, wup), "down": (wdn_h, wdn),
        "branch": (cot, branch), "masks": (masks_h, masks), "table": (table_h, table), "table_t": (table_t_h, table_t), "tap_t": (tap_t_h, tap_t),
    }
    once = ("branch", "masks", "table", "table_t", "tap_t")

    def load(name, l):
        src, dst = sources[name]
        copy = pltpu.make_async_copy(src if name in once else src.at[l], dst, load_sems.at[l, len([k for k in loads if k[1] == l])])
        copy.start()
        loads[name, l] = copy

    def ready(*names, l):
        for name in names:
            loads[name, l].wait()

    def next_load(*names, l):
        if l:
            for name in names:
                load(name, l - 1)

    top = layers - 1
    for name in ("branch", "active", "down"):
        load(name, top)
    greet_all(place)
    bufs = (grads, r0, r1, r2, res)
    bounds = (PIECE_DOWN, PIECE_UP // 2, PIECE_UP, (PIECE_UP + PIECE_OUT) // 2, PIECE_OUT, PIECE_IN, PIECE_GATE, PIECE_ROWS)
    groups = {}
    for l in range(layers):
        for k, letter in enumerate("deuvoij"):
            name = letter + str(l)
            order = BACKWARD_ORDER.get(name, "direct")
            groups[name] = Reduce(place, bufs, red_sems, len(groups), l, bounds[k], bounds[k + 1] - bounds[k], order)
    kernel_grads = [KernelGrad(place, l, (kg_s, kg_z, kg_t, kg_y, kg_u, kg_own), kg_sems) for l in range(layers)]
    norm_grads = NormGrad(place, (norm_s, norm_r, norm_t, norm_u, norm_v), norm_sems)
    out_move = Move(place, out_in, out_o, move_sems.at[0])
    grad_move = Move(place, branch, grad_o, move_sems.at[1], grad_p)
    moving = {"norm": norm_grads, **groups}
    moving.update({"kg" + str(l): kernel_grads[l] for l in range(layers)})

    def visit(l, point):
        for step in BACKWARD_PLAN.get((l, point), ()):
            what, action = step.split(".")
            getattr(moving[what], action)()

    def exchange_start(slot, src, dst, rows):
        for k in range(1, n):
            s, peer = place.partner(k)
            send(src.at[s, rows], dst.at[me, rows], a2a_sems.at[slot, 0], a2a_sems.at[slot, 1], peer)

    def exchange_wait(slot, src, dst, l):
        await_bytes(src.at[pl.ds(0, n - 1)], a2a_sems.at[slot, 0])
        await_bytes(dst.at[pl.ds(0, n - 1)], a2a_sems.at[slot, 1])

    def holder(parity, l):
        mine = 1 - (parity - core) * (parity - core)
        return l * mine + spare * (1 - mine)

    out_move.start()
    for name in ("slope", "hidden_mid", "up", "middle", "out", "gated", "gact", "gslope", "conv_out"):
        load(name, top)
    ready("branch", l=top)

    def widen_grad(j):
        r = rows_of(j, 64)
        grad[r, :] = branch[r, :].astype(F32)

    loop(tokens // 64, widen_grad)

    for l in reversed(range(layers)):
        ready("active", l=l)

        def grad_up(c):
            got = dot_tn(hidden_mid[:, rows_of(c, 128)], up_grad[...]).astype(BF)
            for par in range(2):
                for q in range(n):
                    grads[holder(par, l), c // 2, lax.rem(c, 2), q, PIECE_UP:PIECE_OUT, :] = got[par * 64 : par * 64 + 64, q * (ff // n) : (q + 1) * (ff // n)]

        def grad_down(q):
            got = dot_tn(active[:, rows_of(q, ff // n)], branch[...]).astype(BF)
            for i in range(GROUP):
                grads[holder(i % 2, l), i // 4, i // 2 % 2, q, PIECE_DOWN:PIECE_UP, :] = got[i * 64 : (i + 1) * 64]

        def grad_out():
            got = dot_tn(gated[...], out_grad[...]).astype(BF)
            for q in range(n):
                for i in range(GROUP):
                    at = q * channels + i * 16
                    grads[holder(i % 2, l), i // 4, i // 2 % 2, q, PIECE_OUT:PIECE_IN, :] = got[at : at + 16]

        def grad_in(h):
            got = dot_tn(hidden[...], joined[:, h * width : (h + 1) * width]).astype(BF)
            first = (PIECE_IN, PIECE_GATE)[h]
            for i in range(GROUP):
                for q in range(n):
                    for t in range(4):
                        at = i * 64 + t * 16
                        grads[holder(i % 2, l), i // 4, i // 2 % 2, q, first : first + 16, t * 128 : (t + 1) * 128] = got[
                            at : at + 16, q * channels : (q + 1) * channels
                        ]
            groups["ij"[h] + str(l)].s0()

        loop(n // 2, grad_down)
        visit(l, "down0")
        loop(n // 2, lambda q: grad_down(q + n // 2))
        for letter in "de":
            groups[letter + str(l)].s0()
        visit(l, "down")
        ready("down", "slope", l=l)
        for h in range(2):
            c = slice(h * half, (h + 1) * half)
            up_grad[:, c] = (dot_nt(branch[...], wdn[c, :]) * slope[:, c].astype(F32)).astype(BF)
        next_load("down", "slope", l=l)
        if l == top:
            for name in ("spec_x", "wins", "masks", "table", "table_t", "tap_t", "in", "hidden", "stream"):
                load(name, top)
        visit(l, "activate")
        ready("hidden_mid", l=l)
        loop(GROUP // 4, grad_up)
        visit(l, "up0")
        loop(GROUP // 4, lambda c: grad_up(c + GROUP // 4))
        for letter in "uv":
            groups[letter + str(l)].s0()
        next_load("hidden_mid", l=l)
        visit(l, "up")
        ready("up", l=l)
        big_a[...] = dot_nt(up_grad[...], wup[...])
        next_load("up", l=l)
        visit(l, "narrow")
        ready("middle", l=l)
        sums_mid = norm_back(big_a, middle, grad, gains[l, 1:2, :], middle_grad, out_grad)
        next_load("middle", l=l)
        visit(l, "middle")

        ready("gated", l=l)
        grad_out()
        groups["o" + str(l)].s0()
        next_load("gated", l=l)
        visit(l, "out")
        ready("out", l=l)
        big_b[0:tokens, 0:width] = dot_nt(out_grad[...], wout[...])
        next_load("out", l=l)
        visit(l, "open")
        ready("gact", "gslope", "conv_out", l=l)

        def unmix(j):
            r = rows_of(j, 32)
            for s in range(n):
                c = slice(s * channels, (s + 1) * channels)
                up = big_b[r, c]
                send_c[s, r, :] = (up * gact[r, c].astype(F32)).astype(BF)
                joined[r, slice(width + s * channels, width + (s + 1) * channels)] = (
                    up * conv_out[s, r, :].astype(F32) * gslope[r, c].astype(F32)
                ).astype(BF)

        for j in range(2):
            loop(tokens // 64, lambda k: unmix(k + j * (tokens // 64)))
            exchange_start(2 * l, send_c, recv_c, pl.ds(j * (tokens // 2), tokens // 2))
        next_load("gact", "gslope", "conv_out", l=l)
        recv_c[me] = send_c[me]
        visit(l, "sent")
        if l == top:
            ready("masks", "table", l=l)
        visit(l, "transform")
        exchange_wait(2 * l, send_c, recv_c, l)
        visit(l, "arrived")
        spread_blocks(recv_c, masks, spread)
        big_b[:, 0 : 7 * channels] = dot(table[...], spread[...])
        visit(l, "came")
        ready("wins", "spec_x", l=l)
        back_products(spec_x, big_b, wins, active, up_grad, channels)
        next_load("wins", "spec_x", l=l)
        visit(l, "products")
        if l == top:
            ready("table_t", "tap_t", l=l)

        for j in range(2):
            r = slice(j * (quarter // 2), (j + 1) * (quarter // 2))
            parts = dot(table_t[r, 0:quarter], active[:, 0 : 7 * channels])
            parts += dot(table_t[r, quarter : 2 * quarter], active[:, half : half + 7 * channels])
            for s in range(n):
                send_d[s, r, :] = join_blocks(parts, r, masks, s).astype(BF)
            exchange_start(2 * l + 1, send_d, recv_d, pl.ds(j * (quarter // 2), quarter // 2))
            if j == 0:
                visit(l, "half")
        recv_d[me] = send_d[me]
        next_load("active", l=l)

        taps = None
        for m in range(4):
            c = slice(m * channels, (m + 1) * channels)
            d = slice(half + m * channels, half + (m + 1) * channels)
            got = dot(tap_t[m, :, 0:quarter], up_grad[:, c]) + dot(tap_t[m, :, quarter : 2 * quarter], up_grad[:, d])
            taps = got if taps is None else taps + got
        kg_s[l] = taps.astype(BF)
        kernel_grads[l].start()
        visit(l, "returned")
        ready("in", "hidden", "stream", l=l)
        big_a[...] = dot_nt(joined[:, width : 2 * width], win[1])
        visit(l, "gatep")
        grad_in(1)
        visit(l, "in")
        exchange_wait(2 * l + 1, send_d, recv_d, l)

        def collect(j):
            r = rows_of(j, 64)
            for s in range(n):
                joined[r, s * channels : (s + 1) * channels] = recv_d[s, r, :]

        loop(tokens // 64, collect)
        if l == 0:
            grad_in(0)
        visit(l, "in0")
        big_a[...] = big_a[...] + dot_nt(joined[:, 0:width], win[0])
        next_load("in", l=l)
        visit(l, "project")
        sums_in = norm_back(big_a, stream, middle_grad, gains[l, 0:1, :], grad, branch)
        next_load("stream", l=l)
        if l == 0:
            grad_move.start()
        else:
            grad_in(0)
        next_load("hidden", l=l)
        norm_s[l] = jnp.concatenate(
            [jnp.sum(s, axis=0, keepdims=True) for s in (sums_in[0], sums_mid[0], sums_in[1], sums_mid[1])]
            + [jnp.zeros((4, width), F32)],
            axis=0,
        )
        norm_grads.start(l)
        if l == 0:
            grad_move.pass_on()
        visit(l, "end")

    visit(0, "tail")
    out_norm = pltpu.make_async_copy(norm_v, norm_o, out_sems.at[1])
    out_norm.start()
    for l in range(layers):
        raw, inverse = normal_taps(subs, scales, l)
        k = raw * inverse
        own = kg_own[l].astype(F32)
        along = jnp.sum(own * k, axis=0, keepdims=True)
        sub_s[l] = scales[0] * (own - scales[1] * k * along) * inverse
    out_sub = pltpu.make_async_copy(sub_s, sub_o, out_sems.at[0])
    out_sub.start()
    for group in groups.values():
        group.end()
    out_res = pltpu.make_async_copy(res, res_o, out_sems.at[2])
    out_res.start()
    for m in (out_move, grad_move):
        m.arrive()
        m.finish()
    for g in kernel_grads:
        g.finish()
    out_sub.wait()
    out_norm.wait()
    out_res.wait()


def backward(n, gains, subs, scales, masks, table, table_t, tap_t, out, cot, kept):
    layers, tokens, width = kept[0].shape
    channels = width // n
    ff = kept[-1].shape[1]
    taps = subs.shape[1]

    def sds(*shape, dtype=F32):
        return jax.ShapeDtypeStruct(shape, dtype)

    outs = [
        sds(tokens, width, dtype=BF), sds(tokens, width, dtype=BF), sds(layers, GROUP, PIECE_ROWS, width, dtype=BF),
        sds(layers, taps, channels), sds(layers, 8, width),
    ]
    f32 = lambda *s: pltpu.VMEM(s, F32)
    bf = lambda *s: pltpu.VMEM(s, BF)
    wide, blocks, small = (tokens, width), (n, tokens, channels), (layers, taps, channels)
    scratch = [
        f32(*wide), f32(*wide), f32(*wide), bf(*wide), bf(*wide), bf(*wide), bf(2 * tokens, 7 * channels), bf(*blocks), bf(*wide), f32(*wide), bf(*wide),
        bf(tokens, ff), bf(tokens, ff), f32(4, 2, tokens, channels),
        bf(2, width, width), bf(width, width), bf(width, ff), bf(ff, width),
        bf(layers + 1, 2, 2, n, PIECE_ROWS, width),
        bf(layers, 2, 2, n, PIECE_ROWS, width),
        bf(layers, 3, n, PIECE_ROWS, width),
        bf(layers, n - 1, PIECE_ROWS, width),
        bf(layers, GROUP, PIECE_ROWS, width),
        bf(tokens, ff), bf(*wide), bf(*wide), bf(tokens, 2 * width),
        f32(*wide), f32(2 * tokens, 7 * channels), bf(tokens, 7 * channels),
        bf(*blocks), bf(*blocks), bf(*blocks), bf(*blocks),
        bf(*small), bf(*small), bf(*small), bf(layers, 3, taps, channels), bf(*small), bf(*small), f32(*small),
        bf(10, tokens, channels), bf(2 * tokens, tokens), bf(tokens, 2 * tokens), bf(4, taps, 2 * tokens),
        f32(layers, 8, width), f32(layers, GROUP - 1, 8, width), f32(layers, 8, width), f32(layers, n - 1, 8, width), f32(layers, 8, width), bf(tokens // 2, width),
        pltpu.SemaphoreType.DMA((layers, 21)),
        pltpu.SemaphoreType.DMA((2 * layers, 2)),
        pltpu.SemaphoreType.DMA((7 * layers, 14)),
        pltpu.SemaphoreType.DMA((layers, 10)),
        pltpu.SemaphoreType.DMA((layers, 4)),
        pltpu.SemaphoreType.DMA((3,)),
        pltpu.SemaphoreType.DMA((2, 4)),
    ]
    return pl.pallas_call(
        functools.partial(backward_kernel, n, layers),
        out_shape=outs,
        in_specs=[VMEM] * 3 + [ANY] * (6 + len(kept)),
        out_specs=[ANY] * len(outs),
        scratch_shapes=scratch,
        compiler_params=pltpu.CompilerParams(collective_id=2, has_side_effects=True, vmem_limit_bytes=int(63.5 * 2**20)),
        name="backward",
    )(gains, subs, scales, masks, table, table_t, tap_t, out, cot, *kept)


def finish_kernel(out_i, grad_i, res, norms, sub_i, out, grad, up, down, out_w, in_w, vectors, sub):
    out[...] = out_i[...].astype(F32)
    grad[...] = grad_i[...].astype(F32)
    members = res.shape[1]
    for i in range(members):
        up[0, i * 64 : (i + 1) * 64, :] = res[0, i, PIECE_UP:PIECE_OUT, :].astype(F32)
        down[0, i * 64 : (i + 1) * 64, :] = res[0, i, PIECE_DOWN:PIECE_UP, :].astype(F32)
        out_w[0, i * 16 : (i + 1) * 16, :] = res[0, i, PIECE_OUT:PIECE_IN, :].astype(F32)
        for h, first in enumerate((PIECE_IN, PIECE_GATE)):
            for t in range(4):
                c = t * 128
                in_w[0, i * 64 + t * 16 : i * 64 + (t + 1) * 16, h, :] = res[0, i, first : first + 16, c : c + 128].astype(F32)
    vectors[...] = norms[...]
    sub[...] = sub_i[...]


def finish(out, grad, res, norms, sub):
    layers, members, _, width = res.shape
    tokens = out.shape[0]
    channels = sub.shape[2]
    parts = 1
    m = members // parts
    steps = layers * parts
    rows = tokens // steps

    def sds(*shape):
        return jax.ShapeDtypeStruct(shape, F32)

    def whole(a):
        return pl.BlockSpec(a.shape, lambda j: (0,) * len(a.shape))

    flat = pl.BlockSpec((rows, width), lambda j: (j, 0))

    def mid(*shape):
        return pl.BlockSpec((1, *shape, width), lambda j: (j // parts, j % parts, 0))

    vectors = sds(*norms.shape)
    return pl.pallas_call(
        finish_kernel,
        grid=(steps,),
        out_shape=[
            sds(tokens, width), sds(tokens, width), sds(layers, members * 64, width), sds(layers, members * 64, width),
            sds(layers, members * 16, width), sds(layers, members * 64, 2, channels), vectors, sds(*sub.shape),
        ],
        in_specs=[
            flat, flat, pl.BlockSpec((1, m, PIECE_ROWS, width), lambda j: (j // parts, j % parts, 0, 0)), whole(norms), whole(sub),
        ],
        out_specs=[
            flat, flat, mid(m * 64), mid(m * 64), mid(m * 16),
            pl.BlockSpec((1, m * 64, 2, channels), lambda j: (j // parts, j % parts, 0, 0)), whole(vectors), whole(sub),
        ],
        compiler_params=pltpu.CompilerParams(vmem_limit_bytes=48 * 2**20),
        name="finish",
    )(out, grad, res, norms, sub)


def per_device(
    stream_in, segments, norm_gain, norm_bias, w_in, w_out, sub_kernels, w_up, w_down, cotangent
):
    layers, scales, taps, channels = sub_kernels.shape
    n = lax.axis_size("mp")
    quarter = segments.shape[1] // 4
    table = transform_table(quarter)
    tap_table = tap_tables(quarter, scales, taps) / quarter

    def const(a):
        return jnp.asarray(a, F32).astype(BF)

    factors = jnp.asarray(tap_scales(scales, taps, channels))
    subs = sub_kernels.reshape(layers, -1, channels)
    out, *kept, masks, cot, win, wout, wup, wdn = forward(
        n, stream_in, cotangent, segments, norm_gain, norm_bias, subs, factors, const(table), const(table.T), const(tap_table),
        w_in.transpose(0, 2, 1, 3).reshape(2 * layers, -1, channels), w_out, w_up, w_down,
    )
    out, grad, res, sub, norms = backward(
        n, norm_gain, subs, factors, masks, const(table), const(table.T), const(tap_table.transpose(0, 2, 1)),
        out, cot, (*kept, win.reshape(layers, 2, *win.shape[1:]), wout, wup, wdn),
    )
    if lax.axis_size("dp") > GROUP:
        res, sub, norms = [v * (1.0 / GROUP) for v in lax.psum((res.astype(F32), sub, norms), "dp")]
        res = res.astype(BF)
    out, grad, up, down, out_w, in_w, norms, sub = finish(out, grad, res, norms, sub)
    return out, grad, norms[:, 0:2], norms[:, 2:4], in_w, out_w, sub.reshape(sub_kernels.shape), up, down


def solution(mesh):
    rows = P(("dp", "mp"), None)
    last = P(None, None, None, "mp")
    mid = P(None, "mp", None)
    return jax.shard_map(
        per_device,
        mesh=mesh,
        in_specs=(rows, P("dp", None), P(), P(), last, mid, last, P(None, None, "mp"), mid, rows),
        out_specs=(rows, rows, P(), P(), last, mid, last, P(None, None, "mp"), mid),
        check_vma=False,
    )
```
